128 devices in a mesh: fsdp: 2 (over x_hi), ctx: 64 (over x_lo, y, z, core).
Axes of the slice: x: 4 (x_hi: 2, x_lo: 2; x = x_hi * 2 + x_lo), y: 4, z: 4, core: 2. Of those that a mesh axis runs over, the one named last changes fastest.
Arguments:
- inputs: bfloat16 [2, 8192, 960], P('fsdp', 'ctx'), may hold values from -6 to 6
- cotangent: bfloat16 [2, 8192, 960], P('fsdp', 'ctx'), may hold values from -6 to 6
- positions: int32 [2, 8192], P('fsdp', 'ctx'), may hold values from 0 to 16382, as said below
- pair_index: int32 [2, 64], P('fsdp', 'ctx'), may hold values from 0 to 63, as said below
- input_projection: bfloat16 [960, 1600], P('ctx', 'fsdp'), may hold values from -0.1875 to 0.1875
- project_out: bfloat16 [960, 960], P('ctx', 'fsdp'), may hold values from -0.75 to 0.75
- gate_up: bfloat16 [960, 2, 2560], P('ctx', None, 'fsdp'), may hold values from -0.1875 to 0.1875
- down_weight: bfloat16 [960, 2560], P('ctx', 'fsdp'), may hold values from -0.125 to 0.125
- norm_gains: bfloat16 [960, 2], P('ctx', 'fsdp'), may hold values from 0.25 to 1.75
Outputs:
- layer_out: bfloat16 [2, 8192, 960], P('fsdp', 'ctx')
- input_grad: bfloat16 [2, 8192, 960], P('fsdp', 'ctx')
- grad_project_in: float32 [960, 1600], P('ctx', 'fsdp')
- grad_project_out: float32 [960, 960], P('ctx', 'fsdp')
- grad_gate_up: float32 [960, 2, 2560], P('ctx', None, 'fsdp')
- grad_down: float32 [960, 2560], P('ctx', 'fsdp')
- grad_gains: float32 [960, 2], P('ctx', 'fsdp')
The draws below stay inside these ranges and needn't reach their ends.
Inputs may be any that keep to these rules, and one draw needn't show every extreme that they name: Each row is a permutation of 0 to 64 - 1; device c of a sequence holds block pair_index and block 2 * 64 - 1 - pair_index, each of 64 tokens in order. Taken in the causal order that pair_index gives, a sequence's positions start at 0, rise by 1 to 3 from token to token and end at 16382.
All inputs are finite; a program needn't handle non-finite values.
Results may differ from the reference program's by a relative error of at most 0.029.
Values may be sent and summed in bfloat16 or wider, within the bound.
A program may use at most 192 MiB of HBM per device.

```python
import math
import jax
import jax.numpy as jnp
from jax import lax

MODEL_WIDTH = 960
QUERY_HEADS = 15
KEY_VALUE_HEADS = 5
HEAD_SIZE = 64
FF = 2560
TOK_DEV = 128
KEY_BLOCK_ROWS = 512
SEQS = 2
SEQ = 8192
N_CTX = 64


def layout_pairs(key):
    seeds = jax.random.split(key, SEQS)
    return jnp.stack([jax.random.permutation(seeds[index], N_CTX) for index in range(SEQS)]).astype(jnp.int32)


def draw_pair_index(key, part):
    chosen = layout_pairs(key)
    return chosen


def draw_positions(key, part):
    chosen = layout_pairs(key)
    key = jax.random.fold_in(key, 5)
    stride_draw = jax.random.randint(key, (SEQS, SEQ // 2 - 1), 1, 4).astype(jnp.int32)
    paired = jnp.stack([stride_draw, 4 - stride_draw], axis=2).reshape(SEQS, SEQ - 2)
    between = jnp.concatenate([paired, jnp.full((SEQS, 1), 2, jnp.int32)], axis=1)
    natural = jnp.concatenate([jnp.zeros((SEQS, 1), jnp.int32), jnp.cumsum(between, axis=1).astype(jnp.int32)], axis=1)
    row_ids = jnp.arange(SEQ, dtype=jnp.int32)
    half_block = TOK_DEV // 2
    device = row_ids // TOK_DEV
    within = row_ids % TOK_DEV
    picked = chosen[:, device]
    blocks = jnp.where((within // half_block)[None, :] == 0, picked, 2 * N_CTX - 1 - picked)
    order_ids = (blocks * half_block + (within % half_block)[None, :]).astype(jnp.int32)
    return jnp.take_along_axis(natural, order_ids, axis=1).astype(jnp.int32)


def shard_levels(rng, shape, shards, low, largest):
    loudness = 1.0
    for dim, blocks in shards:
        draws = jax.random.uniform(jax.random.fold_in(jax.random.fold_in(rng, 6), dim), (blocks,), jnp.float32, low / len(shards), largest / len(shards))
        loudness = loudness * jnp.repeat(jnp.exp(draws), shape[dim] // blocks).reshape((-1,) + (1,) * (len(shape) - 1 - dim))
    return loudness


def bell_draw(own_key, extent, scale, most, cuts=(), kind=jnp.bfloat16):
    values = scale * jax.random.normal(own_key, extent, jnp.float32)
    if cuts:
        values = values * shard_levels(own_key, extent, cuts, -0.22, 0.18)
    return jnp.clip(values, -most, most).astype(kind)


def setup_inputs(seed: int = 0) -> dict:
    key_of = jax.random.split(jax.random.key(seed), 10)
    return {
        "inputs": bell_draw(key_of[0], (SEQS, SEQ, MODEL_WIDTH), 1.0, 6.0, ((0, 2), (1, 64))),
        "cotangent": bell_draw(key_of[1], (SEQS, SEQ, MODEL_WIDTH), 1.0, 6.0, ((0, 2), (1, 64))),
        "positions": draw_positions(jax.random.fold_in(key_of[9], 71), 0),
        "pair_index": draw_pair_index(jax.random.fold_in(key_of[9], 71), 0),
        "input_projection": bell_draw(key_of[4], (MODEL_WIDTH, (QUERY_HEADS + 2 * KEY_VALUE_HEADS) * HEAD_SIZE), MODEL_WIDTH ** -0.5, 0.1875, ((0, 64), (1, 2))),
        "project_out": bell_draw(key_of[5], (MODEL_WIDTH, QUERY_HEADS * HEAD_SIZE), HEAD_SIZE ** -0.5, 0.75, ((0, 64), (1, 2))),
        "gate_up": bell_draw(key_of[6], (MODEL_WIDTH, 2, FF), MODEL_WIDTH ** -0.5, 0.1875, ((0, 64), (2, 2))),
        "down_weight": bell_draw(key_of[7], (MODEL_WIDTH, FF), FF ** -0.5, 0.125, ((0, 64), (1, 2))),
        "norm_gains": jnp.clip(1.0 + 0.15 * jax.random.normal(key_of[8], (MODEL_WIDTH, 2), jnp.float32), 0.25, 1.75).astype(jnp.bfloat16),
    }


HIGHEST = lax.Precision.HIGHEST
EPSILON = 1e-05

@jax.custom_vjp
def reduced_copy(v):
    return lax.optimization_barrier(v.astype(jnp.bfloat16)).astype(jnp.float32)

@jax.custom_vjp
def low_back(v):
    return v

def low_keep(v):
    return (reduced_copy(v), None)

def low_pass(kept, grad):
    return (grad,)

def back_keep(v):
    return (v, None)

def back_low(kept, grad):
    return (reduced_copy(grad),)
reduced_copy.defvjp(low_keep, low_pass)
low_back.defvjp(back_keep, back_low)

def order_index(pairs):
    row_ids = jnp.arange(SEQ, dtype=jnp.int32)
    half_block = TOK_DEV // 2
    device = row_ids // TOK_DEV
    within = row_ids % TOK_DEV
    picked = pairs[:, device]
    blocks = jnp.where((within // half_block)[None, :] == 0, picked, 2 * N_CTX - 1 - picked)
    return (blocks * half_block + (within % half_block)[None, :]).astype(jnp.int32)

def rotate(tensor, cosine_table, sine_table):
    middle = tensor.shape[-1] // 2
    first = tensor[..., :middle]
    second = tensor[..., middle:]
    return jnp.concatenate([first * cosine_table - second * sine_table, second * cosine_table + first * sine_table], axis=-1)

def rms_scale(value_rows, gain):
    return value_rows * lax.rsqrt(lax.optimization_barrier(jnp.mean(value_rows * value_rows, axis=-1, keepdims=True)) + EPSILON) * gain

def attend(query_rows, key_rows, value_rows, query_order, key_order):
    scores = jnp.einsum('thgd,khd->hgtk', query_rows, key_rows, precision=HIGHEST) * (1.0 / math.sqrt(HEAD_SIZE))
    scores = low_back(scores)
    visible = key_order[None, :] <= query_order[:, None]
    scores = jnp.where(visible, scores, -1e+30)
    highest = lax.optimization_barrier(jnp.max(scores, axis=-1, keepdims=True))
    weights = jnp.exp(scores - highest)
    totals = lax.optimization_barrier(jnp.sum(weights, axis=-1, keepdims=True))
    attention_output = low_back(jnp.einsum('hgtk,khd->thgd', reduced_copy(weights), value_rows, precision=HIGHEST))
    return attention_output / jnp.transpose(totals, (2, 0, 1, 3))

def layer(start, input_projection, project_out, gate_up, down_weight, norm_gains, cosine_table, sine_table, ordering_row):
    sequence_length = start.shape[0]
    query_groups = QUERY_HEADS // KEY_VALUE_HEADS
    query_width = QUERY_HEADS * HEAD_SIZE
    key_width = KEY_VALUE_HEADS * HEAD_SIZE
    normed = reduced_copy(rms_scale(start, norm_gains[:, 0]))
    projected_rows = low_back(jnp.dot(normed, input_projection, precision=HIGHEST))
    query_rows = projected_rows[:, :query_width].reshape(sequence_length, KEY_VALUE_HEADS, query_groups, HEAD_SIZE)
    key_rows = projected_rows[:, query_width:query_width + key_width].reshape(sequence_length, KEY_VALUE_HEADS, HEAD_SIZE)
    value_rows = reduced_copy(projected_rows[:, query_width + key_width:].reshape(sequence_length, KEY_VALUE_HEADS, HEAD_SIZE))
    query_rows = reduced_copy(rotate(query_rows, cosine_table[:, :, None, :], sine_table[:, :, None, :]))
    key_rows = reduced_copy(rotate(key_rows, cosine_table, sine_table))
    block_count = sequence_length // KEY_BLOCK_ROWS

    def single_block(pieces):
        return attend(pieces[0], key_rows, value_rows, pieces[1], ordering_row)
    attention_output = lax.map(jax.checkpoint(single_block), (query_rows.reshape(block_count, KEY_BLOCK_ROWS, KEY_VALUE_HEADS, query_groups, HEAD_SIZE), ordering_row.reshape(block_count, KEY_BLOCK_ROWS)))
    attention_output = attention_output.reshape(sequence_length, query_width)
    branch = low_back(jnp.dot(reduced_copy(attention_output), project_out.T, precision=HIGHEST))
    resid = start + branch
    normed_two = reduced_copy(rms_scale(resid, norm_gains[:, 1]))
    gate_vals = low_back(jnp.einsum('td,dcf->tcf', normed_two, gate_up, precision=HIGHEST))
    hidden = reduced_copy(jax.nn.silu(gate_vals[:, 0]) * gate_vals[:, 1])
    return resid + low_back(jnp.dot(hidden, down_weight.T, precision=HIGHEST))

def reference(inputs, cotangent, positions, pair_index, input_projection, project_out, gate_up, down_weight, norm_gains):
    weight_a = input_projection.astype(jnp.float32)
    weight_b = project_out.astype(jnp.float32)
    weight_c = gate_up.astype(jnp.float32)
    weight_d = down_weight.astype(jnp.float32)
    weight_e = norm_gains.astype(jnp.float32)
    orders = order_index(pair_index)
    freqs = jnp.exp(-math.log(10000.0) * jnp.arange(HEAD_SIZE // 2, dtype=jnp.float32) * 2.0 / HEAD_SIZE)

    def one_sequence(sums, pieces):
        start, upstream, place, ordering_row = pieces
        angle = place.astype(jnp.float32)[:, None] * freqs[None, :]
        cosine_table = jnp.cos(angle)[:, None, :]
        sine_table = jnp.sin(angle)[:, None, :]

        def forward(value_rows, first, second, third, fourth, fifth):
            return layer(value_rows, first, second, third, fourth, fifth, cosine_table, sine_table, ordering_row)
        result, pull = jax.vjp(forward, start.astype(jnp.float32), weight_a, weight_b, weight_c, weight_d, weight_e)
        grads = pull(upstream.astype(jnp.float32))
        sums = (sums[0] + grads[1], sums[1] + grads[2], sums[2] + grads[3], sums[3] + grads[4], sums[4] + grads[5])
        return (sums, (result.astype(jnp.bfloat16), grads[0].astype(jnp.bfloat16)))
    zero_fill = (jnp.zeros_like(weight_a), jnp.zeros_like(weight_b), jnp.zeros_like(weight_c), jnp.zeros_like(weight_d), jnp.zeros_like(weight_e))
    sums, (results, input_grads) = lax.scan(one_sequence, zero_fill, (inputs, cotangent, positions, orders))
    return (results, input_grads, sums[0], sums[1], sums[2], sums[3], sums[4])
```

```python
import math

import jax
import jax.numpy as jnp
import numpy as np
from jax import lax
from jax.experimental import pallas as pl
from jax.experimental.pallas import tpu as pltpu
from jax.sharding import PartitionSpec as P

WIDTH = 960
QUERY_HEADS = 15
KEY_VALUE_HEADS = 5
GROUP = 3
HEAD_SIZE = 64
FF_HALF = 1280
EPSILON = 1e-05
ROWS = 16
PADDED = 1024
IN_HALF = 800
IN_PAD = 896
OUT_HALF = 480
OUT_PAD = 512
IN_COLS = 2 * IN_PAD
ATT_COLS = IN_COLS + 2 * OUT_PAD
BLOB = ATT_COLS + 3 * FF_HALF
TILE = 512
QROWS = 384
MESH = pl.DeviceIdType.MESH
VMEM_LIMIT = 56 * 1024 * 1024


def slot_to_ctx():
    table = []
    for core in range(2):
        for p2 in range(4):
            for p1 in range(4):
                for x in range(2):
                    y, z = (p1, p2) if core == 0 else (p2, p1)
                    table.append(((x * 4 + y) * 4 + z) * 2 + core)
    return np.array(table, np.int32)


SLOT_CTX = slot_to_ctx()


def column_map():
    cols = np.full((64, ROWS), -1, np.int32)
    cols[:, :15] = SLOT_CTX[:, None] * 15 + np.arange(15)[None, :]
    return cols.reshape(-1)


COLUMN_MAP = column_map()


def coordinates():
    index = lax.axis_index("ctx")
    core = index % 2
    z = (index // 2) % 4
    y = (index // 8) % 4
    x = index // 32
    p1 = y * (1 - core) + z * core
    p2 = z * (1 - core) + y * core
    return x, p1, p2, core


def device_at(x, p1, p2, core):
    y = p1 * (1 - core) + p2 * core
    z = p2 * (1 - core) + p1 * core
    return ((x * 4 + y) * 4 + z) * 2 + core


def neighbours(x, p1, p2, core):
    index = lax.axis_index("ctx")
    return (
        device_at(1 - x, p1, p2, core),
        device_at(x, (p1 + 1) % 4, p2, core),
        device_at(x, (p1 + 3) % 4, p2, core),
        device_at(x, p1, (p2 + 1) % 4, core),
        device_at(x, p1, (p2 + 3) % 4, core),
        index + 1 - 2 * core,
    )


def greet(devices):
    barrier = pltpu.get_barrier_semaphore()
    for device in devices:
        pl.semaphore_signal(barrier, inc=1, device_id={"ctx": device}, device_id_type=MESH)
    pl.semaphore_wait(barrier, len(devices))


def gather_kernel(in_ref, out_ref, local_sem, send_sem, recv_sem):
    x, p1, p2, core = coordinates()
    across, right1, left1, right2, left2, sibling = neighbours(x, p1, p2, core)
    greet((across, right1, left1, right2, left2, sibling))
    p1p, p1m = (p1 + 1) % 4, (p1 + 3) % 4
    p2p, p2m, p2o = (p2 + 1) % 4, (p2 + 3) % 4, (p2 + 2) % 4
    sent = []

    def send(place, to, source=None):
        number = len(sent)
        copy = pltpu.make_async_remote_copy(
            src_ref=place if source is None else source,
            dst_ref=place,
            send_sem=send_sem.at[number],
            recv_sem=recv_sem.at[number],
            device_id={"ctx": to},
            device_id_type=MESH,
        )
        copy.start()
        sent.append(copy)
        return copy

    mine = out_ref.at[core, p2, p1, x]
    local = pltpu.make_async_copy(in_ref, mine, local_sem)
    local.start()
    first = send(mine, across, in_ref)
    local.wait()
    first.wait_recv()
    pair = out_ref.at[core, p2, p1]
    from_left = send(pair, right1)
    from_right = send(pair, left1)
    from_left.wait_recv()
    far_a = send(out_ref.at[core, p2, p1m, 0], right1)
    from_right.wait_recv()
    far_b = send(out_ref.at[core, p2, p1p, 1], left1)
    far_a.wait_recv()
    far_b.wait_recv()
    low = pl.ds(0, 2)
    high = pl.ds(2, 2)
    right_low = send(out_ref.at[core, p2, low], right2)
    left_high = send(out_ref.at[core, p2, high], left2)
    right_high = send(out_ref.at[core, p2, high], right2)
    left_low = send(out_ref.at[core, p2, low], left2)
    last = [send(out_ref.at[core, p2], sibling)]
    right_low.wait_recv()
    far_low = send(out_ref.at[core, p2m, low], right2)
    left_high.wait_recv()
    far_high = send(out_ref.at[core, p2p, high], left2)
    last.append(send(out_ref.at[core, p2m, low], sibling))
    last.append(send(out_ref.at[core, p2p, high], sibling))
    right_high.wait_recv()
    last.append(send(out_ref.at[core, p2m, high], sibling))
    left_low.wait_recv()
    last.append(send(out_ref.at[core, p2p, low], sibling))
    far_low.wait_recv()
    last.append(send(out_ref.at[core, p2o, low], sibling))
    far_high.wait_recv()
    last.append(send(out_ref.at[core, p2o, high], sibling))
    for copy in last:
        copy.wait_recv()
    for copy in sent:
        copy.wait_send()


def gather_blocks(block, collective_id):
    rows, columns = block.shape
    return pl.pallas_call(
        gather_kernel,
        out_shape=jax.ShapeDtypeStruct((2, 4, 4, 2, rows, columns), block.dtype),
        in_specs=[pl.BlockSpec(memory_space=pl.ANY)],
        out_specs=pl.BlockSpec(memory_space=pl.ANY),
        scratch_shapes=[
            pltpu.SemaphoreType.DMA,
            pltpu.SemaphoreType.DMA((18,)),
            pltpu.SemaphoreType.DMA((18,)),
        ],
        compiler_params=pltpu.CompilerParams(
            collective_id=collective_id, has_side_effects=True
        ),
    )(block)


def scatter_kernel(
    g_ref,
    out_ref,
    acc,
    other,
    far_low,
    far_high,
    near_left,
    near_right,
    pair_low,
    pair_high,
    pair_left,
    pair_right,
    last,
    local_sem,
    send_sem,
    recv_sem,
):
    x, p1, p2, core = coordinates()
    across, right1, left1, right2, left2, sibling = neighbours(x, p1, p2, core)
    greet((across, right1, left1, right2, left2, sibling))
    p1p, p1m, p1o = (p1 + 1) % 4, (p1 + 3) % 4, (p1 + 2) % 4
    p2p, p2m, p2o = (p2 + 1) % 4, (p2 + 3) % 4, (p2 + 2) % 4
    sent = []

    def send(source, place, to):
        number = len(sent)
        copy = pltpu.make_async_remote_copy(
            src_ref=source,
            dst_ref=place,
            send_sem=send_sem.at[number],
            recv_sem=recv_sem.at[number],
            device_id={"ctx": to},
            device_id_type=MESH,
        )
        copy.start()
        sent.append(copy)
        return copy

    def add(place, term, blocks):
        @pl.loop(0, blocks)
        def _(step):
            place[step // 2, step % 2] = place[step // 2, step % 2] + term[step // 2, step % 2]

    needed = (p2o, p2m, p2p, p2)
    theirs = (p1o, p1m, p1p, p1)
    crossing = [
        send(g_ref.at[1 - core, theirs[k]], other.at[theirs[k]], sibling) for k in range(4)
    ]
    own = []
    for k in range(4):
        copy = pltpu.make_async_copy(
            g_ref.at[core, needed[k]], acc.at[needed[k]], local_sem.at[k]
        )
        copy.start()
        own.append(copy)

    def merge(k):
        own[k].wait()
        crossing[k].wait_recv()
        add(acc.at[needed[k]], other.at[needed[k]], 8)

    low = pl.ds(0, 2)
    high = pl.ds(2, 2)
    merge(0)
    got_low = send(acc.at[p2o, low], far_low, right2)
    got_high = send(acc.at[p2o, high], far_high, left2)
    merge(1)
    right_low = send(acc.at[p2m, low], near_right.at[low], left2)
    merge(2)
    left_high = send(acc.at[p2p, high], near_left.at[high], right2)
    got_low.wait_recv()
    add(acc.at[p2p, low], far_low, 4)
    left_low = send(acc.at[p2p, low], near_left.at[low], right2)
    got_high.wait_recv()
    add(acc.at[p2m, high], far_high, 4)
    right_high = send(acc.at[p2m, high], near_right.at[high], left2)
    merge(3)
    right_low.wait_recv()
    left_high.wait_recv()
    left_low.wait_recv()
    right_high.wait_recv()

    @pl.loop(0, 8)
    def _(step):
        i, j = step // 2, step % 2
        total = acc[p2, i, j].astype(jnp.float32) + near_left[i, j].astype(jnp.float32)
        total = total + near_right[i, j].astype(jnp.float32)
        acc[p2, i, j] = total.astype(acc.dtype)

    got_low = send(acc.at[p2, p1o, 0], pair_low, right1)
    got_high = send(acc.at[p2, p1o, 1], pair_high, left1)
    right_low = send(acc.at[p2, p1m, 0], pair_right.at[0], left1)
    left_high = send(acc.at[p2, p1p, 1], pair_left.at[1], right1)
    got_low.wait_recv()
    acc[p2, p1p, 0] = acc[p2, p1p, 0] + pair_low[...]
    left_low = send(acc.at[p2, p1p, 0], pair_left.at[0], right1)
    got_high.wait_recv()
    acc[p2, p1m, 1] = acc[p2, p1m, 1] + pair_high[...]
    right_high = send(acc.at[p2, p1m, 1], pair_right.at[1], left1)
    right_low.wait_recv()
    left_high.wait_recv()
    left_low.wait_recv()
    right_high.wait_recv()

    @pl.loop(0, 2)
    def _(j):
        total = acc[p2, p1, j].astype(jnp.float32) + pair_left[j].astype(jnp.float32)
        total = total + pair_right[j].astype(jnp.float32)
        acc[p2, p1, j] = total.astype(acc.dtype)

    final = send(acc.at[p2, p1, 1 - x], last, across)
    final.wait_recv()
    out_ref[...] = acc[p2, p1, x].astype(jnp.float32) + last[...].astype(jnp.float32)
    for copy in sent:
        copy.wait_send()


def scatter_blocks(blocks, collective_id):
    rows, columns = blocks.shape[-2:]
    kind = blocks.dtype
    block = (rows, columns)
    return pl.pallas_call(
        scatter_kernel,
        out_shape=jax.ShapeDtypeStruct(block, jnp.float32),
        in_specs=[pl.BlockSpec(memory_space=pl.ANY)],
        out_specs=pl.BlockSpec(memory_space=pltpu.VMEM),
        scratch_shapes=[
            pltpu.VMEM((4, 4, 2) + block, kind),
            pltpu.VMEM((4, 4, 2) + block, kind),
            pltpu.VMEM((2, 2) + block, kind),
            pltpu.VMEM((2, 2) + block, kind),
            pltpu.VMEM((4, 2) + block, kind),
            pltpu.VMEM((4, 2) + block, kind),
            pltpu.VMEM(block, kind),
            pltpu.VMEM(block, kind),
            pltpu.VMEM((2,) + block, kind),
            pltpu.VMEM((2,) + block, kind),
            pltpu.VMEM(block, kind),
            pltpu.SemaphoreType.DMA((4,)),
            pltpu.SemaphoreType.DMA((17,)),
            pltpu.SemaphoreType.DMA((17,)),
        ],
        compiler_params=pltpu.CompilerParams(
            collective_id=collective_id, has_side_effects=True, vmem_limit_bytes=VMEM_LIMIT
        ),
    )(blocks)


LAST = (((1,), (1,)), ((), ()))
FIRST = (((0,), (0,)), ((), ()))
PLAIN = (((1,), (0,)), ((), ()))


def dot(a, b, dims=PLAIN):
    return lax.dot_general(a, b, dims, preferred_element_type=jnp.float32)


def load_tiles(table_ref, kv_hbm, kv, sems, tiles):
    @pl.loop(0, tiles)
    def _(tile):
        for j in range(8):
            block = tile * 8 + j
            pltpu.make_async_copy(
                kv_hbm.at[table_ref[block]],
                kv.at[pl.ds(pl.multiple_of(block * 64, 64), 64)],
                sems.at[tile],
            ).start()


def wait_tile(kv, sems, tile):
    part = kv.at[pl.ds(pl.multiple_of(tile * TILE, TILE), TILE)]
    pltpu.make_async_copy(part, part, sems.at[tile]).wait()


def visible_keys(tile, pair, first_row, rows):
    key = tile * TILE + lax.broadcasted_iota(jnp.int32, (TILE, rows), 0)
    row = first_row + lax.broadcasted_iota(jnp.int32, (TILE, rows), 1)
    order = jnp.where(row < QROWS // 2, pair, 127 - pair) * 64 + row % 64
    return key <= order


def spread_heads(source, place, offset):
    for g in range(KEY_VALUE_HEADS):
        place[g] = jnp.zeros(place.shape[1:], place.dtype)
        for half in range(2):
            for h in range(GROUP):
                column = (GROUP * g + h) * HEAD_SIZE
                start = (half * GROUP + h) * 64
                place[g, start : start + 64, offset : offset + 64] = source[
                    half * 64 : half * 64 + 64, column : column + 64
                ]


def collect_heads(g, values, place):
    for half in range(2):
        for h in range(GROUP):
            column = (GROUP * g + h) * HEAD_SIZE
            start = (half * GROUP + h) * 64
            place[half * 64 : half * 64 + 64, column : column + 64] = values[start : start + 64]


def run_tiles(pair, step):
    low_tiles = (pair + 8) // 8
    high_tiles = (135 - pair) // 8

    @pl.loop(0, low_tiles - 1)
    def _(tile):
        step(tile, 0, QROWS, False)

    step(low_tiles - 1, 0, QROWS, True)

    @pl.loop(low_tiles, high_tiles - 1)
    def _(tile):
        step(tile, QROWS // 2, QROWS // 2, False)

    step(high_tiles - 1, QROWS // 2, QROWS // 2, True)


def attend_kernel(table_ref, pair_ref, q_ref, kv_hbm, out_ref, stat_ref, kv, q, acc, sems):
    pair = pair_ref[0]
    high_tiles = (135 - pair) // 8
    load_tiles(table_ref, kv_hbm, kv, sems, high_tiles)
    spread_heads(q_ref, q, 0)
    for g in range(KEY_VALUE_HEADS):
        acc[g] = jnp.zeros(acc.shape[1:], jnp.float32)
        stat_ref[g, 0:1, :] = jnp.full((1, QROWS), -1e30, jnp.float32)
        stat_ref[g, 1:8, :] = jnp.zeros((7, QROWS), jnp.float32)

    def step(tile, first_row, rows, masked):
        wait_tile(kv, sems, tile)
        span = slice(first_row, first_row + rows)
        if masked:
            seen = visible_keys(tile, pair, first_row, rows)
        for g in range(KEY_VALUE_HEADS):
            keys = kv[pl.ds(pl.multiple_of(tile * TILE, TILE), TILE), g * 128 : g * 128 + 128]
            scores = dot(keys, q[g, span, :], LAST)
            if masked:
                scores = jnp.where(seen, scores, -1e30)
            before = stat_ref[g, 0:1, span]
            highest = jnp.maximum(before, jnp.max(scores, axis=0, keepdims=True))
            weights = jnp.exp(scores - highest)
            shrink = jnp.exp(before - highest)
            stat_ref[g, 0:1, span] = highest
            stat_ref[g, 1:2, span] = stat_ref[g, 1:2, span] * shrink + jnp.sum(
                weights, axis=0, keepdims=True
            )
            acc[g, :, span] = acc[g, :, span] * shrink + dot(
                keys, weights.astype(jnp.bfloat16), FIRST
            )

    run_tiles(pair, step)
    for g in range(KEY_VALUE_HEADS):
        values = acc[g, 64:128, :] / stat_ref[g, 1:2, :]
        collect_heads(g, values.T, out_ref)


def attend(table, pair, q, kv):
    return pl.pallas_call(
        attend_kernel,
        out_shape=(
            jax.ShapeDtypeStruct((128, WIDTH), jnp.float32),
            jax.ShapeDtypeStruct((KEY_VALUE_HEADS, 8, QROWS), jnp.float32),
        ),
        in_specs=[
            pl.BlockSpec(memory_space=pltpu.SMEM),
            pl.BlockSpec(memory_space=pltpu.SMEM),
            pl.BlockSpec(memory_space=pltpu.VMEM),
            pl.BlockSpec(memory_space=pl.ANY),
        ],
        out_specs=(
            pl.BlockSpec(memory_space=pltpu.VMEM),
            pl.BlockSpec(memory_space=pltpu.VMEM),
        ),
        scratch_shapes=[
            pltpu.VMEM((8192, 640), jnp.bfloat16),
            pltpu.VMEM((KEY_VALUE_HEADS, QROWS, 128), jnp.bfloat16),
            pltpu.VMEM((KEY_VALUE_HEADS, 128, QROWS), jnp.float32),
            pltpu.SemaphoreType.DMA((16,)),
        ],
        compiler_params=pltpu.CompilerParams(vmem_limit_bytes=VMEM_LIMIT),
        cost_estimate=pl.CostEstimate(
            flops=4 * 10**9, bytes_accessed=10**7, transcendentals=8 * 10**6
        ),
    )(table, pair, q, kv)


def attend_back_kernel(
    table_ref,
    pair_ref,
    q_ref,
    g_ref,
    stat_ref,
    kv_hbm,
    dq_ref,
    dkv_hbm,
    kv,
    dkv,
    q,
    gs,
    acc,
    sems,
    out_sems,
):
    pair = pair_ref[0]
    high_tiles = (135 - pair) // 8
    load_tiles(table_ref, kv_hbm, kv, sems, high_tiles)
    spread_heads(q_ref, q, 0)
    spread_heads(g_ref, gs, 64)
    for g in range(KEY_VALUE_HEADS):
        acc[g] = jnp.zeros(acc.shape[1:], jnp.float32)

    def store(tile):
        for j in range(8):
            block = tile * 8 + j
            pltpu.make_async_copy(
                dkv.at[pl.ds(pl.multiple_of(block * 64, 64), 64)],
                dkv_hbm.at[table_ref[block]],
                out_sems.at[tile],
            ).start()

    @pl.loop(high_tiles, 16)
    def _(tile):
        dkv[pl.ds(pl.multiple_of(tile * TILE, TILE), TILE), :] = jnp.zeros(
            (TILE, 640), jnp.bfloat16
        )
        store(tile)

    def step(tile, first_row, rows, masked):
        wait_tile(kv, sems, tile)
        span = slice(first_row, first_row + rows)
        part = pl.ds(pl.multiple_of(tile * TILE, TILE), TILE)
        if masked:
            seen = visible_keys(tile, pair, first_row, rows)
        for g in range(KEY_VALUE_HEADS):
            columns = slice(g * 128, g * 128 + 128)
            keys = kv[part, columns]
            scores = dot(keys, q[g, span, :], LAST)
            if masked:
                scores = jnp.where(seen, scores, -1e30)
            probs = jnp.exp(scores - stat_ref[g, 0:1, span])
            prob_grad = dot(keys, gs[g, span, :], LAST)
            score_grad = (probs * (prob_grad - stat_ref[g, 1:2, span])).astype(jnp.bfloat16)
            acc[g, :, span] = acc[g, :, span] + dot(keys, score_grad, FIRST)
            both = dot(score_grad, q[g, span, :]) + dot(
                probs.astype(jnp.bfloat16), gs[g, span, :]
            )
            dkv[part, columns] = both.astype(jnp.bfloat16)
        store(tile)

    run_tiles(pair, step)
    for g in range(KEY_VALUE_HEADS):
        collect_heads(g, acc[g, 0:64, :].T, dq_ref)

    @pl.loop(0, 16)
    def _(tile):
        part = dkv.at[pl.ds(pl.multiple_of(tile * TILE, TILE), TILE)]
        pltpu.make_async_copy(part, part, out_sems.at[tile]).wait()


def attend_back(table, pair, q, scaled_grad, stats, kv):
    return pl.pallas_call(
        attend_back_kernel,
        out_shape=(
            jax.ShapeDtypeStruct((128, WIDTH), jnp.float32),
            jax.ShapeDtypeStruct((128, 64, 640), jnp.bfloat16),
        ),
        in_specs=[
            pl.BlockSpec(memory_space=pltpu.SMEM),
            pl.BlockSpec(memory_space=pltpu.SMEM),
            pl.BlockSpec(memory_space=pltpu.VMEM),
            pl.BlockSpec(memory_space=pltpu.VMEM),
            pl.BlockSpec(memory_space=pltpu.VMEM),
            pl.BlockSpec(memory_space=pl.ANY),
        ],
        out_specs=(
            pl.BlockSpec(memory_space=pltpu.VMEM),
            pl.BlockSpec(memory_space=pl.ANY),
        ),
        scratch_shapes=[
            pltpu.VMEM((8192, 640), jnp.bfloat16),
            pltpu.VMEM((8192, 640), jnp.bfloat16),
            pltpu.VMEM((KEY_VALUE_HEADS, QROWS, 128), jnp.bfloat16),
            pltpu.VMEM((KEY_VALUE_HEADS, QROWS, 128), jnp.bfloat16),
            pltpu.VMEM((KEY_VALUE_HEADS, 128, QROWS), jnp.float32),
            pltpu.SemaphoreType.DMA((16,)),
            pltpu.SemaphoreType.DMA((16,)),
        ],
        compiler_params=pltpu.CompilerParams(vmem_limit_bytes=VMEM_LIMIT),
        cost_estimate=pl.CostEstimate(
            flops=10**10, bytes_accessed=2 * 10**7, transcendentals=8 * 10**6
        ),
    )(table, pair, q, scaled_grad, stats, kv)


def rotate(values, cosine, sine):
    heads = values.shape[1] // HEAD_SIZE
    shaped = values.reshape(values.shape[0], heads, 2, HEAD_SIZE // 2)
    first, second = shaped[:, :, 0], shaped[:, :, 1]
    return jnp.stack(
        [first * cosine - second * sine, second * cosine + first * sine], axis=2
    ).reshape(values.shape)


def swap(value):
    return lax.ppermute(value, "fsdp", [(0, 1), (1, 0)])


def pad_columns(value, columns):
    return jnp.pad(value, ((0, 0), (0, columns - value.shape[1])))


def pad_halves(value, half, padded):
    return jnp.concatenate(
        [pad_columns(value[:, :half], padded), pad_columns(value[:, half:], padded)], axis=1
    )


def norm_backward(rows, scale, weighted):
    inner = jnp.sum(weighted * rows, axis=-1, keepdims=True)
    return scale * weighted - rows * scale**3 * inner / WIDTH


def on_device(
    inputs,
    cotangent,
    positions,
    pair_index,
    input_projection,
    project_out,
    gate_up,
    down_weight,
    norm_gains,
):
    half = lax.axis_index("fsdp")
    pair = pair_index[0, 0]
    key_width = KEY_VALUE_HEADS * HEAD_SIZE
    select = (
        lax.broadcasted_iota(jnp.int32, (WIDTH, PADDED), 0) == jnp.asarray(COLUMN_MAP)[None, :]
    ).astype(jnp.bfloat16)

    spare = jnp.pad(norm_gains.T, ((0, 0), (0, 1)))
    own_in = jnp.concatenate([input_projection, pad_columns(spare, IN_HALF)], axis=0)
    own_att = jnp.concatenate(
        [
            pad_columns(own_in, IN_PAD),
            jnp.pad(project_out, ((0, 1), (0, OUT_PAD - OUT_HALF))),
        ],
        axis=1,
    )
    other_att = swap(own_att)
    other_cotangent = swap(cotangent[0])
    first_att = jnp.where(half == 0, own_att, other_att)
    second_att = jnp.where(half == 0, other_att, own_att)
    own_ffn = jnp.pad(
        jnp.concatenate([gate_up.reshape(15, 2 * FF_HALF), down_weight], axis=1),
        ((0, 1), (0, 0)),
    )
    blob = jnp.concatenate(
        [
            first_att[:, :IN_PAD],
            second_att[:, :IN_PAD],
            first_att[:, IN_PAD:],
            second_att[:, IN_PAD:],
            own_ffn,
        ],
        axis=1,
    )
    blob = blob.at[15, 32].set(pair.astype(jnp.bfloat16))
    gathered = gather_blocks(blob, 0).reshape(PADDED, BLOB)
    weight_in = gathered[:, :IN_COLS]
    weight_out = gathered[:, IN_COLS:ATT_COLS]
    weight_gu = gathered[:, ATT_COLS : ATT_COLS + 2 * FF_HALF]
    weight_down = gathered[:, ATT_COLS + 2 * FF_HALF :]
    spare_rows = gathered.reshape(64, ROWS, BLOB)[:, 15]
    gain_first = spare_rows[:, :ROWS].reshape(PADDED).astype(jnp.float32)
    gain_second = spare_rows[:, IN_PAD : IN_PAD + ROWS].reshape(PADDED).astype(jnp.float32)
    held = jnp.arange(PADDED) % ROWS < 15
    gain_first = jnp.where(held, gain_first, 0.0)
    gain_second = jnp.where(held, gain_second, 0.0)
    labels = spare_rows[:, 32].astype(jnp.int32)
    slots = jnp.arange(64, dtype=jnp.int32)
    blocks = jnp.stack([labels, 127 - labels], axis=1).reshape(128)
    places = jnp.stack([2 * slots, 2 * slots + 1], axis=1).reshape(128)
    hits = blocks[None, :] == jnp.arange(128, dtype=jnp.int32)[:, None]
    table = jnp.sum(jnp.where(hits, places[None, :], 0), axis=1)

    start = dot(inputs[0], select)
    upstream = dot(cotangent[0], select)
    freqs = jnp.exp(
        -math.log(10000.0) * jnp.arange(HEAD_SIZE // 2, dtype=jnp.float32) * 2.0 / HEAD_SIZE
    )
    angle = positions[0].astype(jnp.float32)[:, None] * freqs[None, :]
    cosine = jnp.cos(angle)[:, None, :]
    sine = jnp.sin(angle)[:, None, :]
    scale_one = lax.rsqrt(jnp.sum(start * start, axis=-1, keepdims=True) / WIDTH + EPSILON)
    normed_low = (start * scale_one * gain_first).astype(jnp.bfloat16)
    projected = dot(normed_low, weight_in)
    projected = jnp.concatenate(
        [projected[:, :IN_HALF], projected[:, IN_PAD : IN_PAD + IN_HALF]], axis=1
    )
    query_low = rotate(projected[:, :WIDTH], cosine, sine).astype(jnp.bfloat16)
    query_scaled = query_low * jnp.bfloat16(0.125)
    key_low = rotate(projected[:, WIDTH : WIDTH + key_width], cosine, sine).astype(jnp.bfloat16)
    value_low = projected[:, WIDTH + key_width :].astype(jnp.bfloat16)
    key_value = jnp.stack(
        [
            key_low.reshape(128, KEY_VALUE_HEADS, HEAD_SIZE),
            value_low.reshape(128, KEY_VALUE_HEADS, HEAD_SIZE),
        ],
        axis=2,
    ).reshape(128, 2 * key_width)
    all_kv = gather_blocks(key_value, 1).reshape(128, 64, 2 * key_width)
    pair_one = pair.reshape(1)
    attention, stats = attend(table, pair_one, query_scaled, all_kv)
    mixed_low = pad_halves(attention.astype(jnp.bfloat16), OUT_HALF, OUT_PAD)
    branch = dot(mixed_low, weight_out, LAST)
    resid = start + jnp.where(held, branch, 0.0)
    scale_two = lax.rsqrt(jnp.sum(resid * resid, axis=-1, keepdims=True) / WIDTH + EPSILON)
    normed_two = (resid * scale_two * gain_second).astype(jnp.bfloat16)
    other_normed = swap(normed_two)
    both_normed = jnp.concatenate([normed_two, other_normed], axis=0)
    both_cotangent = jnp.concatenate(
        [upstream.astype(jnp.bfloat16), dot(other_cotangent, select).astype(jnp.bfloat16)], axis=0
    )
    gate_vals = dot(both_normed, weight_gu)
    gate = gate_vals[:, :FF_HALF]
    upper = gate_vals[:, FF_HALF:]
    sigma = jax.nn.sigmoid(gate)
    silu_vals = gate * sigma
    hidden_low = (silu_vals * upper).astype(jnp.bfloat16)
    ffn_out = dot(hidden_low, weight_down, LAST)
    hidden_grad = dot(both_cotangent, weight_down)
    gate_grad = hidden_grad * upper * sigma * (1.0 + gate * (1.0 - sigma))
    upper_grad = hidden_grad * silu_vals
    gate_up_grad = jnp.concatenate([gate_grad, upper_grad], axis=1).astype(jnp.bfloat16)
    normed_two_grad = dot(gate_up_grad, weight_gu, LAST)
    from_other = swap(
        jnp.concatenate([ffn_out[128:], normed_two_grad[128:]], axis=1).astype(jnp.bfloat16)
    ).astype(jnp.float32)
    ffn_out = ffn_out[:128] + from_other[:, :PADDED]
    normed_two_grad = normed_two_grad[:128] + from_other[:, PADDED:]
    layer_out = dot((resid + ffn_out).astype(jnp.bfloat16), select, LAST).astype(jnp.bfloat16)

    resid_grad = upstream + norm_backward(resid, scale_two, normed_two_grad * gain_second)
    gain_two_grad = jnp.sum(normed_two_grad * resid * scale_two, axis=0)
    branch_grad_low = resid_grad.astype(jnp.bfloat16)
    mixed_grad = dot(branch_grad_low, weight_out)
    mixed_grad = jnp.concatenate(
        [mixed_grad[:, :OUT_HALF], mixed_grad[:, OUT_PAD : OUT_PAD + OUT_HALF]], axis=1
    ).reshape(128, QUERY_HEADS, HEAD_SIZE)
    totals = stats[:, 1]
    totals_by_token = jnp.transpose(
        totals.reshape(KEY_VALUE_HEADS, 2, GROUP, 64), (1, 3, 0, 2)
    ).reshape(128, QUERY_HEADS)
    delta = jnp.sum(mixed_grad * attention.reshape(128, QUERY_HEADS, HEAD_SIZE), axis=-1)
    scaled_grad = (mixed_grad / totals_by_token[..., None]).astype(jnp.bfloat16).reshape(128, WIDTH)
    correction = jnp.transpose(
        (delta / totals_by_token).reshape(2, 64, KEY_VALUE_HEADS, GROUP), (2, 0, 3, 1)
    ).reshape(KEY_VALUE_HEADS, 1, QROWS)
    back_stats = jnp.concatenate(
        [stats[:, 0:1], correction, jnp.zeros((KEY_VALUE_HEADS, 6, QROWS), jnp.float32)], axis=1
    )
    query_grad, all_kv_grad = attend_back(
        table, pair_one, query_scaled, scaled_grad, back_stats, all_kv
    )
    kv_grad = scatter_blocks(all_kv_grad.reshape(2, 4, 4, 2, 128, 2 * key_width), 2)
    kv_grad = kv_grad.reshape(128, KEY_VALUE_HEADS, 2, HEAD_SIZE)
    proj_grad = jnp.concatenate(
        [
            rotate(query_grad * 0.125, cosine, -sine),
            rotate(kv_grad[:, :, 0].reshape(128, key_width), cosine, -sine),
            kv_grad[:, :, 1].reshape(128, key_width),
        ],
        axis=1,
    ).astype(jnp.bfloat16)
    proj_grad = pad_halves(proj_grad, IN_HALF, IN_PAD)
    normed_one_grad = dot(proj_grad, weight_in, LAST)
    gain_one_grad = jnp.sum(normed_one_grad * start * scale_one, axis=0)
    through = norm_backward(start, scale_one, normed_one_grad * gain_first)
    input_grad = dot((resid_grad + through).astype(jnp.bfloat16), select, LAST).astype(jnp.bfloat16)

    grad_in = dot(normed_low, proj_grad, FIRST).astype(jnp.bfloat16)
    grad_out = dot(branch_grad_low, mixed_low, FIRST).astype(jnp.bfloat16)
    grad_gu = dot(both_normed, gate_up_grad, FIRST).astype(jnp.bfloat16)
    grad_down = dot(both_cotangent, hidden_low, FIRST).astype(jnp.bfloat16)
    row = jnp.arange(PADDED)[:, None]
    lane = jnp.arange(IN_COLS)[None, :]
    gains_by_slot = jnp.stack([gain_one_grad, gain_two_grad]).reshape(2, 64, ROWS)
    gains_by_slot = jnp.pad(
        gains_by_slot.transpose(1, 0, 2), ((0, 0), (0, 0), (0, IN_PAD - ROWS))
    ).reshape(64, 1, IN_COLS)
    grad_in = jnp.where(
        row % ROWS == 15,
        jnp.broadcast_to(gains_by_slot, (64, ROWS, IN_COLS)).reshape(PADDED, IN_COLS).astype(jnp.bfloat16),
        grad_in,
    )
    grads = jnp.concatenate([grad_in, grad_out, grad_gu, grad_down], axis=1)
    summed = scatter_blocks(grads.reshape(2, 4, 4, 2, ROWS, BLOB), 3)
    first_sum = jnp.concatenate(
        [summed[:, :IN_PAD], summed[:, IN_COLS : IN_COLS + OUT_PAD]], axis=1
    )
    second_sum = jnp.concatenate(
        [summed[:, IN_PAD:IN_COLS], summed[:, IN_COLS + OUT_PAD : ATT_COLS]], axis=1
    )
    own_sum = jnp.where(half == 0, first_sum, second_sum)
    send_sum = jnp.where(half == 0, second_sum, first_sum).astype(jnp.bfloat16)
    own_sum = own_sum + swap(send_sum).astype(jnp.float32)
    return (
        layer_out[None],
        input_grad[None],
        own_sum[:15, :IN_HALF],
        own_sum[:15, IN_PAD : IN_PAD + OUT_HALF],
        summed[:15, ATT_COLS : ATT_COLS + 2 * FF_HALF].reshape(15, 2, FF_HALF),
        summed[:15, ATT_COLS + 2 * FF_HALF :],
        own_sum[15, :15].reshape(15, 1),
    )


def solution(mesh):
    in_specs = (
        P("fsdp", "ctx", None),
        P("fsdp", "ctx", None),
        P("fsdp", "ctx"),
        P("fsdp", "ctx"),
        P("ctx", "fsdp"),
        P("ctx", "fsdp"),
        P("ctx", None, "fsdp"),
        P("ctx", "fsdp"),
        P("ctx", "fsdp"),
    )
    out_specs = (
        P("fsdp", "ctx", None),
        P("fsdp", "ctx", None),
        P("ctx", "fsdp"),
        P("ctx", "fsdp"),
        P("ctx", None, "fsdp"),
        P("ctx", "fsdp"),
        P("ctx", "fsdp"),
    )
    return jax.shard_map(
        on_device, mesh=mesh, in_specs=in_specs, out_specs=out_specs, check_vma=False
    )
```

```python
import math

import jax
import jax.numpy as jnp
import numpy as np
from jax import lax
from jax.experimental import pallas as pl
from jax.experimental.pallas import tpu as pltpu
from jax.sharding import PartitionSpec as P

WIDTH = 960
QUERY_HEADS = 15
KEY_VALUE_HEADS = 5
GROUP = 3
HEAD_SIZE = 64
FF_HALF = 1280
EPSILON = 1e-05
ROWS = 16
PADDED = 1024
IN_HALF = 800
IN_PAD = 896
OUT_HALF = 480
OUT_PAD = 512
IN_COLS = 2 * IN_PAD
TILE = 512
QROWS = 384
MESH = pl.DeviceIdType.MESH
VMEM_LIMIT = 56 * 1024 * 1024


def column_map():
    cols = np.full((64, ROWS), -1, np.int32)
    cols[:, :15] = np.arange(64)[:, None] * 15 + np.arange(15)[None, :]
    return cols.reshape(-1)


COLUMN_MAP = column_map()


def coordinates():
    index = lax.axis_index("ctx")
    core = index % 2
    z = (index // 2) % 4
    y = (index // 8) % 4
    x = index // 32
    p1 = y * (1 - core) + z * core
    p2 = z * (1 - core) + y * core
    return x, p1, p2, core


def device_at(x, p1, p2, core):
    y = p1 * (1 - core) + p2 * core
    z = p2 * (1 - core) + p1 * core
    return ((x * 4 + y) * 4 + z) * 2 + core


def neighbours(x, p1, p2, core):
    index = lax.axis_index("ctx")
    return (
        device_at(1 - x, p1, p2, core),
        device_at(x, (p1 + 1) % 4, p2, core),
        device_at(x, (p1 + 3) % 4, p2, core),
        device_at(x, p1, (p2 + 1) % 4, core),
        device_at(x, p1, (p2 + 3) % 4, core),
        index + 1 - 2 * core,
    )


def block_of(ref, core, x, p1, p2):
    return ref.at[x, p1, p2, core] if core == 0 else ref.at[x, p2, p1, core]


def half_of(ref, core, x, p2):
    every = pl.ds(0, 4)
    return ref.at[x, every, p2, core] if core == 0 else ref.at[x, p2, every, core]


def slab_of(ref, core, p2):
    every = pl.ds(0, 4)
    both = pl.ds(0, 2)
    return ref.at[both, every, p2, core] if core == 0 else ref.at[both, p2, every, core]


def greet(devices):
    barrier = pltpu.get_barrier_semaphore()
    for device in devices:
        pl.semaphore_signal(barrier, inc=1, device_id={"ctx": device}, device_id_type=MESH)
    pl.semaphore_wait(barrier, len(devices))


def gather_kernel(in_ref, out_ref, local_sem, send_sem, recv_sem):
    x, p1, p2, core = coordinates()
    greet(neighbours(x, p1, p2, core))
    for chosen in range(2):

        @pl.when(core == chosen)
        def _(chosen=chosen):
            gather_body(chosen, in_ref, out_ref, local_sem, send_sem, recv_sem)


def gather_body(core, in_ref, out_ref, local_sem, send_sem, recv_sem):
    x, p1, p2, _ = coordinates()
    across, right1, left1, right2, left2, sibling = neighbours(x, p1, p2, core)
    p1p, p1m, p1o = (p1 + 1) % 4, (p1 + 3) % 4, (p1 + 2) % 4
    p2p, p2m, p2o = (p2 + 1) % 4, (p2 + 3) % 4, (p2 + 2) % 4
    sent = []

    def send(place, to, source=None):
        number = len(sent)
        copy = pltpu.make_async_remote_copy(
            src_ref=place if source is None else source,
            dst_ref=place,
            send_sem=send_sem.at[number],
            recv_sem=recv_sem.at[number],
            device_id={"ctx": to},
            device_id_type=MESH,
        )
        copy.start()
        sent.append(copy)
        return copy

    def block(side, q1):
        return block_of(out_ref, core, side, q1, p2)

    def half(side, q2):
        return half_of(out_ref, core, side, q2)

    mine = block(x, p1)
    local = pltpu.make_async_copy(in_ref, mine, local_sem)
    local.start()
    crossed = send(mine, across, in_ref)
    own_left = send(mine, right1, in_ref)
    own_right = send(mine, left1, in_ref)
    crossed.wait_recv()
    other_left = send(block(1 - x, p1), right1)
    other_right = send(block(1 - x, p1), left1)
    own_left.wait_recv()
    own_far = send(block(x, p1m), right1)
    own_right.wait_recv()
    own_far.wait_recv()
    local.wait()
    own_left = send(half(x, p2), right2)
    own_right = send(half(x, p2), left2)
    last = [send(half(x, p2), sibling)]
    other_right.wait_recv()
    other_far = send(block(1 - x, p1p), left1)
    other_left.wait_recv()
    other_far.wait_recv()
    other_right = send(half(1 - x, p2), left2)
    other_left = send(half(1 - x, p2), right2)
    last.append(send(half(1 - x, p2), sibling))
    own_left.wait_recv()
    own_far = send(half(x, p2m), right2)
    last.append(send(half(x, p2m), sibling))
    own_right.wait_recv()
    last.append(send(half(x, p2p), sibling))
    other_right.wait_recv()
    other_far = send(half(1 - x, p2p), left2)
    last.append(send(half(1 - x, p2p), sibling))
    other_left.wait_recv()
    last.append(send(half(1 - x, p2m), sibling))
    own_far.wait_recv()
    last.append(send(half(x, p2o), sibling))
    other_far.wait_recv()
    last.append(send(half(1 - x, p2o), sibling))
    for copy in last:
        copy.wait_recv()
    for copy in sent:
        copy.wait_send()


def gather_blocks(block, collective_id):
    rows, columns = block.shape
    return pl.pallas_call(
        gather_kernel,
        out_shape=jax.ShapeDtypeStruct((2, 4, 4, 2, rows, columns), block.dtype),
        in_specs=[pl.BlockSpec(memory_space=pl.ANY)],
        out_specs=pl.BlockSpec(memory_space=pl.ANY),
        scratch_shapes=[
            pltpu.SemaphoreType.DMA,
            pltpu.SemaphoreType.DMA((21,)),
            pltpu.SemaphoreType.DMA((21,)),
        ],
        compiler_params=pltpu.CompilerParams(
            collective_id=collective_id, has_side_effects=True
        ),
    )(block)


def scatter_kernel(
    g_ref,
    out_ref,
    acc,
    other,
    far_low,
    far_high,
    near_left,
    near_right,
    pair_low,
    pair_high,
    pair_left,
    pair_right,
    last,
    local_sem,
    cross_send,
    cross_recv,
    send_sem,
    recv_sem,
):
    x, p1, p2, core = coordinates()
    across, right1, left1, right2, left2, sibling = neighbours(x, p1, p2, core)
    greet((across, right1, left1, right2, left2, sibling))
    p1p, p1m, p1o = (p1 + 1) % 4, (p1 + 3) % 4, (p1 + 2) % 4
    p2p, p2m, p2o = (p2 + 1) % 4, (p2 + 3) % 4, (p2 + 2) % 4
    needed = (p2o, p2m, p2p, p2)
    theirs = (p1o, p1m, p1p, p1)
    sent = []

    def crossing(k, source):
        return pltpu.make_async_remote_copy(
            src_ref=source,
            dst_ref=other.at[theirs[k]],
            send_sem=cross_send.at[k],
            recv_sem=cross_recv.at[k],
            device_id={"ctx": sibling},
            device_id_type=MESH,
        )

    for chosen in range(2):

        @pl.when(core == chosen)
        def _(chosen=chosen):
            for k in range(4):
                crossing(k, slab_of(g_ref, 1 - chosen, theirs[k])).start()
                pltpu.make_async_copy(
                    slab_of(g_ref, chosen, needed[k]), acc.at[needed[k]], local_sem.at[k]
                ).start()

    def send(source, place, to):
        number = len(sent)
        copy = pltpu.make_async_remote_copy(
            src_ref=source,
            dst_ref=place,
            send_sem=send_sem.at[number],
            recv_sem=recv_sem.at[number],
            device_id={"ctx": to},
            device_id_type=MESH,
        )
        copy.start()
        sent.append(copy)
        return copy

    def add(place, term):
        @pl.loop(0, 4)
        def _(step):
            place[step] = place[step] + term[step]

    def add_both(side):
        @pl.loop(0, 4)
        def _(step):
            total = acc[p2, side, step].astype(jnp.float32)
            total = total + near_left[side, step].astype(jnp.float32)
            total = total + near_right[side, step].astype(jnp.float32)
            acc[p2, side, step] = total.astype(acc.dtype)

    def merge(k):
        pltpu.make_async_copy(acc.at[needed[k]], acc.at[needed[k]], local_sem.at[k]).wait()
        crossing(k, other.at[theirs[k]]).wait_recv()
        for side in range(2):
            add(acc.at[needed[k], side], other.at[needed[k], side])

    merge(0)
    got_low = send(acc.at[p2o, 0], far_low, right2)
    got_high = send(acc.at[p2o, 1], far_high, left2)
    merge(1)
    right_low = send(acc.at[p2m, 0], near_right.at[0], left2)
    merge(2)
    left_high = send(acc.at[p2p, 1], near_left.at[1], right2)
    got_low.wait_recv()
    add(acc.at[p2p, 0], far_low)
    left_low = send(acc.at[p2p, 0], near_left.at[0], right2)
    got_high.wait_recv()
    add(acc.at[p2m, 1], far_high)
    right_high = send(acc.at[p2m, 1], near_right.at[1], left2)
    merge(3)
    right_low.wait_recv()
    left_low.wait_recv()
    add_both(0)
    got_low = send(acc.at[p2, 0, p1o], pair_low, right1)
    near_low = send(acc.at[p2, 0, p1m], pair_right.at[0], left1)
    left_high.wait_recv()
    right_high.wait_recv()
    add_both(1)
    got_high = send(acc.at[p2, 1, p1o], pair_high, left1)
    near_high = send(acc.at[p2, 1, p1p], pair_left.at[1], right1)
    got_low.wait_recv()
    acc[p2, 0, p1p] = acc[p2, 0, p1p] + pair_low[...]
    left_low = send(acc.at[p2, 0, p1p], pair_left.at[0], right1)
    got_high.wait_recv()
    acc[p2, 1, p1m] = acc[p2, 1, p1m] + pair_high[...]
    right_high = send(acc.at[p2, 1, p1m], pair_right.at[1], left1)
    near_low.wait_recv()
    near_high.wait_recv()
    left_low.wait_recv()
    right_high.wait_recv()

    @pl.loop(0, 2)
    def _(j):
        total = acc[p2, j, p1].astype(jnp.float32) + pair_left[j].astype(jnp.float32)
        total = total + pair_right[j].astype(jnp.float32)
        acc[p2, j, p1] = total.astype(acc.dtype)

    final = send(acc.at[p2, 1 - x, p1], last, across)
    final.wait_recv()
    out_ref[...] = acc[p2, x, p1].astype(jnp.float32) + last[...].astype(jnp.float32)
    for k in range(4):
        crossing(k, other.at[theirs[k]]).wait_send()
    for copy in sent:
        copy.wait_send()


def scatter_blocks(blocks, collective_id):
    rows, columns = blocks.shape[-2:]
    kind = blocks.dtype
    block = (rows, columns)
    return pl.pallas_call(
        scatter_kernel,
        out_shape=jax.ShapeDtypeStruct(block, jnp.float32),
        in_specs=[pl.BlockSpec(memory_space=pl.ANY)],
        out_specs=pl.BlockSpec(memory_space=pltpu.VMEM),
        scratch_shapes=[
            pltpu.VMEM((4, 2, 4) + block, kind),
            pltpu.VMEM((4, 2, 4) + block, kind),
            pltpu.VMEM((4,) + block, kind),
            pltpu.VMEM((4,) + block, kind),
            pltpu.VMEM((2, 4) + block, kind),
            pltpu.VMEM((2, 4) + block, kind),
            pltpu.VMEM(block, kind),
            pltpu.VMEM(block, kind),
            pltpu.VMEM((2,) + block, kind),
            pltpu.VMEM((2,) + block, kind),
            pltpu.VMEM(block, kind),
            pltpu.SemaphoreType.DMA((4,)),
            pltpu.SemaphoreType.DMA((4,)),
            pltpu.SemaphoreType.DMA((4,)),
            pltpu.SemaphoreType.DMA((13,)),
            pltpu.SemaphoreType.DMA((13,)),
        ],
        compiler_params=pltpu.CompilerParams(
            collective_id=collective_id, has_side_effects=True, vmem_limit_bytes=VMEM_LIMIT
        ),
    )(blocks)


LAST = (((1,), (1,)), ((), ()))
FIRST = (((0,), (0,)), ((), ()))
PLAIN = (((1,), (0,)), ((), ()))


def dot(a, b, dims=PLAIN):
    return lax.dot_general(a, b, dims, preferred_element_type=jnp.float32)


def load_tiles(table_ref, kv_hbm, kv, sems, tiles):
    @pl.loop(0, tiles)
    def _(tile):
        for j in range(8):
            block = tile * 8 + j
            pltpu.make_async_copy(
                kv_hbm.at[table_ref[block]],
                kv.at[pl.ds(pl.multiple_of(block * 64, 64), 64)],
                sems.at[tile],
            ).start()


def wait_tile(kv, sems, tile):
    part = kv.at[pl.ds(pl.multiple_of(tile * TILE, TILE), TILE)]
    pltpu.make_async_copy(part, part, sems.at[tile]).wait()


def visible_keys(tile, pair, first_row, rows):
    key = tile * TILE + lax.broadcasted_iota(jnp.int32, (TILE, rows), 0)
    row = first_row + lax.broadcasted_iota(jnp.int32, (TILE, rows), 1)
    order = jnp.where(row < QROWS // 2, pair, 127 - pair) * 64 + row % 64
    return key <= order


def spread_heads(source, place, offset):
    for g in range(KEY_VALUE_HEADS):
        place[g] = jnp.zeros(place.shape[1:], place.dtype)
        for half in range(2):
            for h in range(GROUP):
                column = (GROUP * g + h) * HEAD_SIZE
                start = (half * GROUP + h) * 64
                place[g, start : start + 64, offset : offset + 64] = source[
                    half * 64 : half * 64 + 64, column : column + 64
                ]


def collect_heads(g, values, place):
    for half in range(2):
        for h in range(GROUP):
            column = (GROUP * g + h) * HEAD_SIZE
            start = (half * GROUP + h) * 64
            place[half * 64 : half * 64 + 64, column : column + 64] = values[start : start + 64]


def run_tiles(pair, step):
    low_tiles = (pair + 8) // 8
    high_tiles = (135 - pair) // 8

    @pl.loop(0, low_tiles - 1)
    def _(tile):
        step(tile, 0, QROWS, False)

    step(low_tiles - 1, 0, QROWS, True)

    @pl.loop(low_tiles, high_tiles - 1)
    def _(tile):
        step(tile, QROWS // 2, QROWS // 2, False)

    step(high_tiles - 1, QROWS // 2, QROWS // 2, True)


def attend_kernel(table_ref, pair_ref, q_ref, kv_hbm, out_ref, stat_ref, kv, q, acc, sems):
    pair = pair_ref[0]
    high_tiles = (135 - pair) // 8
    load_tiles(table_ref, kv_hbm, kv, sems, high_tiles)
    spread_heads(q_ref, q, 0)
    for g in range(KEY_VALUE_HEADS):
        acc[g] = jnp.zeros(acc.shape[1:], jnp.float32)
        stat_ref[g, 0:1, :] = jnp.full((1, QROWS), -1e30, jnp.float32)
        stat_ref[g, 1:8, :] = jnp.zeros((7, QROWS), jnp.float32)

    def step(tile, first_row, rows, masked):
        wait_tile(kv, sems, tile)
        span = slice(first_row, first_row + rows)
        if masked:
            seen = visible_keys(tile, pair, first_row, rows)
        for g in range(KEY_VALUE_HEADS):
            keys = kv[pl.ds(pl.multiple_of(tile * TILE, TILE), TILE), g * 128 : g * 128 + 128]
            scores = dot(keys, q[g, span, :], LAST)
            if masked:
                scores = jnp.where(seen, scores, -1e30)
            before = stat_ref[g, 0:1, span]
            highest = jnp.maximum(before, jnp.max(scores, axis=0, keepdims=True))
            weights = jnp.exp(scores - highest)
            shrink = jnp.exp(before - highest)
            stat_ref[g, 0:1, span] = highest
            stat_ref[g, 1:2, span] = stat_ref[g, 1:2, span] * shrink + jnp.sum(
                weights, axis=0, keepdims=True
            )
            acc[g, :, span] = acc[g, :, span] * shrink + dot(
                keys, weights.astype(jnp.bfloat16), FIRST
            )

    run_tiles(pair, step)
    for g in range(KEY_VALUE_HEADS):
        values = acc[g, 64:128, :] / stat_ref[g, 1:2, :]
        collect_heads(g, values.T, out_ref)


def attend(table, pair, q, kv):
    return pl.pallas_call(
        attend_kernel,
        out_shape=(
            jax.ShapeDtypeStruct((128, WIDTH), jnp.float32),
            jax.ShapeDtypeStruct((KEY_VALUE_HEADS, 8, QROWS), jnp.float32),
        ),
        in_specs=[
            pl.BlockSpec(memory_space=pltpu.SMEM),
            pl.BlockSpec(memory_space=pltpu.SMEM),
            pl.BlockSpec(memory_space=pltpu.VMEM),
            pl.BlockSpec(memory_space=pl.ANY),
        ],
        out_specs=(
            pl.BlockSpec(memory_space=pltpu.VMEM),
            pl.BlockSpec(memory_space=pltpu.VMEM),
        ),
        scratch_shapes=[
            pltpu.VMEM((8192, 640), jnp.bfloat16),
            pltpu.VMEM((KEY_VALUE_HEADS, QROWS, 128), jnp.bfloat16),
            pltpu.VMEM((KEY_VALUE_HEADS, 128, QROWS), jnp.float32),
            pltpu.SemaphoreType.DMA((16,)),
        ],
        compiler_params=pltpu.CompilerParams(vmem_limit_bytes=VMEM_LIMIT),
        cost_estimate=pl.CostEstimate(
            flops=4 * 10**9, bytes_accessed=10**7, transcendentals=8 * 10**6
        ),
    )(table, pair, q, kv)


def attend_back_kernel(
    table_ref,
    pair_ref,
    q_ref,
    g_ref,
    stat_ref,
    kv_hbm,
    dq_ref,
    dkv_hbm,
    kv,
    dkv,
    q,
    gs,
    acc,
    sems,
    out_sems,
):
    pair = pair_ref[0]
    high_tiles = (135 - pair) // 8
    load_tiles(table_ref, kv_hbm, kv, sems, high_tiles)
    spread_heads(q_ref, q, 0)
    spread_heads(g_ref, gs, 64)
    for g in range(KEY_VALUE_HEADS):
        acc[g] = jnp.zeros(acc.shape[1:], jnp.float32)

    def store(tile):
        for j in range(8):
            block = tile * 8 + j
            pltpu.make_async_copy(
                dkv.at[pl.ds(pl.multiple_of(block * 64, 64), 64)],
                dkv_hbm.at[table_ref[block]],
                out_sems.at[tile],
            ).start()

    @pl.loop(high_tiles, 16)
    def _(tile):
        dkv[pl.ds(pl.multiple_of(tile * TILE, TILE), TILE), :] = jnp.zeros(
            (TILE, 640), jnp.bfloat16
        )
        store(tile)

    def step(tile, first_row, rows, masked):
        wait_tile(kv, sems, tile)
        span = slice(first_row, first_row + rows)
        part = pl.ds(pl.multiple_of(tile * TILE, TILE), TILE)
        if masked:
            seen = visible_keys(tile, pair, first_row, rows)
        for g in range(KEY_VALUE_HEADS):
            columns = slice(g * 128, g * 128 + 128)
            keys = kv[part, columns]
            scores = dot(keys, q[g, span, :], LAST)
            if masked:
                scores = jnp.where(seen, scores, -1e30)
            probs = jnp.exp(scores - stat_ref[g, 0:1, span])
            prob_grad = dot(keys, gs[g, span, :], LAST)
            score_grad = (probs * (prob_grad - stat_ref[g, 1:2, span])).astype(jnp.bfloat16)
            acc[g, :, span] = acc[g, :, span] + dot(keys, score_grad, FIRST)
            both = dot(score_grad, q[g, span, :]) + dot(
                probs.astype(jnp.bfloat16), gs[g, span, :]
            )
            dkv[part, columns] = both.astype(jnp.bfloat16)
        store(tile)

    run_tiles(pair, step)
    for g in range(KEY_VALUE_HEADS):
        collect_heads(g, acc[g, 0:64, :].T, dq_ref)

    @pl.loop(0, 16)
    def _(tile):
        part = dkv.at[pl.ds(pl.multiple_of(tile * TILE, TILE), TILE)]
        pltpu.make_async_copy(part, part, out_sems.at[tile]).wait()


def attend_back(table, pair, q, scaled_grad, stats, kv):
    return pl.pallas_call(
        attend_back_kernel,
        out_shape=(
            jax.ShapeDtypeStruct((128, WIDTH), jnp.float32),
            jax.ShapeDtypeStruct((128, 64, 640), jnp.bfloat16),
        ),
        in_specs=[
            pl.BlockSpec(memory_space=pltpu.SMEM),
            pl.BlockSpec(memory_space=pltpu.SMEM),
            pl.BlockSpec(memory_space=pltpu.VMEM),
            pl.BlockSpec(memory_space=pltpu.VMEM),
            pl.BlockSpec(memory_space=pltpu.VMEM),
            pl.BlockSpec(memory_space=pl.ANY),
        ],
        out_specs=(
            pl.BlockSpec(memory_space=pltpu.VMEM),
            pl.BlockSpec(memory_space=pl.ANY),
        ),
        scratch_shapes=[
            pltpu.VMEM((8192, 640), jnp.bfloat16),
            pltpu.VMEM((8192, 640), jnp.bfloat16),
            pltpu.VMEM((KEY_VALUE_HEADS, QROWS, 128), jnp.bfloat16),
            pltpu.VMEM((KEY_VALUE_HEADS, QROWS, 128), jnp.bfloat16),
            pltpu.VMEM((KEY_VALUE_HEADS, 128, QROWS), jnp.float32),
            pltpu.SemaphoreType.DMA((16,)),
            pltpu.SemaphoreType.DMA((16,)),
        ],
        compiler_params=pltpu.CompilerParams(vmem_limit_bytes=VMEM_LIMIT),
        cost_estimate=pl.CostEstimate(
            flops=10**10, bytes_accessed=2 * 10**7, transcendentals=8 * 10**6
        ),
    )(table, pair, q, scaled_grad, stats, kv)


def rotate(values, cosine, sine):
    heads = values.shape[1] // HEAD_SIZE
    shaped = values.reshape(values.shape[0], heads, 2, HEAD_SIZE // 2)
    first, second = shaped[:, :, 0], shaped[:, :, 1]
    return jnp.stack(
        [first * cosine - second * sine, second * cosine + first * sine], axis=2
    ).reshape(values.shape)


def swap(value):
    return lax.ppermute(value, "fsdp", [(0, 1), (1, 0)])


def pad_columns(value, columns):
    return jnp.pad(value, ((0, 0), (0, columns - value.shape[1])))


def pad_halves(value, half, padded):
    return jnp.concatenate(
        [pad_columns(value[:, :half], padded), pad_columns(value[:, half:], padded)], axis=1
    )


def norm_backward(rows, scale, weighted):
    inner = jnp.sum(weighted * rows, axis=-1, keepdims=True)
    return scale * weighted - rows * scale**3 * inner / WIDTH


def on_device(
    inputs,
    cotangent,
    positions,
    pair_index,
    input_projection,
    project_out,
    gate_up,
    down_weight,
    norm_gains,
):
    half = lax.axis_index("fsdp")
    pair = pair_index[0, 0]
    key_width = KEY_VALUE_HEADS * HEAD_SIZE
    select = (
        lax.broadcasted_iota(jnp.int32, (WIDTH, PADDED), 0) == jnp.asarray(COLUMN_MAP)[None, :]
    ).astype(jnp.bfloat16)

    spare = jnp.pad(norm_gains.T, ((0, 0), (0, 1)))
    own_in = pad_columns(
        jnp.concatenate([input_projection, pad_columns(spare, IN_HALF)], axis=0), IN_PAD
    )
    other_in = swap(own_in)
    own_out = jnp.pad(project_out, ((0, 1), (0, OUT_PAD - OUT_HALF)))
    other_out = swap(own_out)
    other_cotangent = swap(cotangent[0])

    def in_order(own, other):
        return jnp.concatenate(
            [jnp.where(half == 0, own, other), jnp.where(half == 0, other, own)], axis=1
        )

    def gather(value):
        return lax.all_gather(value, "ctx", axis=0, tiled=True)

    own_ffn = jnp.pad(
        jnp.concatenate([gate_up.reshape(15, 2 * FF_HALF), down_weight], axis=1),
        ((0, 1), (0, 0)),
    )
    gathered = gather(jnp.concatenate([in_order(own_out, other_out), own_ffn], axis=1))
    weight_out = gathered[:, : 2 * OUT_PAD]
    weight_gu = gathered[:, 2 * OUT_PAD : 2 * OUT_PAD + 2 * FF_HALF]
    weight_down = gathered[:, 2 * OUT_PAD + 2 * FF_HALF :]
    blob = in_order(own_in, other_in).at[15, 32].set(pair.astype(jnp.bfloat16))
    weight_in = gather_blocks(blob, 0).reshape(PADDED, IN_COLS)
    spare_rows = weight_in.reshape(64, ROWS, IN_COLS)[:, 15]
    gain_first = spare_rows[:, :ROWS].reshape(PADDED).astype(jnp.float32)
    gain_second = spare_rows[:, IN_PAD : IN_PAD + ROWS].reshape(PADDED).astype(jnp.float32)
    held = jnp.arange(PADDED) % ROWS < 15
    gain_first = jnp.where(held, gain_first, 0.0)
    gain_second = jnp.where(held, gain_second, 0.0)
    labels = spare_rows[:, 32].astype(jnp.int32)
    slots = jnp.arange(64, dtype=jnp.int32)
    blocks = jnp.stack([labels, 127 - labels], axis=1).reshape(128)
    places = jnp.stack([2 * slots, 2 * slots + 1], axis=1).reshape(128)
    hits = blocks[None, :] == jnp.arange(128, dtype=jnp.int32)[:, None]
    table = jnp.sum(jnp.where(hits, places[None, :], 0), axis=1)

    start = dot(inputs[0], select)
    upstream = dot(cotangent[0], select)
    freqs = jnp.exp(
        -math.log(10000.0) * jnp.arange(HEAD_SIZE // 2, dtype=jnp.float32) * 2.0 / HEAD_SIZE
    )
    angle = positions[0].astype(jnp.float32)[:, None] * freqs[None, :]
    cosine = jnp.cos(angle)[:, None, :]
    sine = jnp.sin(angle)[:, None, :]
    scale_one = lax.rsqrt(jnp.sum(start * start, axis=-1, keepdims=True) / WIDTH + EPSILON)
    normed_low = (start * scale_one * gain_first).astype(jnp.bfloat16)
    projected = dot(normed_low, weight_in)
    projected = jnp.concatenate(
        [projected[:, :IN_HALF], projected[:, IN_PAD : IN_PAD + IN_HALF]], axis=1
    )
    query_low = rotate(projected[:, :WIDTH], cosine, sine).astype(jnp.bfloat16)
    query_scaled = query_low * jnp.bfloat16(0.125)
    key_low = rotate(projected[:, WIDTH : WIDTH + key_width], cosine, sine).astype(jnp.bfloat16)
    value_low = projected[:, WIDTH + key_width :].astype(jnp.bfloat16)
    key_value = jnp.stack(
        [
            key_low.reshape(128, KEY_VALUE_HEADS, HEAD_SIZE),
            value_low.reshape(128, KEY_VALUE_HEADS, HEAD_SIZE),
        ],
        axis=2,
    ).reshape(128, 2 * key_width)
    all_kv = gather_blocks(key_value, 1).reshape(128, 64, 2 * key_width)
    pair_one = pair.reshape(1)
    attention, stats = attend(table, pair_one, query_scaled, all_kv)
    mixed_low = pad_halves(attention.astype(jnp.bfloat16), OUT_HALF, OUT_PAD)
    branch = dot(mixed_low, weight_out, LAST)
    resid = start + jnp.where(held, branch, 0.0)
    scale_two = lax.rsqrt(jnp.sum(resid * resid, axis=-1, keepdims=True) / WIDTH + EPSILON)
    normed_two = (resid * scale_two * gain_second).astype(jnp.bfloat16)
    other_normed = swap(normed_two)
    both_normed = jnp.concatenate([normed_two, other_normed], axis=0)
    both_cotangent = jnp.concatenate(
        [upstream.astype(jnp.bfloat16), dot(other_cotangent, select).astype(jnp.bfloat16)], axis=0
    )
    gate_vals = dot(both_normed, weight_gu)
    gate = gate_vals[:, :FF_HALF]
    upper = gate_vals[:, FF_HALF:]
    sigma = jax.nn.sigmoid(gate)
    silu_vals = gate * sigma
    hidden_low = (silu_vals * upper).astype(jnp.bfloat16)
    ffn_out = dot(hidden_low, weight_down, LAST)
    hidden_grad = dot(both_cotangent, weight_down)
    gate_grad = hidden_grad * upper * sigma * (1.0 + gate * (1.0 - sigma))
    upper_grad = hidden_grad * silu_vals
    gate_up_grad = jnp.concatenate([gate_grad, upper_grad], axis=1).astype(jnp.bfloat16)
    normed_two_grad = dot(gate_up_grad, weight_gu, LAST)
    from_other = swap(
        jnp.concatenate([ffn_out[128:], normed_two_grad[128:]], axis=1).astype(jnp.bfloat16)
    ).astype(jnp.float32)
    ffn_out = ffn_out[:128] + from_other[:, :PADDED]
    normed_two_grad = normed_two_grad[:128] + from_other[:, PADDED:]
    layer_out = dot((resid + ffn_out).astype(jnp.bfloat16), select, LAST).astype(jnp.bfloat16)

    resid_grad = upstream + norm_backward(resid, scale_two, normed_two_grad * gain_second)
    gain_two_grad = jnp.sum(normed_two_grad * resid * scale_two, axis=0)
    branch_grad_low = resid_grad.astype(jnp.bfloat16)
    grad_out = dot(branch_grad_low, mixed_low, FIRST).astype(jnp.bfloat16)
    grad_gu = dot(both_normed, gate_up_grad, FIRST).astype(jnp.bfloat16)
    grad_down = dot(both_cotangent, hidden_low, FIRST).astype(jnp.bfloat16)
    rest_sum = lax.psum_scatter(
        jnp.concatenate([grad_out, grad_gu, grad_down], axis=1),
        "ctx",
        scatter_dimension=0,
        tiled=True,
    )
    mixed_grad = dot(branch_grad_low, weight_out)
    mixed_grad = jnp.concatenate(
        [mixed_grad[:, :OUT_HALF], mixed_grad[:, OUT_PAD : OUT_PAD + OUT_HALF]], axis=1
    ).reshape(128, QUERY_HEADS, HEAD_SIZE)
    totals = stats[:, 1]
    totals_by_token = jnp.transpose(
        totals.reshape(KEY_VALUE_HEADS, 2, GROUP, 64), (1, 3, 0, 2)
    ).reshape(128, QUERY_HEADS)
    delta = jnp.sum(mixed_grad * attention.reshape(128, QUERY_HEADS, HEAD_SIZE), axis=-1)
    scaled_grad = (mixed_grad / totals_by_token[..., None]).astype(jnp.bfloat16).reshape(128, WIDTH)
    correction = jnp.transpose(
        (delta / totals_by_token).reshape(2, 64, KEY_VALUE_HEADS, GROUP), (2, 0, 3, 1)
    ).reshape(KEY_VALUE_HEADS, 1, QROWS)
    back_stats = jnp.concatenate(
        [stats[:, 0:1], correction, jnp.zeros((KEY_VALUE_HEADS, 6, QROWS), jnp.float32)], axis=1
    )
    query_grad, all_kv_grad = attend_back(
        table, pair_one, query_scaled, scaled_grad, back_stats, all_kv
    )
    kv_grad = scatter_blocks(all_kv_grad.reshape(2, 4, 4, 2, 128, 2 * key_width), 2)
    kv_grad = kv_grad.reshape(128, KEY_VALUE_HEADS, 2, HEAD_SIZE)
    proj_grad = jnp.concatenate(
        [
            rotate(query_grad * 0.125, cosine, -sine),
            rotate(kv_grad[:, :, 0].reshape(128, key_width), cosine, -sine),
            kv_grad[:, :, 1].reshape(128, key_width),
        ],
        axis=1,
    ).astype(jnp.bfloat16)
    proj_grad = pad_halves(proj_grad, IN_HALF, IN_PAD)
    normed_one_grad = dot(proj_grad, weight_in, LAST)
    gain_one_grad = jnp.sum(normed_one_grad * start * scale_one, axis=0)
    through = norm_backward(start, scale_one, normed_one_grad * gain_first)
    input_grad = dot((resid_grad + through).astype(jnp.bfloat16), select, LAST).astype(jnp.bfloat16)

    grad_in = dot(normed_low, proj_grad, FIRST).astype(jnp.bfloat16)
    row = jnp.arange(PADDED)[:, None]
    lane = jnp.arange(IN_COLS)[None, :]
    gains_by_slot = jnp.stack([gain_one_grad, gain_two_grad]).reshape(2, 64, ROWS)
    gains_by_slot = jnp.pad(
        gains_by_slot.transpose(1, 0, 2), ((0, 0), (0, 0), (0, IN_PAD - ROWS))
    ).reshape(64, 1, IN_COLS)
    grad_in = jnp.where(
        row % ROWS == 15,
        jnp.broadcast_to(gains_by_slot, (64, ROWS, IN_COLS)).reshape(PADDED, IN_COLS).astype(jnp.bfloat16),
        grad_in,
    )
    in_sum = scatter_blocks(grad_in.reshape(2, 4, 4, 2, ROWS, IN_COLS), 3)
    out_sum = rest_sum[:, : 2 * OUT_PAD].astype(jnp.float32)

    def own_and_other(value, width):
        first, second = value[:, :width], value[:, width:]
        return jnp.where(half == 0, first, second), jnp.where(half == 0, second, first)

    own_in_sum, other_in_sum = own_and_other(in_sum, IN_PAD)
    own_out_sum, other_out_sum = own_and_other(out_sum, OUT_PAD)
    own_in_sum = own_in_sum + swap(other_in_sum.astype(jnp.bfloat16)).astype(jnp.float32)
    own_out_sum = own_out_sum + swap(other_out_sum.astype(jnp.bfloat16)).astype(jnp.float32)
    ffn_sum = rest_sum[:15, 2 * OUT_PAD :].astype(jnp.float32)
    return (
        layer_out[None],
        input_grad[None],
        own_in_sum[:15, :IN_HALF],
        own_out_sum[:15, :OUT_HALF],
        ffn_sum[:, : 2 * FF_HALF].reshape(15, 2, FF_HALF),
        ffn_sum[:, 2 * FF_HALF :],
        own_in_sum[15, :15].reshape(15, 1),
    )


def solution(mesh):
    in_specs = (
        P("fsdp", "ctx", None),
        P("fsdp", "ctx", None),
        P("fsdp", "ctx"),
        P("fsdp", "ctx"),
        P("ctx", "fsdp"),
        P("ctx", "fsdp"),
        P("ctx", None, "fsdp"),
        P("ctx", "fsdp"),
        P("ctx", "fsdp"),
    )
    out_specs = (
        P("fsdp", "ctx", None),
        P("fsdp", "ctx", None),
        P("ctx", "fsdp"),
        P("ctx", "fsdp"),
        P("ctx", None, "fsdp"),
        P("ctx", "fsdp"),
        P("ctx", "fsdp"),
    )
    return jax.shard_map(
        on_device, mesh=mesh, in_specs=in_specs, out_specs=out_specs, check_vma=False
    )
```

```python
import math

import jax
import jax.numpy as jnp
import numpy as np
from jax import lax
from jax.experimental import pallas as pl
from jax.experimental.pallas import tpu as pltpu
from jax.sharding import PartitionSpec as P

WIDTH = 960
QUERY_HEADS = 15
KEY_VALUE_HEADS = 5
GROUP = 3
HEAD_SIZE = 64
FF_HALF = 1280
FF_QUARTER = 640
EPSILON = 1e-05
ROWS = 16
PADDED = 1024
IN_HALF = 800
IN_PAD = 896
OUT_HALF = 480
OUT_PAD = 512
IN_COLS = 2 * IN_PAD
TILE = 512
QROWS = 384
MESH = pl.DeviceIdType.MESH
VMEM_LIMIT = 56 * 1024 * 1024


def column_map():
    cols = np.full((64, ROWS), -1, np.int32)
    cols[:, :15] = np.arange(64)[:, None] * 15 + np.arange(15)[None, :]
    return cols.reshape(-1)


COLUMN_MAP = column_map()


def coordinates():
    index = lax.axis_index("ctx")
    core = index % 2
    z = (index // 2) % 4
    y = (index // 8) % 4
    x = index // 32
    p1 = y * (1 - core) + z * core
    p2 = z * (1 - core) + y * core
    return x, p1, p2, core


def device_at(x, p1, p2, core):
    y = p1 * (1 - core) + p2 * core
    z = p2 * (1 - core) + p1 * core
    return ((x * 4 + y) * 4 + z) * 2 + core


def neighbours(x, p1, p2, core):
    index = lax.axis_index("ctx")
    return (
        device_at(1 - x, p1, p2, core),
        device_at(x, (p1 + 1) % 4, p2, core),
        device_at(x, (p1 + 3) % 4, p2, core),
        device_at(x, p1, (p2 + 1) % 4, core),
        device_at(x, p1, (p2 + 3) % 4, core),
        index + 1 - 2 * core,
    )


def block_of(ref, core, x, p1, p2):
    return ref.at[x, p1, p2, core] if core == 0 else ref.at[x, p2, p1, core]


def half_of(ref, core, x, p2):
    every = pl.ds(0, 4)
    return ref.at[x, every, p2, core] if core == 0 else ref.at[x, p2, every, core]


def slab_of(ref, core, p2):
    every = pl.ds(0, 4)
    both = pl.ds(0, 2)
    return ref.at[both, every, p2, core] if core == 0 else ref.at[both, p2, every, core]


def row_place():
    return lax.axis_index("fsdp") * 2 + lax.axis_index("ctx") // 32


def row_device(place):
    index = lax.axis_index("ctx")
    return {"fsdp": place // 2, "ctx": (place % 2) * 32 + index % 32}


def ctx_device(index):
    return {"ctx": index}


class Sender:
    def __init__(self, send_sem, recv_sem):
        self.send_sem, self.recv_sem, self.sent = send_sem, recv_sem, []

    def __call__(self, source, place, device):
        number = len(self.sent)
        copy = pltpu.make_async_remote_copy(
            src_ref=source,
            dst_ref=place,
            send_sem=self.send_sem.at[number],
            recv_sem=self.recv_sem.at[number],
            device_id=device,
            device_id_type=MESH,
        )
        copy.start()
        self.sent.append(copy)
        return copy

    def finish(self):
        for copy in self.sent:
            copy.wait_send()


class RowGather:
    def __init__(self, in_ref, out_ref, local_sem, send):
        self.out, self.send = out_ref, send
        here = row_place()
        self.left, self.right = (here + 3) % 4, (here + 1) % 4
        self.local = pltpu.make_async_copy(in_ref, out_ref.at[here], local_sem)
        self.local.start()
        self.from_left = send(in_ref, out_ref.at[here], row_device(self.right))
        self.from_right = send(in_ref, out_ref.at[here], row_device(self.left))

    def forward(self):
        rows = self.out.shape[1] // 2
        low, high = pl.ds(0, rows), pl.ds(rows, rows)
        self.from_left.wait_recv()
        place = self.out.at[self.left, low]
        self.far_low = self.send(place, place, row_device(self.right))
        self.from_right.wait_recv()
        place = self.out.at[self.right, high]
        self.far_high = self.send(place, place, row_device(self.left))

    def finish(self):
        self.far_low.wait_recv()
        self.far_high.wait_recv()
        self.local.wait()


class RowScatter:
    def __init__(self, in_ref, far, near_left, near_right, stage, send):
        self.p, self.far, self.stage, self.send = in_ref, far, stage, send
        self.near_left, self.near_right = near_left, near_right
        self.here = row_place()
        self.left, self.right = (self.here + 3) % 4, (self.here + 1) % 4
        to_left, to_right = row_device(self.left), row_device(self.right)
        opposite = (self.here + 2) % 4
        rows = in_ref.shape[1] // 2
        self.low, self.high = pl.ds(0, rows), pl.ds(rows, rows)
        low, high = self.low, self.high
        self.got_low = send(in_ref.at[opposite, low], far.at[0], to_right)
        self.got_high = send(in_ref.at[opposite, high], far.at[1], to_left)
        self.waits = [
            send(in_ref.at[self.right, high], near_left.at[high], to_right),
            send(in_ref.at[self.left, low], near_right.at[low], to_left),
        ]

    def forward(self):
        rows = self.p.shape[1] // 2
        self.got_low.wait_recv()
        self.stage[0] = self.p[self.right, 0:rows] + self.far[0]
        self.waits.append(
            self.send(self.stage.at[0], self.near_left.at[self.low], row_device(self.right))
        )
        self.got_high.wait_recv()
        self.stage[1] = self.p[self.left, rows : 2 * rows] + self.far[1]
        self.waits.append(
            self.send(self.stage.at[1], self.near_right.at[self.high], row_device(self.left))
        )

    def finish(self, out_ref):
        for copy in self.waits:
            copy.wait_recv()
        total = self.p[self.here].astype(jnp.float32) + self.near_left[...].astype(jnp.float32)
        out_ref[...] = total + self.near_right[...].astype(jnp.float32)


def greet(devices):
    barrier = pltpu.get_barrier_semaphore()
    for device in devices:
        pl.semaphore_signal(barrier, inc=1, device_id=device, device_id_type=MESH)
    pl.semaphore_wait(barrier, len(devices))


def greet_ctx(with_row):
    devices = [ctx_device(index) for index in neighbours(*coordinates())]
    if with_row:
        here = row_place()
        step = 2 * (here % 2) - 1
        devices.append(row_device((here + step + 4) % 4))
    greet(devices)


def row_kernel_entry():
    here = row_place()
    greet([row_device((here + 3) % 4), row_device((here + 1) % 4)])


def row_gather_kernel(in_ref, out_ref, local_sem, send_sem, recv_sem):
    row_kernel_entry()
    send = Sender(send_sem, recv_sem)
    row = RowGather(in_ref, out_ref, local_sem, send)
    row.forward()
    row.finish()
    send.finish()


def row_gather(block, collective_id):
    return pl.pallas_call(
        row_gather_kernel,
        out_shape=jax.ShapeDtypeStruct((4,) + block.shape, block.dtype),
        in_specs=[pl.BlockSpec(memory_space=pltpu.VMEM)],
        out_specs=pl.BlockSpec(memory_space=pltpu.VMEM),
        scratch_shapes=[
            pltpu.SemaphoreType.DMA,
            pltpu.SemaphoreType.DMA((4,)),
            pltpu.SemaphoreType.DMA((4,)),
        ],
        compiler_params=pltpu.CompilerParams(
            collective_id=collective_id, has_side_effects=True, vmem_limit_bytes=VMEM_LIMIT
        ),
    )(block)


def row_scatter_kernel(in_ref, out_ref, far, near_left, near_right, stage, send_sem, recv_sem):
    row_kernel_entry()
    send = Sender(send_sem, recv_sem)
    row = RowScatter(in_ref, far, near_left, near_right, stage, send)
    row.forward()
    row.finish(out_ref)
    send.finish()


def row_scratch(rows, columns):
    return [
        pltpu.VMEM((2, rows // 2, columns), jnp.bfloat16),
        pltpu.VMEM((rows, columns), jnp.bfloat16),
        pltpu.VMEM((rows, columns), jnp.bfloat16),
        pltpu.VMEM((2, rows // 2, columns), jnp.bfloat16),
        pltpu.SemaphoreType.DMA((6,)),
        pltpu.SemaphoreType.DMA((6,)),
    ]


def row_scatter(blocks, collective_id):
    rows, columns = blocks.shape[1:]
    return pl.pallas_call(
        row_scatter_kernel,
        out_shape=jax.ShapeDtypeStruct((rows, columns), jnp.float32),
        in_specs=[pl.BlockSpec(memory_space=pltpu.VMEM)],
        out_specs=pl.BlockSpec(memory_space=pltpu.VMEM),
        scratch_shapes=row_scratch(rows, columns),
        compiler_params=pltpu.CompilerParams(
            collective_id=collective_id, has_side_effects=True, vmem_limit_bytes=VMEM_LIMIT
        ),
    )(blocks)


class Group:
    def __init__(self, copies):
        self.copies = copies

    def wait_recv(self):
        for copy in self.copies:
            copy.wait_recv()


def gather_kernel(split, with_row, *refs):
    count = len(split)
    ins, refs = refs[: count + with_row], refs[count + with_row :]
    outs, refs = refs[: count + with_row], refs[count + with_row :]
    local_sem, send_sem, recv_sem, row_local, row_send, row_recv = refs
    greet_ctx(with_row)
    if with_row:
        row_sender = Sender(row_send, row_recv)
        row = RowGather(ins[-1], outs[-1], row_local, row_sender)
    core = coordinates()[3]
    for chosen in range(2):

        @pl.when(core == chosen)
        def _(chosen=chosen):
            gather_body(chosen, split, ins, outs, local_sem, send_sem, recv_sem)

    if with_row:
        row.forward()
        row.finish()
        row_sender.finish()


def gather_body(core, split, ins, outs, local_sem, send_sem, recv_sem):
    x, p1, p2, _ = coordinates()
    across, right1, left1, right2, left2, sibling = neighbours(x, p1, p2, core)
    p1p, p1m = (p1 + 1) % 4, (p1 + 3) % 4
    p2p, p2m, p2o = (p2 + 1) % 4, (p2 + 3) % 4, (p2 + 2) % 4
    sender = Sender(send_sem, recv_sem)
    arrays = range(len(split))
    mine = [ins[k].at[x] if split[k] else ins[k] for k in arrays]
    yours = [ins[k].at[1 - x] if split[k] else ins[k] for k in arrays]

    def send(places, to, sources=None):
        sources = places if sources is None else sources
        return Group([sender(sources[k], places[k], ctx_device(to)) for k in arrays])

    def block(side, q1):
        return [block_of(outs[k], core, side, q1, p2) for k in arrays]

    def half(side, q2):
        return [half_of(outs[k], core, side, q2) for k in arrays]

    here = block(x, p1)
    locals_ = [pltpu.make_async_copy(mine[k], here[k], local_sem.at[k]) for k in arrays]
    for copy in locals_:
        copy.start()
    crossed = send(here, across, yours)
    own_left = send(here, right1, mine)
    own_right = send(here, left1, mine)
    crossed.wait_recv()
    other_left = send(block(1 - x, p1), right1)
    other_right = send(block(1 - x, p1), left1)
    own_left.wait_recv()
    own_far = send(block(x, p1m), right1)
    own_right.wait_recv()
    own_far.wait_recv()
    for copy in locals_:
        copy.wait()
    own_left = send(half(x, p2), right2)
    own_right = send(half(x, p2), left2)
    last = [send(half(x, p2), sibling)]
    other_right.wait_recv()
    other_far = send(block(1 - x, p1p), left1)
    other_left.wait_recv()
    other_far.wait_recv()
    other_right = send(half(1 - x, p2), left2)
    other_left = send(half(1 - x, p2), right2)
    last.append(send(half(1 - x, p2), sibling))
    own_left.wait_recv()
    own_far = send(half(x, p2m), right2)
    last.append(send(half(x, p2m), sibling))
    own_right.wait_recv()
    last.append(send(half(x, p2p), sibling))
    other_right.wait_recv()
    other_far = send(half(1 - x, p2p), left2)
    last.append(send(half(1 - x, p2p), sibling))
    other_left.wait_recv()
    last.append(send(half(1 - x, p2m), sibling))
    own_far.wait_recv()
    last.append(send(half(x, p2o), sibling))
    other_far.wait_recv()
    last.append(send(half(1 - x, p2o), sibling))
    for group in last:
        group.wait_recv()
    sender.finish()


def gather_blocks(blocks, split, row_block, collective_id):
    with_row = row_block is not None
    operands = list(blocks)
    shapes = [
        jax.ShapeDtypeStruct((2, 4, 4, 2) + block.shape[-2:], block.dtype) for block in blocks
    ]
    if with_row:
        operands.append(row_block)
        shapes.append(jax.ShapeDtypeStruct((4,) + row_block.shape, row_block.dtype))
    number = 21 * len(blocks)
    return pl.pallas_call(
        lambda *refs: gather_kernel(split, int(with_row), *refs),
        out_shape=tuple(shapes),
        in_specs=[pl.BlockSpec(memory_space=pl.ANY)] * len(operands),
        out_specs=(pl.BlockSpec(memory_space=pl.ANY),) * len(operands),
        scratch_shapes=[
            pltpu.SemaphoreType.DMA((len(blocks),)),
            pltpu.SemaphoreType.DMA((number,)),
            pltpu.SemaphoreType.DMA((number,)),
            pltpu.SemaphoreType.DMA,
            pltpu.SemaphoreType.DMA((4,)),
            pltpu.SemaphoreType.DMA((4,)),
        ],
        compiler_params=pltpu.CompilerParams(
            collective_id=collective_id, has_side_effects=True
        ),
    )(*operands)


def scatter_kernel(widths, summed, with_row, *refs):
    count = len(widths)
    ins, refs = refs[:count], refs[count:]
    if with_row:
        row_in, refs = refs[0], refs[1:]
    out_ref, refs = refs[0], refs[1:]
    columns = sum(widths)
    if summed < columns:
        parts_ref, refs = refs[0], refs[1:]
    if with_row:
        row_out, refs = refs[0], refs[1:]
    (acc, other, far_low, far_high, near_left, near_right) = refs[:6]
    (pair_low, pair_high, pair_left, pair_right, last) = refs[6:11]
    (local_sem, cross_send, cross_recv, send_sem, recv_sem) = refs[11:16]
    x, p1, p2, core = coordinates()
    across, right1, left1, right2, left2, sibling = neighbours(x, p1, p2, core)
    greet_ctx(with_row)
    p1p, p1m, p1o = (p1 + 1) % 4, (p1 + 3) % 4, (p1 + 2) % 4
    p2p, p2m, p2o = (p2 + 1) % 4, (p2 + 3) % 4, (p2 + 2) % 4
    needed = (p2o, p2m, p2p, p2)
    theirs = (p1o, p1m, p1p, p1)
    starts = [sum(widths[:k]) for k in range(count)]
    sender = Sender(send_sem, recv_sem)

    def part(ref, place, array):
        if count == 1:
            return ref.at[place]
        every = [pl.ds(0, size) for size in ref.shape[1:-1]]
        return ref.at[tuple([place] + every + [pl.ds(starts[array], widths[array])])]

    def crossing(k, array, source):
        return pltpu.make_async_remote_copy(
            src_ref=source,
            dst_ref=part(other, theirs[k], array),
            send_sem=cross_send.at[k, array],
            recv_sem=cross_recv.at[k, array],
            device_id=ctx_device(sibling),
            device_id_type=MESH,
        )

    for chosen in range(2):

        @pl.when(core == chosen)
        def _(chosen=chosen):
            for k in range(4):
                for array in range(count):
                    crossing(k, array, slab_of(ins[array], 1 - chosen, theirs[k])).start()
                    pltpu.make_async_copy(
                        slab_of(ins[array], chosen, needed[k]),
                        part(acc, needed[k], array),
                        local_sem.at[k, array],
                    ).start()

    if with_row:
        row_sender = Sender(refs[20], refs[21])
        row = RowScatter(row_in, refs[16], refs[17], refs[18], refs[19], row_sender)

    def send(source, place, to):
        return sender(source, place, ctx_device(to))

    def add(place, term):
        @pl.loop(0, 4)
        def _(step):
            place[step] = place[step] + term[step]

    def add_both(side):
        @pl.loop(0, 4)
        def _(step):
            total = acc[p2, side, step].astype(jnp.float32)
            total = total + near_left[side, step].astype(jnp.float32)
            total = total + near_right[side, step].astype(jnp.float32)
            acc[p2, side, step] = total.astype(acc.dtype)

    def merge(k):
        for array in range(count):
            mine = part(acc, needed[k], array)
            pltpu.make_async_copy(mine, mine, local_sem.at[k, array]).wait()
            crossing(k, array, part(other, theirs[k], array)).wait_recv()
        for side in range(2):
            add(acc.at[needed[k], side], other.at[needed[k], side])

    merge(0)
    got_low = send(acc.at[p2o, 0], far_low, right2)
    got_high = send(acc.at[p2o, 1], far_high, left2)
    merge(1)
    right_low = send(acc.at[p2m, 0], near_right.at[0], left2)
    merge(2)
    left_high = send(acc.at[p2p, 1], near_left.at[1], right2)
    got_low.wait_recv()
    add(acc.at[p2p, 0], far_low)
    left_low = send(acc.at[p2p, 0], near_left.at[0], right2)
    got_high.wait_recv()
    add(acc.at[p2m, 1], far_high)
    right_high = send(acc.at[p2m, 1], near_right.at[1], left2)
    merge(3)
    if with_row:
        row.forward()
    right_low.wait_recv()
    left_low.wait_recv()
    add_both(0)
    got_low = send(acc.at[p2, 0, p1o], pair_low, right1)
    near_low = send(acc.at[p2, 0, p1m], pair_right.at[0], left1)
    left_high.wait_recv()
    right_high.wait_recv()
    add_both(1)
    got_high = send(acc.at[p2, 1, p1o], pair_high, left1)
    near_high = send(acc.at[p2, 1, p1p], pair_left.at[1], right1)
    got_low.wait_recv()
    acc[p2, 0, p1p] = acc[p2, 0, p1p] + pair_low[...]
    left_low = send(acc.at[p2, 0, p1p], pair_left.at[0], right1)
    got_high.wait_recv()
    acc[p2, 1, p1m] = acc[p2, 1, p1m] + pair_high[...]
    right_high = send(acc.at[p2, 1, p1m], pair_right.at[1], left1)
    if with_row:
        row.finish(row_out)
    near_low.wait_recv()
    near_high.wait_recv()
    left_low.wait_recv()
    right_high.wait_recv()

    @pl.loop(0, 2)
    def _(j):
        total = acc[p2, j, p1].astype(jnp.float32) + pair_left[j].astype(jnp.float32)
        total = total + pair_right[j].astype(jnp.float32)
        acc[p2, j, p1] = total.astype(acc.dtype)

    final = send(acc.at[p2, 1 - x, p1], last, across)
    final.wait_recv()
    own = acc[p2, x, p1]
    received = last[...]
    out_ref[...] = own[:, :summed].astype(jnp.float32) + received[:, :summed].astype(jnp.float32)
    if summed < columns:
        parts_ref[x] = own[:, summed:].astype(jnp.float32)
        parts_ref[1 - x] = received[:, summed:].astype(jnp.float32)
    for k in range(4):
        for array in range(count):
            crossing(k, array, part(other, theirs[k], array)).wait_send()
    sender.finish()
    if with_row:
        row_sender.finish()


def scatter_blocks(arrays, summed, row_blocks, collective_id):
    rows = arrays[0].shape[-2]
    widths = tuple(array.shape[-1] for array in arrays)
    columns = sum(widths)
    kind = arrays[0].dtype
    block = (rows, columns)
    with_row = row_blocks is not None
    operands = list(arrays)
    in_specs = [pl.BlockSpec(memory_space=pl.ANY)] * len(arrays)
    shapes = [jax.ShapeDtypeStruct((rows, summed), jnp.float32)]
    if summed < columns:
        shapes.append(jax.ShapeDtypeStruct((2, rows, columns - summed), jnp.float32))
    scratch = []
    if with_row:
        operands.append(row_blocks)
        in_specs.append(pl.BlockSpec(memory_space=pltpu.VMEM))
        shapes.append(jax.ShapeDtypeStruct(row_blocks.shape[1:], jnp.float32))
        scratch = row_scratch(*row_blocks.shape[1:])
    return pl.pallas_call(
        lambda *refs: scatter_kernel(widths, summed, with_row, *refs),
        out_shape=tuple(shapes),
        in_specs=in_specs,
        out_specs=(pl.BlockSpec(memory_space=pltpu.VMEM),) * len(shapes),
        scratch_shapes=[
            pltpu.VMEM((4, 2, 4) + block, kind),
            pltpu.VMEM((4, 2, 4) + block, kind),
            pltpu.VMEM((4,) + block, kind),
            pltpu.VMEM((4,) + block, kind),
            pltpu.VMEM((2, 4) + block, kind),
            pltpu.VMEM((2, 4) + block, kind),
            pltpu.VMEM(block, kind),
            pltpu.VMEM(block, kind),
            pltpu.VMEM((2,) + block, kind),
            pltpu.VMEM((2,) + block, kind),
            pltpu.VMEM(block, kind),
            pltpu.SemaphoreType.DMA((4, len(arrays))),
            pltpu.SemaphoreType.DMA((4, len(arrays))),
            pltpu.SemaphoreType.DMA((4, len(arrays))),
            pltpu.SemaphoreType.DMA((13,)),
            pltpu.SemaphoreType.DMA((13,)),
        ]
        + scratch,
        compiler_params=pltpu.CompilerParams(
            collective_id=collective_id, has_side_effects=True, vmem_limit_bytes=VMEM_LIMIT
        ),
    )(*operands)


LAST = (((1,), (1,)), ((), ()))
FIRST = (((0,), (0,)), ((), ()))
PLAIN = (((1,), (0,)), ((), ()))


def dot(a, b, dims=PLAIN):
    return lax.dot_general(a, b, dims, preferred_element_type=jnp.float32)


def load_tiles(table_ref, kv_hbm, kv, sems, tiles):
    @pl.loop(0, tiles)
    def _(tile):
        for j in range(8):
            block = tile * 8 + j
            pltpu.make_async_copy(
                kv_hbm.at[table_ref[block]],
                kv.at[pl.ds(pl.multiple_of(block * 64, 64), 64)],
                sems.at[tile],
            ).start()


def wait_tile(kv, sems, tile):
    part = kv.at[pl.ds(pl.multiple_of(tile * TILE, TILE), TILE)]
    pltpu.make_async_copy(part, part, sems.at[tile]).wait()


def visible_keys(tile, pair):
    key = tile * TILE + lax.broadcasted_iota(jnp.int32, (TILE, QROWS), 0)
    row = lax.broadcasted_iota(jnp.int32, (TILE, QROWS), 1)
    order = jnp.where(row < QROWS // 2, pair, 127 - pair) * 64 + row % 64
    return key <= order


def visible_high(tile, pair):
    shape = (TILE // 2, QROWS)
    row = lax.broadcasted_iota(jnp.int32, shape, 1)
    key = tile * TILE + lax.broadcasted_iota(jnp.int32, shape, 0)
    key = key + jnp.where(row < QROWS // 2, 0, TILE // 2)
    return key <= (127 - pair) * 64 + row % 64


def first_half():
    return lax.broadcasted_iota(jnp.int32, (128, QROWS), 1) < QROWS // 2


def wide_keys(kv, tile, columns):
    start = pl.multiple_of(tile * TILE, TILE)
    return jnp.concatenate(
        [
            kv[pl.ds(start, TILE // 2), columns],
            kv[pl.ds(pl.multiple_of(start + TILE // 2, TILE // 2), TILE // 2), columns],
        ],
        axis=1,
    )


def widen(source, place):
    for g in range(KEY_VALUE_HEADS):
        place[g] = jnp.zeros(place.shape[1:], place.dtype)
        place[g, : QROWS // 2, :128] = source[g, QROWS // 2 :, :]
        place[g, QROWS // 2 :, 128:] = source[g, QROWS // 2 :, :]


def spread_heads(source, place, offset):
    for g in range(KEY_VALUE_HEADS):
        place[g] = jnp.zeros(place.shape[1:], place.dtype)
        for half in range(2):
            for h in range(GROUP):
                column = (GROUP * g + h) * HEAD_SIZE
                start = (half * GROUP + h) * 64
                place[g, start : start + 64, offset : offset + 64] = source[
                    half * 64 : half * 64 + 64, column : column + 64
                ]


def collect_heads(g, half, values, place):
    for h in range(GROUP):
        column = (GROUP * g + h) * HEAD_SIZE
        place[half * 64 : half * 64 + 64, column : column + 64] = values[h * 64 : h * 64 + 64]


def run_tiles(pair, full_step, turn, high_step):
    low_tiles = (pair + 8) // 8
    high_tiles = (135 - pair) // 8

    @pl.loop(0, low_tiles - 1)
    def _(tile):
        full_step(tile, False)

    full_step(low_tiles - 1, True)
    turn()

    @pl.loop(low_tiles, high_tiles - 1)
    def _(tile):
        high_step(tile, False)

    high_step(high_tiles - 1, True)


def attend_kernel(
    table_ref, pair_ref, q_ref, kv_hbm, out_ref, stat_ref, kv, q, wide_q, acc, work, sems
):
    pair = pair_ref[0]
    high_tiles = (135 - pair) // 8
    load_tiles(table_ref, kv_hbm, kv, sems, high_tiles)
    spread_heads(q_ref, q, 0)
    widen(q, wide_q)
    low = slice(0, QROWS // 2)
    high = slice(QROWS // 2, QROWS)
    for g in range(KEY_VALUE_HEADS):
        acc[g] = jnp.zeros(acc.shape[1:], jnp.float32)
        work[g, 0:1, :] = jnp.full((1, QROWS), -1e30, jnp.float32)
        work[g, 1:8, :] = jnp.zeros((7, QROWS), jnp.float32)

    def soften(g, scores):
        before = work[g, 0:1, :]
        highest = jnp.maximum(before, jnp.max(scores, axis=0, keepdims=True))
        weights = jnp.exp(scores - highest)
        shrink = jnp.exp(before - highest)
        work[g, 0:1, :] = highest
        work[g, 1:2, :] = work[g, 1:2, :] * shrink + jnp.sum(weights, axis=0, keepdims=True)
        return weights.astype(jnp.bfloat16), shrink

    def full_step(tile, masked):
        wait_tile(kv, sems, tile)
        if masked:
            seen = visible_keys(tile, pair)
        for g in range(KEY_VALUE_HEADS):
            keys = kv[pl.ds(pl.multiple_of(tile * TILE, TILE), TILE), g * 128 : g * 128 + 128]
            scores = dot(keys, q[g], LAST)
            if masked:
                scores = jnp.where(seen, scores, -1e30)
            weights, shrink = soften(g, scores)
            acc[g] = acc[g] * shrink + dot(keys, weights, FIRST)

    def turn():
        for g in range(KEY_VALUE_HEADS):
            values = acc[g, 64:128, low] / work[g, 1:2, low]
            collect_heads(g, 0, values.T, out_ref)
            stat_ref[g] = work[g]
            acc[g, :, low] = jnp.zeros((128, QROWS // 2), jnp.float32)
            work[g, 0:1, low] = jnp.full((1, QROWS // 2), -1e30, jnp.float32)
            work[g, 1:2, low] = jnp.zeros((1, QROWS // 2), jnp.float32)

    def high_step(tile, masked):
        wait_tile(kv, sems, tile)
        if masked:
            seen = visible_high(tile, pair)
        for g in range(KEY_VALUE_HEADS):
            keys = wide_keys(kv, tile, slice(g * 128, g * 128 + 128))
            scores = dot(keys, wide_q[g], LAST)
            if masked:
                scores = jnp.where(seen, scores, -1e30)
            weights, shrink = soften(g, scores)
            mixed = dot(keys, weights, FIRST)
            acc[g] = acc[g] * shrink + jnp.where(first_half(), mixed[:128], mixed[128:])

    run_tiles(pair, full_step, turn, high_step)
    for g in range(KEY_VALUE_HEADS):
        first, second = work[g, 0:1, low], work[g, 0:1, high]
        highest = jnp.maximum(first, second)
        first, second = jnp.exp(first - highest), jnp.exp(second - highest)
        total = work[g, 1:2, low] * first + work[g, 1:2, high] * second
        stat_ref[g, 0:1, high] = highest
        stat_ref[g, 1:2, high] = total
        values = (acc[g, 64:128, low] * first + acc[g, 64:128, high] * second) / total
        collect_heads(g, 1, values.T, out_ref)


def attend(table, pair, q, kv):
    return pl.pallas_call(
        attend_kernel,
        out_shape=(
            jax.ShapeDtypeStruct((128, WIDTH), jnp.float32),
            jax.ShapeDtypeStruct((KEY_VALUE_HEADS, 8, QROWS), jnp.float32),
        ),
        in_specs=[
            pl.BlockSpec(memory_space=pltpu.SMEM),
            pl.BlockSpec(memory_space=pltpu.SMEM),
            pl.BlockSpec(memory_space=pltpu.VMEM),
            pl.BlockSpec(memory_space=pl.ANY),
        ],
        out_specs=(
            pl.BlockSpec(memory_space=pltpu.VMEM),
            pl.BlockSpec(memory_space=pltpu.VMEM),
        ),
        scratch_shapes=[
            pltpu.VMEM((8192, 640), jnp.bfloat16),
            pltpu.VMEM((KEY_VALUE_HEADS, QROWS, 128), jnp.bfloat16),
            pltpu.VMEM((KEY_VALUE_HEADS, QROWS, 256), jnp.bfloat16),
            pltpu.VMEM((KEY_VALUE_HEADS, 128, QROWS), jnp.float32),
            pltpu.VMEM((KEY_VALUE_HEADS, 8, QROWS), jnp.float32),
            pltpu.SemaphoreType.DMA((16,)),
        ],
        compiler_params=pltpu.CompilerParams(vmem_limit_bytes=VMEM_LIMIT),
        cost_estimate=pl.CostEstimate(
            flops=4 * 10**9, bytes_accessed=10**7, transcendentals=8 * 10**6
        ),
    )(table, pair, q, kv)


def attend_back_kernel(
    table_ref,
    pair_ref,
    q_ref,
    g_ref,
    stat_ref,
    kv_hbm,
    dq_ref,
    dkv_hbm,
    kv,
    dkv,
    q,
    gs,
    wide_q,
    wide_g,
    acc,
    wide_acc,
    work,
    sems,
    out_sems,
):
    pair = pair_ref[0]
    high_tiles = (135 - pair) // 8
    load_tiles(table_ref, kv_hbm, kv, sems, high_tiles)
    spread_heads(q_ref, q, 0)
    spread_heads(g_ref, gs, 64)
    widen(q, wide_q)
    widen(gs, wide_g)
    low = slice(0, QROWS // 2)
    high = slice(QROWS // 2, QROWS)
    for g in range(KEY_VALUE_HEADS):
        acc[g] = jnp.zeros(acc.shape[1:], jnp.float32)
        wide_acc[g] = jnp.zeros(acc.shape[1:], jnp.float32)
        work[g, :, low] = stat_ref[g, :, high]
        work[g, :, high] = stat_ref[g, :, high]

    def store(tile):
        for j in range(8):
            block = tile * 8 + j
            pltpu.make_async_copy(
                dkv.at[pl.ds(pl.multiple_of(block * 64, 64), 64)],
                dkv_hbm.at[table_ref[block]],
                out_sems.at[tile],
            ).start()

    @pl.loop(high_tiles, 16)
    def _(tile):
        dkv[pl.ds(pl.multiple_of(tile * TILE, TILE), TILE), :] = jnp.zeros(
            (TILE, 640), jnp.bfloat16
        )
        store(tile)

    def gradients(g, stats, keys, queries, grads, seen):
        scores = dot(keys, queries, LAST)
        if seen is not None:
            scores = jnp.where(seen, scores, -1e30)
        probs = jnp.exp(scores - stats[g, 0:1, :])
        prob_grad = dot(keys, grads, LAST)
        score_grad = (probs * (prob_grad - stats[g, 1:2, :])).astype(jnp.bfloat16)
        both = dot(score_grad, queries) + dot(probs.astype(jnp.bfloat16), grads)
        return dot(keys, score_grad, FIRST), both.astype(jnp.bfloat16)

    def full_step(tile, masked):
        wait_tile(kv, sems, tile)
        part = pl.ds(pl.multiple_of(tile * TILE, TILE), TILE)
        seen = visible_keys(tile, pair) if masked else None
        for g in range(KEY_VALUE_HEADS):
            columns = slice(g * 128, g * 128 + 128)
            change, both = gradients(g, stat_ref, kv[part, columns], q[g], gs[g], seen)
            acc[g] = acc[g] + change
            dkv[part, columns] = both
        store(tile)

    def high_step(tile, masked):
        wait_tile(kv, sems, tile)
        start = pl.multiple_of(tile * TILE, TILE)
        middle = pl.multiple_of(start + TILE // 2, TILE // 2)
        seen = visible_high(tile, pair) if masked else None
        for g in range(KEY_VALUE_HEADS):
            columns = slice(g * 128, g * 128 + 128)
            keys = wide_keys(kv, tile, columns)
            change, both = gradients(g, work, keys, wide_q[g], wide_g[g], seen)
            wide_acc[g] = wide_acc[g] + jnp.where(first_half(), change[:128], change[128:])
            dkv[pl.ds(start, TILE // 2), columns] = both[:, :128]
            dkv[pl.ds(middle, TILE // 2), columns] = both[:, 128:]
        store(tile)

    run_tiles(pair, full_step, lambda: None, high_step)
    for g in range(KEY_VALUE_HEADS):
        collect_heads(g, 0, acc[g, 0:64, low].T, dq_ref)
        total = acc[g, 0:64, high] + wide_acc[g, 0:64, low] + wide_acc[g, 0:64, high]
        collect_heads(g, 1, total.T, dq_ref)

    @pl.loop(0, 16)
    def _(tile):
        part = dkv.at[pl.ds(pl.multiple_of(tile * TILE, TILE), TILE)]
        pltpu.make_async_copy(part, part, out_sems.at[tile]).wait()


def attend_back(table, pair, q, scaled_grad, stats, kv):
    return pl.pallas_call(
        attend_back_kernel,
        out_shape=(
            jax.ShapeDtypeStruct((128, WIDTH), jnp.float32),
            jax.ShapeDtypeStruct((128, 64, 640), jnp.bfloat16),
        ),
        in_specs=[
            pl.BlockSpec(memory_space=pltpu.SMEM),
            pl.BlockSpec(memory_space=pltpu.SMEM),
            pl.BlockSpec(memory_space=pltpu.VMEM),
            pl.BlockSpec(memory_space=pltpu.VMEM),
            pl.BlockSpec(memory_space=pltpu.VMEM),
            pl.BlockSpec(memory_space=pl.ANY),
        ],
        out_specs=(
            pl.BlockSpec(memory_space=pltpu.VMEM),
            pl.BlockSpec(memory_space=pl.ANY),
        ),
        scratch_shapes=[
            pltpu.VMEM((8192, 640), jnp.bfloat16),
            pltpu.VMEM((8192, 640), jnp.bfloat16),
            pltpu.VMEM((KEY_VALUE_HEADS, QROWS, 128), jnp.bfloat16),
            pltpu.VMEM((KEY_VALUE_HEADS, QROWS, 128), jnp.bfloat16),
            pltpu.VMEM((KEY_VALUE_HEADS, QROWS, 256), jnp.bfloat16),
            pltpu.VMEM((KEY_VALUE_HEADS, QROWS, 256), jnp.bfloat16),
            pltpu.VMEM((KEY_VALUE_HEADS, 128, QROWS), jnp.float32),
            pltpu.VMEM((KEY_VALUE_HEADS, 128, QROWS), jnp.float32),
            pltpu.VMEM((KEY_VALUE_HEADS, 8, QROWS), jnp.float32),
            pltpu.SemaphoreType.DMA((16,)),
            pltpu.SemaphoreType.DMA((16,)),
        ],
        compiler_params=pltpu.CompilerParams(vmem_limit_bytes=VMEM_LIMIT),
        cost_estimate=pl.CostEstimate(
            flops=10**10, bytes_accessed=2 * 10**7, transcendentals=8 * 10**6
        ),
    )(table, pair, q, scaled_grad, stats, kv)


def rotate(values, cosine, sine):
    heads = values.shape[1] // HEAD_SIZE
    shaped = values.reshape(values.shape[0], heads, 2, HEAD_SIZE // 2)
    first, second = shaped[:, :, 0], shaped[:, :, 1]
    return jnp.stack(
        [first * cosine - second * sine, second * cosine + first * sine], axis=2
    ).reshape(values.shape)


def swap(value):
    return lax.ppermute(value, "fsdp", [(0, 1), (1, 0)])


def pad_columns(value, columns):
    return jnp.pad(value, ((0, 0), (0, columns - value.shape[1])))


def pad_halves(value, half, padded):
    return jnp.concatenate(
        [pad_columns(value[:, :half], padded), pad_columns(value[:, half:], padded)], axis=1
    )


def norm_backward(rows, scale, weighted):
    inner = jnp.sum(weighted * rows, axis=-1, keepdims=True)
    return scale * weighted - rows * scale**3 * inner / WIDTH


def on_device(
    inputs,
    cotangent,
    positions,
    pair_index,
    input_projection,
    project_out,
    gate_up,
    down_weight,
    norm_gains,
):
    half = lax.axis_index("fsdp")
    pair = pair_index[0, 0]
    key_width = KEY_VALUE_HEADS * HEAD_SIZE
    select = (
        lax.broadcasted_iota(jnp.int32, (WIDTH, PADDED), 0) == jnp.asarray(COLUMN_MAP)[None, :]
    ).astype(jnp.bfloat16)

    spare = jnp.pad(norm_gains.T, ((0, 0), (0, 1)))
    own_in = pad_columns(
        jnp.concatenate([input_projection, pad_columns(spare, IN_HALF)], axis=0), IN_PAD
    )
    other_in = swap(own_in)
    own_out = jnp.pad(project_out, ((0, 1), (0, OUT_PAD - OUT_HALF)))
    other_out = swap(own_out)

    def in_order(own, other):
        return jnp.concatenate(
            [jnp.where(half == 0, own, other), jnp.where(half == 0, other, own)], axis=1
        )

    gate_up_parts = gate_up.reshape(15, 2, 2, FF_QUARTER).transpose(2, 0, 1, 3)
    gate_up_parts = gate_up_parts.reshape(2, 15, 2 * FF_QUARTER)
    down_parts = down_weight.reshape(15, 2, FF_QUARTER).transpose(1, 0, 2)
    spare_row = ((0, 0), (0, 1), (0, 0))
    upstream = dot(cotangent[0], select)
    blob = in_order(own_in, other_in).at[15, 32].set(pair.astype(jnp.bfloat16))
    weight_in, weight_out, weight_gu, weight_down, row_cotangent = gather_blocks(
        (
            blob,
            in_order(own_out, other_out),
            jnp.pad(gate_up_parts, spare_row),
            jnp.pad(down_parts, spare_row),
        ),
        (False, False, True, True),
        upstream.astype(jnp.bfloat16),
        0,
    )
    weight_in = weight_in.reshape(PADDED, IN_COLS)
    weight_out = weight_out.reshape(PADDED, 2 * OUT_PAD)
    weight_gu = weight_gu.reshape(PADDED, 2 * FF_QUARTER)
    weight_down = weight_down.reshape(PADDED, FF_QUARTER)
    row_cotangent = row_cotangent.reshape(512, PADDED)
    spare_rows = weight_in.reshape(64, ROWS, IN_COLS)[:, 15]
    gain_first = spare_rows[:, :ROWS].reshape(PADDED).astype(jnp.float32)
    gain_second = spare_rows[:, IN_PAD : IN_PAD + ROWS].reshape(PADDED).astype(jnp.float32)
    held = jnp.arange(PADDED) % ROWS < 15
    gain_first = jnp.where(held, gain_first, 0.0)
    gain_second = jnp.where(held, gain_second, 0.0)
    labels = spare_rows[:, 32].astype(jnp.int32)
    slots = jnp.arange(64, dtype=jnp.int32)
    blocks = jnp.stack([labels, 127 - labels], axis=1).reshape(128)
    places = jnp.stack([2 * slots, 2 * slots + 1], axis=1).reshape(128)
    hits = blocks[None, :] == jnp.arange(128, dtype=jnp.int32)[:, None]
    table = jnp.sum(jnp.where(hits, places[None, :], 0), axis=1)

    start = dot(inputs[0], select)
    freqs = jnp.exp(
        -math.log(10000.0) * jnp.arange(HEAD_SIZE // 2, dtype=jnp.float32) * 2.0 / HEAD_SIZE
    )
    angle = positions[0].astype(jnp.float32)[:, None] * freqs[None, :]
    cosine = jnp.cos(angle)[:, None, :]
    sine = jnp.sin(angle)[:, None, :]
    scale_one = lax.rsqrt(jnp.sum(start * start, axis=-1, keepdims=True) / WIDTH + EPSILON)
    normed_low = (start * scale_one * gain_first).astype(jnp.bfloat16)
    projected = dot(normed_low, weight_in)
    projected = jnp.concatenate(
        [projected[:, :IN_HALF], projected[:, IN_PAD : IN_PAD + IN_HALF]], axis=1
    )
    query_low = rotate(projected[:, :WIDTH], cosine, sine).astype(jnp.bfloat16)
    query_scaled = query_low * jnp.bfloat16(0.125)
    key_low = rotate(projected[:, WIDTH : WIDTH + key_width], cosine, sine).astype(jnp.bfloat16)
    value_low = projected[:, WIDTH + key_width :].astype(jnp.bfloat16)
    key_value = jnp.stack(
        [
            key_low.reshape(128, KEY_VALUE_HEADS, HEAD_SIZE),
            value_low.reshape(128, KEY_VALUE_HEADS, HEAD_SIZE),
        ],
        axis=2,
    ).reshape(128, 2 * key_width)
    all_kv = gather_blocks((key_value,), (False,), None, 1)[0].reshape(128, 64, 2 * key_width)
    pair_one = pair.reshape(1)
    attention, stats = attend(table, pair_one, query_scaled, all_kv)
    mixed_low = pad_halves(attention.astype(jnp.bfloat16), OUT_HALF, OUT_PAD)
    branch = dot(mixed_low, weight_out, LAST)
    resid = start + jnp.where(held, branch, 0.0)
    scale_two = lax.rsqrt(jnp.sum(resid * resid, axis=-1, keepdims=True) / WIDTH + EPSILON)
    normed_two = (resid * scale_two * gain_second).astype(jnp.bfloat16)
    row_normed = row_gather(normed_two, 2).reshape(512, PADDED)
    gate_vals = dot(row_normed, weight_gu)
    gate = gate_vals[:, :FF_QUARTER]
    upper = gate_vals[:, FF_QUARTER:]
    sigma = jax.nn.sigmoid(gate)
    silu_vals = gate * sigma
    hidden_low = (silu_vals * upper).astype(jnp.bfloat16)
    ffn_out = dot(hidden_low, weight_down, LAST)
    hidden_grad = dot(row_cotangent, weight_down)
    gate_grad = hidden_grad * upper * sigma * (1.0 + gate * (1.0 - sigma))
    upper_grad = hidden_grad * silu_vals
    gate_up_grad = jnp.concatenate([gate_grad, upper_grad], axis=1).astype(jnp.bfloat16)
    normed_two_grad = dot(gate_up_grad, weight_gu, LAST)
    normed_two_grad = row_scatter(
        normed_two_grad.astype(jnp.bfloat16).reshape(4, 128, PADDED), 3
    )
    resid_grad = upstream + norm_backward(resid, scale_two, normed_two_grad * gain_second)
    gain_two_grad = jnp.sum(normed_two_grad * resid * scale_two, axis=0)
    branch_grad_low = resid_grad.astype(jnp.bfloat16)
    grad_out = dot(branch_grad_low, mixed_low, FIRST).astype(jnp.bfloat16)
    grad_gu = dot(row_normed, gate_up_grad, FIRST).astype(jnp.bfloat16)
    grad_down = dot(row_cotangent, hidden_low, FIRST).astype(jnp.bfloat16)
    mixed_grad = dot(branch_grad_low, weight_out)
    mixed_grad = jnp.concatenate(
        [mixed_grad[:, :OUT_HALF], mixed_grad[:, OUT_PAD : OUT_PAD + OUT_HALF]], axis=1
    ).reshape(128, QUERY_HEADS, HEAD_SIZE)
    totals = stats[:, 1]
    totals_by_token = jnp.transpose(
        totals.reshape(KEY_VALUE_HEADS, 2, GROUP, 64), (1, 3, 0, 2)
    ).reshape(128, QUERY_HEADS)
    delta = jnp.sum(mixed_grad * attention.reshape(128, QUERY_HEADS, HEAD_SIZE), axis=-1)
    scaled_grad = (mixed_grad / totals_by_token[..., None]).astype(jnp.bfloat16).reshape(128, WIDTH)
    correction = jnp.transpose(
        (delta / totals_by_token).reshape(2, 64, KEY_VALUE_HEADS, GROUP), (2, 0, 3, 1)
    ).reshape(KEY_VALUE_HEADS, 1, QROWS)
    back_stats = jnp.concatenate(
        [stats[:, 0:1], correction, jnp.zeros((KEY_VALUE_HEADS, 6, QROWS), jnp.float32)], axis=1
    )
    query_grad, all_kv_grad = attend_back(
        table, pair_one, query_scaled, scaled_grad, back_stats, all_kv
    )
    kv_grad, ffn_out = scatter_blocks(
        (all_kv_grad.reshape(2, 4, 4, 2, 128, 2 * key_width),),
        2 * key_width,
        ffn_out.astype(jnp.bfloat16).reshape(4, 128, PADDED),
        4,
    )
    layer_out = dot((resid + ffn_out).astype(jnp.bfloat16), select, LAST).astype(jnp.bfloat16)
    kv_grad = kv_grad.reshape(128, KEY_VALUE_HEADS, 2, HEAD_SIZE)
    proj_grad = jnp.concatenate(
        [
            rotate(query_grad * 0.125, cosine, -sine),
            rotate(kv_grad[:, :, 0].reshape(128, key_width), cosine, -sine),
            kv_grad[:, :, 1].reshape(128, key_width),
        ],
        axis=1,
    ).astype(jnp.bfloat16)
    proj_grad = pad_halves(proj_grad, IN_HALF, IN_PAD)
    normed_one_grad = dot(proj_grad, weight_in, LAST)
    gain_one_grad = jnp.sum(normed_one_grad * start * scale_one, axis=0)
    through = norm_backward(start, scale_one, normed_one_grad * gain_first)
    input_grad = dot((resid_grad + through).astype(jnp.bfloat16), select, LAST).astype(jnp.bfloat16)

    grad_in = dot(normed_low, proj_grad, FIRST).astype(jnp.bfloat16)
    row = jnp.arange(PADDED)[:, None]
    lane = jnp.arange(IN_COLS)[None, :]
    gains_by_slot = jnp.stack([gain_one_grad, gain_two_grad]).reshape(2, 64, ROWS)
    gains_by_slot = jnp.pad(
        gains_by_slot.transpose(1, 0, 2), ((0, 0), (0, 0), (0, IN_PAD - ROWS))
    ).reshape(64, 1, IN_COLS)
    grad_in = jnp.where(
        row % ROWS == 15,
        jnp.broadcast_to(gains_by_slot, (64, ROWS, IN_COLS)).reshape(PADDED, IN_COLS).astype(jnp.bfloat16),
        grad_in,
    )
    att_sum, ffn_parts = scatter_blocks(
        tuple(
            grad.reshape(2, 4, 4, 2, ROWS, grad.shape[1])
            for grad in (grad_in, grad_out, grad_gu, grad_down)
        ),
        IN_COLS + 2 * OUT_PAD,
        None,
        5,
    )
    in_sum, out_sum = att_sum[:, :IN_COLS], att_sum[:, IN_COLS:]

    def own_and_other(value, width):
        first, second = value[:, :width], value[:, width:]
        return jnp.where(half == 0, first, second), jnp.where(half == 0, second, first)

    own_in_sum, other_in_sum = own_and_other(in_sum, IN_PAD)
    own_out_sum, other_out_sum = own_and_other(out_sum, OUT_PAD)
    swapped = swap(jnp.concatenate([other_in_sum, other_out_sum], axis=1).astype(jnp.bfloat16))
    own_in_sum = own_in_sum + swapped[:, :IN_PAD].astype(jnp.float32)
    own_out_sum = own_out_sum + swapped[:, IN_PAD:].astype(jnp.float32)
    gu_sum = ffn_parts[:, :15, : 2 * FF_QUARTER].reshape(2, 15, 2, FF_QUARTER)
    return (
        layer_out[None],
        input_grad[None],
        own_in_sum[:15, :IN_HALF],
        own_out_sum[:15, :OUT_HALF],
        gu_sum.transpose(1, 2, 0, 3).reshape(15, 2, FF_HALF),
        ffn_parts[:, :15, 2 * FF_QUARTER :].transpose(1, 0, 2).reshape(15, FF_HALF),
        own_in_sum[15, :15].reshape(15, 1),
    )


def solution(mesh):
    in_specs = (
        P("fsdp", "ctx", None),
        P("fsdp", "ctx", None),
        P("fsdp", "ctx"),
        P("fsdp", "ctx"),
        P("ctx", "fsdp"),
        P("ctx", "fsdp"),
        P("ctx", None, "fsdp"),
        P("ctx", "fsdp"),
        P("ctx", "fsdp"),
    )
    out_specs = (
        P("fsdp", "ctx", None),
        P("fsdp", "ctx", None),
        P("ctx", "fsdp"),
        P("ctx", "fsdp"),
        P("ctx", None, "fsdp"),
        P("ctx", "fsdp"),
        P("ctx", "fsdp"),
    )
    return jax.shard_map(
        on_device, mesh=mesh, in_specs=in_specs, out_specs=out_specs, check_vma=False
    )
```

```python
import math

import jax
import jax.numpy as jnp
import numpy as np
from jax import lax
from jax.experimental import pallas as pl
from jax.experimental.pallas import tpu as pltpu
from jax.sharding import PartitionSpec as P

WIDTH = 960
QUERY_HEADS = 15
KEY_VALUE_HEADS = 5
GROUP = 3
HEAD_SIZE = 64
FF_HALF = 1280
FF_QUARTER = 640
EPSILON = 1e-05
ROWS = 16
PADDED = 1024
IN_HALF = 800
IN_PAD = 896
OUT_HALF = 480
OUT_PAD = 512
IN_COLS = 2 * IN_PAD
TILE = 512
QROWS = 384
MESH = pl.DeviceIdType.MESH
VMEM_LIMIT = 56 * 1024 * 1024


def column_map():
    cols = np.full((64, ROWS), -1, np.int32)
    cols[:, :15] = np.arange(64)[:, None] * 15 + np.arange(15)[None, :]
    return cols.reshape(-1)


COLUMN_MAP = column_map()


def coordinates():
    index = lax.axis_index("ctx")
    core = index % 2
    z = (index // 2) % 4
    y = (index // 8) % 4
    x = index // 32
    p1 = y * (1 - core) + z * core
    p2 = z * (1 - core) + y * core
    return x, p1, p2, core


def device_at(x, p1, p2, core):
    y = p1 * (1 - core) + p2 * core
    z = p2 * (1 - core) + p1 * core
    return ((x * 4 + y) * 4 + z) * 2 + core


def neighbours(x, p1, p2, core):
    index = lax.axis_index("ctx")
    return (
        device_at(1 - x, p1, p2, core),
        device_at(x, (p1 + 1) % 4, p2, core),
        device_at(x, (p1 + 3) % 4, p2, core),
        device_at(x, p1, (p2 + 1) % 4, core),
        device_at(x, p1, (p2 + 3) % 4, core),
        index + 1 - 2 * core,
    )


def block_of(ref, core, x, p1, p2):
    return ref.at[x, p1, p2, core] if core == 0 else ref.at[x, p2, p1, core]


def half_of(ref, core, x, p2):
    every = pl.ds(0, 4)
    return ref.at[x, every, p2, core] if core == 0 else ref.at[x, p2, every, core]


def slab_of(ref, core, p2):
    every = pl.ds(0, 4)
    both = pl.ds(0, 2)
    return ref.at[both, every, p2, core] if core == 0 else ref.at[both, p2, every, core]


def row_place():
    return lax.axis_index("fsdp") * 2 + lax.axis_index("ctx") // 32


def row_device(place):
    index = lax.axis_index("ctx")
    return {"fsdp": place // 2, "ctx": (place % 2) * 32 + index % 32}


def ctx_device(index):
    return {"ctx": index}


class Sender:
    def __init__(self, send_sem, recv_sem):
        self.send_sem, self.recv_sem, self.sent = send_sem, recv_sem, []

    def __call__(self, source, place, device):
        number = len(self.sent)
        copy = pltpu.make_async_remote_copy(
            src_ref=source,
            dst_ref=place,
            send_sem=self.send_sem.at[number],
            recv_sem=self.recv_sem.at[number],
            device_id=device,
            device_id_type=MESH,
        )
        copy.start()
        self.sent.append(copy)
        return copy

    def finish(self):
        for copy in self.sent:
            copy.wait_send()


class RowGather:
    def __init__(self, in_ref, out_ref, local_sem, send):
        self.out, self.send = out_ref, send
        here = row_place()
        self.left, self.right = (here + 3) % 4, (here + 1) % 4
        self.local = pltpu.make_async_copy(in_ref, out_ref.at[here], local_sem)
        self.local.start()
        self.from_left = send(in_ref, out_ref.at[here], row_device(self.right))
        self.from_right = send(in_ref, out_ref.at[here], row_device(self.left))

    def forward(self):
        rows = self.out.shape[1] // 2
        low, high = pl.ds(0, rows), pl.ds(rows, rows)
        self.from_left.wait_recv()
        place = self.out.at[self.left, low]
        self.far_low = self.send(place, place, row_device(self.right))
        self.from_right.wait_recv()
        place = self.out.at[self.right, high]
        self.far_high = self.send(place, place, row_device(self.left))

    def finish(self):
        self.far_low.wait_recv()
        self.far_high.wait_recv()
        self.local.wait()


class RowScatter:
    def __init__(self, in_ref, far, near_left, near_right, stage, send):
        self.p, self.far, self.stage, self.send = in_ref, far, stage, send
        self.near_left, self.near_right = near_left, near_right
        self.here = row_place()
        self.left, self.right = (self.here + 3) % 4, (self.here + 1) % 4
        to_left, to_right = row_device(self.left), row_device(self.right)
        opposite = (self.here + 2) % 4
        rows = in_ref.shape[1] // 2
        self.low, self.high = pl.ds(0, rows), pl.ds(rows, rows)
        low, high = self.low, self.high
        self.got_low = send(in_ref.at[opposite, low], far.at[0], to_right)
        self.got_high = send(in_ref.at[opposite, high], far.at[1], to_left)
        self.waits = [
            send(in_ref.at[self.right, high], near_left.at[high], to_right),
            send(in_ref.at[self.left, low], near_right.at[low], to_left),
        ]

    def forward(self):
        rows = self.p.shape[1] // 2
        self.got_low.wait_recv()
        self.stage[0] = self.p[self.right, 0:rows] + self.far[0]
        self.waits.append(
            self.send(self.stage.at[0], self.near_left.at[self.low], row_device(self.right))
        )
        self.got_high.wait_recv()
        self.stage[1] = self.p[self.left, rows : 2 * rows] + self.far[1]
        self.waits.append(
            self.send(self.stage.at[1], self.near_right.at[self.high], row_device(self.left))
        )

    def finish(self, out_ref):
        for copy in self.waits:
            copy.wait_recv()
        total = self.p[self.here].astype(jnp.float32) + self.near_left[...].astype(jnp.float32)
        out_ref[...] = total + self.near_right[...].astype(jnp.float32)


def greet(devices):
    barrier = pltpu.get_barrier_semaphore()
    for device in devices:
        pl.semaphore_signal(barrier, inc=1, device_id=device, device_id_type=MESH)
    pl.semaphore_wait(barrier, len(devices))


def greet_ctx(with_row):
    devices = [ctx_device(index) for index in neighbours(*coordinates())]
    if with_row:
        here = row_place()
        step = 2 * (here % 2) - 1
        devices.append(row_device((here + step + 4) % 4))
    greet(devices)


def row_kernel_entry():
    here = row_place()
    greet([row_device((here + 3) % 4), row_device((here + 1) % 4)])


def row_gather_kernel(in_ref, out_ref, local_sem, send_sem, recv_sem):
    row_kernel_entry()
    send = Sender(send_sem, recv_sem)
    row = RowGather(in_ref, out_ref, local_sem, send)
    row.forward()
    row.finish()
    send.finish()


def row_gather(block, collective_id):
    return pl.pallas_call(
        row_gather_kernel,
        out_shape=jax.ShapeDtypeStruct((4,) + block.shape, block.dtype),
        in_specs=[pl.BlockSpec(memory_space=pltpu.VMEM)],
        out_specs=pl.BlockSpec(memory_space=pltpu.VMEM),
        scratch_shapes=[
            pltpu.SemaphoreType.DMA,
            pltpu.SemaphoreType.DMA((4,)),
            pltpu.SemaphoreType.DMA((4,)),
        ],
        compiler_params=pltpu.CompilerParams(
            collective_id=collective_id, has_side_effects=True, vmem_limit_bytes=VMEM_LIMIT
        ),
    )(block)


def row_scatter_kernel(in_ref, out_ref, far, near_left, near_right, stage, send_sem, recv_sem):
    row_kernel_entry()
    send = Sender(send_sem, recv_sem)
    row = RowScatter(in_ref, far, near_left, near_right, stage, send)
    row.forward()
    row.finish(out_ref)
    send.finish()


def row_scratch(rows, columns):
    return [
        pltpu.VMEM((2, rows // 2, columns), jnp.bfloat16),
        pltpu.VMEM((rows, columns), jnp.bfloat16),
        pltpu.VMEM((rows, columns), jnp.bfloat16),
        pltpu.VMEM((2, rows // 2, columns), jnp.bfloat16),
        pltpu.SemaphoreType.DMA((6,)),
        pltpu.SemaphoreType.DMA((6,)),
    ]


def row_scatter(blocks, collective_id):
    rows, columns = blocks.shape[1:]
    return pl.pallas_call(
        row_scatter_kernel,
        out_shape=jax.ShapeDtypeStruct((rows, columns), jnp.float32),
        in_specs=[pl.BlockSpec(memory_space=pltpu.VMEM)],
        out_specs=pl.BlockSpec(memory_space=pltpu.VMEM),
        scratch_shapes=row_scratch(rows, columns),
        compiler_params=pltpu.CompilerParams(
            collective_id=collective_id, has_side_effects=True, vmem_limit_bytes=VMEM_LIMIT
        ),
    )(blocks)


class Group:
    def __init__(self, copies):
        self.copies = copies

    def wait_recv(self):
        for copy in self.copies:
            copy.wait_recv()


def gather_kernel(modes, with_row, *refs):
    count = len(modes)
    ins, refs = refs[: count + with_row], refs[count + with_row :]
    outs, refs = refs[: count + with_row], refs[count + with_row :]
    greet_ctx("row" in modes or with_row)
    core = coordinates()[3]
    for chosen in range(2):

        @pl.when(core == chosen)
        def _(chosen=chosen):
            gather_body(chosen, modes, with_row, ins, outs, *refs)


def gather_body(
    core, modes, with_row, ins, outs, local_sem, send_sem, recv_sem, row_local, row_send, row_recv
):
    x, p1, p2, _ = coordinates()
    across, right1, left1, right2, left2, sibling = neighbours(x, p1, p2, core)
    p1p, p1m = (p1 + 1) % 4, (p1 + 3) % 4
    p2p, p2m, p2o = (p2 + 1) % 4, (p2 + 3) % 4, (p2 + 2) % 4
    place = row_place()
    row_left, row_right = (place + 3) % 4, (place + 1) % 4
    sender = Sender(send_sem, recv_sem)
    arrays = range(len(modes))
    plain = [k for k in arrays if modes[k] != "row"]
    rows = [k for k in arrays if modes[k] == "row"]
    mine = [ins[k].at[x] if modes[k] == "split" else ins[k] for k in arrays]
    yours = [ins[k].at[1 - x] if modes[k] == "split" else ins[k] for k in arrays]

    def send(places, to, chosen=arrays, sources=None):
        sources = places if sources is None else sources
        return Group([sender(sources[k], places[k], ctx_device(to)) for k in chosen])

    def block(side, q1):
        return [block_of(outs[k], core, side, q1, p2) for k in arrays]

    def half(side, q2):
        return [half_of(outs[k], core, side, q2) for k in arrays]

    def slot(k, owner):
        width = ins[k].shape[-1]
        columns = pl.ds(pl.multiple_of((owner // 2) * width, 128), width)
        return block_of(outs[k], core, owner % 2, p1, p2).at[pl.ds(0, ROWS), columns]

    here = block(x, p1)
    there = block(1 - x, p1)
    locals_ = [
        pltpu.make_async_copy(
            mine[k], slot(k, place) if k in rows else here[k], local_sem.at[k]
        )
        for k in arrays
    ]
    for copy in locals_:
        copy.start()
    row_near = Group(
        [
            sender(ins[k], slot(k, place), row_device(to))
            for to in (row_right, row_left)
            for k in rows
        ]
    )
    crossed = send(here, across, plain, yours)
    own_left = send(here, right1, plain, mine)
    own_right = send(here, left1, plain, mine)
    row_near.wait_recv()
    row_far = Group(
        [sender(slot(k, row_left), slot(k, row_left), row_device(row_right)) for k in rows]
    )
    crossed.wait_recv()
    other_left = send(there, right1)
    other_right = send(there, left1)
    for copy in locals_:
        copy.wait()
    row_far.wait_recv()
    own_left.copies += send(here, right1, rows).copies
    own_right.copies += send(here, left1, rows).copies
    if with_row:
        row_sender = Sender(row_send, row_recv)
        row = RowGather(ins[-1], outs[-1], row_local, row_sender)
    own_left.wait_recv()
    own_far = send(block(x, p1m), right1)
    own_right.wait_recv()
    own_far.wait_recv()
    own_left = send(half(x, p2), right2)
    own_right = send(half(x, p2), left2)
    last = [send(half(x, p2), sibling)]
    other_right.wait_recv()
    other_far = send(block(1 - x, p1p), left1)
    other_left.wait_recv()
    other_far.wait_recv()
    other_right = send(half(1 - x, p2), left2)
    other_left = send(half(1 - x, p2), right2)
    last.append(send(half(1 - x, p2), sibling))
    own_left.wait_recv()
    own_far = send(half(x, p2m), right2)
    last.append(send(half(x, p2m), sibling))
    own_right.wait_recv()
    last.append(send(half(x, p2p), sibling))
    if with_row:
        row.forward()
    other_right.wait_recv()
    other_far = send(half(1 - x, p2p), left2)
    last.append(send(half(1 - x, p2p), sibling))
    other_left.wait_recv()
    last.append(send(half(1 - x, p2m), sibling))
    own_far.wait_recv()
    last.append(send(half(x, p2o), sibling))
    if with_row:
        row.finish()
    other_far.wait_recv()
    last.append(send(half(1 - x, p2o), sibling))
    for group in last:
        group.wait_recv()
    sender.finish()
    if with_row:
        row_sender.finish()


def gather_blocks(blocks, modes, row_block, collective_id):
    with_row = row_block is not None
    operands = list(blocks)
    shapes = [
        jax.ShapeDtypeStruct(
            (2, 4, 4, 2, block.shape[-2], block.shape[-1] * (2 if mode == "row" else 1)),
            block.dtype,
        )
        for block, mode in zip(blocks, modes)
    ]
    if with_row:
        operands.append(row_block)
        shapes.append(jax.ShapeDtypeStruct((4,) + row_block.shape, row_block.dtype))
    number = 23 * len(blocks)
    return pl.pallas_call(
        lambda *refs: gather_kernel(modes, int(with_row), *refs),
        out_shape=tuple(shapes),
        in_specs=[pl.BlockSpec(memory_space=pl.ANY)] * len(operands),
        out_specs=(pl.BlockSpec(memory_space=pl.ANY),) * len(operands),
        scratch_shapes=[
            pltpu.SemaphoreType.DMA((len(blocks),)),
            pltpu.SemaphoreType.DMA((number,)),
            pltpu.SemaphoreType.DMA((number,)),
            pltpu.SemaphoreType.DMA,
            pltpu.SemaphoreType.DMA((4,)),
            pltpu.SemaphoreType.DMA((4,)),
        ],
        compiler_params=pltpu.CompilerParams(
            collective_id=collective_id, has_side_effects=True
        ),
    )(*operands)


def scatter_kernel(pieces, halved, with_row, *refs):
    count = 1 + max(piece[0] for piece in pieces)
    ins, refs = refs[:count], refs[count:]
    if with_row:
        row_in, refs = refs[0], refs[1:]
    out_ref, refs = refs[0], refs[1:]
    if halved:
        parts_ref, refs = refs[0], refs[1:]
    if with_row:
        row_out, refs = refs[0], refs[1:]
    (acc, other, far_low, far_high, near_left, near_right) = refs[:6]
    (pair_low, pair_high, pair_left, pair_right, last) = refs[6:11]
    (local_sem, cross_send, cross_recv, send_sem, recv_sem) = refs[11:16]
    x, p1, p2, core = coordinates()
    across, right1, left1, right2, left2, sibling = neighbours(x, p1, p2, core)
    greet_ctx(with_row or halved)
    p1p, p1m, p1o = (p1 + 1) % 4, (p1 + 3) % 4, (p1 + 2) % 4
    p2p, p2m, p2o = (p2 + 1) % 4, (p2 + 3) % 4, (p2 + 2) % 4
    needed = (p2o, p2m, p2p, p2)
    theirs = (p1o, p1m, p1p, p1)
    sender = Sender(send_sem, recv_sem)

    def part(ref, place, piece):
        if len(pieces) == 1:
            return ref.at[place]
        every = [pl.ds(0, size) for size in ref.shape[1:-1]]
        return ref.at[tuple([place] + every + [pl.ds(pieces[piece][3], pieces[piece][2])])]

    def source_of(piece, chosen, place):
        array, start, width, _ = pieces[piece]
        slab = slab_of(ins[array], chosen, place)
        if len(pieces) == 1:
            return slab
        every = [pl.ds(0, size) for size in slab.shape[:-1]]
        return slab.at[tuple(every + [pl.ds(start, width)])]

    def crossing(k, piece, source):
        return pltpu.make_async_remote_copy(
            src_ref=source,
            dst_ref=part(other, theirs[k], piece),
            send_sem=cross_send.at[k, piece],
            recv_sem=cross_recv.at[k, piece],
            device_id=ctx_device(sibling),
            device_id_type=MESH,
        )

    for chosen in range(2):

        @pl.when(core == chosen)
        def _(chosen=chosen):
            for k in range(4):
                for piece in range(len(pieces)):
                    crossing(k, piece, source_of(piece, 1 - chosen, theirs[k])).start()
                    pltpu.make_async_copy(
                        source_of(piece, chosen, needed[k]),
                        part(acc, needed[k], piece),
                        local_sem.at[k, piece],
                    ).start()

    if with_row:
        row_sender = Sender(refs[20], refs[21])
        row = RowScatter(row_in, refs[16], refs[17], refs[18], refs[19], row_sender)

    def send(source, place, to):
        return sender(source, place, ctx_device(to))

    def add(place, term):
        @pl.loop(0, 4)
        def _(step):
            place[step] = place[step] + term[step]

    def add_both(side):
        @pl.loop(0, 4)
        def _(step):
            total = acc[p2, side, step].astype(jnp.float32)
            total = total + near_left[side, step].astype(jnp.float32)
            total = total + near_right[side, step].astype(jnp.float32)
            acc[p2, side, step] = total.astype(acc.dtype)

    def merge(k):
        for piece in range(len(pieces)):
            mine = part(acc, needed[k], piece)
            pltpu.make_async_copy(mine, mine, local_sem.at[k, piece]).wait()
            crossing(k, piece, part(other, theirs[k], piece)).wait_recv()
        for side in range(2):
            add(acc.at[needed[k], side], other.at[needed[k], side])

    merge(0)
    got_low = send(acc.at[p2o, 0], far_low, right2)
    got_high = send(acc.at[p2o, 1], far_high, left2)
    merge(1)
    right_low = send(acc.at[p2m, 0], near_right.at[0], left2)
    merge(2)
    left_high = send(acc.at[p2p, 1], near_left.at[1], right2)
    got_low.wait_recv()
    add(acc.at[p2p, 0], far_low)
    left_low = send(acc.at[p2p, 0], near_left.at[0], right2)
    got_high.wait_recv()
    add(acc.at[p2m, 1], far_high)
    right_high = send(acc.at[p2m, 1], near_right.at[1], left2)
    merge(3)
    if with_row:
        row.forward()
    right_low.wait_recv()
    left_low.wait_recv()
    add_both(0)
    got_low = send(acc.at[p2, 0, p1o], pair_low, right1)
    near_low = send(acc.at[p2, 0, p1m], pair_right.at[0], left1)
    left_high.wait_recv()
    right_high.wait_recv()
    add_both(1)
    got_high = send(acc.at[p2, 1, p1o], pair_high, left1)
    near_high = send(acc.at[p2, 1, p1p], pair_left.at[1], right1)
    got_low.wait_recv()
    acc[p2, 0, p1p] = acc[p2, 0, p1p] + pair_low[...]
    left_low = send(acc.at[p2, 0, p1p], pair_left.at[0], right1)
    got_high.wait_recv()
    acc[p2, 1, p1m] = acc[p2, 1, p1m] + pair_high[...]
    right_high = send(acc.at[p2, 1, p1m], pair_right.at[1], left1)
    if with_row:
        row.finish(row_out)
    near_low.wait_recv()
    near_high.wait_recv()
    left_low.wait_recv()
    right_high.wait_recv()

    @pl.loop(0, 2)
    def _(j):
        total = acc[p2, j, p1].astype(jnp.float32) + pair_left[j].astype(jnp.float32)
        total = total + pair_right[j].astype(jnp.float32)
        acc[p2, j, p1] = total.astype(acc.dtype)

    if halved:
        finish_row(halved, acc, p1, p2, refs[16:20], last, sender, out_ref, parts_ref)
    else:
        final = send(acc.at[p2, 1 - x, p1], last, across)
        final.wait_recv()
        out_ref[...] = acc[p2, x, p1].astype(jnp.float32) + last[...].astype(jnp.float32)
    for k in range(4):
        for piece in range(len(pieces)):
            crossing(k, piece, part(other, theirs[k], piece)).wait_send()
    sender.finish()
    if with_row:
        row_sender.finish()


def finish_row(halved, acc, p1, p2, buffers, last, sender, out_ref, parts_ref):
    far, from_left, from_right, stage = buffers
    here = row_place()
    left, right, opposite = (here + 3) % 4, (here + 1) % 4, (here + 2) % 4
    x = here % 2
    every = pl.ds(0, ROWS)
    rest = pl.ds(2 * halved, acc.shape[-1] - 2 * halved)

    def columns(owner):
        return pl.ds(pl.multiple_of((owner // 2) * halved, 128), halved)

    def block(owner):
        return acc.at[p2, owner % 2, p1, every, columns(owner)]

    far_copy = sender(block(opposite), far, row_device(right))
    from_right_copy = sender(block(left), from_right, row_device(left))
    x_neighbour = row_device((here // 2) * 2 + 1 - x)
    parts_copy = sender(acc.at[p2, 1 - x, p1, every, rest], last, x_neighbour)
    far_copy.wait_recv()
    stage[...] = acc[p2, right % 2, p1, :, columns(right)] + far[...]
    from_left_copy = sender(stage, from_left, row_device(right))
    parts_ref[x] = acc[p2, x, p1, :, rest].astype(jnp.float32)
    parts_copy.wait_recv()
    parts_ref[1 - x] = last[...].astype(jnp.float32)
    from_right_copy.wait_recv()
    from_left_copy.wait_recv()
    total = acc[p2, x, p1, :, columns(here)].astype(jnp.float32)
    total = total + from_left[...].astype(jnp.float32)
    out_ref[...] = total + from_right[...].astype(jnp.float32)


def scatter_blocks(arrays, pieces, halved, row_blocks, collective_id):
    rows = arrays[0].shape[-2]
    columns = sum(piece[2] for piece in pieces)
    kind = arrays[0].dtype
    block = (rows, columns)
    with_row = row_blocks is not None
    operands = list(arrays)
    in_specs = [pl.BlockSpec(memory_space=pl.ANY)] * len(arrays)
    shapes = [jax.ShapeDtypeStruct((rows, halved or columns), jnp.float32)]
    last = block
    scratch = []
    if halved:
        last = (rows, columns - 2 * halved)
        shapes.append(jax.ShapeDtypeStruct((2,) + last, jnp.float32))
        scratch = [pltpu.VMEM((rows, halved), kind)] * 4
    if with_row:
        operands.append(row_blocks)
        in_specs.append(pl.BlockSpec(memory_space=pltpu.VMEM))
        shapes.append(jax.ShapeDtypeStruct(row_blocks.shape[1:], jnp.float32))
        scratch = row_scratch(*row_blocks.shape[1:])
    return pl.pallas_call(
        lambda *refs: scatter_kernel(pieces, halved, with_row, *refs),
        out_shape=tuple(shapes),
        in_specs=in_specs,
        out_specs=(pl.BlockSpec(memory_space=pltpu.VMEM),) * len(shapes),
        scratch_shapes=[
            pltpu.VMEM((4, 2, 4) + block, kind),
            pltpu.VMEM((4, 2, 4) + block, kind),
            pltpu.VMEM((4,) + block, kind),
            pltpu.VMEM((4,) + block, kind),
            pltpu.VMEM((2, 4) + block, kind),
            pltpu.VMEM((2, 4) + block, kind),
            pltpu.VMEM(block, kind),
            pltpu.VMEM(block, kind),
            pltpu.VMEM((2,) + block, kind),
            pltpu.VMEM((2,) + block, kind),
            pltpu.VMEM(last, kind),
            pltpu.SemaphoreType.DMA((4, len(pieces))),
            pltpu.SemaphoreType.DMA((4, len(pieces))),
            pltpu.SemaphoreType.DMA((4, len(pieces))),
            pltpu.SemaphoreType.DMA((16,)),
            pltpu.SemaphoreType.DMA((16,)),
        ]
        + scratch,
        compiler_params=pltpu.CompilerParams(
            collective_id=collective_id, has_side_effects=True, vmem_limit_bytes=VMEM_LIMIT
        ),
    )(*operands)


LAST = (((1,), (1,)), ((), ()))
FIRST = (((0,), (0,)), ((), ()))
PLAIN = (((1,), (0,)), ((), ()))


def dot(a, b, dims=PLAIN):
    return lax.dot_general(a, b, dims, preferred_element_type=jnp.float32)


def load_tiles(table_ref, kv_hbm, kv, sems, tiles):
    @pl.loop(0, tiles)
    def _(tile):
        for j in range(8):
            block = tile * 8 + j
            pltpu.make_async_copy(
                kv_hbm.at[table_ref[block]],
                kv.at[pl.ds(pl.multiple_of(block * 64, 64), 64)],
                sems.at[tile],
            ).start()


def wait_tile(kv, sems, tile):
    part = kv.at[pl.ds(pl.multiple_of(tile * TILE, TILE), TILE)]
    pltpu.make_async_copy(part, part, sems.at[tile]).wait()


def visible_keys(tile, pair, first_row, rows):
    shape = (rows, TILE)
    row = first_row + lax.broadcasted_iota(jnp.int32, shape, 0)
    key = tile * TILE + lax.broadcasted_iota(jnp.int32, shape, 1)
    order = jnp.where(row < QROWS // 2, pair, 127 - pair) * 64 + row % 64
    return key <= order


def head_parts():
    for g in range(KEY_VALUE_HEADS):
        for half in range(2):
            for h in range(GROUP):
                rows = slice((half * GROUP + h) * 64, (half * GROUP + h) * 64 + 64)
                column = (GROUP * g + h) * HEAD_SIZE
                yield g, rows, slice(half * 64, half * 64 + 64), slice(column, column + 64)


def run_tiles(pair, step):
    low_tiles = (pair + 8) // 8
    high_tiles = (135 - pair) // 8

    @pl.loop(0, low_tiles - 1)
    def _(tile):
        step(tile, 0, QROWS, False)

    step(low_tiles - 1, 0, QROWS, True)

    @pl.loop(low_tiles, high_tiles - 1)
    def _(tile):
        step(tile, QROWS // 2, QROWS // 2, False)

    step(high_tiles - 1, QROWS // 2, QROWS // 2, True)


def lane_parts(value):
    return [value[:, k * 128 : k * 128 + 128] for k in range(TILE // 128)]


def attend_kernel(table_ref, pair_ref, q_ref, kv_hbm, out_ref, top_ref, sum_ref, kv, q, acc, sems):
    pair = pair_ref[0]
    high_tiles = (135 - pair) // 8
    load_tiles(table_ref, kv_hbm, kv, sems, high_tiles)
    q[...] = jnp.zeros(q.shape, q.dtype)
    for g, rows, tokens, columns in head_parts():
        q[g, rows, 0:64] = q_ref[tokens, columns]
    acc[...] = jnp.zeros(acc.shape, jnp.float32)
    top_ref[...] = jnp.full(top_ref.shape, -1e30, jnp.float32)
    sum_ref[...] = jnp.zeros(sum_ref.shape, jnp.float32)

    def step(tile, first_row, rows, masked):
        wait_tile(kv, sems, tile)
        span = slice(first_row, first_row + rows)
        if masked:
            seen = visible_keys(tile, pair, first_row, rows)
        heads = range(KEY_VALUE_HEADS)
        keys = [
            kv[pl.ds(pl.multiple_of(tile * TILE, TILE), TILE), g * 128 : g * 128 + 128]
            for g in heads
        ]
        scores = [dot(q[g, span, :], keys[g], LAST) for g in heads]
        if masked:
            scores = [jnp.where(seen, score, -1e30) for score in scores]
        parts = [lane_parts(score) for score in scores]
        best = [
            jnp.maximum(jnp.maximum(p[0], p[1]), jnp.maximum(p[2], p[3])) for p in parts
        ]
        before = [top_ref[g, span, :] for g in heads]
        highest = [
            jnp.maximum(before[g], jnp.max(best[g], axis=1, keepdims=True)) for g in heads
        ]
        shrink = [jnp.exp(before[g] - highest[g]) for g in heads]
        parts = [[jnp.exp(part - highest[g]) for part in parts[g]] for g in heads]
        for g in heads:
            p = parts[g]
            top_ref[g, span, :] = highest[g]
            sum_ref[g, span, :] = sum_ref[g, span, :] * shrink[g] + ((p[0] + p[1]) + (p[2] + p[3]))
        mixed = [
            dot(jnp.concatenate([p.astype(jnp.bfloat16) for p in parts[g]], axis=1), keys[g])
            for g in heads
        ]
        for g in heads:
            acc[g, span, :] = acc[g, span, :] * shrink[g] + mixed[g]

    run_tiles(pair, step)
    for g in range(KEY_VALUE_HEADS):
        total = jnp.sum(sum_ref[g], axis=1, keepdims=True)
        sum_ref[g] = jnp.broadcast_to(total, sum_ref.shape[1:])
        acc[g] = acc[g] / sum_ref[g]
    for g, rows, tokens, columns in head_parts():
        out_ref[tokens, columns] = acc[g, rows, 64:128]


def attend(table, pair, q, kv):
    heads = (KEY_VALUE_HEADS, QROWS, 128)
    return pl.pallas_call(
        attend_kernel,
        out_shape=(
            jax.ShapeDtypeStruct((128, WIDTH), jnp.float32),
            jax.ShapeDtypeStruct(heads, jnp.float32),
            jax.ShapeDtypeStruct(heads, jnp.float32),
        ),
        in_specs=[
            pl.BlockSpec(memory_space=pltpu.SMEM),
            pl.BlockSpec(memory_space=pltpu.SMEM),
            pl.BlockSpec(memory_space=pltpu.VMEM),
            pl.BlockSpec(memory_space=pl.ANY),
        ],
        out_specs=(pl.BlockSpec(memory_space=pltpu.VMEM),) * 3,
        scratch_shapes=[
            pltpu.VMEM((8192, 640), jnp.bfloat16),
            pltpu.VMEM(heads, jnp.bfloat16),
            pltpu.VMEM(heads, jnp.float32),
            pltpu.SemaphoreType.DMA((16,)),
        ],
        compiler_params=pltpu.CompilerParams(vmem_limit_bytes=VMEM_LIMIT),
        cost_estimate=pl.CostEstimate(
            flops=4 * 10**9, bytes_accessed=10**7, transcendentals=8 * 10**6
        ),
    )(table, pair, q, kv)


def attend_back_kernel(
    table_ref,
    pair_ref,
    q_ref,
    grad_ref,
    out_ref,
    top_ref,
    sum_ref,
    kv_hbm,
    dq_ref,
    dkv_hbm,
    kv,
    dkv,
    q,
    gs,
    q_turned,
    g_turned,
    shift,
    acc,
    sems,
    out_sems,
):
    pair = pair_ref[0]
    high_tiles = (135 - pair) // 8
    load_tiles(table_ref, kv_hbm, kv, sems, high_tiles)

    def store(tile):
        for j in range(8):
            block = tile * 8 + j
            pltpu.make_async_copy(
                dkv.at[pl.ds(pl.multiple_of(block * 64, 64), 64)],
                dkv_hbm.at[table_ref[block]],
                out_sems.at[tile],
            ).start()

    @pl.loop(high_tiles, 16)
    def _(tile):
        dkv[pl.ds(pl.multiple_of(tile * TILE, TILE), TILE), :] = jnp.zeros(
            (TILE, 640), jnp.bfloat16
        )
        store(tile)

    q[...] = jnp.zeros(q.shape, q.dtype)
    gs[...] = jnp.zeros(gs.shape, gs.dtype)
    for g, rows, tokens, columns in head_parts():
        q[g, rows, 0:64] = q_ref[tokens, columns]
        grad = grad_ref[tokens, columns]
        total = sum_ref[g, rows, :]
        gs[g, rows, 64:128] = (grad / total[:, 0:64]).astype(jnp.bfloat16)
        delta = jnp.sum(grad * out_ref[tokens, columns], axis=1, keepdims=True)
        shift[g, rows, :] = delta / total
    for g in range(KEY_VALUE_HEADS):
        q_turned[g] = q[g].T
        g_turned[g] = gs[g].T
    acc[...] = jnp.zeros(acc.shape, jnp.float32)

    def step(tile, first_row, rows, masked):
        wait_tile(kv, sems, tile)
        span = slice(first_row, first_row + rows)
        part = pl.ds(pl.multiple_of(tile * TILE, TILE), TILE)
        if masked:
            seen = visible_keys(tile, pair, first_row, rows)
        heads = range(KEY_VALUE_HEADS)
        keys = [kv[part, g * 128 : g * 128 + 128] for g in heads]
        scores = [dot(q[g, span, :], keys[g], LAST) for g in heads]
        prob_grad = [dot(gs[g, span, :], keys[g], LAST) for g in heads]
        if masked:
            scores = [jnp.where(seen, score, -1e30) for score in scores]
        score_grad, probs_low = [], []
        for g in heads:
            top, moved = top_ref[g, span, :], shift[g, span, :]
            probs = [jnp.exp(part_ - top) for part_ in lane_parts(scores[g])]
            grads = [
                (probs[k] * (part_ - moved)).astype(jnp.bfloat16)
                for k, part_ in enumerate(lane_parts(prob_grad[g]))
            ]
            score_grad.append(jnp.concatenate(grads, axis=1))
            probs_low.append(
                jnp.concatenate([prob.astype(jnp.bfloat16) for prob in probs], axis=1)
            )
        change = [dot(score_grad[g], keys[g]) for g in heads]
        both = [
            dot(q_turned[g, :, span], score_grad[g]) + dot(g_turned[g, :, span], probs_low[g])
            for g in heads
        ]
        for g in heads:
            acc[g, span, :] = acc[g, span, :] + change[g]
            dkv[part, g * 128 : g * 128 + 128] = both[g].astype(jnp.bfloat16).T
        store(tile)

    run_tiles(pair, step)
    for g, rows, tokens, columns in head_parts():
        dq_ref[tokens, columns] = acc[g, rows, 0:64]

    @pl.loop(0, 16)
    def _(tile):
        part = dkv.at[pl.ds(pl.multiple_of(tile * TILE, TILE), TILE)]
        pltpu.make_async_copy(part, part, out_sems.at[tile]).wait()


def attend_back(table, pair, q, grad, out, top, total, kv):
    heads = (KEY_VALUE_HEADS, QROWS, 128)
    turned = (KEY_VALUE_HEADS, 128, QROWS)
    return pl.pallas_call(
        attend_back_kernel,
        out_shape=(
            jax.ShapeDtypeStruct((128, WIDTH), jnp.float32),
            jax.ShapeDtypeStruct((128, 64, 640), jnp.bfloat16),
        ),
        in_specs=[pl.BlockSpec(memory_space=pltpu.SMEM)] * 2
        + [pl.BlockSpec(memory_space=pltpu.VMEM)] * 5
        + [pl.BlockSpec(memory_space=pl.ANY)],
        out_specs=(
            pl.BlockSpec(memory_space=pltpu.VMEM),
            pl.BlockSpec(memory_space=pl.ANY),
        ),
        scratch_shapes=[
            pltpu.VMEM((8192, 640), jnp.bfloat16),
            pltpu.VMEM((8192, 640), jnp.bfloat16),
            pltpu.VMEM(heads, jnp.bfloat16),
            pltpu.VMEM(heads, jnp.bfloat16),
            pltpu.VMEM(turned, jnp.bfloat16),
            pltpu.VMEM(turned, jnp.bfloat16),
            pltpu.VMEM(heads, jnp.float32),
            pltpu.VMEM(heads, jnp.float32),
            pltpu.SemaphoreType.DMA((16,)),
            pltpu.SemaphoreType.DMA((16,)),
        ],
        compiler_params=pltpu.CompilerParams(vmem_limit_bytes=VMEM_LIMIT),
        cost_estimate=pl.CostEstimate(
            flops=10**10, bytes_accessed=2 * 10**7, transcendentals=8 * 10**6
        ),
    )(table, pair, q, grad, out, top, total, kv)


def rotate(values, cosine, sine):
    heads = values.shape[1] // HEAD_SIZE
    shaped = values.reshape(values.shape[0], heads, 2, HEAD_SIZE // 2)
    first, second = shaped[:, :, 0], shaped[:, :, 1]
    return jnp.stack(
        [first * cosine - second * sine, second * cosine + first * sine], axis=2
    ).reshape(values.shape)


def pad_columns(value, columns):
    return jnp.pad(value, ((0, 0), (0, columns - value.shape[1])))


def pad_halves(value, half, padded):
    return jnp.concatenate(
        [pad_columns(value[:, :half], padded), pad_columns(value[:, half:], padded)], axis=1
    )


def norm_backward(rows, scale, weighted):
    inner = jnp.sum(weighted * rows, axis=-1, keepdims=True)
    return scale * weighted - rows * scale**3 * inner / WIDTH


def on_device(
    inputs,
    cotangent,
    positions,
    pair_index,
    input_projection,
    project_out,
    gate_up,
    down_weight,
    norm_gains,
):
    half = lax.axis_index("fsdp")
    pair = pair_index[0, 0]
    key_width = KEY_VALUE_HEADS * HEAD_SIZE
    select = (
        lax.broadcasted_iota(jnp.int32, (WIDTH, PADDED), 0) == jnp.asarray(COLUMN_MAP)[None, :]
    ).astype(jnp.bfloat16)

    spare = jnp.pad(norm_gains.T, ((0, 0), (0, 1)))
    own_in = pad_columns(
        jnp.concatenate([input_projection, pad_columns(spare, IN_HALF)], axis=0), IN_PAD
    )
    own_in = own_in.at[15, ROWS].set(pair.astype(jnp.bfloat16))
    own_out = jnp.pad(project_out, ((0, 1), (0, OUT_PAD - OUT_HALF)))
    gate_up_parts = gate_up.reshape(15, 2, 2, FF_QUARTER).transpose(2, 0, 1, 3)
    gate_up_parts = gate_up_parts.reshape(2, 15, 2 * FF_QUARTER)
    down_parts = down_weight.reshape(15, 2, FF_QUARTER).transpose(1, 0, 2)
    spare_row = ((0, 0), (0, 1), (0, 0))
    upstream = dot(cotangent[0], select)
    weight_in, weight_out, weight_gu, weight_down, row_cotangent = gather_blocks(
        (
            own_in,
            own_out,
            jnp.pad(gate_up_parts, spare_row),
            jnp.pad(down_parts, spare_row),
        ),
        ("row", "row", "split", "split"),
        upstream.astype(jnp.bfloat16),
        0,
    )
    weight_in = weight_in.reshape(PADDED, IN_COLS)
    weight_out = weight_out.reshape(PADDED, 2 * OUT_PAD)
    weight_gu = weight_gu.reshape(PADDED, 2 * FF_QUARTER)
    weight_down = weight_down.reshape(PADDED, FF_QUARTER)
    row_cotangent = row_cotangent.reshape(512, PADDED)
    blocks_in = weight_in.reshape(64, ROWS, IN_COLS)
    spare_first = blocks_in[:, 15, : 2 * ROWS]
    spare_second = blocks_in[:, 15, IN_PAD : IN_PAD + 2 * ROWS]
    gain_first = spare_first[:, :ROWS].reshape(PADDED).astype(jnp.float32)
    gain_second = spare_second[:, :ROWS].reshape(PADDED).astype(jnp.float32)
    held = jnp.arange(PADDED) % ROWS < 15
    gain_first = jnp.where(held, gain_first, 0.0)
    gain_second = jnp.where(held, gain_second, 0.0)
    labels = jnp.where(half == 0, spare_first, spare_second)[:, ROWS].astype(jnp.int32)
    slots = jnp.arange(64, dtype=jnp.int32)
    blocks = jnp.stack([labels, 127 - labels], axis=1).reshape(128)
    places = jnp.stack([2 * slots, 2 * slots + 1], axis=1).reshape(128)
    hits = blocks[None, :] == jnp.arange(128, dtype=jnp.int32)[:, None]
    table = jnp.sum(jnp.where(hits, places[None, :], 0), axis=1)

    start = dot(inputs[0], select)
    freqs = jnp.exp(
        -math.log(10000.0) * jnp.arange(HEAD_SIZE // 2, dtype=jnp.float32) * 2.0 / HEAD_SIZE
    )
    angle = positions[0].astype(jnp.float32)[:, None] * freqs[None, :]
    cosine = jnp.cos(angle)[:, None, :]
    sine = jnp.sin(angle)[:, None, :]
    scale_one = lax.rsqrt(jnp.sum(start * start, axis=-1, keepdims=True) / WIDTH + EPSILON)
    normed_low = (start * scale_one * gain_first).astype(jnp.bfloat16)
    projected = dot(normed_low, weight_in)
    projected = jnp.concatenate(
        [projected[:, :IN_HALF], projected[:, IN_PAD : IN_PAD + IN_HALF]], axis=1
    )
    query_low = rotate(projected[:, :WIDTH], cosine, sine).astype(jnp.bfloat16)
    query_scaled = query_low * jnp.bfloat16(0.125)
    key_low = rotate(projected[:, WIDTH : WIDTH + key_width], cosine, sine).astype(jnp.bfloat16)
    value_low = projected[:, WIDTH + key_width :].astype(jnp.bfloat16)
    key_value = jnp.stack(
        [
            key_low.reshape(128, KEY_VALUE_HEADS, HEAD_SIZE),
            value_low.reshape(128, KEY_VALUE_HEADS, HEAD_SIZE),
        ],
        axis=2,
    ).reshape(128, 2 * key_width)
    all_kv = gather_blocks((key_value,), ("whole",), None, 1)[0].reshape(128, 64, 2 * key_width)
    pair_one = pair.reshape(1)
    attention, top, total = attend(table, pair_one, query_scaled, all_kv)
    mixed_low = pad_halves(attention.astype(jnp.bfloat16), OUT_HALF, OUT_PAD)
    branch = dot(mixed_low, weight_out, LAST)
    resid = start + jnp.where(held, branch, 0.0)
    scale_two = lax.rsqrt(jnp.sum(resid * resid, axis=-1, keepdims=True) / WIDTH + EPSILON)
    normed_two = (resid * scale_two * gain_second).astype(jnp.bfloat16)
    row_normed = row_gather(normed_two, 2).reshape(512, PADDED)
    gate_vals = dot(row_normed, weight_gu)
    gate = gate_vals[:, :FF_QUARTER]
    upper = gate_vals[:, FF_QUARTER:]
    sigma = jax.nn.sigmoid(gate)
    silu_vals = gate * sigma
    hidden_low = (silu_vals * upper).astype(jnp.bfloat16)
    ffn_out = dot(hidden_low, weight_down, LAST)
    hidden_grad = dot(row_cotangent, weight_down)
    gate_grad = hidden_grad * upper * sigma * (1.0 + gate * (1.0 - sigma))
    upper_grad = hidden_grad * silu_vals
    gate_up_grad = jnp.concatenate([gate_grad, upper_grad], axis=1).astype(jnp.bfloat16)
    normed_two_grad = dot(gate_up_grad, weight_gu, LAST)
    normed_two_grad = row_scatter(
        normed_two_grad.astype(jnp.bfloat16).reshape(4, 128, PADDED), 3
    )
    resid_grad = upstream + norm_backward(resid, scale_two, normed_two_grad * gain_second)
    gain_two_grad = jnp.sum(normed_two_grad * resid * scale_two, axis=0)
    branch_grad_low = resid_grad.astype(jnp.bfloat16)
    grad_out = dot(branch_grad_low, mixed_low, FIRST).astype(jnp.bfloat16)
    grad_gu = dot(row_normed, gate_up_grad, FIRST).astype(jnp.bfloat16)
    grad_down = dot(row_cotangent, hidden_low, FIRST).astype(jnp.bfloat16)
    mixed_grad = dot(branch_grad_low, weight_out)
    mixed_grad = jnp.concatenate(
        [mixed_grad[:, :OUT_HALF], mixed_grad[:, OUT_PAD : OUT_PAD + OUT_HALF]], axis=1
    )
    query_grad, all_kv_grad = attend_back(
        table, pair_one, query_scaled, mixed_grad, attention, top, total, all_kv
    )
    kv_grad, ffn_out = scatter_blocks(
        (all_kv_grad.reshape(2, 4, 4, 2, 128, 2 * key_width),),
        ((0, 0, 2 * key_width, 0),),
        None,
        ffn_out.astype(jnp.bfloat16).reshape(4, 128, PADDED),
        4,
    )
    layer_out = dot((resid + ffn_out).astype(jnp.bfloat16), select, LAST).astype(jnp.bfloat16)
    kv_grad = kv_grad.reshape(128, KEY_VALUE_HEADS, 2, HEAD_SIZE)
    proj_grad = jnp.concatenate(
        [
            rotate(query_grad * 0.125, cosine, -sine),
            rotate(kv_grad[:, :, 0].reshape(128, key_width), cosine, -sine),
            kv_grad[:, :, 1].reshape(128, key_width),
        ],
        axis=1,
    ).astype(jnp.bfloat16)
    proj_grad = pad_halves(proj_grad, IN_HALF, IN_PAD)
    normed_one_grad = dot(proj_grad, weight_in, LAST)
    gain_one_grad = jnp.sum(normed_one_grad * start * scale_one, axis=0)
    through = norm_backward(start, scale_one, normed_one_grad * gain_first)
    input_grad = dot((resid_grad + through).astype(jnp.bfloat16), select, LAST).astype(jnp.bfloat16)

    grad_in = dot(normed_low, proj_grad, FIRST).astype(jnp.bfloat16)
    row = jnp.arange(PADDED)[:, None]
    lane = jnp.arange(IN_COLS)[None, :]
    gains_by_slot = jnp.stack([gain_one_grad, gain_two_grad]).reshape(2, 64, ROWS)
    gains_by_slot = jnp.pad(
        gains_by_slot.transpose(1, 0, 2), ((0, 0), (0, 0), (0, IN_PAD - ROWS))
    ).reshape(64, 1, IN_COLS)
    grad_in = jnp.where(
        row % ROWS == 15,
        jnp.broadcast_to(gains_by_slot, (64, ROWS, IN_COLS)).reshape(PADDED, IN_COLS).astype(jnp.bfloat16),
        grad_in,
    )
    own_cols = IN_PAD + OUT_PAD
    att_sum, ffn_parts = scatter_blocks(
        tuple(
            grad.reshape(2, 4, 4, 2, ROWS, grad.shape[1])
            for grad in (grad_in, grad_out, grad_gu, grad_down)
        ),
        (
            (0, 0, IN_PAD, 0),
            (0, IN_PAD, IN_PAD, own_cols),
            (1, 0, OUT_PAD, IN_PAD),
            (1, OUT_PAD, OUT_PAD, own_cols + IN_PAD),
            (2, 0, 2 * FF_QUARTER, 2 * own_cols),
            (3, 0, FF_QUARTER, 2 * own_cols + 2 * FF_QUARTER),
        ),
        own_cols,
        None,
        5,
    )
    gu_sum = ffn_parts[:, :15, : 2 * FF_QUARTER].reshape(2, 15, 2, FF_QUARTER)
    return (
        layer_out[None],
        input_grad[None],
        att_sum[:15, :IN_HALF],
        att_sum[:15, IN_PAD : IN_PAD + OUT_HALF],
        gu_sum.transpose(1, 2, 0, 3).reshape(15, 2, FF_HALF),
        ffn_parts[:, :15, 2 * FF_QUARTER :].transpose(1, 0, 2).reshape(15, FF_HALF),
        att_sum[15, :15].reshape(15, 1),
    )


def solution(mesh):
    in_specs = (
        P("fsdp", "ctx", None),
        P("fsdp", "ctx", None),
        P("fsdp", "ctx"),
        P("fsdp", "ctx"),
        P("ctx", "fsdp"),
        P("ctx", "fsdp"),
        P("ctx", None, "fsdp"),
        P("ctx", "fsdp"),
        P("ctx", "fsdp"),
    )
    out_specs = (
        P("fsdp", "ctx", None),
        P("fsdp", "ctx", None),
        P("ctx", "fsdp"),
        P("ctx", "fsdp"),
        P("ctx", None, "fsdp"),
        P("ctx", "fsdp"),
        P("ctx", "fsdp"),
    )
    return jax.shard_map(
        on_device, mesh=mesh, in_specs=in_specs, out_specs=out_specs, check_vma=False
    )
```

```python
import math

import jax
import jax.numpy as jnp
import numpy as np
from jax import lax
from jax.experimental import pallas as pl
from jax.experimental.pallas import tpu as pltpu
from jax.sharding import PartitionSpec as P

WIDTH = 960
QUERY_HEADS = 15
KEY_VALUE_HEADS = 5
GROUP = 3
HEAD_SIZE = 64
FF_HALF = 1280
FF_QUARTER = 640
EPSILON = 1e-05
ROWS = 16
PADDED = 1024
IN_HALF = 800
IN_PAD = 896
OUT_HALF = 480
OUT_PAD = 512
IN_COLS = 2 * IN_PAD
TILE = 512
QROWS = 384
MESH = pl.DeviceIdType.MESH
VMEM_LIMIT = 56 * 1024 * 1024


def column_map():
    cols = np.full((64, ROWS), -1, np.int32)
    cols[:, :15] = np.arange(64)[:, None] * 15 + np.arange(15)[None, :]
    return cols.reshape(-1)


COLUMN_MAP = column_map()


def coordinates():
    index = lax.axis_index("ctx")
    core = index % 2
    z = (index // 2) % 4
    y = (index // 8) % 4
    x = index // 32
    p1 = y * (1 - core) + z * core
    p2 = z * (1 - core) + y * core
    return x, p1, p2, core


def device_at(x, p1, p2, core):
    y = p1 * (1 - core) + p2 * core
    z = p2 * (1 - core) + p1 * core
    return ((x * 4 + y) * 4 + z) * 2 + core


def neighbours(x, p1, p2, core):
    index = lax.axis_index("ctx")
    return (
        device_at(1 - x, p1, p2, core),
        device_at(x, (p1 + 1) % 4, p2, core),
        device_at(x, (p1 + 3) % 4, p2, core),
        device_at(x, p1, (p2 + 1) % 4, core),
        device_at(x, p1, (p2 + 3) % 4, core),
        index + 1 - 2 * core,
    )


def block_of(ref, core, x, p1, p2):
    return ref.at[x, p1, p2, core] if core == 0 else ref.at[x, p2, p1, core]


def half_of(ref, core, x, p2):
    every = pl.ds(0, 4)
    return ref.at[x, every, p2, core] if core == 0 else ref.at[x, p2, every, core]


def slab_of(ref, core, p2):
    every = pl.ds(0, 4)
    both = pl.ds(0, 2)
    return ref.at[both, every, p2, core] if core == 0 else ref.at[both, p2, every, core]


def row_place():
    return lax.axis_index("fsdp") * 2 + lax.axis_index("ctx") // 32


def row_device(place):
    index = lax.axis_index("ctx")
    return {"fsdp": place // 2, "ctx": (place % 2) * 32 + index % 32}


def ctx_device(index):
    return {"ctx": index}


class Sender:
    def __init__(self, send_sem, recv_sem):
        self.send_sem, self.recv_sem, self.sent = send_sem, recv_sem, []

    def __call__(self, source, place, device):
        number = len(self.sent)
        copy = pltpu.make_async_remote_copy(
            src_ref=source,
            dst_ref=place,
            send_sem=self.send_sem.at[number],
            recv_sem=self.recv_sem.at[number],
            device_id=device,
            device_id_type=MESH,
        )
        copy.start()
        self.sent.append(copy)
        return copy

    def finish(self):
        for copy in self.sent:
            copy.wait_send()


class RowGather:
    def __init__(self, in_ref, out_ref, local_sem, send):
        self.out, self.send = out_ref, send
        here = row_place()
        self.left, self.right = (here + 3) % 4, (here + 1) % 4
        self.local = pltpu.make_async_copy(in_ref, out_ref.at[here], local_sem)
        self.local.start()
        self.from_left = send(in_ref, out_ref.at[here], row_device(self.right))
        self.from_right = send(in_ref, out_ref.at[here], row_device(self.left))

    def forward(self):
        rows = self.out.shape[1] // 2
        low, high = pl.ds(0, rows), pl.ds(rows, rows)
        self.from_left.wait_recv()
        place = self.out.at[self.left, low]
        self.far_low = self.send(place, place, row_device(self.right))
        self.from_right.wait_recv()
        place = self.out.at[self.right, high]
        self.far_high = self.send(place, place, row_device(self.left))

    def finish(self):
        self.far_low.wait_recv()
        self.far_high.wait_recv()
        self.local.wait()


class RowScatter:
    def __init__(self, in_ref, far, near_left, near_right, stage, send):
        self.p, self.far, self.stage, self.send = in_ref, far, stage, send
        self.near_left, self.near_right = near_left, near_right
        self.here = row_place()
        self.left, self.right = (self.here + 3) % 4, (self.here + 1) % 4
        to_left, to_right = row_device(self.left), row_device(self.right)
        opposite = (self.here + 2) % 4
        rows = in_ref.shape[1] // 2
        self.low, self.high = pl.ds(0, rows), pl.ds(rows, rows)
        low, high = self.low, self.high
        self.got_low = send(in_ref.at[opposite, low], far.at[0], to_right)
        self.got_high = send(in_ref.at[opposite, high], far.at[1], to_left)
        self.waits = [
            send(in_ref.at[self.right, high], near_left.at[high], to_right),
            send(in_ref.at[self.left, low], near_right.at[low], to_left),
        ]

    def forward(self):
        rows = self.p.shape[1] // 2
        self.got_low.wait_recv()
        self.stage[0] = self.p[self.right, 0:rows] + self.far[0]
        self.waits.append(
            self.send(self.stage.at[0], self.near_left.at[self.low], row_device(self.right))
        )
        self.got_high.wait_recv()
        self.stage[1] = self.p[self.left, rows : 2 * rows] + self.far[1]
        self.waits.append(
            self.send(self.stage.at[1], self.near_right.at[self.high], row_device(self.left))
        )

    def finish(self, out_ref):
        for copy in self.waits:
            copy.wait_recv()
        total = self.p[self.here].astype(jnp.float32) + self.near_left[...].astype(jnp.float32)
        out_ref[...] = total + self.near_right[...].astype(jnp.float32)


def greet(devices):
    barrier = pltpu.get_barrier_semaphore()
    for device in devices:
        pl.semaphore_signal(barrier, inc=1, device_id=device, device_id_type=MESH)
    pl.semaphore_wait(barrier, len(devices))


def greet_ctx(with_row):
    devices = [ctx_device(index) for index in neighbours(*coordinates())]
    if with_row:
        here = row_place()
        step = 2 * (here % 2) - 1
        devices.append(row_device((here + step + 4) % 4))
    greet(devices)


def row_kernel_entry():
    here = row_place()
    greet([row_device((here + 3) % 4), row_device((here + 1) % 4)])


def row_scratch(rows, columns):
    return [
        pltpu.VMEM((2, rows // 2, columns), jnp.bfloat16),
        pltpu.VMEM((rows, columns), jnp.bfloat16),
        pltpu.VMEM((rows, columns), jnp.bfloat16),
        pltpu.VMEM((2, rows // 2, columns), jnp.bfloat16),
        pltpu.SemaphoreType.DMA((6,)),
        pltpu.SemaphoreType.DMA((6,)),
    ]


class Group:
    def __init__(self, copies):
        self.copies = copies

    def wait_recv(self):
        for copy in self.copies:
            copy.wait_recv()


def gather_kernel(modes, with_row, *refs):
    count = len(modes)
    ins, refs = refs[: count + with_row], refs[count + with_row :]
    outs, refs = refs[: count + with_row], refs[count + with_row :]
    greet_ctx("row" in modes or with_row)
    core = coordinates()[3]
    for chosen in range(2):

        @pl.when(core == chosen)
        def _(chosen=chosen):
            gather_body(chosen, modes, with_row, ins, outs, *refs)


def gather_body(
    core, modes, with_row, ins, outs, local_sem, send_sem, recv_sem, row_local, row_send, row_recv
):
    x, p1, p2, _ = coordinates()
    across, right1, left1, right2, left2, sibling = neighbours(x, p1, p2, core)
    p1p, p1m = (p1 + 1) % 4, (p1 + 3) % 4
    p2p, p2m, p2o = (p2 + 1) % 4, (p2 + 3) % 4, (p2 + 2) % 4
    place = row_place()
    row_left, row_right = (place + 3) % 4, (place + 1) % 4
    sender = Sender(send_sem, recv_sem)
    arrays = range(len(modes))
    plain = [k for k in arrays if modes[k] != "row"]
    rows = [k for k in arrays if modes[k] == "row"]
    mine = [ins[k].at[x] if modes[k] == "split" else ins[k] for k in arrays]
    yours = [ins[k].at[1 - x] if modes[k] == "split" else ins[k] for k in arrays]

    def send(places, to, chosen=arrays, sources=None):
        sources = places if sources is None else sources
        return Group([sender(sources[k], places[k], ctx_device(to)) for k in chosen])

    def block(side, q1):
        return [block_of(outs[k], core, side, q1, p2) for k in arrays]

    def half(side, q2):
        return [half_of(outs[k], core, side, q2) for k in arrays]

    def slot(k, owner):
        width = ins[k].shape[-1]
        columns = pl.ds(pl.multiple_of((owner // 2) * width, 128), width)
        return block_of(outs[k], core, owner % 2, p1, p2).at[pl.ds(0, ROWS), columns]

    here = block(x, p1)
    there = block(1 - x, p1)
    locals_ = [
        pltpu.make_async_copy(
            mine[k], slot(k, place) if k in rows else here[k], local_sem.at[k]
        )
        for k in arrays
    ]
    for copy in locals_:
        copy.start()
    row_near = Group(
        [
            sender(ins[k], slot(k, place), row_device(to))
            for to in (row_right, row_left)
            for k in rows
        ]
    )
    crossed = send(here, across, plain, yours)
    own_left = send(here, right1, plain, mine)
    own_right = send(here, left1, plain, mine)
    row_near.wait_recv()
    row_far = Group(
        [sender(slot(k, row_left), slot(k, row_left), row_device(row_right)) for k in rows]
    )
    crossed.wait_recv()
    other_left = send(there, right1)
    other_right = send(there, left1)
    for copy in locals_:
        copy.wait()
    row_far.wait_recv()
    own_left.copies += send(here, right1, rows).copies
    own_right.copies += send(here, left1, rows).copies
    if with_row:
        row_sender = Sender(row_send, row_recv)
        row = RowGather(ins[-1], outs[-1], row_local, row_sender)
    own_left.wait_recv()
    own_far = send(block(x, p1m), right1)
    own_right.wait_recv()
    own_far.wait_recv()
    own_left = send(half(x, p2), right2)
    own_right = send(half(x, p2), left2)
    last = [send(half(x, p2), sibling)]
    other_right.wait_recv()
    other_far = send(block(1 - x, p1p), left1)
    other_left.wait_recv()
    other_far.wait_recv()
    other_right = send(half(1 - x, p2), left2)
    other_left = send(half(1 - x, p2), right2)
    last.append(send(half(1 - x, p2), sibling))
    own_left.wait_recv()
    own_far = send(half(x, p2m), right2)
    last.append(send(half(x, p2m), sibling))
    own_right.wait_recv()
    last.append(send(half(x, p2p), sibling))
    if with_row:
        row.forward()
    other_right.wait_recv()
    other_far = send(half(1 - x, p2p), left2)
    last.append(send(half(1 - x, p2p), sibling))
    other_left.wait_recv()
    last.append(send(half(1 - x, p2m), sibling))
    own_far.wait_recv()
    last.append(send(half(x, p2o), sibling))
    if with_row:
        row.finish()
    other_far.wait_recv()
    last.append(send(half(1 - x, p2o), sibling))
    for group in last:
        group.wait_recv()
    sender.finish()
    if with_row:
        row_sender.finish()


def gather_blocks(blocks, modes, row_block, collective_id):
    with_row = row_block is not None
    operands = list(blocks)
    shapes = [
        jax.ShapeDtypeStruct(
            (2, 4, 4, 2, block.shape[-2], block.shape[-1] * (2 if mode == "row" else 1)),
            block.dtype,
        )
        for block, mode in zip(blocks, modes)
    ]
    if with_row:
        operands.append(row_block)
        shapes.append(jax.ShapeDtypeStruct((4,) + row_block.shape, row_block.dtype))
    number = 23 * len(blocks)
    return pl.pallas_call(
        lambda *refs: gather_kernel(modes, int(with_row), *refs),
        out_shape=tuple(shapes),
        in_specs=[pl.BlockSpec(memory_space=pl.ANY)] * len(operands),
        out_specs=(pl.BlockSpec(memory_space=pl.ANY),) * len(operands),
        scratch_shapes=[
            pltpu.SemaphoreType.DMA((len(blocks),)),
            pltpu.SemaphoreType.DMA((number,)),
            pltpu.SemaphoreType.DMA((number,)),
            pltpu.SemaphoreType.DMA,
            pltpu.SemaphoreType.DMA((4,)),
            pltpu.SemaphoreType.DMA((4,)),
        ],
        compiler_params=pltpu.CompilerParams(
            collective_id=collective_id, has_side_effects=True
        ),
    )(*operands)


def scatter_kernel(pieces, halved, with_row, *refs):
    count = 1 + max(piece[0] for piece in pieces)
    ins, refs = refs[:count], refs[count:]
    if with_row:
        row_in, refs = refs[0], refs[1:]
    out_ref, refs = refs[0], refs[1:]
    if halved:
        parts_ref, refs = refs[0], refs[1:]
    if with_row:
        row_out, refs = refs[0], refs[1:]
    (acc, other, far_low, far_high, near_left, near_right) = refs[:6]
    (pair_low, pair_high, pair_left, pair_right, last) = refs[6:11]
    (local_sem, cross_send, cross_recv, send_sem, recv_sem) = refs[11:16]
    x, p1, p2, core = coordinates()
    across, right1, left1, right2, left2, sibling = neighbours(x, p1, p2, core)
    greet_ctx(with_row or halved)
    p1p, p1m, p1o = (p1 + 1) % 4, (p1 + 3) % 4, (p1 + 2) % 4
    p2p, p2m, p2o = (p2 + 1) % 4, (p2 + 3) % 4, (p2 + 2) % 4
    needed = (p2o, p2m, p2p, p2)
    theirs = (p1o, p1m, p1p, p1)
    sender = Sender(send_sem, recv_sem)

    def part(ref, place, piece):
        if len(pieces) == 1:
            return ref.at[place]
        every = [pl.ds(0, size) for size in ref.shape[1:-1]]
        return ref.at[tuple([place] + every + [pl.ds(pieces[piece][3], pieces[piece][2])])]

    def source_of(piece, chosen, place):
        array, start, width, _ = pieces[piece]
        slab = slab_of(ins[array], chosen, place)
        if len(pieces) == 1:
            return slab
        every = [pl.ds(0, size) for size in slab.shape[:-1]]
        return slab.at[tuple(every + [pl.ds(start, width)])]

    def crossing(k, piece, source):
        return pltpu.make_async_remote_copy(
            src_ref=source,
            dst_ref=part(other, theirs[k], piece),
            send_sem=cross_send.at[k, piece],
            recv_sem=cross_recv.at[k, piece],
            device_id=ctx_device(sibling),
            device_id_type=MESH,
        )

    for chosen in range(2):

        @pl.when(core == chosen)
        def _(chosen=chosen):
            for k in range(4):
                for piece in range(len(pieces)):
                    crossing(k, piece, source_of(piece, 1 - chosen, theirs[k])).start()
                    pltpu.make_async_copy(
                        source_of(piece, chosen, needed[k]),
                        part(acc, needed[k], piece),
                        local_sem.at[k, piece],
                    ).start()

    if with_row:
        row_sender = Sender(refs[20], refs[21])
        row = RowScatter(row_in, refs[16], refs[17], refs[18], refs[19], row_sender)

    def send(source, place, to):
        return sender(source, place, ctx_device(to))

    def add(place, term):
        @pl.loop(0, 4)
        def _(step):
            place[step] = place[step] + term[step]

    def add_both(side):
        @pl.loop(0, 4)
        def _(step):
            total = acc[p2, side, step].astype(jnp.float32)
            total = total + near_left[side, step].astype(jnp.float32)
            total = total + near_right[side, step].astype(jnp.float32)
            acc[p2, side, step] = total.astype(acc.dtype)

    def merge(k):
        for piece in range(len(pieces)):
            mine = part(acc, needed[k], piece)
            pltpu.make_async_copy(mine, mine, local_sem.at[k, piece]).wait()
            crossing(k, piece, part(other, theirs[k], piece)).wait_recv()
        for side in range(2):
            add(acc.at[needed[k], side], other.at[needed[k], side])

    merge(0)
    got_low = send(acc.at[p2o, 0], far_low, right2)
    got_high = send(acc.at[p2o, 1], far_high, left2)
    merge(1)
    right_low = send(acc.at[p2m, 0], near_right.at[0], left2)
    merge(2)
    left_high = send(acc.at[p2p, 1], near_left.at[1], right2)
    got_low.wait_recv()
    add(acc.at[p2p, 0], far_low)
    left_low = send(acc.at[p2p, 0], near_left.at[0], right2)
    got_high.wait_recv()
    add(acc.at[p2m, 1], far_high)
    right_high = send(acc.at[p2m, 1], near_right.at[1], left2)
    merge(3)
    if with_row:
        row.forward()
    right_low.wait_recv()
    left_low.wait_recv()
    add_both(0)
    got_low = send(acc.at[p2, 0, p1o], pair_low, right1)
    near_low = send(acc.at[p2, 0, p1m], pair_right.at[0], left1)
    left_high.wait_recv()
    right_high.wait_recv()
    add_both(1)
    got_high = send(acc.at[p2, 1, p1o], pair_high, left1)
    near_high = send(acc.at[p2, 1, p1p], pair_left.at[1], right1)
    got_low.wait_recv()
    acc[p2, 0, p1p] = acc[p2, 0, p1p] + pair_low[...]
    left_low = send(acc.at[p2, 0, p1p], pair_left.at[0], right1)
    got_high.wait_recv()
    acc[p2, 1, p1m] = acc[p2, 1, p1m] + pair_high[...]
    right_high = send(acc.at[p2, 1, p1m], pair_right.at[1], left1)
    if with_row:
        row.finish(row_out)
    near_low.wait_recv()
    near_high.wait_recv()
    left_low.wait_recv()
    right_high.wait_recv()

    @pl.loop(0, 2)
    def _(j):
        total = acc[p2, j, p1].astype(jnp.float32) + pair_left[j].astype(jnp.float32)
        total = total + pair_right[j].astype(jnp.float32)
        acc[p2, j, p1] = total.astype(acc.dtype)

    if halved:
        finish_row(halved, acc, p1, p2, refs[16:20], last, sender, out_ref, parts_ref)
    else:
        final = send(acc.at[p2, 1 - x, p1], last, across)
        final.wait_recv()
        out_ref[...] = acc[p2, x, p1].astype(jnp.float32) + last[...].astype(jnp.float32)
    for k in range(4):
        for piece in range(len(pieces)):
            crossing(k, piece, part(other, theirs[k], piece)).wait_send()
    sender.finish()
    if with_row:
        row_sender.finish()


def finish_row(halved, acc, p1, p2, buffers, last, sender, out_ref, parts_ref):
    far, from_left, from_right, stage = buffers
    here = row_place()
    left, right, opposite = (here + 3) % 4, (here + 1) % 4, (here + 2) % 4
    x = here % 2
    every = pl.ds(0, ROWS)
    rest = pl.ds(2 * halved, acc.shape[-1] - 2 * halved)

    def columns(owner):
        return pl.ds(pl.multiple_of((owner // 2) * halved, 128), halved)

    def block(owner):
        return acc.at[p2, owner % 2, p1, every, columns(owner)]

    far_copy = sender(block(opposite), far, row_device(right))
    from_right_copy = sender(block(left), from_right, row_device(left))
    x_neighbour = row_device((here // 2) * 2 + 1 - x)
    parts_copy = sender(acc.at[p2, 1 - x, p1, every, rest], last, x_neighbour)
    far_copy.wait_recv()
    stage[...] = acc[p2, right % 2, p1, :, columns(right)] + far[...]
    from_left_copy = sender(stage, from_left, row_device(right))
    parts_ref[x] = acc[p2, x, p1, :, rest].astype(jnp.float32)
    parts_copy.wait_recv()
    parts_ref[1 - x] = last[...].astype(jnp.float32)
    from_right_copy.wait_recv()
    from_left_copy.wait_recv()
    total = acc[p2, x, p1, :, columns(here)].astype(jnp.float32)
    total = total + from_left[...].astype(jnp.float32)
    out_ref[...] = total + from_right[...].astype(jnp.float32)


def scatter_blocks(arrays, pieces, halved, row_blocks, collective_id):
    rows = arrays[0].shape[-2]
    columns = sum(piece[2] for piece in pieces)
    kind = arrays[0].dtype
    block = (rows, columns)
    with_row = row_blocks is not None
    operands = list(arrays)
    in_specs = [pl.BlockSpec(memory_space=pl.ANY)] * len(arrays)
    shapes = [jax.ShapeDtypeStruct((rows, halved or columns), jnp.float32)]
    last = block
    scratch = []
    if halved:
        last = (rows, columns - 2 * halved)
        shapes.append(jax.ShapeDtypeStruct((2,) + last, jnp.float32))
        scratch = [pltpu.VMEM((rows, halved), kind)] * 4
    if with_row:
        operands.append(row_blocks)
        in_specs.append(pl.BlockSpec(memory_space=pltpu.VMEM))
        shapes.append(jax.ShapeDtypeStruct(row_blocks.shape[1:], jnp.float32))
        scratch = row_scratch(*row_blocks.shape[1:])
    return pl.pallas_call(
        lambda *refs: scatter_kernel(pieces, halved, with_row, *refs),
        out_shape=tuple(shapes),
        in_specs=in_specs,
        out_specs=(pl.BlockSpec(memory_space=pltpu.VMEM),) * len(shapes),
        scratch_shapes=[
            pltpu.VMEM((4, 2, 4) + block, kind),
            pltpu.VMEM((4, 2, 4) + block, kind),
            pltpu.VMEM((4,) + block, kind),
            pltpu.VMEM((4,) + block, kind),
            pltpu.VMEM((2, 4) + block, kind),
            pltpu.VMEM((2, 4) + block, kind),
            pltpu.VMEM(block, kind),
            pltpu.VMEM(block, kind),
            pltpu.VMEM((2,) + block, kind),
            pltpu.VMEM((2,) + block, kind),
            pltpu.VMEM(last, kind),
            pltpu.SemaphoreType.DMA((4, len(pieces))),
            pltpu.SemaphoreType.DMA((4, len(pieces))),
            pltpu.SemaphoreType.DMA((4, len(pieces))),
            pltpu.SemaphoreType.DMA((16,)),
            pltpu.SemaphoreType.DMA((16,)),
        ]
        + scratch,
        compiler_params=pltpu.CompilerParams(
            collective_id=collective_id, has_side_effects=True, vmem_limit_bytes=VMEM_LIMIT
        ),
    )(*operands)


LAST = (((1,), (1,)), ((), ()))
FIRST = (((0,), (0,)), ((), ()))
PLAIN = (((1,), (0,)), ((), ()))


def dot(a, b, dims=PLAIN):
    return lax.dot_general(a, b, dims, preferred_element_type=jnp.float32)


def feed_forward_kernel(
    n_ref,
    c_ref,
    gu_ref,
    down_ref,
    dn_ref,
    part_ref,
    grad_gu_ref,
    grad_down_ref,
    normed,
    partial,
    hidden,
    gate_up_grad,
    far,
    near_left,
    near_right,
    stage,
    send_sem,
    recv_sem,
):
    row_kernel_entry()
    here = row_place()
    left, right, opposite = (here + 3) % 4, (here + 1) % 4, (here + 2) % 4
    to_left, to_right = row_device(left), row_device(right)

    def rows(owner, start=0, size=128):
        return pl.ds(pl.multiple_of(owner * 128 + start, 64), size)

    def copy(number, source, place, device):
        return pltpu.make_async_remote_copy(
            src_ref=source,
            dst_ref=place,
            send_sem=send_sem.at[number],
            recv_sem=recv_sem.at[number],
            device_id=device,
            device_id_type=MESH,
        )

    mine = normed.at[rows(here)]
    low, high = pl.ds(0, 64), pl.ds(64, 64)
    normed_right = copy(0, n_ref, mine, to_right)
    normed_left = copy(1, n_ref, mine, to_left)
    place = normed.at[rows(left, 0, 64)]
    normed_far_low = copy(2, place, place, to_right)
    place = normed.at[rows(right, 64, 64)]
    normed_far_high = copy(3, place, place, to_left)
    far_low = copy(4, partial.at[rows(opposite, 0, 64)], far.at[0], to_right)
    far_high = copy(5, partial.at[rows(opposite, 64, 64)], far.at[1], to_left)
    near_low = copy(6, partial.at[rows(left, 0, 64)], near_right.at[low], to_left)
    near_high = copy(7, partial.at[rows(right, 64, 64)], near_left.at[high], to_right)
    sum_low = copy(8, stage.at[0], near_left.at[low], to_right)
    sum_high = copy(9, stage.at[1], near_right.at[high], to_left)
    normed_right.start()
    normed_left.start()
    normed[rows(here), :] = n_ref[...]

    @pl.loop(0, 4)
    def _(step):
        turn = jnp.where(step == 1, 3, jnp.where(step == 2, 1, jnp.where(step == 3, 2, 0)))
        owner = (here + turn) % 4

        @pl.when(step == 1)
        def _():
            normed_right.wait_recv()
            normed_far_low.start()

        @pl.when(step == 2)
        def _():
            normed_left.wait_recv()
            normed_far_high.start()

        @pl.when(step == 3)
        def _():
            normed_far_low.wait_recv()
            normed_far_high.wait_recv()

        gate_vals = dot(normed[rows(owner), :], gu_ref[...])
        hidden_grad = dot(c_ref[rows(owner), :], down_ref[...])
        gate = gate_vals[:, :FF_QUARTER]
        upper = gate_vals[:, FF_QUARTER:]
        sigma = jax.nn.sigmoid(gate)
        silu_vals = gate * sigma
        hidden[rows(owner), :] = (silu_vals * upper).astype(jnp.bfloat16)
        gate_grad = hidden_grad * upper * sigma * (1.0 + gate * (1.0 - sigma))
        upper_grad = hidden_grad * silu_vals
        both = jnp.concatenate([gate_grad, upper_grad], axis=1).astype(jnp.bfloat16)
        gate_up_grad[rows(owner), :] = both
        partial[rows(owner), :] = dot(both, gu_ref[...], LAST).astype(jnp.bfloat16)

        @pl.when(step == 1)
        def _():
            near_low.start()

        @pl.when(step == 2)
        def _():
            near_high.start()

        @pl.when(step == 3)
        def _():
            far_low.start()
            far_high.start()

    @pl.loop(0, 4)
    def _(owner):
        part_ref[rows(owner), :] = dot(hidden[rows(owner), :], down_ref[...], LAST).astype(
            jnp.bfloat16
        )

    far_low.wait_recv()
    stage[0] = partial[rows(right, 0, 64), :] + far[0]
    sum_low.start()
    far_high.wait_recv()
    stage[1] = partial[rows(left, 64, 64), :] + far[1]
    sum_high.start()

    @pl.loop(0, PADDED // 256)
    def _(step):
        span = pl.ds(pl.multiple_of(step * 256, 256), 256)
        grad_gu_ref[span, :] = dot(normed[:, span], gate_up_grad[...], FIRST).astype(jnp.bfloat16)
        grad_down_ref[span, :] = dot(c_ref[:, span], hidden[...], FIRST).astype(jnp.bfloat16)

    for arrived in (near_low, near_high, sum_low, sum_high):
        arrived.wait_recv()
    total = partial[rows(here), :].astype(jnp.float32) + near_left[...].astype(jnp.float32)
    dn_ref[...] = total + near_right[...].astype(jnp.float32)
    for sent in (normed_right, normed_left, normed_far_low, normed_far_high, far_low, far_high):
        sent.wait_send()
    for sent in (near_low, near_high, sum_low, sum_high):
        sent.wait_send()


def feed_forward(normed, cotangent, weight_gu, weight_down, collective_id):
    kind = jnp.bfloat16
    return pl.pallas_call(
        feed_forward_kernel,
        out_shape=(
            jax.ShapeDtypeStruct((128, PADDED), jnp.float32),
            jax.ShapeDtypeStruct((512, PADDED), kind),
            jax.ShapeDtypeStruct(weight_gu.shape, kind),
            jax.ShapeDtypeStruct(weight_down.shape, kind),
        ),
        in_specs=[pl.BlockSpec(memory_space=pltpu.VMEM)] * 4,
        out_specs=(pl.BlockSpec(memory_space=pltpu.VMEM),) * 4,
        scratch_shapes=[
            pltpu.VMEM((512, PADDED), kind),
            pltpu.VMEM((512, PADDED), kind),
            pltpu.VMEM((512, FF_QUARTER), kind),
            pltpu.VMEM((512, 2 * FF_QUARTER), kind),
            pltpu.VMEM((2, 64, PADDED), kind),
            pltpu.VMEM((128, PADDED), kind),
            pltpu.VMEM((128, PADDED), kind),
            pltpu.VMEM((2, 64, PADDED), kind),
            pltpu.SemaphoreType.DMA((10,)),
            pltpu.SemaphoreType.DMA((10,)),
        ],
        compiler_params=pltpu.CompilerParams(
            collective_id=collective_id, has_side_effects=True, vmem_limit_bytes=VMEM_LIMIT
        ),
        cost_estimate=pl.CostEstimate(
            flops=7 * 10**9, bytes_accessed=10**7, transcendentals=4 * 10**5
        ),
    )(normed, cotangent, weight_gu, weight_down)


def load_tiles(table_ref, kv_hbm, kv, sems, tiles):
    @pl.loop(0, tiles)
    def _(tile):
        for j in range(8):
            block = tile * 8 + j
            pltpu.make_async_copy(
                kv_hbm.at[table_ref[block]],
                kv.at[pl.ds(pl.multiple_of(block * 64, 64), 64)],
                sems.at[tile],
            ).start()


def wait_tile(kv, sems, tile):
    part = kv.at[pl.ds(pl.multiple_of(tile * TILE, TILE), TILE)]
    pltpu.make_async_copy(part, part, sems.at[tile]).wait()


def visible_keys(tile, pair, first_row, rows):
    shape = (rows, TILE)
    row = first_row + lax.broadcasted_iota(jnp.int32, shape, 0)
    key = tile * TILE + lax.broadcasted_iota(jnp.int32, shape, 1)
    order = jnp.where(row < QROWS // 2, pair, 127 - pair) * 64 + row % 64
    return key <= order


def head_parts():
    for g in range(KEY_VALUE_HEADS):
        for half in range(2):
            for h in range(GROUP):
                rows = slice((half * GROUP + h) * 64, (half * GROUP + h) * 64 + 64)
                column = (GROUP * g + h) * HEAD_SIZE
                yield g, rows, slice(half * 64, half * 64 + 64), slice(column, column + 64)


def run_tiles(pair, step):
    low_tiles = (pair + 8) // 8
    high_tiles = (135 - pair) // 8

    @pl.loop(0, low_tiles - 1)
    def _(tile):
        step(tile, 0, QROWS, False)

    step(low_tiles - 1, 0, QROWS, True)

    @pl.loop(low_tiles, high_tiles - 1)
    def _(tile):
        step(tile, QROWS // 2, QROWS // 2, False)

    step(high_tiles - 1, QROWS // 2, QROWS // 2, True)


def lane_parts(value):
    return [value[:, k * 128 : k * 128 + 128] for k in range(TILE // 128)]


def attend_kernel(table_ref, pair_ref, q_ref, kv_hbm, out_ref, top_ref, sum_ref, kv, q, acc, sems):
    pair = pair_ref[0]
    high_tiles = (135 - pair) // 8
    load_tiles(table_ref, kv_hbm, kv, sems, high_tiles)
    q[...] = jnp.zeros(q.shape, q.dtype)
    for g, rows, tokens, columns in head_parts():
        q[g, rows, 0:64] = q_ref[tokens, columns]
    acc[...] = jnp.zeros(acc.shape, jnp.float32)
    top_ref[...] = jnp.full(top_ref.shape, -1e30, jnp.float32)
    sum_ref[...] = jnp.zeros(sum_ref.shape, jnp.float32)

    def step(tile, first_row, rows, masked):
        wait_tile(kv, sems, tile)
        span = slice(first_row, first_row + rows)
        if masked:
            seen = visible_keys(tile, pair, first_row, rows)
        heads = range(KEY_VALUE_HEADS)
        keys = [
            kv[pl.ds(pl.multiple_of(tile * TILE, TILE), TILE), g * 128 : g * 128 + 128]
            for g in heads
        ]
        scores = [dot(q[g, span, :], keys[g], LAST) for g in heads]
        if masked:
            scores = [jnp.where(seen, score, -1e30) for score in scores]
        parts = [lane_parts(score) for score in scores]
        best = [
            jnp.maximum(jnp.maximum(p[0], p[1]), jnp.maximum(p[2], p[3])) for p in parts
        ]
        before = [top_ref[g, span, :] for g in heads]
        highest = [
            jnp.maximum(before[g], jnp.max(best[g], axis=1, keepdims=True)) for g in heads
        ]
        shrink = [jnp.exp(before[g] - highest[g]) for g in heads]
        parts = [[jnp.exp(part - highest[g]) for part in parts[g]] for g in heads]
        for g in heads:
            p = parts[g]
            top_ref[g, span, :] = highest[g]
            sum_ref[g, span, :] = sum_ref[g, span, :] * shrink[g] + ((p[0] + p[1]) + (p[2] + p[3]))
        mixed = [
            dot(jnp.concatenate([p.astype(jnp.bfloat16) for p in parts[g]], axis=1), keys[g])
            for g in heads
        ]
        for g in heads:
            acc[g, span, :] = acc[g, span, :] * shrink[g] + mixed[g]

    run_tiles(pair, step)
    for g in range(KEY_VALUE_HEADS):
        total = jnp.sum(sum_ref[g], axis=1, keepdims=True)
        sum_ref[g] = jnp.broadcast_to(total, sum_ref.shape[1:])
        acc[g] = acc[g] / sum_ref[g]
    for g, rows, tokens, columns in head_parts():
        out_ref[tokens, columns] = acc[g, rows, 64:128]


def attend(table, pair, q, kv):
    heads = (KEY_VALUE_HEADS, QROWS, 128)
    return pl.pallas_call(
        attend_kernel,
        out_shape=(
            jax.ShapeDtypeStruct((128, WIDTH), jnp.float32),
            jax.ShapeDtypeStruct(heads, jnp.float32),
            jax.ShapeDtypeStruct(heads, jnp.float32),
        ),
        in_specs=[
            pl.BlockSpec(memory_space=pltpu.SMEM),
            pl.BlockSpec(memory_space=pltpu.SMEM),
            pl.BlockSpec(memory_space=pltpu.VMEM),
            pl.BlockSpec(memory_space=pl.ANY),
        ],
        out_specs=(pl.BlockSpec(memory_space=pltpu.VMEM),) * 3,
        scratch_shapes=[
            pltpu.VMEM((8192, 640), jnp.bfloat16),
            pltpu.VMEM(heads, jnp.bfloat16),
            pltpu.VMEM(heads, jnp.float32),
            pltpu.SemaphoreType.DMA((16,)),
        ],
        compiler_params=pltpu.CompilerParams(vmem_limit_bytes=VMEM_LIMIT),
        cost_estimate=pl.CostEstimate(
            flops=4 * 10**9, bytes_accessed=10**7, transcendentals=8 * 10**6
        ),
    )(table, pair, q, kv)


def attend_back_kernel(
    table_ref,
    pair_ref,
    q_ref,
    grad_ref,
    out_ref,
    top_ref,
    sum_ref,
    kv_hbm,
    dq_ref,
    dkv_hbm,
    kv,
    dkv,
    q,
    gs,
    q_turned,
    g_turned,
    shift,
    acc,
    sems,
    out_sems,
):
    pair = pair_ref[0]
    high_tiles = (135 - pair) // 8
    load_tiles(table_ref, kv_hbm, kv, sems, high_tiles)

    def store(tile):
        for j in range(8):
            block = tile * 8 + j
            pltpu.make_async_copy(
                dkv.at[pl.ds(pl.multiple_of(block * 64, 64), 64)],
                dkv_hbm.at[table_ref[block]],
                out_sems.at[tile],
            ).start()

    @pl.loop(high_tiles, 16)
    def _(tile):
        dkv[pl.ds(pl.multiple_of(tile * TILE, TILE), TILE), :] = jnp.zeros(
            (TILE, 640), jnp.bfloat16
        )
        store(tile)

    q[...] = jnp.zeros(q.shape, q.dtype)
    gs[...] = jnp.zeros(gs.shape, gs.dtype)
    for g, rows, tokens, columns in head_parts():
        q[g, rows, 0:64] = q_ref[tokens, columns]
        grad = grad_ref[tokens, columns]
        total = sum_ref[g, rows, :]
        gs[g, rows, 64:128] = (grad / total[:, 0:64]).astype(jnp.bfloat16)
        delta = jnp.sum(grad * out_ref[tokens, columns], axis=1, keepdims=True)
        shift[g, rows, :] = delta / total
    for g in range(KEY_VALUE_HEADS):
        q_turned[g] = q[g].T
        g_turned[g] = gs[g].T
    acc[...] = jnp.zeros(acc.shape, jnp.float32)

    def step(tile, first_row, rows, masked):
        wait_tile(kv, sems, tile)
        span = slice(first_row, first_row + rows)
        part = pl.ds(pl.multiple_of(tile * TILE, TILE), TILE)
        if masked:
            seen = visible_keys(tile, pair, first_row, rows)
        heads = range(KEY_VALUE_HEADS)
        keys = [kv[part, g * 128 : g * 128 + 128] for g in heads]
        scores = [dot(q[g, span, :], keys[g], LAST) for g in heads]
        prob_grad = [dot(gs[g, span, :], keys[g], LAST) for g in heads]
        if masked:
            scores = [jnp.where(seen, score, -1e30) for score in scores]
        score_grad, probs_low = [], []
        for g in heads:
            top, moved = top_ref[g, span, :], shift[g, span, :]
            probs = [jnp.exp(part_ - top) for part_ in lane_parts(scores[g])]
            grads = [
                (probs[k] * (part_ - moved)).astype(jnp.bfloat16)
                for k, part_ in enumerate(lane_parts(prob_grad[g]))
            ]
            score_grad.append(jnp.concatenate(grads, axis=1))
            probs_low.append(
                jnp.concatenate([prob.astype(jnp.bfloat16) for prob in probs], axis=1)
            )
        change = [dot(score_grad[g], keys[g]) for g in heads]
        both = [
            dot(q_turned[g, :, span], score_grad[g]) + dot(g_turned[g, :, span], probs_low[g])
            for g in heads
        ]
        for g in heads:
            acc[g, span, :] = acc[g, span, :] + change[g]
            dkv[part, g * 128 : g * 128 + 128] = both[g].astype(jnp.bfloat16).T
        store(tile)

    run_tiles(pair, step)
    for g, rows, tokens, columns in head_parts():
        dq_ref[tokens, columns] = acc[g, rows, 0:64]

    @pl.loop(0, 16)
    def _(tile):
        part = dkv.at[pl.ds(pl.multiple_of(tile * TILE, TILE), TILE)]
        pltpu.make_async_copy(part, part, out_sems.at[tile]).wait()


def attend_back(table, pair, q, grad, out, top, total, kv):
    heads = (KEY_VALUE_HEADS, QROWS, 128)
    turned = (KEY_VALUE_HEADS, 128, QROWS)
    return pl.pallas_call(
        attend_back_kernel,
        out_shape=(
            jax.ShapeDtypeStruct((128, WIDTH), jnp.float32),
            jax.ShapeDtypeStruct((128, 64, 640), jnp.bfloat16),
        ),
        in_specs=[pl.BlockSpec(memory_space=pltpu.SMEM)] * 2
        + [pl.BlockSpec(memory_space=pltpu.VMEM)] * 5
        + [pl.BlockSpec(memory_space=pl.ANY)],
        out_specs=(
            pl.BlockSpec(memory_space=pltpu.VMEM),
            pl.BlockSpec(memory_space=pl.ANY),
        ),
        scratch_shapes=[
            pltpu.VMEM((8192, 640), jnp.bfloat16),
            pltpu.VMEM((8192, 640), jnp.bfloat16),
            pltpu.VMEM(heads, jnp.bfloat16),
            pltpu.VMEM(heads, jnp.bfloat16),
            pltpu.VMEM(turned, jnp.bfloat16),
            pltpu.VMEM(turned, jnp.bfloat16),
            pltpu.VMEM(heads, jnp.float32),
            pltpu.VMEM(heads, jnp.float32),
            pltpu.SemaphoreType.DMA((16,)),
            pltpu.SemaphoreType.DMA((16,)),
        ],
        compiler_params=pltpu.CompilerParams(vmem_limit_bytes=VMEM_LIMIT),
        cost_estimate=pl.CostEstimate(
            flops=10**10, bytes_accessed=2 * 10**7, transcendentals=8 * 10**6
        ),
    )(table, pair, q, grad, out, top, total, kv)


def rotate(values, cosine, sine):
    heads = values.shape[1] // HEAD_SIZE
    shaped = values.reshape(values.shape[0], heads, 2, HEAD_SIZE // 2)
    first, second = shaped[:, :, 0], shaped[:, :, 1]
    return jnp.stack(
        [first * cosine - second * sine, second * cosine + first * sine], axis=2
    ).reshape(values.shape)


def pad_columns(value, columns):
    return jnp.pad(value, ((0, 0), (0, columns - value.shape[1])))


def pad_halves(value, half, padded):
    return jnp.concatenate(
        [pad_columns(value[:, :half], padded), pad_columns(value[:, half:], padded)], axis=1
    )


def norm_backward(rows, scale, weighted):
    inner = jnp.sum(weighted * rows, axis=-1, keepdims=True)
    return scale * weighted - rows * scale**3 * inner / WIDTH


def on_device(
    inputs,
    cotangent,
    positions,
    pair_index,
    input_projection,
    project_out,
    gate_up,
    down_weight,
    norm_gains,
):
    half = lax.axis_index("fsdp")
    pair = pair_index[0, 0]
    key_width = KEY_VALUE_HEADS * HEAD_SIZE
    select = (
        lax.broadcasted_iota(jnp.int32, (WIDTH, PADDED), 0) == jnp.asarray(COLUMN_MAP)[None, :]
    ).astype(jnp.bfloat16)

    spare = jnp.pad(norm_gains.T, ((0, 0), (0, 1)))
    own_in = pad_columns(
        jnp.concatenate([input_projection, pad_columns(spare, IN_HALF)], axis=0), IN_PAD
    )
    own_in = own_in.at[15, ROWS].set(pair.astype(jnp.bfloat16))
    own_out = jnp.pad(project_out, ((0, 1), (0, OUT_PAD - OUT_HALF)))
    gate_up_parts = gate_up.reshape(15, 2, 2, FF_QUARTER).transpose(2, 0, 1, 3)
    gate_up_parts = gate_up_parts.reshape(2, 15, 2 * FF_QUARTER)
    down_parts = down_weight.reshape(15, 2, FF_QUARTER).transpose(1, 0, 2)
    spare_row = ((0, 0), (0, 1), (0, 0))
    upstream = dot(cotangent[0], select)
    weight_in, weight_out, weight_gu, weight_down, row_cotangent = gather_blocks(
        (
            own_in,
            own_out,
            jnp.pad(gate_up_parts, spare_row),
            jnp.pad(down_parts, spare_row),
        ),
        ("row", "row", "split", "split"),
        upstream.astype(jnp.bfloat16),
        0,
    )
    weight_in = weight_in.reshape(PADDED, IN_COLS)
    weight_out = weight_out.reshape(PADDED, 2 * OUT_PAD)
    weight_gu = weight_gu.reshape(PADDED, 2 * FF_QUARTER)
    weight_down = weight_down.reshape(PADDED, FF_QUARTER)
    row_cotangent = row_cotangent.reshape(512, PADDED)
    blocks_in = weight_in.reshape(64, ROWS, IN_COLS)
    spare_first = blocks_in[:, 15, : 2 * ROWS]
    spare_second = blocks_in[:, 15, IN_PAD : IN_PAD + 2 * ROWS]
    gain_first = spare_first[:, :ROWS].reshape(PADDED).astype(jnp.float32)
    gain_second = spare_second[:, :ROWS].reshape(PADDED).astype(jnp.float32)
    held = jnp.arange(PADDED) % ROWS < 15
    gain_first = jnp.where(held, gain_first, 0.0)
    gain_second = jnp.where(held, gain_second, 0.0)
    labels = jnp.where(half == 0, spare_first, spare_second)[:, ROWS].astype(jnp.int32)
    slots = jnp.arange(64, dtype=jnp.int32)
    blocks = jnp.stack([labels, 127 - labels], axis=1).reshape(128)
    places = jnp.stack([2 * slots, 2 * slots + 1], axis=1).reshape(128)
    hits = blocks[None, :] == jnp.arange(128, dtype=jnp.int32)[:, None]
    table = jnp.sum(jnp.where(hits, places[None, :], 0), axis=1)

    start = dot(inputs[0], select)
    freqs = jnp.exp(
        -math.log(10000.0) * jnp.arange(HEAD_SIZE // 2, dtype=jnp.float32) * 2.0 / HEAD_SIZE
    )
    angle = positions[0].astype(jnp.float32)[:, None] * freqs[None, :]
    cosine = jnp.cos(angle)[:, None, :]
    sine = jnp.sin(angle)[:, None, :]
    scale_one = lax.rsqrt(jnp.sum(start * start, axis=-1, keepdims=True) / WIDTH + EPSILON)
    normed_low = (start * scale_one * gain_first).astype(jnp.bfloat16)
    projected = dot(normed_low, weight_in)
    projected = jnp.concatenate(
        [projected[:, :IN_HALF], projected[:, IN_PAD : IN_PAD + IN_HALF]], axis=1
    )
    query_low = rotate(projected[:, :WIDTH], cosine, sine).astype(jnp.bfloat16)
    query_scaled = query_low * jnp.bfloat16(0.125)
    key_low = rotate(projected[:, WIDTH : WIDTH + key_width], cosine, sine).astype(jnp.bfloat16)
    value_low = projected[:, WIDTH + key_width :].astype(jnp.bfloat16)
    key_value = jnp.stack(
        [
            key_low.reshape(128, KEY_VALUE_HEADS, HEAD_SIZE),
            value_low.reshape(128, KEY_VALUE_HEADS, HEAD_SIZE),
        ],
        axis=2,
    ).reshape(128, 2 * key_width)
    all_kv = gather_blocks((key_value,), ("whole",), None, 1)[0].reshape(128, 64, 2 * key_width)
    pair_one = pair.reshape(1)
    attention, top, total = attend(table, pair_one, query_scaled, all_kv)
    mixed_low = pad_halves(attention.astype(jnp.bfloat16), OUT_HALF, OUT_PAD)
    branch = dot(mixed_low, weight_out, LAST)
    resid = start + jnp.where(held, branch, 0.0)
    scale_two = lax.rsqrt(jnp.sum(resid * resid, axis=-1, keepdims=True) / WIDTH + EPSILON)
    normed_two = (resid * scale_two * gain_second).astype(jnp.bfloat16)
    normed_two_grad, ffn_out, grad_gu, grad_down = feed_forward(
        normed_two, row_cotangent, weight_gu, weight_down, 2
    )
    resid_grad = upstream + norm_backward(resid, scale_two, normed_two_grad * gain_second)
    gain_two_grad = jnp.sum(normed_two_grad * resid * scale_two, axis=0)
    branch_grad_low = resid_grad.astype(jnp.bfloat16)
    grad_out = dot(branch_grad_low, mixed_low, FIRST).astype(jnp.bfloat16)
    mixed_grad = dot(branch_grad_low, weight_out)
    mixed_grad = jnp.concatenate(
        [mixed_grad[:, :OUT_HALF], mixed_grad[:, OUT_PAD : OUT_PAD + OUT_HALF]], axis=1
    )
    query_grad, all_kv_grad = attend_back(
        table, pair_one, query_scaled, mixed_grad, attention, top, total, all_kv
    )
    kv_grad, ffn_out = scatter_blocks(
        (all_kv_grad.reshape(2, 4, 4, 2, 128, 2 * key_width),),
        ((0, 0, 2 * key_width, 0),),
        None,
        ffn_out.reshape(4, 128, PADDED),
        3,
    )
    layer_out = dot((resid + ffn_out).astype(jnp.bfloat16), select, LAST).astype(jnp.bfloat16)
    kv_grad = kv_grad.reshape(128, KEY_VALUE_HEADS, 2, HEAD_SIZE)
    proj_grad = jnp.concatenate(
        [
            rotate(query_grad * 0.125, cosine, -sine),
            rotate(kv_grad[:, :, 0].reshape(128, key_width), cosine, -sine),
            kv_grad[:, :, 1].reshape(128, key_width),
        ],
        axis=1,
    ).astype(jnp.bfloat16)
    proj_grad = pad_halves(proj_grad, IN_HALF, IN_PAD)
    normed_one_grad = dot(proj_grad, weight_in, LAST)
    gain_one_grad = jnp.sum(normed_one_grad * start * scale_one, axis=0)
    through = norm_backward(start, scale_one, normed_one_grad * gain_first)
    input_grad = dot((resid_grad + through).astype(jnp.bfloat16), select, LAST).astype(jnp.bfloat16)

    grad_in = dot(normed_low, proj_grad, FIRST).astype(jnp.bfloat16)
    row = jnp.arange(PADDED)[:, None]
    lane = jnp.arange(IN_COLS)[None, :]
    gains_by_slot = jnp.stack([gain_one_grad, gain_two_grad]).reshape(2, 64, ROWS)
    gains_by_slot = jnp.pad(
        gains_by_slot.transpose(1, 0, 2), ((0, 0), (0, 0), (0, IN_PAD - ROWS))
    ).reshape(64, 1, IN_COLS)
    grad_in = jnp.where(
        row % ROWS == 15,
        jnp.broadcast_to(gains_by_slot, (64, ROWS, IN_COLS)).reshape(PADDED, IN_COLS).astype(jnp.bfloat16),
        grad_in,
    )
    own_cols = IN_PAD + OUT_PAD
    att_sum, ffn_parts = scatter_blocks(
        tuple(
            grad.reshape(2, 4, 4, 2, ROWS, grad.shape[1])
            for grad in (grad_in, grad_out, grad_gu, grad_down)
        ),
        (
            (0, 0, IN_PAD, 0),
            (0, IN_PAD, IN_PAD, own_cols),
            (1, 0, OUT_PAD, IN_PAD),
            (1, OUT_PAD, OUT_PAD, own_cols + IN_PAD),
            (2, 0, 2 * FF_QUARTER, 2 * own_cols),
            (3, 0, FF_QUARTER, 2 * own_cols + 2 * FF_QUARTER),
        ),
        own_cols,
        None,
        4,
    )
    gu_sum = ffn_parts[:, :15, : 2 * FF_QUARTER].reshape(2, 15, 2, FF_QUARTER)
    return (
        layer_out[None],
        input_grad[None],
        att_sum[:15, :IN_HALF],
        att_sum[:15, IN_PAD : IN_PAD + OUT_HALF],
        gu_sum.transpose(1, 2, 0, 3).reshape(15, 2, FF_HALF),
        ffn_parts[:, :15, 2 * FF_QUARTER :].transpose(1, 0, 2).reshape(15, FF_HALF),
        att_sum[15, :15].reshape(15, 1),
    )


def solution(mesh):
    in_specs = (
        P("fsdp", "ctx", None),
        P("fsdp", "ctx", None),
        P("fsdp", "ctx"),
        P("fsdp", "ctx"),
        P("ctx", "fsdp"),
        P("ctx", "fsdp"),
        P("ctx", None, "fsdp"),
        P("ctx", "fsdp"),
        P("ctx", "fsdp"),
    )
    out_specs = (
        P("fsdp", "ctx", None),
        P("fsdp", "ctx", None),
        P("ctx", "fsdp"),
        P("ctx", "fsdp"),
        P("ctx", None, "fsdp"),
        P("ctx", "fsdp"),
        P("ctx", "fsdp"),
    )
    return jax.shard_map(
        on_device, mesh=mesh, in_specs=in_specs, out_specs=out_specs, check_vma=False
    )
```

```python
import math

import jax
import jax.numpy as jnp
import numpy as np
from jax import lax
from jax.experimental import pallas as pl
from jax.experimental.pallas import tpu as pltpu
from jax.sharding import PartitionSpec as P

WIDTH = 960
QUERY_HEADS = 15
KEY_VALUE_HEADS = 5
GROUP = 3
HEAD_SIZE = 64
FF_HALF = 1280
FF_QUARTER = 640
EPSILON = 1e-05
ROWS = 16
PADDED = 1024
IN_HALF = 800
IN_PAD = 896
OUT_HALF = 480
OUT_PAD = 512
IN_COLS = 2 * IN_PAD
TILE = 512
QROWS = 384
MESH = pl.DeviceIdType.MESH
VMEM_LIMIT = 56 * 1024 * 1024


def column_map():
    cols = np.full((64, ROWS), -1, np.int32)
    cols[:, :15] = np.arange(64)[:, None] * 15 + np.arange(15)[None, :]
    return cols.reshape(-1)


COLUMN_MAP = column_map()


def coordinates():
    index = lax.axis_index("ctx")
    core = index % 2
    z = (index // 2) % 4
    y = (index // 8) % 4
    x = index // 32
    p1 = y * (1 - core) + z * core
    p2 = z * (1 - core) + y * core
    return x, p1, p2, core


def device_at(x, p1, p2, core):
    y = p1 * (1 - core) + p2 * core
    z = p2 * (1 - core) + p1 * core
    return ((x * 4 + y) * 4 + z) * 2 + core


def neighbours(x, p1, p2, core):
    index = lax.axis_index("ctx")
    return (
        device_at(1 - x, p1, p2, core),
        device_at(x, (p1 + 1) % 4, p2, core),
        device_at(x, (p1 + 3) % 4, p2, core),
        device_at(x, p1, (p2 + 1) % 4, core),
        device_at(x, p1, (p2 + 3) % 4, core),
        index + 1 - 2 * core,
    )


def block_of(ref, core, x, p1, p2):
    return ref.at[x, p1, p2, core] if core == 0 else ref.at[x, p2, p1, core]


def half_of(ref, core, x, p2):
    every = pl.ds(0, 4)
    return ref.at[x, every, p2, core] if core == 0 else ref.at[x, p2, every, core]


def slab_of(ref, core, p2):
    every = pl.ds(0, 4)
    both = pl.ds(0, 2)
    return ref.at[both, every, p2, core] if core == 0 else ref.at[both, p2, every, core]


def row_place():
    return lax.axis_index("fsdp") * 2 + lax.axis_index("ctx") // 32


def row_device(place):
    index = lax.axis_index("ctx")
    return {"fsdp": place // 2, "ctx": (place % 2) * 32 + index % 32}


def ctx_device(index):
    return {"ctx": index}


class Sender:
    def __init__(self, send_sem, recv_sem):
        self.send_sem, self.recv_sem, self.sent = send_sem, recv_sem, []

    def __call__(self, source, place, device):
        number = len(self.sent)
        copy = pltpu.make_async_remote_copy(
            src_ref=source,
            dst_ref=place,
            send_sem=self.send_sem.at[number],
            recv_sem=self.recv_sem.at[number],
            device_id=device,
            device_id_type=MESH,
        )
        copy.start()
        self.sent.append(copy)
        return copy

    def finish(self):
        for copy in self.sent:
            copy.wait_send()


class RowGather:
    def __init__(self, in_ref, out_ref, local_sem, send):
        self.out, self.send = out_ref, send
        here = row_place()
        self.left, self.right = (here + 3) % 4, (here + 1) % 4
        self.local = pltpu.make_async_copy(in_ref, out_ref.at[here], local_sem)
        self.local.start()
        self.from_left = send(in_ref, out_ref.at[here], row_device(self.right))
        self.from_right = send(in_ref, out_ref.at[here], row_device(self.left))

    def forward(self):
        rows = self.out.shape[1] // 2
        low, high = pl.ds(0, rows), pl.ds(rows, rows)
        self.from_left.wait_recv()
        place = self.out.at[self.left, low]
        self.far_low = self.send(place, place, row_device(self.right))
        self.from_right.wait_recv()
        place = self.out.at[self.right, high]
        self.far_high = self.send(place, place, row_device(self.left))

    def finish(self):
        self.far_low.wait_recv()
        self.far_high.wait_recv()
        self.local.wait()


class RowScatter:
    def __init__(self, in_ref, far, near_left, near_right, stage, send):
        self.p, self.far, self.stage, self.send = in_ref, far, stage, send
        self.near_left, self.near_right = near_left, near_right
        self.here = row_place()
        self.left, self.right = (self.here + 3) % 4, (self.here + 1) % 4
        to_left, to_right = row_device(self.left), row_device(self.right)
        opposite = (self.here + 2) % 4
        rows = in_ref.shape[1] // 2
        self.low, self.high = pl.ds(0, rows), pl.ds(rows, rows)
        low, high = self.low, self.high
        self.got_low = send(in_ref.at[opposite, low], far.at[0], to_right)
        self.got_high = send(in_ref.at[opposite, high], far.at[1], to_left)
        self.waits = [
            send(in_ref.at[self.right, high], near_left.at[high], to_right),
            send(in_ref.at[self.left, low], near_right.at[low], to_left),
        ]

    def forward(self):
        rows = self.p.shape[1] // 2
        self.got_low.wait_recv()
        self.stage[0] = self.p[self.right, 0:rows] + self.far[0]
        self.waits.append(
            self.send(self.stage.at[0], self.near_left.at[self.low], row_device(self.right))
        )
        self.got_high.wait_recv()
        self.stage[1] = self.p[self.left, rows : 2 * rows] + self.far[1]
        self.waits.append(
            self.send(self.stage.at[1], self.near_right.at[self.high], row_device(self.left))
        )

    def finish(self, out_ref):
        for copy in self.waits:
            copy.wait_recv()
        total = self.p[self.here].astype(jnp.float32) + self.near_left[...].astype(jnp.float32)
        out_ref[...] = total + self.near_right[...].astype(jnp.float32)


def greet(devices):
    barrier = pltpu.get_barrier_semaphore()
    for device in devices:
        pl.semaphore_signal(barrier, inc=1, device_id=device, device_id_type=MESH)
    pl.semaphore_wait(barrier, len(devices))


def greet_ctx(with_row):
    devices = [ctx_device(index) for index in neighbours(*coordinates())]
    if with_row:
        here = row_place()
        step = 2 * (here % 2) - 1
        devices.append(row_device((here + step + 4) % 4))
    greet(devices)


def row_kernel_entry():
    here = row_place()
    greet([row_device((here + 3) % 4), row_device((here + 1) % 4)])


def row_scratch(rows, columns):
    return [
        pltpu.VMEM((2, rows // 2, columns), jnp.bfloat16),
        pltpu.VMEM((rows, columns), jnp.bfloat16),
        pltpu.VMEM((rows, columns), jnp.bfloat16),
        pltpu.VMEM((2, rows // 2, columns), jnp.bfloat16),
        pltpu.SemaphoreType.DMA((6,)),
        pltpu.SemaphoreType.DMA((6,)),
    ]


class Group:
    def __init__(self, copies):
        self.copies = copies

    def wait_recv(self):
        for copy in self.copies:
            copy.wait_recv()


def gather_kernel(modes, with_row, *refs):
    count = len(modes)
    ins, refs = refs[: count + with_row], refs[count + with_row :]
    outs, refs = refs[: count + with_row], refs[count + with_row :]
    greet_ctx("row" in modes or with_row)
    core = coordinates()[3]
    for chosen in range(2):

        @pl.when(core == chosen)
        def _(chosen=chosen):
            gather_body(chosen, modes, with_row, ins, outs, *refs)


def gather_body(
    core, modes, with_row, ins, outs, local_sem, send_sem, recv_sem, row_local, row_send, row_recv
):
    x, p1, p2, _ = coordinates()
    across, right1, left1, right2, left2, sibling = neighbours(x, p1, p2, core)
    p1p, p1m = (p1 + 1) % 4, (p1 + 3) % 4
    p2p, p2m, p2o = (p2 + 1) % 4, (p2 + 3) % 4, (p2 + 2) % 4
    place = row_place()
    row_left, row_right = (place + 3) % 4, (place + 1) % 4
    sender = Sender(send_sem, recv_sem)
    arrays = range(len(modes))
    plain = [k for k in arrays if modes[k] != "row"]
    rows = [k for k in arrays if modes[k] == "row"]
    mine = [ins[k].at[x] if modes[k] == "split" else ins[k] for k in arrays]
    yours = [ins[k].at[1 - x] if modes[k] == "split" else ins[k] for k in arrays]

    def send(places, to, chosen=arrays, sources=None):
        sources = places if sources is None else sources
        return Group([sender(sources[k], places[k], ctx_device(to)) for k in chosen])

    def block(side, q1):
        return [block_of(outs[k], core, side, q1, p2) for k in arrays]

    def half(side, q2):
        return [half_of(outs[k], core, side, q2) for k in arrays]

    def slot(k, owner):
        width = ins[k].shape[-1]
        columns = pl.ds(pl.multiple_of((owner // 2) * width, 128), width)
        return block_of(outs[k], core, owner % 2, p1, p2).at[pl.ds(0, ROWS), columns]

    here = block(x, p1)
    there = block(1 - x, p1)
    locals_ = [
        pltpu.make_async_copy(
            mine[k], slot(k, place) if k in rows else here[k], local_sem.at[k]
        )
        for k in arrays
    ]
    for copy in locals_:
        copy.start()
    row_near = Group(
        [
            sender(ins[k], slot(k, place), row_device(to))
            for to in (row_right, row_left)
            for k in rows
        ]
    )
    crossed = send(here, across, plain, yours)
    own_left = send(here, right1, plain, mine)
    own_right = send(here, left1, plain, mine)
    row_near.wait_recv()
    row_far = Group(
        [sender(slot(k, row_left), slot(k, row_left), row_device(row_right)) for k in rows]
    )
    crossed.wait_recv()
    other_left = send(there, right1)
    other_right = send(there, left1)
    for copy in locals_:
        copy.wait()
    row_far.wait_recv()
    own_left.copies += send(here, right1, rows).copies
    own_right.copies += send(here, left1, rows).copies
    if with_row:
        row_sender = Sender(row_send, row_recv)
        row = RowGather(ins[-1], outs[-1], row_local, row_sender)
    own_left.wait_recv()
    own_far = send(block(x, p1m), right1)
    own_right.wait_recv()
    own_far.wait_recv()
    own_left = send(half(x, p2), right2)
    own_right = send(half(x, p2), left2)
    last = [send(half(x, p2), sibling)]
    other_right.wait_recv()
    other_far = send(block(1 - x, p1p), left1)
    other_left.wait_recv()
    other_far.wait_recv()
    other_right = send(half(1 - x, p2), left2)
    other_left = send(half(1 - x, p2), right2)
    last.append(send(half(1 - x, p2), sibling))
    own_left.wait_recv()
    own_far = send(half(x, p2m), right2)
    last.append(send(half(x, p2m), sibling))
    own_right.wait_recv()
    last.append(send(half(x, p2p), sibling))
    if with_row:
        row.forward()
    other_right.wait_recv()
    other_far = send(half(1 - x, p2p), left2)
    last.append(send(half(1 - x, p2p), sibling))
    other_left.wait_recv()
    last.append(send(half(1 - x, p2m), sibling))
    own_far.wait_recv()
    last.append(send(half(x, p2o), sibling))
    if with_row:
        row.finish()
    other_far.wait_recv()
    last.append(send(half(1 - x, p2o), sibling))
    for group in last:
        group.wait_recv()
    sender.finish()
    if with_row:
        row_sender.finish()


def gather_blocks(blocks, modes, row_block, collective_id):
    with_row = row_block is not None
    operands = list(blocks)
    shapes = [
        jax.ShapeDtypeStruct(
            (2, 4, 4, 2, block.shape[-2], block.shape[-1] * (2 if mode == "row" else 1)),
            block.dtype,
        )
        for block, mode in zip(blocks, modes)
    ]
    if with_row:
        operands.append(row_block)
        shapes.append(jax.ShapeDtypeStruct((4,) + row_block.shape, row_block.dtype))
    number = 23 * len(blocks)
    return pl.pallas_call(
        lambda *refs: gather_kernel(modes, int(with_row), *refs),
        out_shape=tuple(shapes),
        in_specs=[pl.BlockSpec(memory_space=pl.ANY)] * len(operands),
        out_specs=(pl.BlockSpec(memory_space=pl.ANY),) * len(operands),
        scratch_shapes=[
            pltpu.SemaphoreType.DMA((len(blocks),)),
            pltpu.SemaphoreType.DMA((number,)),
            pltpu.SemaphoreType.DMA((number,)),
            pltpu.SemaphoreType.DMA,
            pltpu.SemaphoreType.DMA((4,)),
            pltpu.SemaphoreType.DMA((4,)),
        ],
        compiler_params=pltpu.CompilerParams(
            collective_id=collective_id, has_side_effects=True
        ),
    )(*operands)


def scatter_kernel(pieces, halved, with_row, side, *refs):
    count = 1 + max(piece[0] for piece in pieces)
    ins, refs = refs[:count], refs[count:]
    if with_row:
        row_in, refs = refs[0], refs[1:]
    side_work, side_in, side_out = side
    side_ins, refs = refs[:side_in], refs[side_in:]
    results = 5 if halved else 1
    out_refs, refs = refs[:results], refs[results:]
    if with_row:
        row_out, refs = refs[0], refs[1:]
    side_outs, refs = refs[:side_out], refs[side_out:]
    (acc, other, far_low, far_high, near_left, near_right) = refs[:6]
    (pair_low, pair_high, pair_left, pair_right, last) = refs[6:11]
    (local_sem, cross_send, cross_recv, send_sem, recv_sem) = refs[11:16]
    x, p1, p2, core = coordinates()
    across, right1, left1, right2, left2, sibling = neighbours(x, p1, p2, core)
    greet_ctx(with_row or halved)
    p1p, p1m, p1o = (p1 + 1) % 4, (p1 + 3) % 4, (p1 + 2) % 4
    p2p, p2m, p2o = (p2 + 1) % 4, (p2 + 3) % 4, (p2 + 2) % 4
    needed = (p2o, p2m, p2p, p2)
    theirs = (p1o, p1m, p1p, p1)
    sender = Sender(send_sem, recv_sem)

    def part(ref, place, piece):
        if len(pieces) == 1:
            return ref.at[place]
        every = [pl.ds(0, size) for size in ref.shape[1:-1]]
        return ref.at[tuple([place] + every + [pl.ds(pieces[piece][3], pieces[piece][2])])]

    def source_of(piece, chosen, place):
        array, start, width, _ = pieces[piece]
        slab = slab_of(ins[array], chosen, place)
        if len(pieces) == 1:
            return slab
        every = [pl.ds(0, size) for size in slab.shape[:-1]]
        return slab.at[tuple(every + [pl.ds(start, width)])]

    def crossing(k, piece, source):
        return pltpu.make_async_remote_copy(
            src_ref=source,
            dst_ref=part(other, theirs[k], piece),
            send_sem=cross_send.at[k, piece],
            recv_sem=cross_recv.at[k, piece],
            device_id=ctx_device(sibling),
            device_id_type=MESH,
        )

    for chosen in range(2):

        @pl.when(core == chosen)
        def _(chosen=chosen):
            for k in range(4):
                for piece in range(len(pieces)):
                    crossing(k, piece, source_of(piece, 1 - chosen, theirs[k])).start()
                    pltpu.make_async_copy(
                        source_of(piece, chosen, needed[k]),
                        part(acc, needed[k], piece),
                        local_sem.at[k, piece],
                    ).start()

    if with_row:
        row_sender = Sender(refs[20], refs[21])
        row = RowScatter(row_in, refs[16], refs[17], refs[18], refs[19], row_sender)

    def send(source, place, to):
        return sender(source, place, ctx_device(to))

    def add(place, term):
        @pl.loop(0, 4)
        def _(step):
            place[step] = place[step] + term[step]

    def add_both(side):
        @pl.loop(0, 4)
        def _(step):
            total = acc[p2, side, step].astype(jnp.float32)
            total = total + near_left[side, step].astype(jnp.float32)
            total = total + near_right[side, step].astype(jnp.float32)
            acc[p2, side, step] = total.astype(acc.dtype)

    def merge(k):
        for piece in range(len(pieces)):
            mine = part(acc, needed[k], piece)
            pltpu.make_async_copy(mine, mine, local_sem.at[k, piece]).wait()
            crossing(k, piece, part(other, theirs[k], piece)).wait_recv()
        for side in range(2):
            add(acc.at[needed[k], side], other.at[needed[k], side])

    merge(0)
    got_low = send(acc.at[p2o, 0], far_low, right2)
    got_high = send(acc.at[p2o, 1], far_high, left2)
    merge(1)
    right_low = send(acc.at[p2m, 0], near_right.at[0], left2)
    merge(2)
    left_high = send(acc.at[p2p, 1], near_left.at[1], right2)
    side_work(side_ins, side_outs)
    got_low.wait_recv()
    add(acc.at[p2p, 0], far_low)
    left_low = send(acc.at[p2p, 0], near_left.at[0], right2)
    got_high.wait_recv()
    add(acc.at[p2m, 1], far_high)
    right_high = send(acc.at[p2m, 1], near_right.at[1], left2)
    merge(3)
    if with_row:
        row.forward()
    right_low.wait_recv()
    left_low.wait_recv()
    add_both(0)
    got_low = send(acc.at[p2, 0, p1o], pair_low, right1)
    near_low = send(acc.at[p2, 0, p1m], pair_right.at[0], left1)
    left_high.wait_recv()
    right_high.wait_recv()
    add_both(1)
    got_high = send(acc.at[p2, 1, p1o], pair_high, left1)
    near_high = send(acc.at[p2, 1, p1p], pair_left.at[1], right1)
    got_low.wait_recv()
    acc[p2, 0, p1p] = acc[p2, 0, p1p] + pair_low[...]
    left_low = send(acc.at[p2, 0, p1p], pair_left.at[0], right1)
    got_high.wait_recv()
    acc[p2, 1, p1m] = acc[p2, 1, p1m] + pair_high[...]
    right_high = send(acc.at[p2, 1, p1m], pair_right.at[1], left1)
    if with_row:
        row.finish(row_out)
    near_low.wait_recv()
    near_high.wait_recv()
    left_low.wait_recv()
    right_high.wait_recv()

    @pl.loop(0, 2)
    def _(j):
        total = acc[p2, j, p1].astype(jnp.float32) + pair_left[j].astype(jnp.float32)
        total = total + pair_right[j].astype(jnp.float32)
        acc[p2, j, p1] = total.astype(acc.dtype)

    if halved:
        finish_row(halved, acc, p1, p2, refs[16:20], last, sender, out_refs)
    else:
        final = send(acc.at[p2, 1 - x, p1], last, across)
        final.wait_recv()
        total = acc[p2, x, p1].astype(jnp.float32) + last[...].astype(jnp.float32)
        out_refs[0][...] = total
    for k in range(4):
        for piece in range(len(pieces)):
            crossing(k, piece, part(other, theirs[k], piece)).wait_send()
    sender.finish()
    if with_row:
        row_sender.finish()


def finish_row(halved, acc, p1, p2, buffers, last, sender, out_refs):
    in_ref, out_ref, gu_ref, down_ref, spare_ref = out_refs
    far, from_left, from_right, stage = buffers
    here = row_place()
    left, right, opposite = (here + 3) % 4, (here + 1) % 4, (here + 2) % 4
    x = here % 2
    every = pl.ds(0, ROWS)
    rest = pl.ds(2 * halved, acc.shape[-1] - 2 * halved)

    def columns(owner):
        return pl.ds(pl.multiple_of((owner // 2) * halved, 128), halved)

    def block(owner):
        return acc.at[p2, owner % 2, p1, every, columns(owner)]

    def keep_part(side, value):
        value = value.astype(jnp.float32)[: ROWS - 1]
        span = pl.ds(pl.multiple_of(side * FF_QUARTER, 128), FF_QUARTER)
        gu_ref[:, 0, span] = value[:, :FF_QUARTER]
        gu_ref[:, 1, span] = value[:, FF_QUARTER : 2 * FF_QUARTER]
        down_ref[:, span] = value[:, 2 * FF_QUARTER :]

    far_copy = sender(block(opposite), far, row_device(right))
    from_right_copy = sender(block(left), from_right, row_device(left))
    x_neighbour = row_device((here // 2) * 2 + 1 - x)
    parts_copy = sender(acc.at[p2, 1 - x, p1, every, rest], last, x_neighbour)
    far_copy.wait_recv()
    stage[...] = acc[p2, right % 2, p1, :, columns(right)] + far[...]
    from_left_copy = sender(stage, from_left, row_device(right))
    keep_part(x, acc[p2, x, p1, :, rest])
    parts_copy.wait_recv()
    keep_part(1 - x, last[...])
    from_right_copy.wait_recv()
    from_left_copy.wait_recv()
    total = acc[p2, x, p1, :, columns(here)].astype(jnp.float32)
    total = total + from_left[...].astype(jnp.float32)
    total = total + from_right[...].astype(jnp.float32)
    in_ref[...] = total[: ROWS - 1, :IN_HALF]
    out_ref[...] = total[: ROWS - 1, IN_PAD : IN_PAD + OUT_HALF]
    spare_ref[...] = total[ROWS - 1 :, :128]


def scatter_blocks(arrays, pieces, halved, row_blocks, side, collective_id):
    rows = arrays[0].shape[-2]
    columns = sum(piece[2] for piece in pieces)
    kind = arrays[0].dtype
    block = (rows, columns)
    with_row = row_blocks is not None
    operands = list(arrays)
    in_specs = [pl.BlockSpec(memory_space=pl.ANY)] * len(arrays)
    results = [block]
    last = block
    scratch = []
    if halved:
        last = (rows, columns - 2 * halved)
        results = [
            (rows - 1, IN_HALF),
            (rows - 1, OUT_HALF),
            (rows - 1, 2, FF_HALF),
            (rows - 1, FF_HALF),
            (1, 128),
        ]
        scratch = [pltpu.VMEM((rows, halved), kind)] * 4
    shapes = [jax.ShapeDtypeStruct(shape, jnp.float32) for shape in results]
    if with_row:
        operands.append(row_blocks)
        in_specs.append(pl.BlockSpec(memory_space=pltpu.VMEM))
        shapes.append(jax.ShapeDtypeStruct(row_blocks.shape[1:], jnp.float32))
        scratch = row_scratch(*row_blocks.shape[1:])
    side_work, side_operands, side_shapes = side
    operands += list(side_operands)
    in_specs += [pl.BlockSpec(memory_space=pltpu.VMEM)] * len(side_operands)
    shapes += list(side_shapes)
    side = (side_work, len(side_operands), len(side_shapes))
    return pl.pallas_call(
        lambda *refs: scatter_kernel(pieces, halved, with_row, side, *refs),
        out_shape=tuple(shapes),
        in_specs=in_specs,
        out_specs=(pl.BlockSpec(memory_space=pltpu.VMEM),) * len(shapes),
        scratch_shapes=[
            pltpu.VMEM((4, 2, 4) + block, kind),
            pltpu.VMEM((4, 2, 4) + block, kind),
            pltpu.VMEM((4,) + block, kind),
            pltpu.VMEM((4,) + block, kind),
            pltpu.VMEM((2, 4) + block, kind),
            pltpu.VMEM((2, 4) + block, kind),
            pltpu.VMEM(block, kind),
            pltpu.VMEM(block, kind),
            pltpu.VMEM((2,) + block, kind),
            pltpu.VMEM((2,) + block, kind),
            pltpu.VMEM(last, kind),
            pltpu.SemaphoreType.DMA((4, len(pieces))),
            pltpu.SemaphoreType.DMA((4, len(pieces))),
            pltpu.SemaphoreType.DMA((4, len(pieces))),
            pltpu.SemaphoreType.DMA((16,)),
            pltpu.SemaphoreType.DMA((16,)),
        ]
        + scratch,
        compiler_params=pltpu.CompilerParams(
            collective_id=collective_id, has_side_effects=True, vmem_limit_bytes=VMEM_LIMIT
        ),
    )(*operands)


def weight_grad_work(ins, outs):
    @pl.loop(0, PADDED // 256)
    def _(step):
        span = pl.ds(pl.multiple_of(step * 256, 256), 256)
        outs[0][span, :] = dot(ins[0][:, span], ins[1][...], FIRST).astype(jnp.bfloat16)


def unpad_work(ins, outs):
    for k in range(2):
        outs[k][...] = dot(ins[2][...], ins[k][...], LAST).astype(jnp.bfloat16)


LAST = (((1,), (1,)), ((), ()))
FIRST = (((0,), (0,)), ((), ()))
PLAIN = (((1,), (0,)), ((), ()))


def dot(a, b, dims=PLAIN):
    return lax.dot_general(a, b, dims, preferred_element_type=jnp.float32)


def feed_forward_kernel(
    n_ref,
    c_ref,
    gu_ref,
    down_ref,
    dn_ref,
    part_ref,
    grad_gu_ref,
    grad_down_ref,
    normed,
    partial,
    hidden,
    gate_up_grad,
    far,
    near_left,
    near_right,
    stage,
    send_sem,
    recv_sem,
):
    row_kernel_entry()
    here = row_place()
    left, right, opposite = (here + 3) % 4, (here + 1) % 4, (here + 2) % 4
    to_left, to_right = row_device(left), row_device(right)

    def rows(owner, start=0, size=128):
        return pl.ds(pl.multiple_of(owner * 128 + start, 64), size)

    def copy(number, source, place, device):
        return pltpu.make_async_remote_copy(
            src_ref=source,
            dst_ref=place,
            send_sem=send_sem.at[number],
            recv_sem=recv_sem.at[number],
            device_id=device,
            device_id_type=MESH,
        )

    mine = normed.at[rows(here)]
    low, high = pl.ds(0, 64), pl.ds(64, 64)
    normed_right = copy(0, n_ref, mine, to_right)
    normed_left = copy(1, n_ref, mine, to_left)
    place = normed.at[rows(left, 0, 64)]
    normed_far_low = copy(2, place, place, to_right)
    place = normed.at[rows(right, 64, 64)]
    normed_far_high = copy(3, place, place, to_left)
    far_low = copy(4, partial.at[rows(opposite, 0, 64)], far.at[0], to_right)
    far_high = copy(5, partial.at[rows(opposite, 64, 64)], far.at[1], to_left)
    near_low = copy(6, partial.at[rows(left, 0, 64)], near_right.at[low], to_left)
    near_high = copy(7, partial.at[rows(right, 64, 64)], near_left.at[high], to_right)
    sum_low = copy(8, stage.at[0], near_left.at[low], to_right)
    sum_high = copy(9, stage.at[1], near_right.at[high], to_left)
    normed_right.start()
    normed_left.start()
    normed[rows(here), :] = n_ref[...]

    @pl.loop(0, 4)
    def _(step):
        turn = jnp.where(step == 1, 3, jnp.where(step == 2, 1, jnp.where(step == 3, 2, 0)))
        owner = (here + turn) % 4

        @pl.when(step == 1)
        def _():
            normed_right.wait_recv()
            normed_far_low.start()

        @pl.when(step == 2)
        def _():
            normed_left.wait_recv()
            normed_far_high.start()

        @pl.when(step == 3)
        def _():
            normed_far_low.wait_recv()
            normed_far_high.wait_recv()

        gate_vals = dot(normed[rows(owner), :], gu_ref[...])
        hidden_grad = dot(c_ref[rows(owner), :], down_ref[...])
        gate = gate_vals[:, :FF_QUARTER]
        upper = gate_vals[:, FF_QUARTER:]
        sigma = jax.nn.sigmoid(gate)
        silu_vals = gate * sigma
        hidden[rows(owner), :] = (silu_vals * upper).astype(jnp.bfloat16)
        gate_grad = hidden_grad * upper * sigma * (1.0 + gate * (1.0 - sigma))
        upper_grad = hidden_grad * silu_vals
        both = jnp.concatenate([gate_grad, upper_grad], axis=1).astype(jnp.bfloat16)
        gate_up_grad[rows(owner), :] = both
        partial[rows(owner), :] = dot(both, gu_ref[...], LAST).astype(jnp.bfloat16)

        @pl.when(step == 1)
        def _():
            near_low.start()

        @pl.when(step == 2)
        def _():
            near_high.start()

        @pl.when(step == 3)
        def _():
            far_low.start()
            far_high.start()

    @pl.loop(0, 4)
    def _(owner):
        part_ref[rows(owner), :] = dot(hidden[rows(owner), :], down_ref[...], LAST).astype(
            jnp.bfloat16
        )

    far_low.wait_recv()
    stage[0] = partial[rows(right, 0, 64), :] + far[0]
    sum_low.start()
    far_high.wait_recv()
    stage[1] = partial[rows(left, 64, 64), :] + far[1]
    sum_high.start()

    @pl.loop(0, PADDED // 256)
    def _(step):
        span = pl.ds(pl.multiple_of(step * 256, 256), 256)
        grad_gu_ref[span, :] = dot(normed[:, span], gate_up_grad[...], FIRST).astype(jnp.bfloat16)
        grad_down_ref[span, :] = dot(c_ref[:, span], hidden[...], FIRST).astype(jnp.bfloat16)

    for arrived in (near_low, near_high, sum_low, sum_high):
        arrived.wait_recv()
    total = partial[rows(here), :].astype(jnp.float32) + near_left[...].astype(jnp.float32)
    dn_ref[...] = total + near_right[...].astype(jnp.float32)
    for sent in (normed_right, normed_left, normed_far_low, normed_far_high, far_low, far_high):
        sent.wait_send()
    for sent in (near_low, near_high, sum_low, sum_high):
        sent.wait_send()


def feed_forward(normed, cotangent, weight_gu, weight_down, collective_id):
    kind = jnp.bfloat16
    return pl.pallas_call(
        feed_forward_kernel,
        out_shape=(
            jax.ShapeDtypeStruct((128, PADDED), jnp.float32),
            jax.ShapeDtypeStruct((512, PADDED), kind),
            jax.ShapeDtypeStruct(weight_gu.shape, kind),
            jax.ShapeDtypeStruct(weight_down.shape, kind),
        ),
        in_specs=[pl.BlockSpec(memory_space=pltpu.VMEM)] * 4,
        out_specs=(pl.BlockSpec(memory_space=pltpu.VMEM),) * 4,
        scratch_shapes=[
            pltpu.VMEM((512, PADDED), kind),
            pltpu.VMEM((512, PADDED), kind),
            pltpu.VMEM((512, FF_QUARTER), kind),
            pltpu.VMEM((512, 2 * FF_QUARTER), kind),
            pltpu.VMEM((2, 64, PADDED), kind),
            pltpu.VMEM((128, PADDED), kind),
            pltpu.VMEM((128, PADDED), kind),
            pltpu.VMEM((2, 64, PADDED), kind),
            pltpu.SemaphoreType.DMA((10,)),
            pltpu.SemaphoreType.DMA((10,)),
        ],
        compiler_params=pltpu.CompilerParams(
            collective_id=collective_id, has_side_effects=True, vmem_limit_bytes=VMEM_LIMIT
        ),
        cost_estimate=pl.CostEstimate(
            flops=7 * 10**9, bytes_accessed=10**7, transcendentals=4 * 10**5
        ),
    )(normed, cotangent, weight_gu, weight_down)


def load_tiles(table_ref, kv_hbm, kv, sems, tiles):
    @pl.loop(0, tiles)
    def _(tile):
        for j in range(8):
            block = tile * 8 + j
            pltpu.make_async_copy(
                kv_hbm.at[table_ref[block]],
                kv.at[pl.ds(pl.multiple_of(block * 64, 64), 64)],
                sems.at[tile],
            ).start()


def wait_tile(kv, sems, tile):
    part = kv.at[pl.ds(pl.multiple_of(tile * TILE, TILE), TILE)]
    pltpu.make_async_copy(part, part, sems.at[tile]).wait()


def visible_keys(tile, pair, first_row, rows):
    shape = (rows, TILE)
    row = first_row + lax.broadcasted_iota(jnp.int32, shape, 0)
    key = tile * TILE + lax.broadcasted_iota(jnp.int32, shape, 1)
    order = jnp.where(row < QROWS // 2, pair, 127 - pair) * 64 + row % 64
    return key <= order


def head_parts():
    for g in range(KEY_VALUE_HEADS):
        for half in range(2):
            for h in range(GROUP):
                rows = slice((half * GROUP + h) * 64, (half * GROUP + h) * 64 + 64)
                column = (GROUP * g + h) * HEAD_SIZE
                yield g, rows, slice(half * 64, half * 64 + 64), slice(column, column + 64)


def run_tiles(pair, step):
    low_tiles = (pair + 8) // 8
    high_tiles = (135 - pair) // 8

    @pl.loop(0, low_tiles - 1)
    def _(tile):
        step(tile, 0, QROWS, False)

    step(low_tiles - 1, 0, QROWS, True)

    @pl.loop(low_tiles, high_tiles - 1)
    def _(tile):
        step(tile, QROWS // 2, QROWS // 2, False)

    step(high_tiles - 1, QROWS // 2, QROWS // 2, True)


def lane_parts(value):
    return [value[:, k * 128 : k * 128 + 128] for k in range(TILE // 128)]


def attend_kernel(table_ref, pair_ref, q_ref, kv_hbm, out_ref, top_ref, sum_ref, kv, q, acc, sems):
    pair = pair_ref[0]
    high_tiles = (135 - pair) // 8
    load_tiles(table_ref, kv_hbm, kv, sems, high_tiles)
    q[...] = jnp.zeros(q.shape, q.dtype)
    for g, rows, tokens, columns in head_parts():
        q[g, rows, 0:64] = q_ref[tokens, columns]
    acc[...] = jnp.zeros(acc.shape, jnp.float32)
    top_ref[...] = jnp.full(top_ref.shape, -1e30, jnp.float32)
    sum_ref[...] = jnp.zeros(sum_ref.shape, jnp.float32)

    def step(tile, first_row, rows, masked):
        wait_tile(kv, sems, tile)
        span = slice(first_row, first_row + rows)
        if masked:
            seen = visible_keys(tile, pair, first_row, rows)
        heads = range(KEY_VALUE_HEADS)
        keys = [
            kv[pl.ds(pl.multiple_of(tile * TILE, TILE), TILE), g * 128 : g * 128 + 128]
            for g in heads
        ]
        scores = [dot(q[g, span, :], keys[g], LAST) for g in heads]
        if masked:
            scores = [jnp.where(seen, score, -1e30) for score in scores]
        parts = [lane_parts(score) for score in scores]
        best = [
            jnp.maximum(jnp.maximum(p[0], p[1]), jnp.maximum(p[2], p[3])) for p in parts
        ]
        before = [top_ref[g, span, :] for g in heads]
        highest = [
            jnp.maximum(before[g], jnp.max(best[g], axis=1, keepdims=True)) for g in heads
        ]
        shrink = [jnp.exp(before[g] - highest[g]) for g in heads]
        parts = [[jnp.exp(part - highest[g]) for part in parts[g]] for g in heads]
        for g in heads:
            p = parts[g]
            top_ref[g, span, :] = highest[g]
            sum_ref[g, span, :] = sum_ref[g, span, :] * shrink[g] + ((p[0] + p[1]) + (p[2] + p[3]))
        mixed = [
            dot(jnp.concatenate([p.astype(jnp.bfloat16) for p in parts[g]], axis=1), keys[g])
            for g in heads
        ]
        for g in heads:
            acc[g, span, :] = acc[g, span, :] * shrink[g] + mixed[g]

    run_tiles(pair, step)
    for g in range(KEY_VALUE_HEADS):
        total = jnp.sum(sum_ref[g], axis=1, keepdims=True)
        sum_ref[g] = jnp.broadcast_to(total, sum_ref.shape[1:])
        acc[g] = acc[g] / sum_ref[g]
    for g, rows, tokens, columns in head_parts():
        out_ref[tokens, columns] = acc[g, rows, 64:128]


def attend(table, pair, q, kv):
    heads = (KEY_VALUE_HEADS, QROWS, 128)
    return pl.pallas_call(
        attend_kernel,
        out_shape=(
            jax.ShapeDtypeStruct((128, WIDTH), jnp.float32),
            jax.ShapeDtypeStruct(heads, jnp.float32),
            jax.ShapeDtypeStruct(heads, jnp.float32),
        ),
        in_specs=[
            pl.BlockSpec(memory_space=pltpu.SMEM),
            pl.BlockSpec(memory_space=pltpu.SMEM),
            pl.BlockSpec(memory_space=pltpu.VMEM),
            pl.BlockSpec(memory_space=pl.ANY),
        ],
        out_specs=(pl.BlockSpec(memory_space=pltpu.VMEM),) * 3,
        scratch_shapes=[
            pltpu.VMEM((8192, 640), jnp.bfloat16),
            pltpu.VMEM(heads, jnp.bfloat16),
            pltpu.VMEM(heads, jnp.float32),
            pltpu.SemaphoreType.DMA((16,)),
        ],
        compiler_params=pltpu.CompilerParams(vmem_limit_bytes=VMEM_LIMIT),
        cost_estimate=pl.CostEstimate(
            flops=4 * 10**9, bytes_accessed=10**7, transcendentals=8 * 10**6
        ),
    )(table, pair, q, kv)


def attend_back_kernel(
    table_ref,
    pair_ref,
    q_ref,
    grad_ref,
    out_ref,
    top_ref,
    sum_ref,
    kv_hbm,
    dq_ref,
    dkv_hbm,
    kv,
    dkv,
    q,
    gs,
    q_turned,
    g_turned,
    shift,
    acc,
    sems,
    out_sems,
):
    pair = pair_ref[0]
    high_tiles = (135 - pair) // 8
    load_tiles(table_ref, kv_hbm, kv, sems, high_tiles)

    def store(tile):
        for j in range(8):
            block = tile * 8 + j
            pltpu.make_async_copy(
                dkv.at[pl.ds(pl.multiple_of(block * 64, 64), 64)],
                dkv_hbm.at[table_ref[block]],
                out_sems.at[tile],
            ).start()

    @pl.loop(high_tiles, 16)
    def _(tile):
        dkv[pl.ds(pl.multiple_of(tile * TILE, TILE), TILE), :] = jnp.zeros(
            (TILE, 640), jnp.bfloat16
        )
        store(tile)

    q[...] = jnp.zeros(q.shape, q.dtype)
    gs[...] = jnp.zeros(gs.shape, gs.dtype)
    for g, rows, tokens, columns in head_parts():
        q[g, rows, 0:64] = q_ref[tokens, columns]
        grad = grad_ref[tokens, columns]
        total = sum_ref[g, rows, :]
        gs[g, rows, 64:128] = (grad / total[:, 0:64]).astype(jnp.bfloat16)
        delta = jnp.sum(grad * out_ref[tokens, columns], axis=1, keepdims=True)
        shift[g, rows, :] = delta / total
    for g in range(KEY_VALUE_HEADS):
        q_turned[g] = q[g].T
        g_turned[g] = gs[g].T
    acc[...] = jnp.zeros(acc.shape, jnp.float32)

    def step(tile, first_row, rows, masked):
        wait_tile(kv, sems, tile)
        span = slice(first_row, first_row + rows)
        part = pl.ds(pl.multiple_of(tile * TILE, TILE), TILE)
        if masked:
            seen = visible_keys(tile, pair, first_row, rows)
        heads = range(KEY_VALUE_HEADS)
        keys = [kv[part, g * 128 : g * 128 + 128] for g in heads]
        scores = [dot(q[g, span, :], keys[g], LAST) for g in heads]
        prob_grad = [dot(gs[g, span, :], keys[g], LAST) for g in heads]
        if masked:
            scores = [jnp.where(seen, score, -1e30) for score in scores]
        for g in heads:
            top, moved = top_ref[g, span, :], shift[g, span, :]
            probs = [jnp.exp(part_ - top) for part_ in lane_parts(scores[g])]
            grads = [
                (probs[k] * (part_ - moved)).astype(jnp.bfloat16)
                for k, part_ in enumerate(lane_parts(prob_grad[g]))
            ]
            score_grad = jnp.concatenate(grads, axis=1)
            probs_low = jnp.concatenate([prob.astype(jnp.bfloat16) for prob in probs], axis=1)
            both = dot(
                jnp.concatenate([q_turned[g, :, span], g_turned[g, :, span]], axis=1),
                jnp.concatenate([score_grad, probs_low], axis=0),
            )
            acc[g, span, :] = acc[g, span, :] + dot(score_grad, keys[g])
            dkv[part, g * 128 : g * 128 + 128] = both.astype(jnp.bfloat16).T
        store(tile)

    run_tiles(pair, step)
    for g, rows, tokens, columns in head_parts():
        dq_ref[tokens, columns] = acc[g, rows, 0:64]

    @pl.loop(0, 16)
    def _(tile):
        part = dkv.at[pl.ds(pl.multiple_of(tile * TILE, TILE), TILE)]
        pltpu.make_async_copy(part, part, out_sems.at[tile]).wait()


def attend_back(table, pair, q, grad, out, top, total, kv):
    heads = (KEY_VALUE_HEADS, QROWS, 128)
    turned = (KEY_VALUE_HEADS, 128, QROWS)
    return pl.pallas_call(
        attend_back_kernel,
        out_shape=(
            jax.ShapeDtypeStruct((128, WIDTH), jnp.float32),
            jax.ShapeDtypeStruct((128, 64, 640), jnp.bfloat16),
        ),
        in_specs=[pl.BlockSpec(memory_space=pltpu.SMEM)] * 2
        + [pl.BlockSpec(memory_space=pltpu.VMEM)] * 5
        + [pl.BlockSpec(memory_space=pl.ANY)],
        out_specs=(
            pl.BlockSpec(memory_space=pltpu.VMEM),
            pl.BlockSpec(memory_space=pl.ANY),
        ),
        scratch_shapes=[
            pltpu.VMEM((8192, 640), jnp.bfloat16),
            pltpu.VMEM((8192, 640), jnp.bfloat16),
            pltpu.VMEM(heads, jnp.bfloat16),
            pltpu.VMEM(heads, jnp.bfloat16),
            pltpu.VMEM(turned, jnp.bfloat16),
            pltpu.VMEM(turned, jnp.bfloat16),
            pltpu.VMEM(heads, jnp.float32),
            pltpu.VMEM(heads, jnp.float32),
            pltpu.SemaphoreType.DMA((16,)),
            pltpu.SemaphoreType.DMA((16,)),
        ],
        compiler_params=pltpu.CompilerParams(vmem_limit_bytes=VMEM_LIMIT),
        cost_estimate=pl.CostEstimate(
            flops=10**10, bytes_accessed=2 * 10**7, transcendentals=8 * 10**6
        ),
    )(table, pair, q, grad, out, top, total, kv)


def pad_columns(value, columns):
    return jnp.pad(value, ((0, 0), (0, columns - value.shape[1])))


def pad_halves(value, half, padded):
    return jnp.concatenate(
        [pad_columns(value[:, :half], padded), pad_columns(value[:, half:], padded)], axis=1
    )


def norm_backward(rows, scale, weighted):
    inner = jnp.sum(weighted * rows, axis=-1, keepdims=True)
    return scale * weighted - rows * scale**3 * inner / WIDTH


def rotate_tiles(values, cosine, sine):
    lane = lax.broadcasted_iota(jnp.int32, (128, 128), 1)
    turned = []
    for k in range(values.shape[1] // 128):
        part = values[:, k * 128 : k * 128 + 128]
        partner = jnp.where(lane % 64 < 32, pltpu.roll(part, 96, 1), pltpu.roll(part, 32, 1))
        turned.append(part * cosine + partner * sine)
    return jnp.concatenate(turned, axis=1)


def project_kernel(
    start_ref, scale_ref, spare_ref, w_ref, cos_ref, sin_ref, n_ref, q_ref, kv_ref, gain_ref
):
    lane = lax.broadcasted_iota(jnp.int32, (ROWS, PADDED), 1)
    row = lax.broadcasted_iota(jnp.int32, (ROWS, PADDED), 0)
    spread = dot(spare_ref[...], jnp.where(lane % ROWS == row, 1.0, 0.0).astype(jnp.bfloat16))
    lane = lax.broadcasted_iota(jnp.int32, (128, PADDED), 1)
    slot = lax.broadcasted_iota(jnp.int32, (128, PADDED), 0)
    spread = jnp.where(lane // ROWS == slot % 64, spread, 0.0)
    gain_first = jnp.sum(spread[:64], axis=0, keepdims=True)
    gain_ref[0:1, :] = gain_first
    gain_ref[1:2, :] = jnp.sum(spread[64:], axis=0, keepdims=True)
    normed = (start_ref[...] * scale_ref[...] * gain_first).astype(jnp.bfloat16)
    n_ref[...] = normed
    projected = dot(normed, w_ref[...])
    natural = jnp.concatenate(
        [projected[:, :IN_HALF], projected[:, IN_PAD : IN_PAD + IN_HALF]], axis=1
    )
    key_width = KEY_VALUE_HEADS * HEAD_SIZE
    turned = rotate_tiles(natural[:, : WIDTH + key_width], cos_ref[...], sin_ref[...])
    q_ref[...] = turned[:, :WIDTH].astype(jnp.bfloat16) * jnp.bfloat16(0.125)
    keys, values = turned[:, WIDTH:], natural[:, WIDTH + key_width :]
    pieces = []
    for g in range(KEY_VALUE_HEADS):
        span = slice(g * HEAD_SIZE, (g + 1) * HEAD_SIZE)
        pieces += [keys[:, span], values[:, span]]
    kv_ref[...] = jnp.concatenate(pieces, axis=1).astype(jnp.bfloat16)


def local_call(kernel, shapes, flops):
    return pl.pallas_call(
        kernel,
        out_shape=tuple(jax.ShapeDtypeStruct(shape, kind) for shape, kind in shapes),
        compiler_params=pltpu.CompilerParams(vmem_limit_bytes=VMEM_LIMIT),
        cost_estimate=pl.CostEstimate(flops=flops, bytes_accessed=6 * 10**6, transcendentals=0),
    )


def project(start, scale, spare, weight, cosine, sine):
    low, full = jnp.bfloat16, jnp.float32
    shapes = (
        ((128, PADDED), low),
        ((128, WIDTH), low),
        ((128, 2 * KEY_VALUE_HEADS * HEAD_SIZE), low),
        ((2, PADDED), full),
    )
    return local_call(project_kernel, shapes, 5 * 10**8)(start, scale, spare, weight, cosine, sine)


def project_back_kernel(
    dq_ref,
    kv_ref,
    start_ref,
    scale_ref,
    gain_ref,
    gain_two_ref,
    resid_ref,
    n_ref,
    w_ref,
    cos_ref,
    sin_ref,
    grad_ref,
    input_ref,
):
    key_width = KEY_VALUE_HEADS * HEAD_SIZE
    kv = kv_ref[...]
    keys = [kv[:, g * 128 : g * 128 + 64] for g in range(KEY_VALUE_HEADS)]
    values = [kv[:, g * 128 + 64 : g * 128 + 128] for g in range(KEY_VALUE_HEADS)]
    turned = rotate_tiles(
        jnp.concatenate([dq_ref[...] * 0.125] + keys, axis=1), cos_ref[...], -sin_ref[...]
    )
    natural = jnp.concatenate([turned] + values, axis=1).astype(jnp.bfloat16)
    blank = jnp.zeros((128, IN_PAD - IN_HALF), jnp.bfloat16)
    grads = jnp.concatenate([natural[:, :IN_HALF], blank, natural[:, IN_HALF:], blank], axis=1)
    back = dot(grads, w_ref[...], LAST)
    start, scale = start_ref[...], scale_ref[...]
    gain_grad = jnp.sum(back * start * scale, axis=0, keepdims=True)
    through = norm_backward(start, scale, back * gain_ref[0:1, :])
    input_ref[...] = (resid_ref[...] + through).astype(jnp.bfloat16)
    for k in range(PADDED // 256):
        span = slice(k * 256, k * 256 + 256)
        grad_ref[span, :] = dot(n_ref[:, span], grads, FIRST).astype(jnp.bfloat16)
    slot = lax.broadcasted_iota(jnp.int32, (64, PADDED), 0)
    lane = lax.broadcasted_iota(jnp.int32, (64, PADDED), 1)
    picks = jnp.where((lane // ROWS == slot) & (lane % ROWS < ROWS - 1), 1.0, 0.0)
    row = lax.broadcasted_iota(jnp.int32, (PADDED, 128), 0)
    column = lax.broadcasted_iota(jnp.int32, (PADDED, 128), 1)
    fold = jnp.where(row % ROWS == column, 1.0, 0.0).astype(jnp.bfloat16)
    row = lax.broadcasted_iota(jnp.int32, (PADDED, 64), 0)
    column = lax.broadcasted_iota(jnp.int32, (PADDED, 64), 1)
    place = jnp.where(row == column * ROWS + ROWS - 1, 1.0, 0.0).astype(jnp.bfloat16)
    for start_column, gain in ((0, gain_grad), (IN_PAD, gain_two_ref[...])):
        by_slot = dot((picks * gain).astype(jnp.bfloat16), fold).astype(jnp.bfloat16)
        span = slice(start_column, start_column + 128)
        grad_ref[:, span] = grad_ref[:, span] + dot(place, by_slot).astype(jnp.bfloat16)


def project_back(*operands):
    shapes = (((PADDED, IN_COLS), jnp.bfloat16), ((128, PADDED), jnp.bfloat16))
    return local_call(project_back_kernel, shapes, 10**9)(*operands)


def on_device(
    inputs,
    cotangent,
    positions,
    pair_index,
    input_projection,
    project_out,
    gate_up,
    down_weight,
    norm_gains,
):
    half = lax.axis_index("fsdp")
    pair = pair_index[0, 0]
    key_width = KEY_VALUE_HEADS * HEAD_SIZE
    select = (
        lax.broadcasted_iota(jnp.int32, (WIDTH, PADDED), 0) == jnp.asarray(COLUMN_MAP)[None, :]
    ).astype(jnp.bfloat16)

    spare = jnp.pad(norm_gains.T, ((0, 0), (0, 1)))
    own_in = pad_columns(
        jnp.concatenate([input_projection, pad_columns(spare, IN_HALF)], axis=0), IN_PAD
    )
    own_in = own_in.at[15, ROWS].set(pair.astype(jnp.bfloat16))
    own_out = jnp.pad(project_out, ((0, 1), (0, OUT_PAD - OUT_HALF)))
    gate_up_parts = gate_up.reshape(15, 2, 2, FF_QUARTER).transpose(2, 0, 1, 3)
    gate_up_parts = gate_up_parts.reshape(2, 15, 2 * FF_QUARTER)
    down_parts = down_weight.reshape(15, 2, FF_QUARTER).transpose(1, 0, 2)
    spare_row = ((0, 0), (0, 1), (0, 0))
    upstream = dot(cotangent[0], select)
    weight_in, weight_out, weight_gu, weight_down, row_cotangent = gather_blocks(
        (
            own_in,
            own_out,
            jnp.pad(gate_up_parts, spare_row),
            jnp.pad(down_parts, spare_row),
        ),
        ("row", "row", "split", "split"),
        upstream.astype(jnp.bfloat16),
        0,
    )
    weight_in = weight_in.reshape(PADDED, IN_COLS)
    weight_out = weight_out.reshape(PADDED, 2 * OUT_PAD)
    weight_gu = weight_gu.reshape(PADDED, 2 * FF_QUARTER)
    weight_down = weight_down.reshape(PADDED, FF_QUARTER)
    row_cotangent = row_cotangent.reshape(512, PADDED)
    blocks_in = weight_in.reshape(64, ROWS, IN_COLS)
    spare_first = blocks_in[:, 15, : 2 * ROWS]
    spare_second = blocks_in[:, 15, IN_PAD : IN_PAD + 2 * ROWS]
    held = jnp.arange(PADDED) % ROWS < 15
    labels = jnp.where(half == 0, spare_first, spare_second)[:, ROWS].astype(jnp.int32)
    slots = jnp.arange(64, dtype=jnp.int32)
    blocks = jnp.stack([labels, 127 - labels], axis=1).reshape(128)
    places = jnp.stack([2 * slots, 2 * slots + 1], axis=1).reshape(128)
    hits = blocks[None, :] == jnp.arange(128, dtype=jnp.int32)[:, None]
    table = jnp.sum(jnp.where(hits, places[None, :], 0), axis=1)

    start = dot(inputs[0], select)
    freqs = jnp.exp(
        -math.log(10000.0) * jnp.arange(HEAD_SIZE // 2, dtype=jnp.float32) * 2.0 / HEAD_SIZE
    )
    angle = positions[0].astype(jnp.float32)[:, None] * freqs[None, :]
    cosine = jnp.tile(jnp.cos(angle), (1, 4))
    sine = jnp.sin(angle)
    sine = jnp.tile(jnp.concatenate([-sine, sine], axis=1), (1, 2))
    scale_one = lax.rsqrt(jnp.sum(start * start, axis=-1, keepdims=True) / WIDTH + EPSILON)
    spare = jnp.concatenate([spare_first[:, :ROWS], spare_second[:, :ROWS]], axis=0)
    normed_low, query_scaled, key_value, gains = project(
        start, scale_one, spare, weight_in, cosine, sine
    )
    gain_second = gains[1]
    all_kv = gather_blocks((key_value,), ("whole",), None, 1)[0].reshape(128, 64, 2 * key_width)
    pair_one = pair.reshape(1)
    attention, top, total = attend(table, pair_one, query_scaled, all_kv)
    mixed_low = pad_halves(attention.astype(jnp.bfloat16), OUT_HALF, OUT_PAD)
    branch = dot(mixed_low, weight_out, LAST)
    resid = start + jnp.where(held, branch, 0.0)
    scale_two = lax.rsqrt(jnp.sum(resid * resid, axis=-1, keepdims=True) / WIDTH + EPSILON)
    normed_two = (resid * scale_two * gain_second).astype(jnp.bfloat16)
    normed_two_grad, ffn_out, grad_gu, grad_down = feed_forward(
        normed_two, row_cotangent, weight_gu, weight_down, 2
    )
    resid_grad = upstream + norm_backward(resid, scale_two, normed_two_grad * gain_second)
    gain_two_grad = jnp.sum(normed_two_grad * resid * scale_two, axis=0, keepdims=True)
    branch_grad_low = resid_grad.astype(jnp.bfloat16)
    mixed_grad = dot(branch_grad_low, weight_out)
    mixed_grad = jnp.concatenate(
        [mixed_grad[:, :OUT_HALF], mixed_grad[:, OUT_PAD : OUT_PAD + OUT_HALF]], axis=1
    )
    query_grad, all_kv_grad = attend_back(
        table, pair_one, query_scaled, mixed_grad, attention, top, total, all_kv
    )
    kv_grad, ffn_out, grad_out = scatter_blocks(
        (all_kv_grad.reshape(2, 4, 4, 2, 128, 2 * key_width),),
        ((0, 0, 2 * key_width, 0),),
        None,
        ffn_out.reshape(4, 128, PADDED),
        (
            weight_grad_work,
            (branch_grad_low, mixed_low),
            (jax.ShapeDtypeStruct((PADDED, 2 * OUT_PAD), jnp.bfloat16),),
        ),
        3,
    )
    layer_out = (resid + ffn_out).astype(jnp.bfloat16)
    grad_in, input_grad = project_back(
        query_grad,
        kv_grad,
        start,
        scale_one,
        gains,
        gain_two_grad,
        resid_grad,
        normed_low,
        weight_in,
        cosine,
        sine,
    )
    own_cols = IN_PAD + OUT_PAD
    narrow = jax.ShapeDtypeStruct((WIDTH, 128), jnp.bfloat16)
    sum_in, sum_out, sum_gu, sum_down, spare, layer_out, input_grad = scatter_blocks(
        tuple(
            grad.reshape(2, 4, 4, 2, ROWS, grad.shape[1])
            for grad in (grad_in, grad_out, grad_gu, grad_down)
        ),
        (
            (0, 0, IN_PAD, 0),
            (0, IN_PAD, IN_PAD, own_cols),
            (1, 0, OUT_PAD, IN_PAD),
            (1, OUT_PAD, OUT_PAD, own_cols + IN_PAD),
            (2, 0, 2 * FF_QUARTER, 2 * own_cols),
            (3, 0, FF_QUARTER, 2 * own_cols + 2 * FF_QUARTER),
        ),
        own_cols,
        None,
        (unpad_work, (layer_out, input_grad, select), (narrow, narrow)),
        4,
    )
    return (
        layer_out.T[None],
        input_grad.T[None],
        sum_in,
        sum_out,
        sum_gu,
        sum_down,
        spare[0, :15].reshape(15, 1),
    )


def solution(mesh):
    in_specs = (
        P("fsdp", "ctx", None),
        P("fsdp", "ctx", None),
        P("fsdp", "ctx"),
        P("fsdp", "ctx"),
        P("ctx", "fsdp"),
        P("ctx", "fsdp"),
        P("ctx", None, "fsdp"),
        P("ctx", "fsdp"),
        P("ctx", "fsdp"),
    )
    out_specs = (
        P("fsdp", "ctx", None),
        P("fsdp", "ctx", None),
        P("ctx", "fsdp"),
        P("ctx", "fsdp"),
        P("ctx", None, "fsdp"),
        P("ctx", "fsdp"),
        P("ctx", "fsdp"),
    )
    return jax.shard_map(
        on_device, mesh=mesh, in_specs=in_specs, out_specs=out_specs, check_vma=False
    )
```

```python
import math

import jax
import jax.numpy as jnp
import numpy as np
from jax import lax
from jax.experimental import pallas as pl
from jax.experimental.pallas import tpu as pltpu
from jax.sharding import PartitionSpec as P

WIDTH = 960
QUERY_HEADS = 15
KEY_VALUE_HEADS = 5
GROUP = 3
HEAD_SIZE = 64
FF_HALF = 1280
FF_QUARTER = 640
EPSILON = 1e-05
ROWS = 16
PADDED = 1024
IN_HALF = 800
IN_PAD = 896
OUT_HALF = 480
OUT_PAD = 512
IN_COLS = 2 * IN_PAD
TILE = 512
QROWS = 384
MESH = pl.DeviceIdType.MESH
VMEM_LIMIT = 56 * 1024 * 1024


def column_map():
    cols = np.full((64, ROWS), -1, np.int32)
    cols[:, :15] = np.arange(64)[:, None] * 15 + np.arange(15)[None, :]
    return cols.reshape(-1)


COLUMN_MAP = column_map()


def coordinates():
    index = lax.axis_index("ctx")
    core = index % 2
    z = (index // 2) % 4
    y = (index // 8) % 4
    x = index // 32
    p1 = y * (1 - core) + z * core
    p2 = z * (1 - core) + y * core
    return x, p1, p2, core


def device_at(x, p1, p2, core):
    y = p1 * (1 - core) + p2 * core
    z = p2 * (1 - core) + p1 * core
    return ((x * 4 + y) * 4 + z) * 2 + core


def neighbours(x, p1, p2, core):
    index = lax.axis_index("ctx")
    return (
        device_at(1 - x, p1, p2, core),
        device_at(x, (p1 + 1) % 4, p2, core),
        device_at(x, (p1 + 3) % 4, p2, core),
        device_at(x, p1, (p2 + 1) % 4, core),
        device_at(x, p1, (p2 + 3) % 4, core),
        index + 1 - 2 * core,
    )


def block_of(ref, core, x, p1, p2):
    return ref.at[x, p1, p2, core] if core == 0 else ref.at[x, p2, p1, core]


def half_of(ref, core, x, p2):
    every = pl.ds(0, 4)
    return ref.at[x, every, p2, core] if core == 0 else ref.at[x, p2, every, core]


def slab_of(ref, core, p2):
    every = pl.ds(0, 4)
    both = pl.ds(0, 2)
    return ref.at[both, every, p2, core] if core == 0 else ref.at[both, p2, every, core]


def row_place():
    return lax.axis_index("fsdp") * 2 + lax.axis_index("ctx") // 32


def row_device(place):
    index = lax.axis_index("ctx")
    return {"fsdp": place // 2, "ctx": (place % 2) * 32 + index % 32}


def ctx_device(index):
    return {"ctx": index}


class Sender:
    def __init__(self, send_sem, recv_sem):
        self.send_sem, self.recv_sem, self.sent = send_sem, recv_sem, []

    def __call__(self, source, place, device):
        number = len(self.sent)
        copy = pltpu.make_async_remote_copy(
            src_ref=source,
            dst_ref=place,
            send_sem=self.send_sem.at[number],
            recv_sem=self.recv_sem.at[number],
            device_id=device,
            device_id_type=MESH,
        )
        copy.start()
        self.sent.append(copy)
        return copy

    def finish(self):
        for copy in self.sent:
            copy.wait_send()


class RowGather:
    def __init__(self, in_ref, out_ref, local_sem, send):
        self.out, self.send = out_ref, send
        here = row_place()
        self.left, self.right = (here + 3) % 4, (here + 1) % 4
        self.local = pltpu.make_async_copy(in_ref, out_ref.at[here], local_sem)
        self.local.start()
        self.from_left = send(in_ref, out_ref.at[here], row_device(self.right))
        self.from_right = send(in_ref, out_ref.at[here], row_device(self.left))

    def forward(self):
        rows = self.out.shape[1] // 2
        low, high = pl.ds(0, rows), pl.ds(rows, rows)
        self.from_left.wait_recv()
        place = self.out.at[self.left, low]
        self.far_low = self.send(place, place, row_device(self.right))
        self.from_right.wait_recv()
        place = self.out.at[self.right, high]
        self.far_high = self.send(place, place, row_device(self.left))

    def finish(self):
        self.far_low.wait_recv()
        self.far_high.wait_recv()
        self.local.wait()


class RowScatter:
    def __init__(self, in_ref, far, near_left, near_right, stage, send):
        self.p, self.far, self.stage, self.send = in_ref, far, stage, send
        self.near_left, self.near_right = near_left, near_right
        self.here = row_place()
        self.left, self.right = (self.here + 3) % 4, (self.here + 1) % 4
        to_left, to_right = row_device(self.left), row_device(self.right)
        opposite = (self.here + 2) % 4
        rows = in_ref.shape[1] // 2
        self.low, self.high = pl.ds(0, rows), pl.ds(rows, rows)
        low, high = self.low, self.high
        self.got_low = send(in_ref.at[opposite, low], far.at[0], to_right)
        self.got_high = send(in_ref.at[opposite, high], far.at[1], to_left)
        self.waits = [
            send(in_ref.at[self.right, high], near_left.at[high], to_right),
            send(in_ref.at[self.left, low], near_right.at[low], to_left),
        ]

    def forward(self):
        rows = self.p.shape[1] // 2
        self.got_low.wait_recv()
        self.stage[0] = self.p[self.right, 0:rows] + self.far[0]
        self.waits.append(
            self.send(self.stage.at[0], self.near_left.at[self.low], row_device(self.right))
        )
        self.got_high.wait_recv()
        self.stage[1] = self.p[self.left, rows : 2 * rows] + self.far[1]
        self.waits.append(
            self.send(self.stage.at[1], self.near_right.at[self.high], row_device(self.left))
        )

    def finish(self, out_ref):
        for copy in self.waits:
            copy.wait_recv()
        total = self.p[self.here].astype(jnp.float32) + self.near_left[...].astype(jnp.float32)
        out_ref[...] = total + self.near_right[...].astype(jnp.float32)


def greet(devices):
    barrier = pltpu.get_barrier_semaphore()
    for device in devices:
        pl.semaphore_signal(barrier, inc=1, device_id=device, device_id_type=MESH)
    pl.semaphore_wait(barrier, len(devices))


def greet_ctx(with_row):
    devices = [ctx_device(index) for index in neighbours(*coordinates())]
    if with_row:
        here = row_place()
        step = 2 * (here % 2) - 1
        devices.append(row_device((here + step + 4) % 4))
    greet(devices)


def row_kernel_entry():
    here = row_place()
    greet([row_device((here + 3) % 4), row_device((here + 1) % 4)])


def row_scratch(rows, columns):
    return [
        pltpu.VMEM((2, rows // 2, columns), jnp.bfloat16),
        pltpu.VMEM((rows, columns), jnp.bfloat16),
        pltpu.VMEM((rows, columns), jnp.bfloat16),
        pltpu.VMEM((2, rows // 2, columns), jnp.bfloat16),
        pltpu.SemaphoreType.DMA((6,)),
        pltpu.SemaphoreType.DMA((6,)),
    ]


class Group:
    def __init__(self, copies):
        self.copies = copies

    def wait_recv(self):
        for copy in self.copies:
            copy.wait_recv()


def gather_kernel(modes, with_row, *refs):
    count = len(modes)
    ins, refs = refs[: count + with_row], refs[count + with_row :]
    outs, refs = refs[: count + with_row], refs[count + with_row :]
    greet_ctx("row" in modes or with_row)
    core = coordinates()[3]
    for chosen in range(2):

        @pl.when(core == chosen)
        def _(chosen=chosen):
            if modes == ("whole",):
                gather_fine(chosen, ins[0], outs[0], *refs[:3])
            else:
                gather_body(chosen, modes, with_row, ins, outs, *refs)


def gather_body(
    core, modes, with_row, ins, outs, local_sem, send_sem, recv_sem, row_local, row_send, row_recv
):
    x, p1, p2, _ = coordinates()
    across, right1, left1, right2, left2, sibling = neighbours(x, p1, p2, core)
    p1p, p1m = (p1 + 1) % 4, (p1 + 3) % 4
    p2p, p2m, p2o = (p2 + 1) % 4, (p2 + 3) % 4, (p2 + 2) % 4
    place = row_place()
    row_left, row_right = (place + 3) % 4, (place + 1) % 4
    sender = Sender(send_sem, recv_sem)
    arrays = range(len(modes))
    plain = [k for k in arrays if modes[k] != "row"]
    rows = [k for k in arrays if modes[k] == "row"]
    mine = [ins[k].at[x] if modes[k] == "split" else ins[k] for k in arrays]
    yours = [ins[k].at[1 - x] if modes[k] == "split" else ins[k] for k in arrays]

    def send(places, to, chosen=arrays, sources=None):
        sources = places if sources is None else sources
        return Group([sender(sources[k], places[k], ctx_device(to)) for k in chosen])

    def block(side, q1):
        return [block_of(outs[k], core, side, q1, p2) for k in arrays]

    def half(side, q2):
        return [half_of(outs[k], core, side, q2) for k in arrays]

    def slot(k, owner):
        width = ins[k].shape[-1]
        columns = pl.ds(pl.multiple_of((owner // 2) * width, 128), width)
        return block_of(outs[k], core, owner % 2, p1, p2).at[pl.ds(0, ROWS), columns]

    here = block(x, p1)
    there = block(1 - x, p1)
    locals_ = [
        pltpu.make_async_copy(
            mine[k], slot(k, place) if k in rows else here[k], local_sem.at[k]
        )
        for k in arrays
    ]
    for copy in locals_:
        copy.start()
    row_near = Group(
        [
            sender(ins[k], slot(k, place), row_device(to))
            for to in (row_right, row_left)
            for k in rows
        ]
    )
    crossed = send(here, across, plain, yours)
    own_left = send(here, right1, plain, mine)
    own_right = send(here, left1, plain, mine)
    row_near.wait_recv()
    row_far = Group(
        [sender(slot(k, row_left), slot(k, row_left), row_device(row_right)) for k in rows]
    )
    crossed.wait_recv()
    other_left = send(there, right1)
    other_right = send(there, left1)
    for copy in locals_:
        copy.wait()
    row_far.wait_recv()
    own_left.copies += send(here, right1, rows).copies
    own_right.copies += send(here, left1, rows).copies
    if with_row:
        row_sender = Sender(row_send, row_recv)
        row = RowGather(ins[-1], outs[-1], row_local, row_sender)
    own_left.wait_recv()
    own_far = send(block(x, p1m), right1)
    own_right.wait_recv()
    own_far.wait_recv()
    own_left = send(half(x, p2), right2)
    own_right = send(half(x, p2), left2)
    last = [send(half(x, p2), sibling)]
    other_right.wait_recv()
    other_far = send(block(1 - x, p1p), left1)
    other_left.wait_recv()
    other_far.wait_recv()
    other_right = send(half(1 - x, p2), left2)
    other_left = send(half(1 - x, p2), right2)
    last.append(send(half(1 - x, p2), sibling))
    own_left.wait_recv()
    own_far = send(half(x, p2m), right2)
    last.append(send(half(x, p2m), sibling))
    own_right.wait_recv()
    last.append(send(half(x, p2p), sibling))
    if with_row:
        row.forward()
    other_right.wait_recv()
    other_far = send(half(1 - x, p2p), left2)
    last.append(send(half(1 - x, p2p), sibling))
    other_left.wait_recv()
    last.append(send(half(1 - x, p2m), sibling))
    own_far.wait_recv()
    last.append(send(half(x, p2o), sibling))
    if with_row:
        row.finish()
    other_far.wait_recv()
    last.append(send(half(1 - x, p2o), sibling))
    for group in last:
        group.wait_recv()
    sender.finish()
    if with_row:
        row_sender.finish()


def gather_fine(core, in_ref, out_ref, local_sem, send_sem, recv_sem):
    x, p1, p2, _ = coordinates()
    across, right1, left1, right2, left2, sibling = neighbours(x, p1, p2, core)
    p1p, p1m, p1o = (p1 + 1) % 4, (p1 + 3) % 4, (p1 + 2) % 4
    p2p, p2m, p2o = (p2 + 1) % 4, (p2 + 3) % 4, (p2 + 2) % 4
    sender = Sender(send_sem, recv_sem)

    def block(side, q1, q2):
        return block_of(out_ref, core, side, q1, q2)

    def send(place, to, source=None):
        return sender(place if source is None else source, place, ctx_device(to))

    def near(side, q1, source=None):
        place = block(side, q1, p2)
        return send(place, right2, source), send(place, left2, source)

    def cross(side, q2):
        return send(half_of(out_ref, core, side, q2), sibling)

    def onward_right(copies, q1):
        copies[0].wait_recv()
        return send(block(x, q1, p2m), right2)

    def onward_left(copies, q1):
        copies[1].wait_recv()
        return send(block(1 - x, q1, p2p), left2)

    mine = block(x, p1, p2)
    local = pltpu.make_async_copy(in_ref, mine, local_sem.at[0])
    local.start()
    crossed = send(mine, across, in_ref)
    own_right = send(mine, right1, in_ref)
    own_left = send(mine, left1, in_ref)
    own = near(x, p1, in_ref)
    own_right.wait_recv()
    own_far = send(block(x, p1m, p2), right1)
    own_m = near(x, p1m)
    own_left.wait_recv()
    own_p = near(x, p1p)
    crossed.wait_recv()
    there = block(1 - x, p1, p2)
    other_left = send(there, left1)
    other_right = send(there, right1)
    other = near(1 - x, p1)
    far_own = [onward_right(own, p1)]
    own_far.wait_recv()
    own_o = near(x, p1o)
    far_own.append(onward_right(own_m, p1m))
    far_own.append(onward_right(own_p, p1p))
    local.wait()
    last = [cross(x, p2)]
    other_left.wait_recv()
    other_far = send(block(1 - x, p1p, p2), left1)
    other_p = near(1 - x, p1p)
    other_right.wait_recv()
    other_m = near(1 - x, p1m)
    far_other = [onward_left(other, p1)]
    other_far.wait_recv()
    other_o = near(1 - x, p1o)
    last.append(cross(1 - x, p2))
    far_own.append(onward_right(own_o, p1o))
    last.append(cross(x, p2m))
    far_other.append(onward_left(other_p, p1p))
    far_other.append(onward_left(other_m, p1m))
    for copies in (own, own_m, own_p, own_o):
        copies[1].wait_recv()
    last.append(cross(x, p2p))
    far_other.append(onward_left(other_o, p1o))
    last.append(cross(1 - x, p2p))
    for copies in (other, other_m, other_p, other_o):
        copies[0].wait_recv()
    last.append(cross(1 - x, p2m))
    for side, copies in ((x, far_own), (1 - x, far_other)):
        for copy in copies:
            copy.wait_recv()
        last.append(cross(side, p2o))
    for copy in last:
        copy.wait_recv()
    sender.finish()


def gather_blocks(blocks, modes, row_block, collective_id):
    with_row = row_block is not None
    operands = list(blocks)
    shapes = [
        jax.ShapeDtypeStruct(
            (2, 4, 4, 2, block.shape[-2], block.shape[-1] * (2 if mode == "row" else 1)),
            block.dtype,
        )
        for block, mode in zip(blocks, modes)
    ]
    if with_row:
        operands.append(row_block)
        shapes.append(jax.ShapeDtypeStruct((4,) + row_block.shape, row_block.dtype))
    number = 39 if modes == ("whole",) else 23 * len(blocks)
    return pl.pallas_call(
        lambda *refs: gather_kernel(modes, int(with_row), *refs),
        out_shape=tuple(shapes),
        in_specs=[pl.BlockSpec(memory_space=pl.ANY)] * len(operands),
        out_specs=(pl.BlockSpec(memory_space=pl.ANY),) * len(operands),
        scratch_shapes=[
            pltpu.SemaphoreType.DMA((len(blocks),)),
            pltpu.SemaphoreType.DMA((number,)),
            pltpu.SemaphoreType.DMA((number,)),
            pltpu.SemaphoreType.DMA,
            pltpu.SemaphoreType.DMA((4,)),
            pltpu.SemaphoreType.DMA((4,)),
        ],
        compiler_params=pltpu.CompilerParams(
            collective_id=collective_id, has_side_effects=True
        ),
    )(*operands)


def scatter_kernel(pieces, halved, with_row, side, *refs):
    count = 1 + max(piece[0] for piece in pieces)
    ins, refs = refs[:count], refs[count:]
    if with_row:
        row_in, refs = refs[0], refs[1:]
    side_work, side_in, side_out = side
    side_ins, refs = refs[:side_in], refs[side_in:]
    results = 5 if halved else 1
    out_refs, refs = refs[:results], refs[results:]
    if with_row:
        row_out, refs = refs[0], refs[1:]
    side_outs, refs = refs[:side_out], refs[side_out:]
    (acc, other, far_low, far_high, near_left, near_right) = refs[:6]
    (pair_low, pair_high, pair_left, pair_right, last) = refs[6:11]
    (local_sem, cross_send, cross_recv, send_sem, recv_sem) = refs[11:16]
    x, p1, p2, core = coordinates()
    across, right1, left1, right2, left2, sibling = neighbours(x, p1, p2, core)
    greet_ctx(with_row or halved)
    p1p, p1m, p1o = (p1 + 1) % 4, (p1 + 3) % 4, (p1 + 2) % 4
    p2p, p2m, p2o = (p2 + 1) % 4, (p2 + 3) % 4, (p2 + 2) % 4
    needed = (p2o, p2m, p2p, p2)
    theirs = (p1o, p1m, p1p, p1)
    sender = Sender(send_sem, recv_sem)

    def part(ref, place, piece):
        if len(pieces) == 1:
            return ref.at[place]
        every = [pl.ds(0, size) for size in ref.shape[1:-1]]
        return ref.at[tuple([place] + every + [pl.ds(pieces[piece][3], pieces[piece][2])])]

    def source_of(piece, chosen, place):
        array, start, width, _ = pieces[piece]
        slab = slab_of(ins[array], chosen, place)
        if len(pieces) == 1:
            return slab
        every = [pl.ds(0, size) for size in slab.shape[:-1]]
        return slab.at[tuple(every + [pl.ds(start, width)])]

    def crossing(k, piece, source):
        return pltpu.make_async_remote_copy(
            src_ref=source,
            dst_ref=part(other, theirs[k], piece),
            send_sem=cross_send.at[k, piece],
            recv_sem=cross_recv.at[k, piece],
            device_id=ctx_device(sibling),
            device_id_type=MESH,
        )

    for chosen in range(2):

        @pl.when(core == chosen)
        def _(chosen=chosen):
            for k in range(4):
                for piece in range(len(pieces)):
                    crossing(k, piece, source_of(piece, 1 - chosen, theirs[k])).start()
                    pltpu.make_async_copy(
                        source_of(piece, chosen, needed[k]),
                        part(acc, needed[k], piece),
                        local_sem.at[k, piece],
                    ).start()

    if with_row:
        row_sender = Sender(refs[20], refs[21])
        row = RowScatter(row_in, refs[16], refs[17], refs[18], refs[19], row_sender)

    def send(source, place, to):
        return sender(source, place, ctx_device(to))

    def add(place, term):
        @pl.loop(0, 4)
        def _(step):
            place[step] = place[step] + term[step]

    def add_both(side):
        @pl.loop(0, 4)
        def _(step):
            total = acc[p2, side, step].astype(jnp.float32)
            total = total + near_left[side, step].astype(jnp.float32)
            total = total + near_right[side, step].astype(jnp.float32)
            acc[p2, side, step] = total.astype(acc.dtype)

    def merge(k):
        for piece in range(len(pieces)):
            mine = part(acc, needed[k], piece)
            pltpu.make_async_copy(mine, mine, local_sem.at[k, piece]).wait()
            crossing(k, piece, part(other, theirs[k], piece)).wait_recv()
        for side in range(2):
            add(acc.at[needed[k], side], other.at[needed[k], side])

    merge(0)
    got_low = send(acc.at[p2o, 0], far_low, right2)
    got_high = send(acc.at[p2o, 1], far_high, left2)
    merge(1)
    right_low = send(acc.at[p2m, 0], near_right.at[0], left2)
    merge(2)
    left_high = send(acc.at[p2p, 1], near_left.at[1], right2)
    side_work(side_ins, side_outs)
    got_low.wait_recv()
    add(acc.at[p2p, 0], far_low)
    left_low = send(acc.at[p2p, 0], near_left.at[0], right2)
    got_high.wait_recv()
    add(acc.at[p2m, 1], far_high)
    right_high = send(acc.at[p2m, 1], near_right.at[1], left2)
    merge(3)
    if with_row:
        row.forward()
    right_low.wait_recv()
    left_low.wait_recv()
    add_both(0)
    got_low = send(acc.at[p2, 0, p1o], pair_low, right1)
    near_low = send(acc.at[p2, 0, p1m], pair_right.at[0], left1)
    left_high.wait_recv()
    right_high.wait_recv()
    add_both(1)
    got_high = send(acc.at[p2, 1, p1o], pair_high, left1)
    near_high = send(acc.at[p2, 1, p1p], pair_left.at[1], right1)
    got_low.wait_recv()
    acc[p2, 0, p1p] = acc[p2, 0, p1p] + pair_low[...]
    left_low = send(acc.at[p2, 0, p1p], pair_left.at[0], right1)
    got_high.wait_recv()
    acc[p2, 1, p1m] = acc[p2, 1, p1m] + pair_high[...]
    right_high = send(acc.at[p2, 1, p1m], pair_right.at[1], left1)
    if with_row:
        row.finish(row_out)
    near_low.wait_recv()
    near_high.wait_recv()
    left_low.wait_recv()
    right_high.wait_recv()

    @pl.loop(0, 2)
    def _(j):
        total = acc[p2, j, p1].astype(jnp.float32) + pair_left[j].astype(jnp.float32)
        total = total + pair_right[j].astype(jnp.float32)
        acc[p2, j, p1] = total.astype(acc.dtype)

    if halved:
        finish_row(halved, acc, p1, p2, refs[16:20], last, sender, out_refs)
    else:
        final = send(acc.at[p2, 1 - x, p1], last, across)
        final.wait_recv()
        total = acc[p2, x, p1].astype(jnp.float32) + last[...].astype(jnp.float32)
        out_refs[0][...] = total
    for k in range(4):
        for piece in range(len(pieces)):
            crossing(k, piece, part(other, theirs[k], piece)).wait_send()
    sender.finish()
    if with_row:
        row_sender.finish()


def finish_row(halved, acc, p1, p2, buffers, last, sender, out_refs):
    in_ref, out_ref, gu_ref, down_ref, spare_ref = out_refs
    far, from_left, from_right, stage = buffers
    here = row_place()
    left, right, opposite = (here + 3) % 4, (here + 1) % 4, (here + 2) % 4
    x = here % 2
    every = pl.ds(0, ROWS)
    rest = pl.ds(2 * halved, acc.shape[-1] - 2 * halved)

    def columns(owner):
        return pl.ds(pl.multiple_of((owner // 2) * halved, 128), halved)

    def block(owner):
        return acc.at[p2, owner % 2, p1, every, columns(owner)]

    def keep_part(side, value):
        value = value.astype(jnp.float32)[: ROWS - 1]
        span = pl.ds(pl.multiple_of(side * FF_QUARTER, 128), FF_QUARTER)
        gu_ref[:, 0, span] = value[:, :FF_QUARTER]
        gu_ref[:, 1, span] = value[:, FF_QUARTER : 2 * FF_QUARTER]
        down_ref[:, span] = value[:, 2 * FF_QUARTER :]

    far_copy = sender(block(opposite), far, row_device(right))
    from_right_copy = sender(block(left), from_right, row_device(left))
    x_neighbour = row_device((here // 2) * 2 + 1 - x)
    parts_copy = sender(acc.at[p2, 1 - x, p1, every, rest], last, x_neighbour)
    far_copy.wait_recv()
    stage[...] = acc[p2, right % 2, p1, :, columns(right)] + far[...]
    from_left_copy = sender(stage, from_left, row_device(right))
    keep_part(x, acc[p2, x, p1, :, rest])
    parts_copy.wait_recv()
    keep_part(1 - x, last[...])
    from_right_copy.wait_recv()
    from_left_copy.wait_recv()
    total = acc[p2, x, p1, :, columns(here)].astype(jnp.float32)
    total = total + from_left[...].astype(jnp.float32)
    total = total + from_right[...].astype(jnp.float32)
    in_ref[...] = total[: ROWS - 1, :IN_HALF]
    out_ref[...] = total[: ROWS - 1, IN_PAD : IN_PAD + OUT_HALF]
    spare_ref[...] = total[ROWS - 1 :, :128]


def scatter_blocks(arrays, pieces, halved, row_blocks, side, collective_id):
    rows = arrays[0].shape[-2]
    columns = sum(piece[2] for piece in pieces)
    kind = arrays[0].dtype
    block = (rows, columns)
    with_row = row_blocks is not None
    operands = list(arrays)
    in_specs = [pl.BlockSpec(memory_space=pl.ANY)] * len(arrays)
    results = [block]
    last = block
    scratch = []
    if halved:
        last = (rows, columns - 2 * halved)
        results = [
            (rows - 1, IN_HALF),
            (rows - 1, OUT_HALF),
            (rows - 1, 2, FF_HALF),
            (rows - 1, FF_HALF),
            (1, 128),
        ]
        scratch = [pltpu.VMEM((rows, halved), kind)] * 4
    shapes = [jax.ShapeDtypeStruct(shape, jnp.float32) for shape in results]
    if with_row:
        operands.append(row_blocks)
        in_specs.append(pl.BlockSpec(memory_space=pltpu.VMEM))
        shapes.append(jax.ShapeDtypeStruct(row_blocks.shape[1:], jnp.float32))
        scratch = row_scratch(*row_blocks.shape[1:])
    side_work, side_operands, side_shapes = side
    operands += list(side_operands)
    in_specs += [pl.BlockSpec(memory_space=pltpu.VMEM)] * len(side_operands)
    shapes += list(side_shapes)
    side = (side_work, len(side_operands), len(side_shapes))
    return pl.pallas_call(
        lambda *refs: scatter_kernel(pieces, halved, with_row, side, *refs),
        out_shape=tuple(shapes),
        in_specs=in_specs,
        out_specs=(pl.BlockSpec(memory_space=pltpu.VMEM),) * len(shapes),
        scratch_shapes=[
            pltpu.VMEM((4, 2, 4) + block, kind),
            pltpu.VMEM((4, 2, 4) + block, kind),
            pltpu.VMEM((4,) + block, kind),
            pltpu.VMEM((4,) + block, kind),
            pltpu.VMEM((2, 4) + block, kind),
            pltpu.VMEM((2, 4) + block, kind),
            pltpu.VMEM(block, kind),
            pltpu.VMEM(block, kind),
            pltpu.VMEM((2,) + block, kind),
            pltpu.VMEM((2,) + block, kind),
            pltpu.VMEM(last, kind),
            pltpu.SemaphoreType.DMA((4, len(pieces))),
            pltpu.SemaphoreType.DMA((4, len(pieces))),
            pltpu.SemaphoreType.DMA((4, len(pieces))),
            pltpu.SemaphoreType.DMA((16,)),
            pltpu.SemaphoreType.DMA((16,)),
        ]
        + scratch,
        compiler_params=pltpu.CompilerParams(
            collective_id=collective_id, has_side_effects=True, vmem_limit_bytes=VMEM_LIMIT
        ),
    )(*operands)


def weight_grad_work(ins, outs):
    @pl.loop(0, PADDED // 256)
    def _(step):
        span = pl.ds(pl.multiple_of(step * 256, 256), 256)
        outs[0][span, :] = dot(ins[0][:, span], ins[1][...], FIRST).astype(jnp.bfloat16)


def unpad_work(ins, outs):
    for k in range(2):
        outs[k][...] = dot(ins[2][...], ins[k][...], LAST).astype(jnp.bfloat16)


LAST = (((1,), (1,)), ((), ()))
FIRST = (((0,), (0,)), ((), ()))
PLAIN = (((1,), (0,)), ((), ()))


def dot(a, b, dims=PLAIN):
    return lax.dot_general(a, b, dims, preferred_element_type=jnp.float32)


def feed_forward_kernel(
    n_ref,
    c_ref,
    gu_ref,
    down_ref,
    dn_ref,
    part_ref,
    grad_gu_ref,
    grad_down_ref,
    normed,
    partial,
    hidden,
    gate_up_grad,
    far,
    near_left,
    near_right,
    stage,
    send_sem,
    recv_sem,
):
    row_kernel_entry()
    here = row_place()
    left, right, opposite = (here + 3) % 4, (here + 1) % 4, (here + 2) % 4
    to_left, to_right = row_device(left), row_device(right)

    def rows(owner, start=0, size=128):
        return pl.ds(pl.multiple_of(owner * 128 + start, 64), size)

    def copy(number, source, place, device):
        return pltpu.make_async_remote_copy(
            src_ref=source,
            dst_ref=place,
            send_sem=send_sem.at[number],
            recv_sem=recv_sem.at[number],
            device_id=device,
            device_id_type=MESH,
        )

    mine = normed.at[rows(here)]
    low, high = pl.ds(0, 64), pl.ds(64, 64)
    normed_right = copy(0, n_ref, mine, to_right)
    normed_left = copy(1, n_ref, mine, to_left)
    place = normed.at[rows(left, 0, 64)]
    normed_far_low = copy(2, place, place, to_right)
    place = normed.at[rows(right, 64, 64)]
    normed_far_high = copy(3, place, place, to_left)
    far_low = copy(4, partial.at[rows(opposite, 0, 64)], far.at[0], to_right)
    far_high = copy(5, partial.at[rows(opposite, 64, 64)], far.at[1], to_left)
    near_low = copy(6, partial.at[rows(left, 0, 64)], near_right.at[low], to_left)
    near_high = copy(7, partial.at[rows(right, 64, 64)], near_left.at[high], to_right)
    sum_low = copy(8, stage.at[0], near_left.at[low], to_right)
    sum_high = copy(9, stage.at[1], near_right.at[high], to_left)
    normed_right.start()
    normed_left.start()
    normed[rows(here), :] = n_ref[...]

    @pl.loop(0, 4)
    def _(step):
        turn = jnp.where(step == 1, 3, jnp.where(step == 2, 1, jnp.where(step == 3, 2, 0)))
        owner = (here + turn) % 4

        @pl.when(step == 1)
        def _():
            normed_right.wait_recv()
            normed_far_low.start()

        @pl.when(step == 2)
        def _():
            normed_left.wait_recv()
            normed_far_high.start()

        @pl.when(step == 3)
        def _():
            normed_far_low.wait_recv()
            normed_far_high.wait_recv()

        gate_vals = dot(normed[rows(owner), :], gu_ref[...])
        hidden_grad = dot(c_ref[rows(owner), :], down_ref[...])
        gate = gate_vals[:, :FF_QUARTER]
        upper = gate_vals[:, FF_QUARTER:]
        sigma = jax.nn.sigmoid(gate)
        silu_vals = gate * sigma
        hidden[rows(owner), :] = (silu_vals * upper).astype(jnp.bfloat16)
        gate_grad = hidden_grad * upper * sigma * (1.0 + gate * (1.0 - sigma))
        upper_grad = hidden_grad * silu_vals
        both = jnp.concatenate([gate_grad, upper_grad], axis=1).astype(jnp.bfloat16)
        gate_up_grad[rows(owner), :] = both
        partial[rows(owner), :] = dot(both, gu_ref[...], LAST).astype(jnp.bfloat16)

        @pl.when(step == 1)
        def _():
            near_low.start()

        @pl.when(step == 2)
        def _():
            near_high.start()

        @pl.when(step == 3)
        def _():
            far_low.start()
            far_high.start()

    @pl.loop(0, 4)
    def _(owner):
        part_ref[rows(owner), :] = dot(hidden[rows(owner), :], down_ref[...], LAST).astype(
            jnp.bfloat16
        )

    far_low.wait_recv()
    stage[0] = partial[rows(right, 0, 64), :] + far[0]
    sum_low.start()
    far_high.wait_recv()
    stage[1] = partial[rows(left, 64, 64), :] + far[1]
    sum_high.start()

    @pl.loop(0, PADDED // 256)
    def _(step):
        span = pl.ds(pl.multiple_of(step * 256, 256), 256)
        grad_gu_ref[span, :] = dot(normed[:, span], gate_up_grad[...], FIRST).astype(jnp.bfloat16)
        grad_down_ref[span, :] = dot(c_ref[:, span], hidden[...], FIRST).astype(jnp.bfloat16)

    for arrived in (near_low, near_high, sum_low, sum_high):
        arrived.wait_recv()
    total = partial[rows(here), :].astype(jnp.float32) + near_left[...].astype(jnp.float32)
    dn_ref[...] = total + near_right[...].astype(jnp.float32)
    for sent in (normed_right, normed_left, normed_far_low, normed_far_high, far_low, far_high):
        sent.wait_send()
    for sent in (near_low, near_high, sum_low, sum_high):
        sent.wait_send()


def feed_forward(normed, cotangent, weight_gu, weight_down, collective_id):
    kind = jnp.bfloat16
    return pl.pallas_call(
        feed_forward_kernel,
        out_shape=(
            jax.ShapeDtypeStruct((128, PADDED), jnp.float32),
            jax.ShapeDtypeStruct((512, PADDED), kind),
            jax.ShapeDtypeStruct(weight_gu.shape, kind),
            jax.ShapeDtypeStruct(weight_down.shape, kind),
        ),
        in_specs=[pl.BlockSpec(memory_space=pltpu.VMEM)] * 4,
        out_specs=(pl.BlockSpec(memory_space=pltpu.VMEM),) * 4,
        scratch_shapes=[
            pltpu.VMEM((512, PADDED), kind),
            pltpu.VMEM((512, PADDED), kind),
            pltpu.VMEM((512, FF_QUARTER), kind),
            pltpu.VMEM((512, 2 * FF_QUARTER), kind),
            pltpu.VMEM((2, 64, PADDED), kind),
            pltpu.VMEM((128, PADDED), kind),
            pltpu.VMEM((128, PADDED), kind),
            pltpu.VMEM((2, 64, PADDED), kind),
            pltpu.SemaphoreType.DMA((10,)),
            pltpu.SemaphoreType.DMA((10,)),
        ],
        compiler_params=pltpu.CompilerParams(
            collective_id=collective_id, has_side_effects=True, vmem_limit_bytes=VMEM_LIMIT
        ),
        cost_estimate=pl.CostEstimate(
            flops=7 * 10**9, bytes_accessed=10**7, transcendentals=4 * 10**5
        ),
    )(normed, cotangent, weight_gu, weight_down)


def load_tiles(table_ref, kv_hbm, kv, sems, tiles):
    @pl.loop(0, tiles)
    def _(tile):
        for j in range(8):
            block = tile * 8 + j
            pltpu.make_async_copy(
                kv_hbm.at[table_ref[block]],
                kv.at[pl.ds(pl.multiple_of(block * 64, 64), 64)],
                sems.at[tile],
            ).start()


def wait_tile(kv, sems, tile):
    part = kv.at[pl.ds(pl.multiple_of(tile * TILE, TILE), TILE)]
    pltpu.make_async_copy(part, part, sems.at[tile]).wait()


def visible_keys(tile, pair, first_row, rows):
    shape = (rows, TILE)
    row = first_row + lax.broadcasted_iota(jnp.int32, shape, 0)
    key = tile * TILE + lax.broadcasted_iota(jnp.int32, shape, 1)
    order = jnp.where(row < QROWS // 2, pair, 127 - pair) * 64 + row % 64
    return key <= order


def head_parts():
    for g in range(KEY_VALUE_HEADS):
        for half in range(2):
            for h in range(GROUP):
                rows = slice((half * GROUP + h) * 64, (half * GROUP + h) * 64 + 64)
                column = (GROUP * g + h) * HEAD_SIZE
                yield g, rows, slice(half * 64, half * 64 + 64), slice(column, column + 64)


def run_tiles(pair, step):
    low_tiles = (pair + 8) // 8
    high_tiles = (135 - pair) // 8

    @pl.loop(0, low_tiles - 1)
    def _(tile):
        step(tile, 0, QROWS, False)

    step(low_tiles - 1, 0, QROWS, True)

    @pl.loop(low_tiles, high_tiles - 1)
    def _(tile):
        step(tile, QROWS // 2, QROWS // 2, False)

    step(high_tiles - 1, QROWS // 2, QROWS // 2, True)


def lane_parts(value):
    return [value[:, k * 128 : k * 128 + 128] for k in range(TILE // 128)]


def attend_kernel(table_ref, pair_ref, q_ref, kv_hbm, out_ref, top_ref, sum_ref, kv, q, acc, sems):
    pair = pair_ref[0]
    high_tiles = (135 - pair) // 8
    load_tiles(table_ref, kv_hbm, kv, sems, high_tiles)
    q[...] = jnp.zeros(q.shape, q.dtype)
    for g, rows, tokens, columns in head_parts():
        q[g, rows, 0:64] = q_ref[tokens, columns]
    acc[...] = jnp.zeros(acc.shape, jnp.float32)
    top_ref[...] = jnp.full(top_ref.shape, -1e30, jnp.float32)
    sum_ref[...] = jnp.zeros(sum_ref.shape, jnp.float32)

    def step(tile, first_row, rows, masked):
        wait_tile(kv, sems, tile)
        span = slice(first_row, first_row + rows)
        if masked:
            seen = visible_keys(tile, pair, first_row, rows)
        heads = range(KEY_VALUE_HEADS)
        keys = [
            kv[pl.ds(pl.multiple_of(tile * TILE, TILE), TILE), g * 128 : g * 128 + 128]
            for g in heads
        ]
        scores = [dot(q[g, span, :], keys[g], LAST) for g in heads]
        if masked:
            scores = [jnp.where(seen, score, -1e30) for score in scores]
        parts = [lane_parts(score) for score in scores]
        best = [
            jnp.maximum(jnp.maximum(p[0], p[1]), jnp.maximum(p[2], p[3])) for p in parts
        ]
        before = [top_ref[g, span, :] for g in heads]
        highest = [
            jnp.maximum(before[g], jnp.max(best[g], axis=1, keepdims=True)) for g in heads
        ]
        shrink = [jnp.exp(before[g] - highest[g]) for g in heads]
        parts = [[jnp.exp(part - highest[g]) for part in parts[g]] for g in heads]
        for g in heads:
            p = parts[g]
            top_ref[g, span, :] = highest[g]
            sum_ref[g, span, :] = sum_ref[g, span, :] * shrink[g] + ((p[0] + p[1]) + (p[2] + p[3]))
        mixed = [
            dot(jnp.concatenate([p.astype(jnp.bfloat16) for p in parts[g]], axis=1), keys[g])
            for g in heads
        ]
        for g in heads:
            acc[g, span, :] = acc[g, span, :] * shrink[g] + mixed[g]

    run_tiles(pair, step)
    for g in range(KEY_VALUE_HEADS):
        total = jnp.sum(sum_ref[g], axis=1, keepdims=True)
        sum_ref[g] = jnp.broadcast_to(total, sum_ref.shape[1:])
        acc[g] = acc[g] / sum_ref[g]
    for g, rows, tokens, columns in head_parts():
        out_ref[tokens, columns] = acc[g, rows, 64:128]


def attend(table, pair, q, kv):
    heads = (KEY_VALUE_HEADS, QROWS, 128)
    return pl.pallas_call(
        attend_kernel,
        out_shape=(
            jax.ShapeDtypeStruct((128, WIDTH), jnp.float32),
            jax.ShapeDtypeStruct(heads, jnp.float32),
            jax.ShapeDtypeStruct(heads, jnp.float32),
        ),
        in_specs=[
            pl.BlockSpec(memory_space=pltpu.SMEM),
            pl.BlockSpec(memory_space=pltpu.SMEM),
            pl.BlockSpec(memory_space=pltpu.VMEM),
            pl.BlockSpec(memory_space=pl.ANY),
        ],
        out_specs=(pl.BlockSpec(memory_space=pltpu.VMEM),) * 3,
        scratch_shapes=[
            pltpu.VMEM((8192, 640), jnp.bfloat16),
            pltpu.VMEM(heads, jnp.bfloat16),
            pltpu.VMEM(heads, jnp.float32),
            pltpu.SemaphoreType.DMA((16,)),
        ],
        compiler_params=pltpu.CompilerParams(vmem_limit_bytes=VMEM_LIMIT),
        cost_estimate=pl.CostEstimate(
            flops=4 * 10**9, bytes_accessed=10**7, transcendentals=8 * 10**6
        ),
    )(table, pair, q, kv)


def attend_back_kernel(
    table_ref,
    pair_ref,
    q_ref,
    grad_ref,
    out_ref,
    top_ref,
    sum_ref,
    kv_hbm,
    dq_ref,
    dkv_hbm,
    kv,
    dkv,
    q,
    gs,
    q_turned,
    g_turned,
    shift,
    acc,
    sems,
    out_sems,
):
    pair = pair_ref[0]
    high_tiles = (135 - pair) // 8
    load_tiles(table_ref, kv_hbm, kv, sems, high_tiles)

    def store(tile):
        for j in range(8):
            block = tile * 8 + j
            pltpu.make_async_copy(
                dkv.at[pl.ds(pl.multiple_of(block * 64, 64), 64)],
                dkv_hbm.at[table_ref[block]],
                out_sems.at[tile],
            ).start()

    @pl.loop(high_tiles, 16)
    def _(tile):
        dkv[pl.ds(pl.multiple_of(tile * TILE, TILE), TILE), :] = jnp.zeros(
            (TILE, 640), jnp.bfloat16
        )
        store(tile)

    q[...] = jnp.zeros(q.shape, q.dtype)
    gs[...] = jnp.zeros(gs.shape, gs.dtype)
    for g, rows, tokens, columns in head_parts():
        q[g, rows, 0:64] = q_ref[tokens, columns]
        grad = grad_ref[tokens, columns]
        total = sum_ref[g, rows, :]
        gs[g, rows, 64:128] = (grad / total[:, 0:64]).astype(jnp.bfloat16)
        delta = jnp.sum(grad * out_ref[tokens, columns], axis=1, keepdims=True)
        shift[g, rows, :] = delta / total
    for g in range(KEY_VALUE_HEADS):
        q_turned[g] = q[g].T
        g_turned[g] = gs[g].T
    acc[...] = jnp.zeros(acc.shape, jnp.float32)

    def step(tile, first_row, rows, masked):
        wait_tile(kv, sems, tile)
        span = slice(first_row, first_row + rows)
        part = pl.ds(pl.multiple_of(tile * TILE, TILE), TILE)
        if masked:
            seen = visible_keys(tile, pair, first_row, rows)
        heads = range(KEY_VALUE_HEADS)
        keys = [kv[part, g * 128 : g * 128 + 128] for g in heads]
        scores = [dot(q[g, span, :], keys[g], LAST) for g in heads]
        prob_grad = [dot(gs[g, span, :], keys[g], LAST) for g in heads]
        if masked:
            scores = [jnp.where(seen, score, -1e30) for score in scores]
        for g in heads:
            top, moved = top_ref[g, span, :], shift[g, span, :]
            probs = [jnp.exp(part_ - top) for part_ in lane_parts(scores[g])]
            grads = [
                (probs[k] * (part_ - moved)).astype(jnp.bfloat16)
                for k, part_ in enumerate(lane_parts(prob_grad[g]))
            ]
            score_grad = jnp.concatenate(grads, axis=1)
            probs_low = jnp.concatenate([prob.astype(jnp.bfloat16) for prob in probs], axis=1)
            both = dot(
                jnp.concatenate([q_turned[g, :, span], g_turned[g, :, span]], axis=1),
                jnp.concatenate([score_grad, probs_low], axis=0),
            )
            acc[g, span, :] = acc[g, span, :] + dot(score_grad, keys[g])
            dkv[part, g * 128 : g * 128 + 128] = both.astype(jnp.bfloat16).T
        store(tile)

    run_tiles(pair, step)
    for g, rows, tokens, columns in head_parts():
        dq_ref[tokens, columns] = acc[g, rows, 0:64]

    @pl.loop(0, 16)
    def _(tile):
        part = dkv.at[pl.ds(pl.multiple_of(tile * TILE, TILE), TILE)]
        pltpu.make_async_copy(part, part, out_sems.at[tile]).wait()


def attend_back(table, pair, q, grad, out, top, total, kv):
    heads = (KEY_VALUE_HEADS, QROWS, 128)
    turned = (KEY_VALUE_HEADS, 128, QROWS)
    return pl.pallas_call(
        attend_back_kernel,
        out_shape=(
            jax.ShapeDtypeStruct((128, WIDTH), jnp.float32),
            jax.ShapeDtypeStruct((128, 64, 640), jnp.bfloat16),
        ),
        in_specs=[pl.BlockSpec(memory_space=pltpu.SMEM)] * 2
        + [pl.BlockSpec(memory_space=pltpu.VMEM)] * 5
        + [pl.BlockSpec(memory_space=pl.ANY)],
        out_specs=(
            pl.BlockSpec(memory_space=pltpu.VMEM),
            pl.BlockSpec(memory_space=pl.ANY),
        ),
        scratch_shapes=[
            pltpu.VMEM((8192, 640), jnp.bfloat16),
            pltpu.VMEM((8192, 640), jnp.bfloat16),
            pltpu.VMEM(heads, jnp.bfloat16),
            pltpu.VMEM(heads, jnp.bfloat16),
            pltpu.VMEM(turned, jnp.bfloat16),
            pltpu.VMEM(turned, jnp.bfloat16),
            pltpu.VMEM(heads, jnp.float32),
            pltpu.VMEM(heads, jnp.float32),
            pltpu.SemaphoreType.DMA((16,)),
            pltpu.SemaphoreType.DMA((16,)),
        ],
        compiler_params=pltpu.CompilerParams(vmem_limit_bytes=VMEM_LIMIT),
        cost_estimate=pl.CostEstimate(
            flops=10**10, bytes_accessed=2 * 10**7, transcendentals=8 * 10**6
        ),
    )(table, pair, q, grad, out, top, total, kv)


def pad_columns(value, columns):
    return jnp.pad(value, ((0, 0), (0, columns - value.shape[1])))


def pad_halves(value, half, padded):
    return jnp.concatenate(
        [pad_columns(value[:, :half], padded), pad_columns(value[:, half:], padded)], axis=1
    )


def norm_backward(rows, scale, weighted):
    inner = jnp.sum(weighted * rows, axis=-1, keepdims=True)
    return scale * weighted - rows * scale**3 * inner / WIDTH


def rotate_tiles(values, cosine, sine):
    lane = lax.broadcasted_iota(jnp.int32, (128, 128), 1)
    turned = []
    for k in range(values.shape[1] // 128):
        part = values[:, k * 128 : k * 128 + 128]
        partner = jnp.where(lane % 64 < 32, pltpu.roll(part, 96, 1), pltpu.roll(part, 32, 1))
        turned.append(part * cosine + partner * sine)
    return jnp.concatenate(turned, axis=1)


def project_kernel(
    start_ref, scale_ref, spare_ref, w_ref, cos_ref, sin_ref, n_ref, q_ref, kv_ref, gain_ref
):
    lane = lax.broadcasted_iota(jnp.int32, (ROWS, PADDED), 1)
    row = lax.broadcasted_iota(jnp.int32, (ROWS, PADDED), 0)
    spread = dot(spare_ref[...], jnp.where(lane % ROWS == row, 1.0, 0.0).astype(jnp.bfloat16))
    lane = lax.broadcasted_iota(jnp.int32, (128, PADDED), 1)
    slot = lax.broadcasted_iota(jnp.int32, (128, PADDED), 0)
    spread = jnp.where(lane // ROWS == slot % 64, spread, 0.0)
    gain_first = jnp.sum(spread[:64], axis=0, keepdims=True)
    gain_ref[0:1, :] = gain_first
    gain_ref[1:2, :] = jnp.sum(spread[64:], axis=0, keepdims=True)
    normed = (start_ref[...] * scale_ref[...] * gain_first).astype(jnp.bfloat16)
    n_ref[...] = normed
    projected = dot(normed, w_ref[...])
    natural = jnp.concatenate(
        [projected[:, :IN_HALF], projected[:, IN_PAD : IN_PAD + IN_HALF]], axis=1
    )
    key_width = KEY_VALUE_HEADS * HEAD_SIZE
    turned = rotate_tiles(natural[:, : WIDTH + key_width], cos_ref[...], sin_ref[...])
    q_ref[...] = turned[:, :WIDTH].astype(jnp.bfloat16) * jnp.bfloat16(0.125)
    keys, values = turned[:, WIDTH:], natural[:, WIDTH + key_width :]
    pieces = []
    for g in range(KEY_VALUE_HEADS):
        span = slice(g * HEAD_SIZE, (g + 1) * HEAD_SIZE)
        pieces += [keys[:, span], values[:, span]]
    kv_ref[...] = jnp.concatenate(pieces, axis=1).astype(jnp.bfloat16)


def local_call(kernel, shapes, flops):
    return pl.pallas_call(
        kernel,
        out_shape=tuple(jax.ShapeDtypeStruct(shape, kind) for shape, kind in shapes),
        compiler_params=pltpu.CompilerParams(vmem_limit_bytes=VMEM_LIMIT),
        cost_estimate=pl.CostEstimate(flops=flops, bytes_accessed=6 * 10**6, transcendentals=0),
    )


def project(start, scale, spare, weight, cosine, sine):
    low, full = jnp.bfloat16, jnp.float32
    shapes = (
        ((128, PADDED), low),
        ((128, WIDTH), low),
        ((128, 2 * KEY_VALUE_HEADS * HEAD_SIZE), low),
        ((2, PADDED), full),
    )
    return local_call(project_kernel, shapes, 5 * 10**8)(start, scale, spare, weight, cosine, sine)


def project_back_kernel(
    dq_ref,
    kv_ref,
    start_ref,
    scale_ref,
    gain_ref,
    gain_two_ref,
    resid_ref,
    n_ref,
    w_ref,
    cos_ref,
    sin_ref,
    grad_ref,
    input_ref,
):
    key_width = KEY_VALUE_HEADS * HEAD_SIZE
    kv = kv_ref[...]
    keys = [kv[:, g * 128 : g * 128 + 64] for g in range(KEY_VALUE_HEADS)]
    values = [kv[:, g * 128 + 64 : g * 128 + 128] for g in range(KEY_VALUE_HEADS)]
    turned = rotate_tiles(
        jnp.concatenate([dq_ref[...] * 0.125] + keys, axis=1), cos_ref[...], -sin_ref[...]
    )
    natural = jnp.concatenate([turned] + values, axis=1).astype(jnp.bfloat16)
    blank = jnp.zeros((128, IN_PAD - IN_HALF), jnp.bfloat16)
    grads = jnp.concatenate([natural[:, :IN_HALF], blank, natural[:, IN_HALF:], blank], axis=1)
    back = dot(grads, w_ref[...], LAST)
    start, scale = start_ref[...], scale_ref[...]
    gain_grad = jnp.sum(back * start * scale, axis=0, keepdims=True)
    through = norm_backward(start, scale, back * gain_ref[0:1, :])
    input_ref[...] = (resid_ref[...] + through).astype(jnp.bfloat16)
    for k in range(PADDED // 256):
        span = slice(k * 256, k * 256 + 256)
        grad_ref[span, :] = dot(n_ref[:, span], grads, FIRST).astype(jnp.bfloat16)
    slot = lax.broadcasted_iota(jnp.int32, (64, PADDED), 0)
    lane = lax.broadcasted_iota(jnp.int32, (64, PADDED), 1)
    picks = jnp.where((lane // ROWS == slot) & (lane % ROWS < ROWS - 1), 1.0, 0.0)
    row = lax.broadcasted_iota(jnp.int32, (PADDED, 128), 0)
    column = lax.broadcasted_iota(jnp.int32, (PADDED, 128), 1)
    fold = jnp.where(row % ROWS == column, 1.0, 0.0).astype(jnp.bfloat16)
    row = lax.broadcasted_iota(jnp.int32, (PADDED, 64), 0)
    column = lax.broadcasted_iota(jnp.int32, (PADDED, 64), 1)
    place = jnp.where(row == column * ROWS + ROWS - 1, 1.0, 0.0).astype(jnp.bfloat16)
    for start_column, gain in ((0, gain_grad), (IN_PAD, gain_two_ref[...])):
        by_slot = dot((picks * gain).astype(jnp.bfloat16), fold).astype(jnp.bfloat16)
        span = slice(start_column, start_column + 128)
        grad_ref[:, span] = grad_ref[:, span] + dot(place, by_slot).astype(jnp.bfloat16)


def project_back(*operands):
    shapes = (((PADDED, IN_COLS), jnp.bfloat16), ((128, PADDED), jnp.bfloat16))
    return local_call(project_back_kernel, shapes, 10**9)(*operands)


def on_device(
    inputs,
    cotangent,
    positions,
    pair_index,
    input_projection,
    project_out,
    gate_up,
    down_weight,
    norm_gains,
):
    half = lax.axis_index("fsdp")
    pair = pair_index[0, 0]
    key_width = KEY_VALUE_HEADS * HEAD_SIZE
    select = (
        lax.broadcasted_iota(jnp.int32, (WIDTH, PADDED), 0) == jnp.asarray(COLUMN_MAP)[None, :]
    ).astype(jnp.bfloat16)

    spare = jnp.pad(norm_gains.T, ((0, 0), (0, 1)))
    own_in = pad_columns(
        jnp.concatenate([input_projection, pad_columns(spare, IN_HALF)], axis=0), IN_PAD
    )
    own_in = own_in.at[15, ROWS].set(pair.astype(jnp.bfloat16))
    own_out = jnp.pad(project_out, ((0, 1), (0, OUT_PAD - OUT_HALF)))
    gate_up_parts = gate_up.reshape(15, 2, 2, FF_QUARTER).transpose(2, 0, 1, 3)
    gate_up_parts = gate_up_parts.reshape(2, 15, 2 * FF_QUARTER)
    down_parts = down_weight.reshape(15, 2, FF_QUARTER).transpose(1, 0, 2)
    spare_row = ((0, 0), (0, 1), (0, 0))
    upstream = dot(cotangent[0], select)
    weight_in, weight_out, weight_gu, weight_down, row_cotangent = gather_blocks(
        (
            own_in,
            own_out,
            jnp.pad(gate_up_parts, spare_row),
            jnp.pad(down_parts, spare_row),
        ),
        ("row", "row", "split", "split"),
        upstream.astype(jnp.bfloat16),
        0,
    )
    weight_in = weight_in.reshape(PADDED, IN_COLS)
    weight_out = weight_out.reshape(PADDED, 2 * OUT_PAD)
    weight_gu = weight_gu.reshape(PADDED, 2 * FF_QUARTER)
    weight_down = weight_down.reshape(PADDED, FF_QUARTER)
    row_cotangent = row_cotangent.reshape(512, PADDED)
    blocks_in = weight_in.reshape(64, ROWS, IN_COLS)
    spare_first = blocks_in[:, 15, : 2 * ROWS]
    spare_second = blocks_in[:, 15, IN_PAD : IN_PAD + 2 * ROWS]
    held = jnp.arange(PADDED) % ROWS < 15
    labels = jnp.where(half == 0, spare_first, spare_second)[:, ROWS].astype(jnp.int32)
    slots = jnp.arange(64, dtype=jnp.int32)
    blocks = jnp.stack([labels, 127 - labels], axis=1).reshape(128)
    places = jnp.stack([2 * slots, 2 * slots + 1], axis=1).reshape(128)
    hits = blocks[None, :] == jnp.arange(128, dtype=jnp.int32)[:, None]
    table = jnp.sum(jnp.where(hits, places[None, :], 0), axis=1)

    start = dot(inputs[0], select)
    freqs = jnp.exp(
        -math.log(10000.0) * jnp.arange(HEAD_SIZE // 2, dtype=jnp.float32) * 2.0 / HEAD_SIZE
    )
    angle = positions[0].astype(jnp.float32)[:, None] * freqs[None, :]
    cosine = jnp.tile(jnp.cos(angle), (1, 4))
    sine = jnp.sin(angle)
    sine = jnp.tile(jnp.concatenate([-sine, sine], axis=1), (1, 2))
    scale_one = lax.rsqrt(jnp.sum(start * start, axis=-1, keepdims=True) / WIDTH + EPSILON)
    spare = jnp.concatenate([spare_first[:, :ROWS], spare_second[:, :ROWS]], axis=0)
    normed_low, query_scaled, key_value, gains = project(
        start, scale_one, spare, weight_in, cosine, sine
    )
    gain_second = gains[1]
    all_kv = gather_blocks((key_value,), ("whole",), None, 1)[0].reshape(128, 64, 2 * key_width)
    pair_one = pair.reshape(1)
    attention, top, total = attend(table, pair_one, query_scaled, all_kv)
    mixed_low = pad_halves(attention.astype(jnp.bfloat16), OUT_HALF, OUT_PAD)
    branch = dot(mixed_low, weight_out, LAST)
    resid = start + jnp.where(held, branch, 0.0)
    scale_two = lax.rsqrt(jnp.sum(resid * resid, axis=-1, keepdims=True) / WIDTH + EPSILON)
    normed_two = (resid * scale_two * gain_second).astype(jnp.bfloat16)
    normed_two_grad, ffn_out, grad_gu, grad_down = feed_forward(
        normed_two, row_cotangent, weight_gu, weight_down, 2
    )
    resid_grad = upstream + norm_backward(resid, scale_two, normed_two_grad * gain_second)
    gain_two_grad = jnp.sum(normed_two_grad * resid * scale_two, axis=0, keepdims=True)
    branch_grad_low = resid_grad.astype(jnp.bfloat16)
    mixed_grad = dot(branch_grad_low, weight_out)
    mixed_grad = jnp.concatenate(
        [mixed_grad[:, :OUT_HALF], mixed_grad[:, OUT_PAD : OUT_PAD + OUT_HALF]], axis=1
    )
    query_grad, all_kv_grad = attend_back(
        table, pair_one, query_scaled, mixed_grad, attention, top, total, all_kv
    )
    kv_grad, ffn_out, grad_out = scatter_blocks(
        (all_kv_grad.reshape(2, 4, 4, 2, 128, 2 * key_width),),
        ((0, 0, 2 * key_width, 0),),
        None,
        ffn_out.reshape(4, 128, PADDED),
        (
            weight_grad_work,
            (branch_grad_low, mixed_low),
            (jax.ShapeDtypeStruct((PADDED, 2 * OUT_PAD), jnp.bfloat16),),
        ),
        3,
    )
    layer_out = (resid + ffn_out).astype(jnp.bfloat16)
    grad_in, input_grad = project_back(
        query_grad,
        kv_grad,
        start,
        scale_one,
        gains,
        gain_two_grad,
        resid_grad,
        normed_low,
        weight_in,
        cosine,
        sine,
    )
    own_cols = IN_PAD + OUT_PAD
    narrow = jax.ShapeDtypeStruct((WIDTH, 128), jnp.bfloat16)
    sum_in, sum_out, sum_gu, sum_down, spare, layer_out, input_grad = scatter_blocks(
        tuple(
            grad.reshape(2, 4, 4, 2, ROWS, grad.shape[1])
            for grad in (grad_in, grad_out, grad_gu, grad_down)
        ),
        (
            (0, 0, IN_PAD, 0),
            (0, IN_PAD, IN_PAD, own_cols),
            (1, 0, OUT_PAD, IN_PAD),
            (1, OUT_PAD, OUT_PAD, own_cols + IN_PAD),
            (2, 0, 2 * FF_QUARTER, 2 * own_cols),
            (3, 0, FF_QUARTER, 2 * own_cols + 2 * FF_QUARTER),
        ),
        own_cols,
        None,
        (unpad_work, (layer_out, input_grad, select), (narrow, narrow)),
        4,
    )
    return (
        layer_out.T[None],
        input_grad.T[None],
        sum_in,
        sum_out,
        sum_gu,
        sum_down,
        spare[0, :15].reshape(15, 1),
    )


def solution(mesh):
    in_specs = (
        P("fsdp", "ctx", None),
        P("fsdp", "ctx", None),
        P("fsdp", "ctx"),
        P("fsdp", "ctx"),
        P("ctx", "fsdp"),
        P("ctx", "fsdp"),
        P("ctx", None, "fsdp"),
        P("ctx", "fsdp"),
        P("ctx", "fsdp"),
    )
    out_specs = (
        P("fsdp", "ctx", None),
        P("fsdp", "ctx", None),
        P("ctx", "fsdp"),
        P("ctx", "fsdp"),
        P("ctx", None, "fsdp"),
        P("ctx", "fsdp"),
        P("ctx", "fsdp"),
    )
    return jax.shard_map(
        on_device, mesh=mesh, in_specs=in_specs, out_specs=out_specs, check_vma=False
    )
```

```python
import math

import jax
import jax.numpy as jnp
import numpy as np
from jax import lax
from jax.experimental import pallas as pl
from jax.experimental.pallas import tpu as pltpu
from jax.sharding import PartitionSpec as P

WIDTH = 960
QUERY_HEADS = 15
KEY_VALUE_HEADS = 5
GROUP = 3
HEAD_SIZE = 64
FF_HALF = 1280
FF_QUARTER = 640
EPSILON = 1e-05
ROWS = 16
PADDED = 1024
IN_HALF = 800
IN_PAD = 896
OUT_HALF = 480
OUT_PAD = 512
IN_COLS = 2 * IN_PAD
TILE = 512
QROWS = 384
MESH = pl.DeviceIdType.MESH
VMEM_LIMIT = 56 * 1024 * 1024


def column_map():
    cols = np.full((64, ROWS), -1, np.int32)
    cols[:, :15] = np.arange(64)[:, None] * 15 + np.arange(15)[None, :]
    return cols.reshape(-1)


COLUMN_MAP = column_map()


def coordinates():
    index = lax.axis_index("ctx")
    core = index % 2
    z = (index // 2) % 4
    y = (index // 8) % 4
    x = index // 32
    p1 = y * (1 - core) + z * core
    p2 = z * (1 - core) + y * core
    return x, p1, p2, core


def device_at(x, p1, p2, core):
    y = p1 * (1 - core) + p2 * core
    z = p2 * (1 - core) + p1 * core
    return ((x * 4 + y) * 4 + z) * 2 + core


def neighbours(x, p1, p2, core):
    index = lax.axis_index("ctx")
    return (
        device_at(1 - x, p1, p2, core),
        device_at(x, (p1 + 1) % 4, p2, core),
        device_at(x, (p1 + 3) % 4, p2, core),
        device_at(x, p1, (p2 + 1) % 4, core),
        device_at(x, p1, (p2 + 3) % 4, core),
        index + 1 - 2 * core,
    )


def block_of(ref, core, x, p1, p2):
    return ref.at[x, p1, p2, core] if core == 0 else ref.at[x, p2, p1, core]


def half_of(ref, core, x, p2):
    every = pl.ds(0, 4)
    return ref.at[x, every, p2, core] if core == 0 else ref.at[x, p2, every, core]


def slab_of(ref, core, p2):
    every = pl.ds(0, 4)
    both = pl.ds(0, 2)
    return ref.at[both, every, p2, core] if core == 0 else ref.at[both, p2, every, core]


def row_place():
    return lax.axis_index("fsdp") * 2 + lax.axis_index("ctx") // 32


def row_device(place):
    index = lax.axis_index("ctx")
    return {"fsdp": place // 2, "ctx": (place % 2) * 32 + index % 32}


def ctx_device(index):
    return {"ctx": index}


class Sender:
    def __init__(self, send_sem, recv_sem):
        self.send_sem, self.recv_sem, self.sent = send_sem, recv_sem, []

    def __call__(self, source, place, device):
        number = len(self.sent)
        copy = pltpu.make_async_remote_copy(
            src_ref=source,
            dst_ref=place,
            send_sem=self.send_sem.at[number],
            recv_sem=self.recv_sem.at[number],
            device_id=device,
            device_id_type=MESH,
        )
        copy.start()
        self.sent.append(copy)
        return copy

    def finish(self):
        for copy in self.sent:
            copy.wait_send()


class RowGather:
    def __init__(self, in_ref, out_ref, local_sem, send):
        self.out, self.send = out_ref, send
        here = row_place()
        self.left, self.right = (here + 3) % 4, (here + 1) % 4
        self.local = pltpu.make_async_copy(in_ref, out_ref.at[here], local_sem)
        self.local.start()
        self.from_left = send(in_ref, out_ref.at[here], row_device(self.right))
        self.from_right = send(in_ref, out_ref.at[here], row_device(self.left))

    def forward(self):
        rows = self.out.shape[1] // 2
        low, high = pl.ds(0, rows), pl.ds(rows, rows)
        self.from_left.wait_recv()
        place = self.out.at[self.left, low]
        self.far_low = self.send(place, place, row_device(self.right))
        self.from_right.wait_recv()
        place = self.out.at[self.right, high]
        self.far_high = self.send(place, place, row_device(self.left))

    def finish(self):
        self.far_low.wait_recv()
        self.far_high.wait_recv()
        self.local.wait()


class RowScatter:
    def __init__(self, in_ref, far, near_left, near_right, stage, send):
        self.p, self.far, self.stage, self.send = in_ref, far, stage, send
        self.near_left, self.near_right = near_left, near_right
        self.here = row_place()
        self.left, self.right = (self.here + 3) % 4, (self.here + 1) % 4
        to_left, to_right = row_device(self.left), row_device(self.right)
        opposite = (self.here + 2) % 4
        rows = in_ref.shape[1] // 2
        self.low, self.high = pl.ds(0, rows), pl.ds(rows, rows)
        low, high = self.low, self.high
        self.got_low = send(in_ref.at[opposite, low], far.at[0], to_right)
        self.got_high = send(in_ref.at[opposite, high], far.at[1], to_left)
        self.waits = [
            send(in_ref.at[self.right, high], near_left.at[high], to_right),
            send(in_ref.at[self.left, low], near_right.at[low], to_left),
        ]

    def forward(self):
        rows = self.p.shape[1] // 2
        self.got_low.wait_recv()
        self.stage[0] = self.p[self.right, 0:rows] + self.far[0]
        self.waits.append(
            self.send(self.stage.at[0], self.near_left.at[self.low], row_device(self.right))
        )
        self.got_high.wait_recv()
        self.stage[1] = self.p[self.left, rows : 2 * rows] + self.far[1]
        self.waits.append(
            self.send(self.stage.at[1], self.near_right.at[self.high], row_device(self.left))
        )

    def finish(self, out_ref):
        for copy in self.waits:
            copy.wait_recv()
        total = self.p[self.here].astype(jnp.float32) + self.near_left[...].astype(jnp.float32)
        out_ref[...] = total + self.near_right[...].astype(jnp.float32)


def greet(devices):
    barrier = pltpu.get_barrier_semaphore()
    for device in devices:
        pl.semaphore_signal(barrier, inc=1, device_id=device, device_id_type=MESH)
    pl.semaphore_wait(barrier, len(devices))


def greet_ctx(with_row):
    devices = [ctx_device(index) for index in neighbours(*coordinates())]
    if with_row:
        here = row_place()
        step = 2 * (here % 2) - 1
        devices.append(row_device((here + step + 4) % 4))
    greet(devices)


def row_kernel_entry():
    here = row_place()
    greet([row_device((here + 3) % 4), row_device((here + 1) % 4)])


def row_scratch(rows, columns):
    return [
        pltpu.VMEM((2, rows // 2, columns), jnp.bfloat16),
        pltpu.VMEM((rows, columns), jnp.bfloat16),
        pltpu.VMEM((rows, columns), jnp.bfloat16),
        pltpu.VMEM((2, rows // 2, columns), jnp.bfloat16),
        pltpu.SemaphoreType.DMA((6,)),
        pltpu.SemaphoreType.DMA((6,)),
    ]


def gather_kernel(count, *refs):
    ins, refs = refs[:count], refs[count:]
    outs, refs = refs[:count], refs[count:]
    greet_ctx(count > 1)
    core = coordinates()[3]
    for chosen in range(2):

        @pl.when(core == chosen)
        def _(chosen=chosen):
            gather_body(chosen, ins, outs, *refs)


def gather_body(core, ins, outs, local_sem, send_sem, recv_sem, row_local, row_send, row_recv):
    x, p1, p2, _ = coordinates()
    across = neighbours(x, p1, p2, core)[0]
    sender = Sender(send_sem, recv_sem)
    if len(ins) == 1:
        mine = block_of(outs[0], core, x, p1, p2)
        local = pltpu.make_async_copy(ins[0], mine, local_sem.at[0])
        local.start()
        crossed = sender(ins[0], mine, ctx_device(across))
        run_all([gather_steps(core, outs[0], sender, x, lambda: None, crossed.wait_recv, ins[0], [local])])
        sender.finish()
        return
    place = row_place()
    left, right = (place + 3) % 4, (place + 1) % 4
    width = ins[0].shape[-1]

    def slot(owner):
        columns = pl.ds(pl.multiple_of((owner // 2) * width, 128), width)
        return block_of(outs[0], core, owner % 2, p1, p2).at[pl.ds(0, ROWS), columns]

    mine = block_of(outs[1], core, x, p1, p2)
    locals_ = [
        pltpu.make_async_copy(ins[0], slot(place), local_sem.at[0]),
        pltpu.make_async_copy(ins[1].at[x], mine, local_sem.at[1]),
    ]
    for copy in locals_:
        copy.start()
    from_left = sender(ins[0], slot(place), row_device(right))
    from_right = sender(ins[0], slot(place), row_device(left))
    crossed = sender(ins[1].at[1 - x], mine, ctx_device(across))
    far = []

    def first_ready():
        from_left.wait_recv()
        far.append(sender(slot(left), slot(left), row_device(right)))
        from_right.wait_recv()

    def second_ready():
        far[0].wait_recv()
        locals_[0].wait()

    row_sender = Sender(row_send, row_recv)

    def row_steps():
        for _ in range(4):
            yield
        row = RowGather(ins[2], outs[2], row_local, row_sender)
        for _ in range(8):
            yield
        row.forward()
        for _ in range(6):
            yield
        row.finish()

    run_all(
        [
            gather_steps(
                core, outs[1], sender, x, lambda: None, crossed.wait_recv, ins[1].at[x], locals_[1:]
            ),
            gather_steps(core, outs[0], sender, 1 - x, first_ready, second_ready, None, []),
            row_steps(),
        ]
    )
    sender.finish()
    row_sender.finish()


def run_all(steps):
    while steps:
        going = []
        for step in steps:
            try:
                next(step)
                going.append(step)
            except StopIteration:
                pass
        steps = going


def gather_steps(core, out_ref, sender, first, first_ready, second_ready, source, locals_):
    x, p1, p2, _ = coordinates()
    _, right1, left1, right2, left2, sibling = neighbours(x, p1, p2, core)
    p1p, p1m, p1o = (p1 + 1) % 4, (p1 + 3) % 4, (p1 + 2) % 4
    p2p, p2m, p2o = (p2 + 1) % 4, (p2 + 3) % 4, (p2 + 2) % 4
    second = 1 - first

    def block(side, q1, q2):
        return block_of(out_ref, core, side, q1, q2)

    def send(place, to, origin=None):
        return sender(place if origin is None else origin, place, ctx_device(to))

    def near(side, q1, origin=None):
        place = block(side, q1, p2)
        return send(place, right2, origin), send(place, left2, origin)

    def cross(side, q2):
        return send(half_of(out_ref, core, side, q2), sibling)

    def onward_right(copies, q1):
        copies[0].wait_recv()
        return send(block(first, q1, p2m), right2)

    def onward_left(copies, q1):
        copies[1].wait_recv()
        return send(block(second, q1, p2p), left2)

    first_ready()
    mine = block(first, p1, p2)
    own_right = send(mine, right1, source)
    own_left = send(mine, left1, source)
    own = near(first, p1, source)
    yield
    own_right.wait_recv()
    own_far = send(block(first, p1m, p2), right1)
    own_m = near(first, p1m)
    yield
    own_left.wait_recv()
    own_p = near(first, p1p)
    yield
    second_ready()
    there = block(second, p1, p2)
    other_left = send(there, left1)
    other_right = send(there, right1)
    other = near(second, p1)
    yield
    far_own = [onward_right(own, p1)]
    yield
    own_far.wait_recv()
    own_o = near(first, p1o)
    yield
    far_own.append(onward_right(own_m, p1m))
    yield
    far_own.append(onward_right(own_p, p1p))
    yield
    for copy in locals_:
        copy.wait()
    last = [cross(first, p2)]
    other_left.wait_recv()
    other_far = send(block(second, p1p, p2), left1)
    other_p = near(second, p1p)
    yield
    other_right.wait_recv()
    other_m = near(second, p1m)
    yield
    far_other = [onward_left(other, p1)]
    yield
    other_far.wait_recv()
    other_o = near(second, p1o)
    last.append(cross(second, p2))
    yield
    far_own.append(onward_right(own_o, p1o))
    last.append(cross(first, p2m))
    yield
    far_other.append(onward_left(other_p, p1p))
    yield
    far_other.append(onward_left(other_m, p1m))
    yield
    for copies in (own, own_m, own_p, own_o):
        copies[1].wait_recv()
    last.append(cross(first, p2p))
    yield
    far_other.append(onward_left(other_o, p1o))
    last.append(cross(second, p2p))
    yield
    for copies in (other, other_m, other_p, other_o):
        copies[0].wait_recv()
    last.append(cross(second, p2m))
    yield
    for side, copies in ((first, far_own), (second, far_other)):
        for copy in copies:
            copy.wait_recv()
        last.append(cross(side, p2o))
        yield
    for copy in last:
        copy.wait_recv()


def gather_blocks(blocks, collective_id):
    kind = jnp.bfloat16
    if len(blocks) == 1:
        shapes = [(2, 4, 4, 2) + blocks[0].shape]
    else:
        att, parts, row = blocks
        shapes = [
            (2, 4, 4, 2, att.shape[0], 2 * att.shape[1]),
            (2, 4, 4, 2) + parts.shape[1:],
            (4,) + row.shape,
        ]
    number = 39 if len(blocks) == 1 else 80
    return pl.pallas_call(
        lambda *refs: gather_kernel(len(blocks), *refs),
        out_shape=tuple(jax.ShapeDtypeStruct(shape, kind) for shape in shapes),
        in_specs=[pl.BlockSpec(memory_space=pl.ANY)] * len(blocks),
        out_specs=(pl.BlockSpec(memory_space=pl.ANY),) * len(blocks),
        scratch_shapes=[
            pltpu.SemaphoreType.DMA((2,)),
            pltpu.SemaphoreType.DMA((number,)),
            pltpu.SemaphoreType.DMA((number,)),
            pltpu.SemaphoreType.DMA,
            pltpu.SemaphoreType.DMA((4,)),
            pltpu.SemaphoreType.DMA((4,)),
        ],
        compiler_params=pltpu.CompilerParams(
            collective_id=collective_id, has_side_effects=True
        ),
    )(*blocks)


def scatter_kernel(pieces, halved, with_row, side, *refs):
    count = 1 + max(piece[0] for piece in pieces)
    ins, refs = refs[:count], refs[count:]
    if with_row:
        row_in, refs = refs[0], refs[1:]
    side_work, side_in, side_out = side
    side_ins, refs = refs[:side_in], refs[side_in:]
    results = 5 if halved else 1
    out_refs, refs = refs[:results], refs[results:]
    if with_row:
        row_out, refs = refs[0], refs[1:]
    side_outs, refs = refs[:side_out], refs[side_out:]
    (acc, other, far_low, far_high, near_left, near_right) = refs[:6]
    (pair_low, pair_high, pair_left, pair_right, last) = refs[6:11]
    (local_sem, cross_send, cross_recv, send_sem, recv_sem) = refs[11:16]
    x, p1, p2, core = coordinates()
    across, right1, left1, right2, left2, sibling = neighbours(x, p1, p2, core)
    greet_ctx(with_row or halved)
    p1p, p1m, p1o = (p1 + 1) % 4, (p1 + 3) % 4, (p1 + 2) % 4
    p2p, p2m, p2o = (p2 + 1) % 4, (p2 + 3) % 4, (p2 + 2) % 4
    needed = (p2o, p2m, p2p, p2)
    theirs = (p1o, p1m, p1p, p1)
    sender = Sender(send_sem, recv_sem)

    def part(ref, place, piece):
        if len(pieces) == 1:
            return ref.at[place]
        every = [pl.ds(0, size) for size in ref.shape[1:-1]]
        return ref.at[tuple([place] + every + [pl.ds(pieces[piece][3], pieces[piece][2])])]

    def source_of(piece, chosen, place):
        array, start, width, _ = pieces[piece]
        slab = slab_of(ins[array], chosen, place)
        if len(pieces) == 1:
            return slab
        every = [pl.ds(0, size) for size in slab.shape[:-1]]
        return slab.at[tuple(every + [pl.ds(start, width)])]

    def crossing(k, piece, source):
        return pltpu.make_async_remote_copy(
            src_ref=source,
            dst_ref=part(other, theirs[k], piece),
            send_sem=cross_send.at[k, piece],
            recv_sem=cross_recv.at[k, piece],
            device_id=ctx_device(sibling),
            device_id_type=MESH,
        )

    for chosen in range(2):

        @pl.when(core == chosen)
        def _(chosen=chosen):
            for k in range(4):
                for piece in range(len(pieces)):
                    crossing(k, piece, source_of(piece, 1 - chosen, theirs[k])).start()
                    pltpu.make_async_copy(
                        source_of(piece, chosen, needed[k]),
                        part(acc, needed[k], piece),
                        local_sem.at[k, piece],
                    ).start()

    if with_row:
        row_sender = Sender(refs[20], refs[21])
        row = RowScatter(row_in, refs[16], refs[17], refs[18], refs[19], row_sender)

    def send(source, place, to):
        return sender(source, place, ctx_device(to))

    def add(place, term):
        @pl.loop(0, 4)
        def _(step):
            place[step] = place[step] + term[step]

    def add_both(side):
        @pl.loop(0, 4)
        def _(step):
            total = acc[p2, side, step].astype(jnp.float32)
            total = total + near_left[side, step].astype(jnp.float32)
            total = total + near_right[side, step].astype(jnp.float32)
            acc[p2, side, step] = total.astype(acc.dtype)

    def merge(k):
        for piece in range(len(pieces)):
            mine = part(acc, needed[k], piece)
            pltpu.make_async_copy(mine, mine, local_sem.at[k, piece]).wait()
            crossing(k, piece, part(other, theirs[k], piece)).wait_recv()
        for side in range(2):
            add(acc.at[needed[k], side], other.at[needed[k], side])

    merge(0)
    got_low = send(acc.at[p2o, 0], far_low, right2)
    got_high = send(acc.at[p2o, 1], far_high, left2)
    merge(1)
    right_low = send(acc.at[p2m, 0], near_right.at[0], left2)
    merge(2)
    left_high = send(acc.at[p2p, 1], near_left.at[1], right2)
    side_work(side_ins, side_outs)
    got_low.wait_recv()
    add(acc.at[p2p, 0], far_low)
    left_low = send(acc.at[p2p, 0], near_left.at[0], right2)
    got_high.wait_recv()
    add(acc.at[p2m, 1], far_high)
    right_high = send(acc.at[p2m, 1], near_right.at[1], left2)
    merge(3)
    if with_row:
        row.forward()
    right_low.wait_recv()
    left_low.wait_recv()
    add_both(0)
    got_low = send(acc.at[p2, 0, p1o], pair_low, right1)
    near_low = send(acc.at[p2, 0, p1m], pair_right.at[0], left1)
    left_high.wait_recv()
    right_high.wait_recv()
    add_both(1)
    got_high = send(acc.at[p2, 1, p1o], pair_high, left1)
    near_high = send(acc.at[p2, 1, p1p], pair_left.at[1], right1)
    got_low.wait_recv()
    acc[p2, 0, p1p] = acc[p2, 0, p1p] + pair_low[...]
    left_low = send(acc.at[p2, 0, p1p], pair_left.at[0], right1)
    got_high.wait_recv()
    acc[p2, 1, p1m] = acc[p2, 1, p1m] + pair_high[...]
    right_high = send(acc.at[p2, 1, p1m], pair_right.at[1], left1)
    if with_row:
        row.finish(row_out)
    near_low.wait_recv()
    near_high.wait_recv()
    left_low.wait_recv()
    right_high.wait_recv()

    @pl.loop(0, 2)
    def _(j):
        total = acc[p2, j, p1].astype(jnp.float32) + pair_left[j].astype(jnp.float32)
        total = total + pair_right[j].astype(jnp.float32)
        acc[p2, j, p1] = total.astype(acc.dtype)

    if halved:
        finish_row(halved, acc, p1, p2, refs[16:20], last, sender, out_refs)
    else:
        final = send(acc.at[p2, 1 - x, p1], last, across)
        final.wait_recv()
        total = acc[p2, x, p1].astype(jnp.float32) + last[...].astype(jnp.float32)
        out_refs[0][...] = total
    for k in range(4):
        for piece in range(len(pieces)):
            crossing(k, piece, part(other, theirs[k], piece)).wait_send()
    sender.finish()
    if with_row:
        row_sender.finish()


def finish_row(halved, acc, p1, p2, buffers, last, sender, out_refs):
    in_ref, out_ref, gu_ref, down_ref, spare_ref = out_refs
    far, from_left, from_right, stage = buffers
    here = row_place()
    left, right, opposite = (here + 3) % 4, (here + 1) % 4, (here + 2) % 4
    x = here % 2
    every = pl.ds(0, ROWS)
    rest = pl.ds(2 * halved, acc.shape[-1] - 2 * halved)

    def columns(owner):
        return pl.ds(pl.multiple_of((owner // 2) * halved, 128), halved)

    def block(owner):
        return acc.at[p2, owner % 2, p1, every, columns(owner)]

    def keep_part(side, value):
        value = value.astype(jnp.float32)[: ROWS - 1]
        span = pl.ds(pl.multiple_of(side * FF_QUARTER, 128), FF_QUARTER)
        gu_ref[:, 0, span] = value[:, :FF_QUARTER]
        gu_ref[:, 1, span] = value[:, FF_QUARTER : 2 * FF_QUARTER]
        down_ref[:, span] = value[:, 2 * FF_QUARTER :]

    far_copy = sender(block(opposite), far, row_device(right))
    from_right_copy = sender(block(left), from_right, row_device(left))
    x_neighbour = row_device((here // 2) * 2 + 1 - x)
    parts_copy = sender(acc.at[p2, 1 - x, p1, every, rest], last, x_neighbour)
    far_copy.wait_recv()
    stage[...] = acc[p2, right % 2, p1, :, columns(right)] + far[...]
    from_left_copy = sender(stage, from_left, row_device(right))
    keep_part(x, acc[p2, x, p1, :, rest])
    parts_copy.wait_recv()
    keep_part(1 - x, last[...])
    from_right_copy.wait_recv()
    from_left_copy.wait_recv()
    total = acc[p2, x, p1, :, columns(here)].astype(jnp.float32)
    total = total + from_left[...].astype(jnp.float32)
    total = total + from_right[...].astype(jnp.float32)
    in_ref[...] = total[: ROWS - 1, :IN_HALF]
    out_ref[...] = total[: ROWS - 1, IN_PAD : IN_PAD + OUT_HALF]
    spare_ref[...] = total[ROWS - 1 :, :128]


def scatter_blocks(arrays, pieces, halved, row_blocks, side, collective_id):
    rows = arrays[0].shape[-2]
    columns = sum(piece[2] for piece in pieces)
    kind = arrays[0].dtype
    block = (rows, columns)
    with_row = row_blocks is not None
    operands = list(arrays)
    in_specs = [pl.BlockSpec(memory_space=pl.ANY)] * len(arrays)
    results = [block]
    last = block
    scratch = []
    if halved:
        last = (rows, columns - 2 * halved)
        results = [
            (rows - 1, IN_HALF),
            (rows - 1, OUT_HALF),
            (rows - 1, 2, FF_HALF),
            (rows - 1, FF_HALF),
            (1, 128),
        ]
        scratch = [pltpu.VMEM((rows, halved), kind)] * 4
    shapes = [jax.ShapeDtypeStruct(shape, jnp.float32) for shape in results]
    if with_row:
        operands.append(row_blocks)
        in_specs.append(pl.BlockSpec(memory_space=pltpu.VMEM))
        shapes.append(jax.ShapeDtypeStruct(row_blocks.shape[1:], jnp.float32))
        scratch = row_scratch(*row_blocks.shape[1:])
    side_work, side_operands, side_shapes = side
    operands += list(side_operands)
    in_specs += [pl.BlockSpec(memory_space=pltpu.VMEM)] * len(side_operands)
    shapes += list(side_shapes)
    side = (side_work, len(side_operands), len(side_shapes))
    return pl.pallas_call(
        lambda *refs: scatter_kernel(pieces, halved, with_row, side, *refs),
        out_shape=tuple(shapes),
        in_specs=in_specs,
        out_specs=(pl.BlockSpec(memory_space=pltpu.VMEM),) * len(shapes),
        scratch_shapes=[
            pltpu.VMEM((4, 2, 4) + block, kind),
            pltpu.VMEM((4, 2, 4) + block, kind),
            pltpu.VMEM((4,) + block, kind),
            pltpu.VMEM((4,) + block, kind),
            pltpu.VMEM((2, 4) + block, kind),
            pltpu.VMEM((2, 4) + block, kind),
            pltpu.VMEM(block, kind),
            pltpu.VMEM(block, kind),
            pltpu.VMEM((2,) + block, kind),
            pltpu.VMEM((2,) + block, kind),
            pltpu.VMEM(last, kind),
            pltpu.SemaphoreType.DMA((4, len(pieces))),
            pltpu.SemaphoreType.DMA((4, len(pieces))),
            pltpu.SemaphoreType.DMA((4, len(pieces))),
            pltpu.SemaphoreType.DMA((16,)),
            pltpu.SemaphoreType.DMA((16,)),
        ]
        + scratch,
        compiler_params=pltpu.CompilerParams(
            collective_id=collective_id, has_side_effects=True, vmem_limit_bytes=VMEM_LIMIT
        ),
    )(*operands)


def weight_grad_work(ins, outs):
    @pl.loop(0, PADDED // 256)
    def _(step):
        span = pl.ds(pl.multiple_of(step * 256, 256), 256)
        outs[0][span, :] = dot(ins[0][:, span], ins[1][...], FIRST).astype(jnp.bfloat16)


LAST = (((1,), (1,)), ((), ()))
FIRST = (((0,), (0,)), ((), ()))
PLAIN = (((1,), (0,)), ((), ()))


def dot(a, b, dims=PLAIN):
    return lax.dot_general(a, b, dims, preferred_element_type=jnp.float32)


def feed_forward_kernel(
    n_ref,
    c_ref,
    w_ref,
    dn_ref,
    part_ref,
    grad_gu_ref,
    grad_down_ref,
    normed,
    partial,
    hidden,
    gate_up_grad,
    far,
    near_left,
    near_right,
    stage,
    send_sem,
    recv_sem,
):
    row_kernel_entry()
    gu_ref = w_ref.at[:, pl.ds(0, 2 * FF_QUARTER)]
    down_ref = w_ref.at[:, pl.ds(2 * FF_QUARTER, FF_QUARTER)]
    here = row_place()
    left, right, opposite = (here + 3) % 4, (here + 1) % 4, (here + 2) % 4
    to_left, to_right = row_device(left), row_device(right)

    def rows(owner, start=0, size=128):
        return pl.ds(pl.multiple_of(owner * 128 + start, 64), size)

    def copy(number, source, place, device):
        return pltpu.make_async_remote_copy(
            src_ref=source,
            dst_ref=place,
            send_sem=send_sem.at[number],
            recv_sem=recv_sem.at[number],
            device_id=device,
            device_id_type=MESH,
        )

    mine = normed.at[rows(here)]
    low, high = pl.ds(0, 64), pl.ds(64, 64)
    normed_right = copy(0, n_ref, mine, to_right)
    normed_left = copy(1, n_ref, mine, to_left)
    place = normed.at[rows(left, 0, 64)]
    normed_far_low = copy(2, place, place, to_right)
    place = normed.at[rows(right, 64, 64)]
    normed_far_high = copy(3, place, place, to_left)
    far_low = copy(4, partial.at[rows(opposite, 0, 64)], far.at[0], to_right)
    far_high = copy(5, partial.at[rows(opposite, 64, 64)], far.at[1], to_left)
    near_low = copy(6, partial.at[rows(left, 0, 64)], near_right.at[low], to_left)
    near_high = copy(7, partial.at[rows(right, 64, 64)], near_left.at[high], to_right)
    sum_low = copy(8, stage.at[0], near_left.at[low], to_right)
    sum_high = copy(9, stage.at[1], near_right.at[high], to_left)
    normed_right.start()
    normed_left.start()
    normed[rows(here), :] = n_ref[...]

    @pl.loop(0, 4)
    def _(step):
        turn = jnp.where(step == 1, 3, jnp.where(step == 2, 1, jnp.where(step == 3, 2, 0)))
        owner = (here + turn) % 4

        @pl.when(step == 1)
        def _():
            normed_right.wait_recv()
            normed_far_low.start()

        @pl.when(step == 2)
        def _():
            normed_left.wait_recv()
            normed_far_high.start()

        @pl.when(step == 3)
        def _():
            normed_far_low.wait_recv()
            normed_far_high.wait_recv()

        gate_vals = dot(normed[rows(owner), :], gu_ref[...])
        hidden_grad = dot(c_ref[rows(owner), :], down_ref[...])
        gate = gate_vals[:, :FF_QUARTER]
        upper = gate_vals[:, FF_QUARTER:]
        sigma = jax.nn.sigmoid(gate)
        silu_vals = gate * sigma
        hidden[rows(owner), :] = (silu_vals * upper).astype(jnp.bfloat16)
        gate_grad = hidden_grad * upper * sigma * (1.0 + gate * (1.0 - sigma))
        upper_grad = hidden_grad * silu_vals
        both = jnp.concatenate([gate_grad, upper_grad], axis=1).astype(jnp.bfloat16)
        gate_up_grad[rows(owner), :] = both
        partial[rows(owner), :] = dot(both, gu_ref[...], LAST).astype(jnp.bfloat16)

        @pl.when(step == 1)
        def _():
            near_low.start()

        @pl.when(step == 2)
        def _():
            near_high.start()

        @pl.when(step == 3)
        def _():
            far_low.start()
            far_high.start()

    @pl.loop(0, 4)
    def _(owner):
        part_ref[rows(owner), :] = dot(hidden[rows(owner), :], down_ref[...], LAST).astype(
            jnp.bfloat16
        )

    far_low.wait_recv()
    stage[0] = partial[rows(right, 0, 64), :] + far[0]
    sum_low.start()
    far_high.wait_recv()
    stage[1] = partial[rows(left, 64, 64), :] + far[1]
    sum_high.start()

    @pl.loop(0, PADDED // 256)
    def _(step):
        span = pl.ds(pl.multiple_of(step * 256, 256), 256)
        grad_gu_ref[span, :] = dot(normed[:, span], gate_up_grad[...], FIRST).astype(jnp.bfloat16)
        grad_down_ref[span, :] = dot(c_ref[:, span], hidden[...], FIRST).astype(jnp.bfloat16)

    for arrived in (near_low, near_high, sum_low, sum_high):
        arrived.wait_recv()
    total = partial[rows(here), :].astype(jnp.float32) + near_left[...].astype(jnp.float32)
    dn_ref[...] = total + near_right[...].astype(jnp.float32)
    for sent in (normed_right, normed_left, normed_far_low, normed_far_high, far_low, far_high):
        sent.wait_send()
    for sent in (near_low, near_high, sum_low, sum_high):
        sent.wait_send()


def feed_forward(normed, cotangent, weights, collective_id):
    kind = jnp.bfloat16
    return pl.pallas_call(
        feed_forward_kernel,
        out_shape=(
            jax.ShapeDtypeStruct((128, PADDED), jnp.float32),
            jax.ShapeDtypeStruct((512, PADDED), kind),
            jax.ShapeDtypeStruct((PADDED, 2 * FF_QUARTER), kind),
            jax.ShapeDtypeStruct((PADDED, FF_QUARTER), kind),
        ),
        in_specs=[pl.BlockSpec(memory_space=pltpu.VMEM)] * 3,
        out_specs=(pl.BlockSpec(memory_space=pltpu.VMEM),) * 4,
        scratch_shapes=[
            pltpu.VMEM((512, PADDED), kind),
            pltpu.VMEM((512, PADDED), kind),
            pltpu.VMEM((512, FF_QUARTER), kind),
            pltpu.VMEM((512, 2 * FF_QUARTER), kind),
            pltpu.VMEM((2, 64, PADDED), kind),
            pltpu.VMEM((128, PADDED), kind),
            pltpu.VMEM((128, PADDED), kind),
            pltpu.VMEM((2, 64, PADDED), kind),
            pltpu.SemaphoreType.DMA((10,)),
            pltpu.SemaphoreType.DMA((10,)),
        ],
        compiler_params=pltpu.CompilerParams(
            collective_id=collective_id, has_side_effects=True, vmem_limit_bytes=VMEM_LIMIT
        ),
        cost_estimate=pl.CostEstimate(
            flops=7 * 10**9, bytes_accessed=10**7, transcendentals=4 * 10**5
        ),
    )(normed, cotangent, weights)


def load_tiles(table_ref, kv_hbm, kv, sems, tiles):
    @pl.loop(0, tiles)
    def _(tile):
        for j in range(8):
            block = tile * 8 + j
            pltpu.make_async_copy(
                kv_hbm.at[table_ref[block]],
                kv.at[pl.ds(pl.multiple_of(block * 64, 64), 64)],
                sems.at[tile],
            ).start()


def wait_tile(kv, sems, tile):
    part = kv.at[pl.ds(pl.multiple_of(tile * TILE, TILE), TILE)]
    pltpu.make_async_copy(part, part, sems.at[tile]).wait()


def visible_keys(tile, pair, first_row, rows):
    shape = (rows, TILE)
    row = first_row + lax.broadcasted_iota(jnp.int32, shape, 0)
    key = tile * TILE + lax.broadcasted_iota(jnp.int32, shape, 1)
    order = jnp.where(row < QROWS // 2, pair, 127 - pair) * 64 + row % 64
    return key <= order


def head_parts():
    for g in range(KEY_VALUE_HEADS):
        for half in range(2):
            for h in range(GROUP):
                rows = slice((half * GROUP + h) * 64, (half * GROUP + h) * 64 + 64)
                column = (GROUP * g + h) * HEAD_SIZE
                yield g, rows, slice(half * 64, half * 64 + 64), slice(column, column + 64)


def run_tiles(pair, step):
    low_tiles = (pair + 8) // 8
    high_tiles = (135 - pair) // 8

    @pl.loop(0, low_tiles - 1)
    def _(tile):
        step(tile, 0, QROWS, False)

    step(low_tiles - 1, 0, QROWS, True)

    @pl.loop(low_tiles, high_tiles - 1)
    def _(tile):
        step(tile, QROWS // 2, QROWS // 2, False)

    step(high_tiles - 1, QROWS // 2, QROWS // 2, True)


def lane_parts(value):
    return [value[:, k * 128 : k * 128 + 128] for k in range(TILE // 128)]


def load_halves(w_hbm, place, sems, start):
    width = place.shape[-1]
    copies = []
    for k in range(2):
        columns = pl.ds(k * (IN_PAD + OUT_PAD) + start, width)
        copies.append(
            pltpu.make_async_copy(w_hbm.at[pl.ds(0, PADDED), columns], place.at[k], sems.at[k])
        )
        copies[-1].start()
    return copies


def held_lanes():
    return lax.broadcasted_iota(jnp.int32, (128, PADDED), 1) % ROWS < ROWS - 1


def norm_scale(values):
    return lax.rsqrt(jnp.sum(values * values, axis=-1, keepdims=True) / WIDTH + EPSILON)


def attend_kernel(
    table_ref,
    pair_ref,
    q_ref,
    start_ref,
    gain_ref,
    kv_hbm,
    w_hbm,
    out_ref,
    top_ref,
    sum_ref,
    mixed_ref,
    resid_ref,
    normed_ref,
    kv,
    q,
    acc,
    weight,
    sems,
    w_sems,
):
    pair = pair_ref[0]
    high_tiles = (135 - pair) // 8
    loads = load_halves(w_hbm, weight, w_sems, IN_PAD)
    load_tiles(table_ref, kv_hbm, kv, sems, high_tiles)
    q[...] = jnp.zeros(q.shape, q.dtype)
    for g, rows, tokens, columns in head_parts():
        q[g, rows, 0:64] = q_ref[tokens, columns]
    acc[...] = jnp.zeros(acc.shape, jnp.float32)
    top_ref[...] = jnp.full(top_ref.shape, -1e30, jnp.float32)
    sum_ref[...] = jnp.zeros(sum_ref.shape, jnp.float32)

    def step(tile, first_row, rows, masked):
        wait_tile(kv, sems, tile)
        span = slice(first_row, first_row + rows)
        if masked:
            seen = visible_keys(tile, pair, first_row, rows)
        heads = range(KEY_VALUE_HEADS)
        keys = [
            kv[pl.ds(pl.multiple_of(tile * TILE, TILE), TILE), g * 128 : g * 128 + 128]
            for g in heads
        ]
        scores = [dot(q[g, span, :], keys[g], LAST) for g in heads]
        if masked:
            scores = [jnp.where(seen, score, -1e30) for score in scores]
        parts = [lane_parts(score) for score in scores]
        best = [
            jnp.maximum(jnp.maximum(p[0], p[1]), jnp.maximum(p[2], p[3])) for p in parts
        ]
        before = [top_ref[g, span, :] for g in heads]
        highest = [
            jnp.maximum(before[g], jnp.max(best[g], axis=1, keepdims=True)) for g in heads
        ]
        shrink = [jnp.exp(before[g] - highest[g]) for g in heads]
        parts = [[jnp.exp(part - highest[g]) for part in parts[g]] for g in heads]
        for g in heads:
            p = parts[g]
            top_ref[g, span, :] = highest[g]
            sum_ref[g, span, :] = sum_ref[g, span, :] * shrink[g] + ((p[0] + p[1]) + (p[2] + p[3]))
        mixed = [
            dot(jnp.concatenate([p.astype(jnp.bfloat16) for p in parts[g]], axis=1), keys[g])
            for g in heads
        ]
        for g in heads:
            acc[g, span, :] = acc[g, span, :] * shrink[g] + mixed[g]

    run_tiles(pair, step)
    for g in range(KEY_VALUE_HEADS):
        total = jnp.sum(sum_ref[g], axis=1, keepdims=True)
        sum_ref[g] = jnp.broadcast_to(total, sum_ref.shape[1:])
        acc[g] = acc[g] / sum_ref[g]
    for g, rows, tokens, columns in head_parts():
        out_ref[tokens, columns] = acc[g, rows, 64:128]
    mixed_ref[...] = jnp.zeros(mixed_ref.shape, mixed_ref.dtype)
    mixed_ref[:, :OUT_HALF] = out_ref[:, :OUT_HALF].astype(jnp.bfloat16)
    mixed_ref[:, OUT_PAD : OUT_PAD + OUT_HALF] = out_ref[:, OUT_HALF:].astype(jnp.bfloat16)
    for copy in loads:
        copy.wait()
    branch = dot(mixed_ref[:, :OUT_PAD], weight[0], LAST)
    branch = branch + dot(mixed_ref[:, OUT_PAD:], weight[1], LAST)
    resid = start_ref[...] + jnp.where(held_lanes(), branch, 0.0)
    resid_ref[...] = resid
    normed_ref[...] = (resid * norm_scale(resid) * gain_ref[1:2, :]).astype(jnp.bfloat16)


def attend(table, pair, q, start, gains, kv, weights):
    heads = (KEY_VALUE_HEADS, QROWS, 128)
    return pl.pallas_call(
        attend_kernel,
        out_shape=(
            jax.ShapeDtypeStruct((128, WIDTH), jnp.float32),
            jax.ShapeDtypeStruct(heads, jnp.float32),
            jax.ShapeDtypeStruct(heads, jnp.float32),
            jax.ShapeDtypeStruct((128, PADDED), jnp.bfloat16),
            jax.ShapeDtypeStruct((128, PADDED), jnp.float32),
            jax.ShapeDtypeStruct((128, PADDED), jnp.bfloat16),
        ),
        in_specs=[pl.BlockSpec(memory_space=pltpu.SMEM)] * 2
        + [pl.BlockSpec(memory_space=pltpu.VMEM)] * 3
        + [pl.BlockSpec(memory_space=pl.ANY)] * 2,
        out_specs=(pl.BlockSpec(memory_space=pltpu.VMEM),) * 6,
        scratch_shapes=[
            pltpu.VMEM((8192, 640), jnp.bfloat16),
            pltpu.VMEM(heads, jnp.bfloat16),
            pltpu.VMEM(heads, jnp.float32),
            pltpu.VMEM((2, PADDED, OUT_PAD), jnp.bfloat16),
            pltpu.SemaphoreType.DMA((16,)),
            pltpu.SemaphoreType.DMA((2,)),
        ],
        compiler_params=pltpu.CompilerParams(vmem_limit_bytes=VMEM_LIMIT),
        cost_estimate=pl.CostEstimate(
            flops=4 * 10**9, bytes_accessed=10**7, transcendentals=8 * 10**6
        ),
    )(table, pair, q, start, gains, kv, weights)


def attend_back_kernel(
    table_ref,
    pair_ref,
    q_ref,
    normed_grad_ref,
    resid_ref,
    upstream_ref,
    gain_ref,
    out_ref,
    top_ref,
    sum_ref,
    kv_hbm,
    w_hbm,
    dq_ref,
    dkv_hbm,
    resid_grad_ref,
    branch_grad_ref,
    gain_grad_ref,
    grad_ref,
    weight,
    w_sems,
    kv,
    dkv,
    q,
    gs,
    q_turned,
    g_turned,
    shift,
    acc,
    sems,
    out_sems,
):
    pair = pair_ref[0]
    high_tiles = (135 - pair) // 8
    loads = load_halves(w_hbm, weight, w_sems, IN_PAD)
    load_tiles(table_ref, kv_hbm, kv, sems, high_tiles)

    def store(tile):
        for j in range(8):
            block = tile * 8 + j
            pltpu.make_async_copy(
                dkv.at[pl.ds(pl.multiple_of(block * 64, 64), 64)],
                dkv_hbm.at[table_ref[block]],
                out_sems.at[tile],
            ).start()

    @pl.loop(high_tiles, 16)
    def _(tile):
        dkv[pl.ds(pl.multiple_of(tile * TILE, TILE), TILE), :] = jnp.zeros(
            (TILE, 640), jnp.bfloat16
        )
        store(tile)

    resid, normed_grad = resid_ref[...], normed_grad_ref[...]
    scale = norm_scale(resid)
    gain_grad_ref[...] = jnp.sum(normed_grad * resid * scale, axis=0, keepdims=True)
    resid_grad = upstream_ref[...] + norm_backward(resid, scale, normed_grad * gain_ref[1:2, :])
    resid_grad_ref[...] = resid_grad
    branch_grad = resid_grad.astype(jnp.bfloat16)
    branch_grad_ref[...] = branch_grad
    for copy in loads:
        copy.wait()
    for k in range(2):
        mixed_grad = dot(branch_grad, weight[k])
        grad_ref[:, k * OUT_HALF : (k + 1) * OUT_HALF] = mixed_grad[:, :OUT_HALF]
    q[...] = jnp.zeros(q.shape, q.dtype)
    gs[...] = jnp.zeros(gs.shape, gs.dtype)
    for g, rows, tokens, columns in head_parts():
        q[g, rows, 0:64] = q_ref[tokens, columns]
        grad = grad_ref[tokens, columns]
        total = sum_ref[g, rows, :]
        gs[g, rows, 64:128] = (grad / total[:, 0:64]).astype(jnp.bfloat16)
        delta = jnp.sum(grad * out_ref[tokens, columns], axis=1, keepdims=True)
        shift[g, rows, :] = delta / total
    for g in range(KEY_VALUE_HEADS):
        q_turned[g] = q[g].T
        g_turned[g] = gs[g].T
    acc[...] = jnp.zeros(acc.shape, jnp.float32)

    def step(tile, first_row, rows, masked):
        wait_tile(kv, sems, tile)
        span = slice(first_row, first_row + rows)
        part = pl.ds(pl.multiple_of(tile * TILE, TILE), TILE)
        if masked:
            seen = visible_keys(tile, pair, first_row, rows)
        heads = range(KEY_VALUE_HEADS)
        keys = [kv[part, g * 128 : g * 128 + 128] for g in heads]
        scores = [dot(q[g, span, :], keys[g], LAST) for g in heads]
        prob_grad = [dot(gs[g, span, :], keys[g], LAST) for g in heads]
        if masked:
            scores = [jnp.where(seen, score, -1e30) for score in scores]
        for g in heads:
            top, moved = top_ref[g, span, :], shift[g, span, :]
            probs = [jnp.exp(part_ - top) for part_ in lane_parts(scores[g])]
            grads = [
                (probs[k] * (part_ - moved)).astype(jnp.bfloat16)
                for k, part_ in enumerate(lane_parts(prob_grad[g]))
            ]
            score_grad = jnp.concatenate(grads, axis=1)
            probs_low = jnp.concatenate([prob.astype(jnp.bfloat16) for prob in probs], axis=1)
            both = dot(
                jnp.concatenate([q_turned[g, :, span], g_turned[g, :, span]], axis=1),
                jnp.concatenate([score_grad, probs_low], axis=0),
            )
            acc[g, span, :] = acc[g, span, :] + dot(score_grad, keys[g])
            dkv[part, g * 128 : g * 128 + 128] = both.astype(jnp.bfloat16).T
        store(tile)

    run_tiles(pair, step)
    for g, rows, tokens, columns in head_parts():
        dq_ref[tokens, columns] = acc[g, rows, 0:64]

    @pl.loop(0, 16)
    def _(tile):
        part = dkv.at[pl.ds(pl.multiple_of(tile * TILE, TILE), TILE)]
        pltpu.make_async_copy(part, part, out_sems.at[tile]).wait()


def attend_back(table, pair, q, normed_grad, resid, upstream, gains, out, top, total, kv, weights):
    heads = (KEY_VALUE_HEADS, QROWS, 128)
    turned = (KEY_VALUE_HEADS, 128, QROWS)
    return pl.pallas_call(
        attend_back_kernel,
        out_shape=(
            jax.ShapeDtypeStruct((128, WIDTH), jnp.float32),
            jax.ShapeDtypeStruct((128, 64, 640), jnp.bfloat16),
            jax.ShapeDtypeStruct((128, PADDED), jnp.float32),
            jax.ShapeDtypeStruct((128, PADDED), jnp.bfloat16),
            jax.ShapeDtypeStruct((1, PADDED), jnp.float32),
        ),
        in_specs=[pl.BlockSpec(memory_space=pltpu.SMEM)] * 2
        + [pl.BlockSpec(memory_space=pltpu.VMEM)] * 8
        + [pl.BlockSpec(memory_space=pl.ANY)] * 2,
        out_specs=(
            pl.BlockSpec(memory_space=pltpu.VMEM),
            pl.BlockSpec(memory_space=pl.ANY),
        )
        + (pl.BlockSpec(memory_space=pltpu.VMEM),) * 3,
        scratch_shapes=[
            pltpu.VMEM((128, WIDTH), jnp.float32),
            pltpu.VMEM((2, PADDED, OUT_PAD), jnp.bfloat16),
            pltpu.SemaphoreType.DMA((2,)),
            pltpu.VMEM((8192, 640), jnp.bfloat16),
            pltpu.VMEM((8192, 640), jnp.bfloat16),
            pltpu.VMEM(heads, jnp.bfloat16),
            pltpu.VMEM(heads, jnp.bfloat16),
            pltpu.VMEM(turned, jnp.bfloat16),
            pltpu.VMEM(turned, jnp.bfloat16),
            pltpu.VMEM(heads, jnp.float32),
            pltpu.VMEM(heads, jnp.float32),
            pltpu.SemaphoreType.DMA((16,)),
            pltpu.SemaphoreType.DMA((16,)),
        ],
        compiler_params=pltpu.CompilerParams(vmem_limit_bytes=VMEM_LIMIT),
        cost_estimate=pl.CostEstimate(
            flops=10**10, bytes_accessed=2 * 10**7, transcendentals=8 * 10**6
        ),
    )(table, pair, q, normed_grad, resid, upstream, gains, out, top, total, kv, weights)


def pad_columns(value, columns):
    return jnp.pad(value, ((0, 0), (0, columns - value.shape[1])))


def pad_halves(value, half, padded):
    return jnp.concatenate(
        [pad_columns(value[:, :half], padded), pad_columns(value[:, half:], padded)], axis=1
    )


def norm_backward(rows, scale, weighted):
    inner = jnp.sum(weighted * rows, axis=-1, keepdims=True)
    return scale * weighted - rows * scale**3 * inner / WIDTH


def rotate_tiles(values, cosine, sine):
    lane = lax.broadcasted_iota(jnp.int32, (128, 128), 1)
    turned = []
    for k in range(values.shape[1] // 128):
        part = values[:, k * 128 : k * 128 + 128]
        partner = jnp.where(lane % 64 < 32, pltpu.roll(part, 96, 1), pltpu.roll(part, 32, 1))
        turned.append(part * cosine + partner * sine)
    return jnp.concatenate(turned, axis=1)


def project_kernel(
    start_ref,
    spare_ref,
    cos_ref,
    sin_ref,
    w_hbm,
    n_ref,
    q_ref,
    kv_ref,
    gain_ref,
    weight,
    w_sems,
):
    loads = load_halves(w_hbm, weight, w_sems, 0)
    lane = lax.broadcasted_iota(jnp.int32, (ROWS, PADDED), 1)
    row = lax.broadcasted_iota(jnp.int32, (ROWS, PADDED), 0)
    spread = dot(spare_ref[...], jnp.where(lane % ROWS == row, 1.0, 0.0).astype(jnp.bfloat16))
    lane = lax.broadcasted_iota(jnp.int32, (128, PADDED), 1)
    slot = lax.broadcasted_iota(jnp.int32, (128, PADDED), 0)
    spread = jnp.where(lane // ROWS == slot % 64, spread, 0.0)
    gain_first = jnp.sum(spread[:64], axis=0, keepdims=True)
    gain_ref[0:1, :] = gain_first
    gain_ref[1:2, :] = jnp.sum(spread[64:], axis=0, keepdims=True)
    start = start_ref[...]
    normed = (start * norm_scale(start) * gain_first).astype(jnp.bfloat16)
    n_ref[...] = normed
    for copy in loads:
        copy.wait()
    natural = jnp.concatenate([dot(normed, weight[k])[:, :IN_HALF] for k in range(2)], axis=1)
    key_width = KEY_VALUE_HEADS * HEAD_SIZE
    turned = rotate_tiles(natural[:, : WIDTH + key_width], cos_ref[...], sin_ref[...])
    q_ref[...] = turned[:, :WIDTH].astype(jnp.bfloat16) * jnp.bfloat16(0.125)
    keys, values = turned[:, WIDTH:], natural[:, WIDTH + key_width :]
    pieces = []
    for g in range(KEY_VALUE_HEADS):
        span = slice(g * HEAD_SIZE, (g + 1) * HEAD_SIZE)
        pieces += [keys[:, span], values[:, span]]
    kv_ref[...] = jnp.concatenate(pieces, axis=1).astype(jnp.bfloat16)


def local_call(kernel, shapes, operands, weights, flops):
    return pl.pallas_call(
        kernel,
        out_shape=tuple(jax.ShapeDtypeStruct(shape, kind) for shape, kind in shapes),
        in_specs=[pl.BlockSpec(memory_space=pltpu.VMEM)] * len(operands)
        + [pl.BlockSpec(memory_space=pl.ANY)],
        scratch_shapes=[
            pltpu.VMEM((2, PADDED, IN_PAD), jnp.bfloat16),
            pltpu.SemaphoreType.DMA((2,)),
        ],
        compiler_params=pltpu.CompilerParams(vmem_limit_bytes=VMEM_LIMIT),
        cost_estimate=pl.CostEstimate(flops=flops, bytes_accessed=6 * 10**6, transcendentals=0),
    )(*operands, weights)


def project(start, spare, cosine, sine, weights):
    low, full = jnp.bfloat16, jnp.float32
    shapes = (
        ((128, PADDED), low),
        ((128, WIDTH), low),
        ((128, 2 * KEY_VALUE_HEADS * HEAD_SIZE), low),
        ((2, PADDED), full),
    )
    return local_call(project_kernel, shapes, (start, spare, cosine, sine), weights, 5 * 10**8)


def project_back_kernel(
    dq_ref,
    kv_ref,
    start_ref,
    gain_ref,
    gain_two_ref,
    resid_grad_ref,
    n_ref,
    cos_ref,
    sin_ref,
    resid_ref,
    ffn_ref,
    map_ref,
    w_hbm,
    grad_ref,
    layer_ref,
    input_ref,
    weight,
    w_sems,
):
    loads = load_halves(w_hbm, weight, w_sems, 0)
    row = lax.broadcasted_iota(jnp.int32, (WIDTH, PADDED), 0)
    select = jnp.where(row == map_ref[...], 1.0, 0.0).astype(jnp.bfloat16)
    layer = (resid_ref[...] + ffn_ref[...]).astype(jnp.bfloat16)
    layer_ref[...] = dot(select, layer, LAST).astype(jnp.bfloat16)
    key_width = KEY_VALUE_HEADS * HEAD_SIZE
    kv = kv_ref[...]
    keys = [kv[:, g * 128 : g * 128 + 64] for g in range(KEY_VALUE_HEADS)]
    values = [kv[:, g * 128 + 64 : g * 128 + 128] for g in range(KEY_VALUE_HEADS)]
    turned = rotate_tiles(
        jnp.concatenate([dq_ref[...] * 0.125] + keys, axis=1), cos_ref[...], -sin_ref[...]
    )
    natural = jnp.concatenate([turned] + values, axis=1).astype(jnp.bfloat16)
    blank = jnp.zeros((128, IN_PAD - IN_HALF), jnp.bfloat16)
    grads = jnp.concatenate([natural[:, :IN_HALF], blank, natural[:, IN_HALF:], blank], axis=1)
    for copy in loads:
        copy.wait()
    back = dot(grads[:, :IN_PAD], weight[0], LAST) + dot(grads[:, IN_PAD:], weight[1], LAST)
    start = start_ref[...]
    scale = norm_scale(start)
    gain_grad = jnp.sum(back * start * scale, axis=0, keepdims=True)
    through = norm_backward(start, scale, back * gain_ref[0:1, :])
    change = (resid_grad_ref[...] + through).astype(jnp.bfloat16)
    input_ref[...] = dot(select, change, LAST).astype(jnp.bfloat16)
    for k in range(PADDED // 256):
        span = slice(k * 256, k * 256 + 256)
        grad_ref[span, :] = dot(n_ref[:, span], grads, FIRST).astype(jnp.bfloat16)
    slot = lax.broadcasted_iota(jnp.int32, (64, PADDED), 0)
    lane = lax.broadcasted_iota(jnp.int32, (64, PADDED), 1)
    picks = jnp.where((lane // ROWS == slot) & (lane % ROWS < ROWS - 1), 1.0, 0.0)
    row = lax.broadcasted_iota(jnp.int32, (PADDED, 128), 0)
    column = lax.broadcasted_iota(jnp.int32, (PADDED, 128), 1)
    fold = jnp.where(row % ROWS == column, 1.0, 0.0).astype(jnp.bfloat16)
    row = lax.broadcasted_iota(jnp.int32, (PADDED, 64), 0)
    column = lax.broadcasted_iota(jnp.int32, (PADDED, 64), 1)
    place = jnp.where(row == column * ROWS + ROWS - 1, 1.0, 0.0).astype(jnp.bfloat16)
    for start_column, gain in ((0, gain_grad), (IN_PAD, gain_two_ref[...])):
        by_slot = dot((picks * gain).astype(jnp.bfloat16), fold).astype(jnp.bfloat16)
        span = slice(start_column, start_column + 128)
        grad_ref[:, span] = grad_ref[:, span] + dot(place, by_slot).astype(jnp.bfloat16)


def project_back(operands, weights):
    low = jnp.bfloat16
    shapes = (((PADDED, IN_COLS), low), ((WIDTH, 128), low), ((WIDTH, 128), low))
    return local_call(project_back_kernel, shapes, operands, weights, 10**9)


def store_kernel(*refs):
    count = len(refs) // 2
    for source, place in zip(refs[:count], refs[count:]):
        place[...] = source[...]


def store(arrays):
    return pl.pallas_call(
        store_kernel,
        out_shape=tuple(jax.ShapeDtypeStruct(array.shape, array.dtype) for array in arrays),
        compiler_params=pltpu.CompilerParams(vmem_limit_bytes=VMEM_LIMIT),
    )(*arrays)


def on_device(
    inputs,
    cotangent,
    positions,
    pair_index,
    input_projection,
    project_out,
    gate_up,
    down_weight,
    norm_gains,
):
    half = lax.axis_index("fsdp")
    pair = pair_index[0, 0]
    key_width = KEY_VALUE_HEADS * HEAD_SIZE
    select = (
        lax.broadcasted_iota(jnp.int32, (WIDTH, PADDED), 0) == jnp.asarray(COLUMN_MAP)[None, :]
    ).astype(jnp.bfloat16)

    spare = jnp.pad(norm_gains.T, ((0, 0), (0, 1)))
    own_in = jnp.concatenate([input_projection, pad_columns(spare, IN_HALF)], axis=0)
    own_in = own_in.at[15, ROWS].set(pair.astype(jnp.bfloat16))
    own_out = jnp.pad(project_out, ((0, 1), (0, OUT_PAD - OUT_HALF)))
    own_att = jnp.concatenate([pad_columns(own_in, IN_PAD), own_out], axis=1)
    parts = jnp.concatenate([gate_up, down_weight[:, None]], axis=1)
    parts = parts.reshape(15, 3, 2, FF_QUARTER).transpose(2, 0, 1, 3)
    parts = jnp.pad(parts.reshape(2, 15, 3 * FF_QUARTER), ((0, 0), (0, 1), (0, 0)))
    upstream = dot(cotangent[0], select)
    weight_att, weight_ffn, row_cotangent = gather_blocks(
        (own_att, parts, upstream.astype(jnp.bfloat16)), 0
    )
    weight_att = weight_att.reshape(PADDED, 2 * (IN_PAD + OUT_PAD))
    weight_ffn = weight_ffn.reshape(PADDED, 3 * FF_QUARTER)
    row_cotangent = row_cotangent.reshape(512, PADDED)
    blocks_att = weight_att.reshape(64, ROWS, 2 * (IN_PAD + OUT_PAD))
    spare_first = blocks_att[:, 15, : 2 * ROWS]
    spare_second = blocks_att[:, 15, IN_PAD + OUT_PAD : IN_PAD + OUT_PAD + 2 * ROWS]
    labels = jnp.where(half == 0, spare_first, spare_second)[:, ROWS].astype(jnp.int32)
    slots = jnp.arange(64, dtype=jnp.int32)
    blocks = jnp.stack([labels, 127 - labels], axis=1).reshape(128)
    places = jnp.stack([2 * slots, 2 * slots + 1], axis=1).reshape(128)
    hits = blocks[None, :] == jnp.arange(128, dtype=jnp.int32)[:, None]
    table = jnp.sum(jnp.where(hits, places[None, :], 0), axis=1)

    start = dot(inputs[0], select)
    freqs = jnp.exp(
        -math.log(10000.0) * jnp.arange(HEAD_SIZE // 2, dtype=jnp.float32) * 2.0 / HEAD_SIZE
    )
    angle = positions[0].astype(jnp.float32)[:, None] * freqs[None, :]
    cosine = jnp.tile(jnp.cos(angle), (1, 4))
    sine = jnp.sin(angle)
    sine = jnp.tile(jnp.concatenate([-sine, sine], axis=1), (1, 2))
    spare = jnp.concatenate([spare_first[:, :ROWS], spare_second[:, :ROWS]], axis=0)
    normed_low, query_scaled, key_value, gains = project(
        start, spare, cosine, sine, weight_att
    )
    all_kv = gather_blocks((key_value,), 1)[0].reshape(128, 64, 2 * key_width)
    pair_one = pair.reshape(1)
    attention, top, total, mixed_low, resid, normed_two = attend(
        table, pair_one, query_scaled, start, gains, all_kv, weight_att
    )
    normed_two_grad, ffn_out, grad_gu, grad_down = feed_forward(
        normed_two, row_cotangent, weight_ffn, 2
    )
    query_grad, all_kv_grad, resid_grad, branch_grad_low, gain_two_grad = attend_back(
        table,
        pair_one,
        query_scaled,
        normed_two_grad,
        resid,
        upstream,
        gains,
        attention,
        top,
        total,
        all_kv,
        weight_att,
    )
    kv_grad, ffn_out, grad_out = scatter_blocks(
        (all_kv_grad.reshape(2, 4, 4, 2, 128, 2 * key_width),),
        ((0, 0, 2 * key_width, 0),),
        None,
        ffn_out.reshape(4, 128, PADDED),
        (
            weight_grad_work,
            (branch_grad_low, mixed_low),
            (jax.ShapeDtypeStruct((PADDED, 2 * OUT_PAD), jnp.bfloat16),),
        ),
        3,
    )
    grad_in, layer_out, input_grad = project_back(
        (
            query_grad,
            kv_grad,
            start,
            gains,
            gain_two_grad,
            resid_grad,
            normed_low,
            cosine,
            sine,
            resid,
            ffn_out,
            jnp.asarray(COLUMN_MAP)[None, :],
        ),
        weight_att,
    )
    own_cols = IN_PAD + OUT_PAD
    sums = scatter_blocks(
        tuple(
            grad.reshape(2, 4, 4, 2, ROWS, grad.shape[1])
            for grad in (grad_in, grad_out, grad_gu, grad_down)
        ),
        (
            (0, 0, IN_PAD, 0),
            (0, IN_PAD, IN_PAD, own_cols),
            (1, 0, OUT_PAD, IN_PAD),
            (1, OUT_PAD, OUT_PAD, own_cols + IN_PAD),
            (2, 0, 2 * FF_QUARTER, 2 * own_cols),
            (3, 0, FF_QUARTER, 2 * own_cols + 2 * FF_QUARTER),
        ),
        own_cols,
        None,
        (lambda ins, outs: None, (), ()),
        4,
    )
    sum_in, sum_out, sum_gu, sum_down, spare = store(sums)
    return (
        layer_out.T[None],
        input_grad.T[None],
        sum_in,
        sum_out,
        sum_gu,
        sum_down,
        spare[0, :15].reshape(15, 1),
    )


def solution(mesh):
    in_specs = (
        P("fsdp", "ctx", None),
        P("fsdp", "ctx", None),
        P("fsdp", "ctx"),
        P("fsdp", "ctx"),
        P("ctx", "fsdp"),
        P("ctx", "fsdp"),
        P("ctx", None, "fsdp"),
        P("ctx", "fsdp"),
        P("ctx", "fsdp"),
    )
    out_specs = (
        P("fsdp", "ctx", None),
        P("fsdp", "ctx", None),
        P("ctx", "fsdp"),
        P("ctx", "fsdp"),
        P("ctx", None, "fsdp"),
        P("ctx", "fsdp"),
        P("ctx", "fsdp"),
    )
    return jax.shard_map(
        on_device, mesh=mesh, in_specs=in_specs, out_specs=out_specs, check_vma=False
    )
```

```python
import math

import jax
import jax.numpy as jnp
import numpy as np
from jax import lax
from jax.experimental import pallas as pl
from jax.experimental.pallas import tpu as pltpu
from jax.sharding import PartitionSpec as P

WIDTH = 960
QUERY_HEADS = 15
KEY_VALUE_HEADS = 5
GROUP = 3
HEAD_SIZE = 64
FF_HALF = 1280
FF_QUARTER = 640
EPSILON = 1e-05
ROWS = 16
PADDED = 1024
IN_HALF = 800
IN_PAD = 896
OUT_HALF = 480
OUT_PAD = 512
IN_COLS = 2 * IN_PAD
TILE = 512
QROWS = 384
MESH = pl.DeviceIdType.MESH
VMEM_LIMIT = 56 * 1024 * 1024


def column_map():
    cols = np.full((64, ROWS), -1, np.int32)
    cols[:, :15] = np.arange(64)[:, None] * 15 + np.arange(15)[None, :]
    return cols.reshape(-1)


COLUMN_MAP = column_map()


def coordinates():
    index = lax.axis_index("ctx")
    core = index % 2
    z = (index // 2) % 4
    y = (index // 8) % 4
    x = index // 32
    p1 = y * (1 - core) + z * core
    p2 = z * (1 - core) + y * core
    return x, p1, p2, core


def device_at(x, p1, p2, core):
    y = p1 * (1 - core) + p2 * core
    z = p2 * (1 - core) + p1 * core
    return ((x * 4 + y) * 4 + z) * 2 + core


def neighbours(x, p1, p2, core):
    index = lax.axis_index("ctx")
    return (
        device_at(1 - x, p1, p2, core),
        device_at(x, (p1 + 1) % 4, p2, core),
        device_at(x, (p1 + 3) % 4, p2, core),
        device_at(x, p1, (p2 + 1) % 4, core),
        device_at(x, p1, (p2 + 3) % 4, core),
        index + 1 - 2 * core,
    )


def block_of(ref, core, x, p1, p2):
    return ref.at[x, p1, p2, core] if core == 0 else ref.at[x, p2, p1, core]


def half_of(ref, core, x, p2):
    every = pl.ds(0, 4)
    return ref.at[x, every, p2, core] if core == 0 else ref.at[x, p2, every, core]


def row_place():
    return lax.axis_index("fsdp") * 2 + lax.axis_index("ctx") // 32


def row_device(place):
    index = lax.axis_index("ctx")
    return {"fsdp": place // 2, "ctx": (place % 2) * 32 + index % 32}


def ctx_device(index):
    return {"ctx": index}


class Sender:
    def __init__(self, send_sem, recv_sem):
        self.send_sem, self.recv_sem, self.sent = send_sem, recv_sem, []

    def __call__(self, source, place, device):
        number = len(self.sent)
        copy = pltpu.make_async_remote_copy(
            src_ref=source,
            dst_ref=place,
            send_sem=self.send_sem.at[number],
            recv_sem=self.recv_sem.at[number],
            device_id=device,
            device_id_type=MESH,
        )
        copy.start()
        self.sent.append(copy)
        return copy

    def finish(self):
        for copy in self.sent:
            copy.wait_send()


class RowGather:
    def __init__(self, in_ref, out_ref, local_sem, send):
        self.out, self.send = out_ref, send
        here = row_place()
        self.left, self.right = (here + 3) % 4, (here + 1) % 4
        self.local = pltpu.make_async_copy(in_ref, out_ref.at[here], local_sem)
        self.local.start()
        self.from_left = send(in_ref, out_ref.at[here], row_device(self.right))
        self.from_right = send(in_ref, out_ref.at[here], row_device(self.left))

    def forward(self):
        rows = self.out.shape[1] // 2
        low, high = pl.ds(0, rows), pl.ds(rows, rows)
        self.from_left.wait_recv()
        place = self.out.at[self.left, low]
        self.far_low = self.send(place, place, row_device(self.right))
        self.from_right.wait_recv()
        place = self.out.at[self.right, high]
        self.far_high = self.send(place, place, row_device(self.left))

    def finish(self):
        self.far_low.wait_recv()
        self.far_high.wait_recv()
        self.local.wait()


class RowScatter:
    def __init__(self, in_ref, far, near_left, near_right, stage, send):
        self.p, self.far, self.stage, self.send = in_ref, far, stage, send
        self.near_left, self.near_right = near_left, near_right
        self.here = row_place()
        self.left, self.right = (self.here + 3) % 4, (self.here + 1) % 4
        to_left, to_right = row_device(self.left), row_device(self.right)
        opposite = (self.here + 2) % 4
        rows = in_ref.shape[1] // 2
        self.low, self.high = pl.ds(0, rows), pl.ds(rows, rows)
        low, high = self.low, self.high
        self.got_low = send(in_ref.at[opposite, low], far.at[0], to_right)
        self.got_high = send(in_ref.at[opposite, high], far.at[1], to_left)
        self.waits = [
            send(in_ref.at[self.right, high], near_left.at[high], to_right),
            send(in_ref.at[self.left, low], near_right.at[low], to_left),
        ]

    def forward(self):
        rows = self.p.shape[1] // 2
        self.got_low.wait_recv()
        self.stage[0] = self.p[self.right, 0:rows] + self.far[0]
        self.waits.append(
            self.send(self.stage.at[0], self.near_left.at[self.low], row_device(self.right))
        )
        self.got_high.wait_recv()
        self.stage[1] = self.p[self.left, rows : 2 * rows] + self.far[1]
        self.waits.append(
            self.send(self.stage.at[1], self.near_right.at[self.high], row_device(self.left))
        )

    def finish(self, out_ref):
        for copy in self.waits:
            copy.wait_recv()
        total = self.p[self.here].astype(jnp.float32) + self.near_left[...].astype(jnp.float32)
        out_ref[...] = total + self.near_right[...].astype(jnp.float32)


def greet(devices):
    barrier = pltpu.get_barrier_semaphore()
    for device in devices:
        pl.semaphore_signal(barrier, inc=1, device_id=device, device_id_type=MESH)
    pl.semaphore_wait(barrier, len(devices))


def greet_ctx(with_row):
    devices = [ctx_device(index) for index in neighbours(*coordinates())]
    if with_row:
        here = row_place()
        step = 2 * (here % 2) - 1
        devices.append(row_device((here + step + 4) % 4))
    greet(devices)


def row_kernel_entry():
    here = row_place()
    greet([row_device((here + 3) % 4), row_device((here + 1) % 4)])


def row_scratch(rows, columns):
    return [
        pltpu.VMEM((2, rows // 2, columns), jnp.bfloat16),
        pltpu.VMEM((rows, columns), jnp.bfloat16),
        pltpu.VMEM((rows, columns), jnp.bfloat16),
        pltpu.VMEM((2, rows // 2, columns), jnp.bfloat16),
        pltpu.SemaphoreType.DMA((6,)),
        pltpu.SemaphoreType.DMA((6,)),
    ]


def gather_kernel(count, *refs):
    ins, refs = refs[:count], refs[count:]
    outs, refs = refs[:count], refs[count:]
    greet_ctx(count > 1)
    core = coordinates()[3]
    for chosen in range(2):

        @pl.when(core == chosen)
        def _(chosen=chosen):
            gather_body(chosen, ins, outs, *refs)


def gather_body(core, ins, outs, local_sem, send_sem, recv_sem, row_local, row_send, row_recv):
    x, p1, p2, _ = coordinates()
    across = neighbours(x, p1, p2, core)[0]
    sender = Sender(send_sem, recv_sem)
    if len(ins) == 1:
        mine = block_of(outs[0], core, x, p1, p2)
        local = pltpu.make_async_copy(ins[0], mine, local_sem.at[0])
        local.start()
        crossed = sender(ins[0], mine, ctx_device(across))
        run_all([gather_steps(core, outs[0], sender, x, lambda: None, crossed.wait_recv, ins[0], [local])])
        sender.finish()
        return
    place = row_place()
    left, right = (place + 3) % 4, (place + 1) % 4
    width = ins[0].shape[-1]

    def slot(owner):
        columns = pl.ds(pl.multiple_of((owner // 2) * width, 128), width)
        return block_of(outs[0], core, owner % 2, p1, p2).at[pl.ds(0, ROWS), columns]

    mine = block_of(outs[1], core, x, p1, p2)
    locals_ = [
        pltpu.make_async_copy(ins[0], slot(place), local_sem.at[0]),
        pltpu.make_async_copy(ins[1].at[x], mine, local_sem.at[1]),
    ]
    for copy in locals_:
        copy.start()
    from_left = sender(ins[0], slot(place), row_device(right))
    from_right = sender(ins[0], slot(place), row_device(left))
    crossed = sender(ins[1].at[1 - x], mine, ctx_device(across))
    far = []

    def first_ready():
        from_left.wait_recv()
        far.append(sender(slot(left), slot(left), row_device(right)))
        from_right.wait_recv()

    def second_ready():
        far[0].wait_recv()
        locals_[0].wait()

    row_sender = Sender(row_send, row_recv)

    def row_steps():
        for _ in range(4):
            yield
        row = RowGather(ins[2], outs[2], row_local, row_sender)
        for _ in range(8):
            yield
        row.forward()
        for _ in range(6):
            yield
        row.finish()

    run_all(
        [
            gather_steps(
                core, outs[1], sender, x, lambda: None, crossed.wait_recv, ins[1].at[x], locals_[1:]
            ),
            gather_steps(core, outs[0], sender, 1 - x, first_ready, second_ready, None, []),
            row_steps(),
        ]
    )
    sender.finish()
    row_sender.finish()


def run_all(steps):
    while steps:
        going = []
        for step in steps:
            try:
                next(step)
                going.append(step)
            except StopIteration:
                pass
        steps = going


def gather_steps(core, out_ref, sender, first, first_ready, second_ready, source, locals_):
    x, p1, p2, _ = coordinates()
    _, right1, left1, right2, left2, sibling = neighbours(x, p1, p2, core)
    p1p, p1m, p1o = (p1 + 1) % 4, (p1 + 3) % 4, (p1 + 2) % 4
    p2p, p2m, p2o = (p2 + 1) % 4, (p2 + 3) % 4, (p2 + 2) % 4
    second = 1 - first

    def block(side, q1, q2):
        return block_of(out_ref, core, side, q1, q2)

    def send(place, to, origin=None):
        return sender(place if origin is None else origin, place, ctx_device(to))

    def near(side, q1, origin=None):
        place = block(side, q1, p2)
        return send(place, right2, origin), send(place, left2, origin)

    def cross(side, q2):
        return send(half_of(out_ref, core, side, q2), sibling)

    def onward_right(copies, q1):
        copies[0].wait_recv()
        return send(block(first, q1, p2m), right2)

    def onward_left(copies, q1):
        copies[1].wait_recv()
        return send(block(second, q1, p2p), left2)

    first_ready()
    mine = block(first, p1, p2)
    own_right = send(mine, right1, source)
    own_left = send(mine, left1, source)
    own = near(first, p1, source)
    yield
    own_right.wait_recv()
    own_far = send(block(first, p1m, p2), right1)
    own_m = near(first, p1m)
    yield
    own_left.wait_recv()
    own_p = near(first, p1p)
    yield
    second_ready()
    there = block(second, p1, p2)
    other_left = send(there, left1)
    other_right = send(there, right1)
    other = near(second, p1)
    yield
    far_own = [onward_right(own, p1)]
    yield
    own_far.wait_recv()
    own_o = near(first, p1o)
    yield
    far_own.append(onward_right(own_m, p1m))
    yield
    far_own.append(onward_right(own_p, p1p))
    yield
    for copy in locals_:
        copy.wait()
    last = [cross(first, p2)]
    other_left.wait_recv()
    other_far = send(block(second, p1p, p2), left1)
    other_p = near(second, p1p)
    yield
    other_right.wait_recv()
    other_m = near(second, p1m)
    yield
    far_other = [onward_left(other, p1)]
    yield
    other_far.wait_recv()
    other_o = near(second, p1o)
    last.append(cross(second, p2))
    yield
    far_own.append(onward_right(own_o, p1o))
    last.append(cross(first, p2m))
    yield
    far_other.append(onward_left(other_p, p1p))
    yield
    far_other.append(onward_left(other_m, p1m))
    yield
    for copies in (own, own_m, own_p, own_o):
        copies[1].wait_recv()
    last.append(cross(first, p2p))
    yield
    far_other.append(onward_left(other_o, p1o))
    last.append(cross(second, p2p))
    yield
    for copies in (other, other_m, other_p, other_o):
        copies[0].wait_recv()
    last.append(cross(second, p2m))
    yield
    for side, copies in ((first, far_own), (second, far_other)):
        for copy in copies:
            copy.wait_recv()
        last.append(cross(side, p2o))
        yield
    for copy in last:
        copy.wait_recv()


def gather_blocks(blocks, collective_id):
    kind = jnp.bfloat16
    if len(blocks) == 1:
        shapes = [(2, 4, 4, 2) + blocks[0].shape]
    else:
        att, parts, row = blocks
        shapes = [
            (2, 4, 4, 2, att.shape[0], 2 * att.shape[1]),
            (2, 4, 4, 2) + parts.shape[1:],
            (4,) + row.shape,
        ]
    number = 39 if len(blocks) == 1 else 80
    return pl.pallas_call(
        lambda *refs: gather_kernel(len(blocks), *refs),
        out_shape=tuple(jax.ShapeDtypeStruct(shape, kind) for shape in shapes),
        in_specs=[pl.BlockSpec(memory_space=pl.ANY)] * len(blocks),
        out_specs=(pl.BlockSpec(memory_space=pl.ANY),) * len(blocks),
        scratch_shapes=[
            pltpu.SemaphoreType.DMA((2,)),
            pltpu.SemaphoreType.DMA((number,)),
            pltpu.SemaphoreType.DMA((number,)),
            pltpu.SemaphoreType.DMA,
            pltpu.SemaphoreType.DMA((4,)),
            pltpu.SemaphoreType.DMA((4,)),
        ],
        compiler_params=pltpu.CompilerParams(
            collective_id=collective_id, has_side_effects=True
        ),
    )(*blocks)


def scatter_kernel(pieces, halved, with_row, side, *refs):
    count = 1 + max(piece[0] for piece in pieces)
    ins, refs = refs[:count], refs[count:]
    if with_row:
        row_in, refs = refs[0], refs[1:]
    side_work, side_in, side_out = side
    side_ins, refs = refs[:side_in], refs[side_in:]
    results = 5 if halved else 1
    out_refs, refs = refs[:results], refs[results:]
    if with_row:
        row_out, refs = refs[0], refs[1:]
    side_outs, refs = refs[:side_out], refs[side_out:]
    (acc, other, far_low, far_high, near_left, near_right) = refs[:6]
    (pair_low, pair_high, pair_left, pair_right, last) = refs[6:11]
    (local_sem, cross_send, cross_recv, send_sem, recv_sem) = refs[11:16]
    x, p1, p2, core = coordinates()
    across, right1, left1, right2, left2, sibling = neighbours(x, p1, p2, core)
    greet_ctx(with_row or halved)
    p1p, p1m, p1o = (p1 + 1) % 4, (p1 + 3) % 4, (p1 + 2) % 4
    p2p, p2m, p2o = (p2 + 1) % 4, (p2 + 3) % 4, (p2 + 2) % 4
    needed = (p2o, p2m, p2p, p2)
    theirs = (p1o, p1m, p1p, p1)
    sender = Sender(send_sem, recv_sem)

    def part(ref, place, side, piece):
        if len(pieces) == 1:
            return ref.at[place, side]
        every = [pl.ds(0, size) for size in ref.shape[2:-1]]
        return ref.at[tuple([place, side] + every + [pl.ds(pieces[piece][3], pieces[piece][2])])]

    def source_of(piece, chosen, place, side):
        array, start, width, _ = pieces[piece]
        half = half_of(ins[array], chosen, side, place)
        if len(pieces) == 1:
            return half
        every = [pl.ds(0, size) for size in half.shape[:-1]]
        return half.at[tuple(every + [pl.ds(start, width)])]

    def crossing(k, side, piece, source):
        return pltpu.make_async_remote_copy(
            src_ref=source,
            dst_ref=part(other, theirs[k], side, piece),
            send_sem=cross_send.at[2 * k + side, piece],
            recv_sem=cross_recv.at[2 * k + side, piece],
            device_id=ctx_device(sibling),
            device_id_type=MESH,
        )

    order = ((0, 0), (0, 1), (1, 0), (2, 1), (2, 0), (1, 1), (3, 0), (3, 1))
    for chosen in range(2):

        @pl.when(core == chosen)
        def _(chosen=chosen):
            for k, side in order:
                for piece in range(len(pieces)):
                    crossing(k, side, piece, source_of(piece, 1 - chosen, theirs[k], side)).start()
                    pltpu.make_async_copy(
                        source_of(piece, chosen, needed[k], side),
                        part(acc, needed[k], side, piece),
                        local_sem.at[2 * k + side, piece],
                    ).start()

    if with_row:
        row_sender = Sender(refs[20], refs[21])
        row = RowScatter(row_in, refs[16], refs[17], refs[18], refs[19], row_sender)

    def send(source, place, to):
        return sender(source, place, ctx_device(to))

    def add(place, term):
        @pl.loop(0, 4)
        def _(step):
            place[step] = place[step] + term[step]

    def total(side, q1):
        value = acc[p2, side, q1].astype(jnp.float32)
        value = value + near_left[side, q1].astype(jnp.float32)
        value = value + near_right[side, q1].astype(jnp.float32)
        acc[p2, side, q1] = value.astype(acc.dtype)

    def merge(k, side):
        for piece in range(len(pieces)):
            mine = part(acc, needed[k], side, piece)
            pltpu.make_async_copy(mine, mine, local_sem.at[2 * k + side, piece]).wait()
            crossing(k, side, piece, part(other, theirs[k], side, piece)).wait_recv()
        add(acc.at[needed[k], side], other.at[needed[k], side])

    merge(0, 0)
    got_low = send(acc.at[p2o, 0], far_low, right2)
    merge(0, 1)
    got_high = send(acc.at[p2o, 1], far_high, left2)
    merge(1, 0)
    right_low = send(acc.at[p2m, 0], near_right.at[0], left2)
    merge(2, 1)
    left_high = send(acc.at[p2p, 1], near_left.at[1], right2)
    side_work(side_ins, side_outs)
    merge(2, 0)
    merge(1, 1)
    turns = (p1o, p1m, p1p, p1)
    got_low.wait_recv()
    add(acc.at[p2p, 0], far_low)
    left_low = [send(acc.at[p2p, 0, q1], near_left.at[0, q1], right2) for q1 in turns]
    got_high.wait_recv()
    add(acc.at[p2m, 1], far_high)
    right_high = [send(acc.at[p2m, 1, q1], near_right.at[1, q1], left2) for q1 in turns]
    merge(3, 0)
    merge(3, 1)
    if with_row:
        row.forward()
    right_low.wait_recv()
    left_high.wait_recv()
    left_low[0].wait_recv()
    total(0, p1o)
    got_low = send(acc.at[p2, 0, p1o], pair_low, right1)
    right_high[0].wait_recv()
    total(1, p1o)
    got_high = send(acc.at[p2, 1, p1o], pair_high, left1)
    left_low[1].wait_recv()
    total(0, p1m)
    near_low = send(acc.at[p2, 0, p1m], pair_right.at[0], left1)
    right_high[1].wait_recv()
    total(1, p1m)
    right_high[2].wait_recv()
    total(1, p1p)
    near_high = send(acc.at[p2, 1, p1p], pair_left.at[1], right1)
    left_low[2].wait_recv()
    total(0, p1p)
    got_low.wait_recv()
    acc[p2, 0, p1p] = acc[p2, 0, p1p] + pair_low[...]
    pair_first = send(acc.at[p2, 0, p1p], pair_left.at[0], right1)
    got_high.wait_recv()
    acc[p2, 1, p1m] = acc[p2, 1, p1m] + pair_high[...]
    pair_second = send(acc.at[p2, 1, p1m], pair_right.at[1], left1)
    left_low[3].wait_recv()
    total(0, p1)
    right_high[3].wait_recv()
    total(1, p1)
    if with_row:
        row.finish(row_out)
    near_low.wait_recv()
    near_high.wait_recv()
    pair_first.wait_recv()
    pair_second.wait_recv()

    @pl.loop(0, 2)
    def _(j):
        total = acc[p2, j, p1].astype(jnp.float32) + pair_left[j].astype(jnp.float32)
        total = total + pair_right[j].astype(jnp.float32)
        acc[p2, j, p1] = total.astype(acc.dtype)

    if halved:
        finish_row(halved, acc, p1, p2, refs[16:20], last, sender, out_refs)
    else:
        final = send(acc.at[p2, 1 - x, p1], last, across)
        final.wait_recv()
        total = acc[p2, x, p1].astype(jnp.float32) + last[...].astype(jnp.float32)
        out_refs[0][...] = total
    for k, side in order:
        for piece in range(len(pieces)):
            crossing(k, side, piece, part(other, theirs[k], side, piece)).wait_send()
    sender.finish()
    if with_row:
        row_sender.finish()


def finish_row(halved, acc, p1, p2, buffers, last, sender, out_refs):
    in_ref, out_ref, gu_ref, down_ref, spare_ref = out_refs
    far, from_left, from_right, stage = buffers
    here = row_place()
    left, right, opposite = (here + 3) % 4, (here + 1) % 4, (here + 2) % 4
    x = here % 2
    every = pl.ds(0, ROWS)
    rest = pl.ds(2 * halved, acc.shape[-1] - 2 * halved)

    def columns(owner):
        return pl.ds(pl.multiple_of((owner // 2) * halved, 128), halved)

    def block(owner):
        return acc.at[p2, owner % 2, p1, every, columns(owner)]

    def keep_part(side, value):
        value = value.astype(jnp.float32)[: ROWS - 1]
        span = pl.ds(pl.multiple_of(side * FF_QUARTER, 128), FF_QUARTER)
        gu_ref[:, 0, span] = value[:, :FF_QUARTER]
        gu_ref[:, 1, span] = value[:, FF_QUARTER : 2 * FF_QUARTER]
        down_ref[:, span] = value[:, 2 * FF_QUARTER :]

    far_copy = sender(block(opposite), far, row_device(right))
    from_right_copy = sender(block(left), from_right, row_device(left))
    x_neighbour = row_device((here // 2) * 2 + 1 - x)
    parts_copy = sender(acc.at[p2, 1 - x, p1, every, rest], last, x_neighbour)
    far_copy.wait_recv()
    stage[...] = acc[p2, right % 2, p1, :, columns(right)] + far[...]
    from_left_copy = sender(stage, from_left, row_device(right))
    keep_part(x, acc[p2, x, p1, :, rest])
    parts_copy.wait_recv()
    keep_part(1 - x, last[...])
    from_right_copy.wait_recv()
    from_left_copy.wait_recv()
    total = acc[p2, x, p1, :, columns(here)].astype(jnp.float32)
    total = total + from_left[...].astype(jnp.float32)
    total = total + from_right[...].astype(jnp.float32)
    in_ref[...] = total[: ROWS - 1, :IN_HALF]
    out_ref[...] = total[: ROWS - 1, IN_PAD : IN_PAD + OUT_HALF]
    spare_ref[...] = total[ROWS - 1 :, :128]


def scatter_blocks(arrays, pieces, halved, row_blocks, side, collective_id):
    rows = arrays[0].shape[-2]
    columns = sum(piece[2] for piece in pieces)
    kind = arrays[0].dtype
    block = (rows, columns)
    with_row = row_blocks is not None
    operands = list(arrays)
    in_specs = [pl.BlockSpec(memory_space=pl.ANY)] * len(arrays)
    results = [block]
    last = block
    scratch = []
    if halved:
        last = (rows, columns - 2 * halved)
        results = [
            (rows - 1, IN_HALF),
            (rows - 1, OUT_HALF),
            (rows - 1, 2, FF_HALF),
            (rows - 1, FF_HALF),
            (1, 128),
        ]
        scratch = [pltpu.VMEM((rows, halved), kind)] * 4
    shapes = [jax.ShapeDtypeStruct(shape, jnp.float32) for shape in results]
    if with_row:
        operands.append(row_blocks)
        in_specs.append(pl.BlockSpec(memory_space=pltpu.VMEM))
        shapes.append(jax.ShapeDtypeStruct(row_blocks.shape[1:], jnp.float32))
        scratch = row_scratch(*row_blocks.shape[1:])
    side_work, side_operands, side_shapes = side
    operands += list(side_operands)
    in_specs += [pl.BlockSpec(memory_space=pltpu.VMEM)] * len(side_operands)
    shapes += list(side_shapes)
    side = (side_work, len(side_operands), len(side_shapes))
    return pl.pallas_call(
        lambda *refs: scatter_kernel(pieces, halved, with_row, side, *refs),
        out_shape=tuple(shapes),
        in_specs=in_specs,
        out_specs=(pl.BlockSpec(memory_space=pltpu.VMEM),) * len(shapes),
        scratch_shapes=[
            pltpu.VMEM((4, 2, 4) + block, kind),
            pltpu.VMEM((4, 2, 4) + block, kind),
            pltpu.VMEM((4,) + block, kind),
            pltpu.VMEM((4,) + block, kind),
            pltpu.VMEM((2, 4) + block, kind),
            pltpu.VMEM((2, 4) + block, kind),
            pltpu.VMEM(block, kind),
            pltpu.VMEM(block, kind),
            pltpu.VMEM((2,) + block, kind),
            pltpu.VMEM((2,) + block, kind),
            pltpu.VMEM(last, kind),
            pltpu.SemaphoreType.DMA((8, len(pieces))),
            pltpu.SemaphoreType.DMA((8, len(pieces))),
            pltpu.SemaphoreType.DMA((8, len(pieces))),
            pltpu.SemaphoreType.DMA((24,)),
            pltpu.SemaphoreType.DMA((24,)),
        ]
        + scratch,
        compiler_params=pltpu.CompilerParams(
            collective_id=collective_id, has_side_effects=True, vmem_limit_bytes=VMEM_LIMIT
        ),
    )(*operands)


def weight_grad_work(ins, outs):
    @pl.loop(0, PADDED // 256)
    def _(step):
        span = pl.ds(pl.multiple_of(step * 256, 256), 256)
        outs[0][span, :] = dot(ins[0][:, span], ins[1][...], FIRST).astype(jnp.bfloat16)


LAST = (((1,), (1,)), ((), ()))
FIRST = (((0,), (0,)), ((), ()))
PLAIN = (((1,), (0,)), ((), ()))


def dot(a, b, dims=PLAIN):
    return lax.dot_general(a, b, dims, preferred_element_type=jnp.float32)


def feed_forward_kernel(
    n_ref,
    c_ref,
    w_ref,
    dn_ref,
    part_ref,
    grad_gu_ref,
    grad_down_ref,
    normed,
    partial,
    hidden,
    gate_up_grad,
    far,
    near_left,
    near_right,
    stage,
    send_sem,
    recv_sem,
):
    row_kernel_entry()
    gu_ref = w_ref.at[:, pl.ds(0, 2 * FF_QUARTER)]
    down_ref = w_ref.at[:, pl.ds(2 * FF_QUARTER, FF_QUARTER)]
    here = row_place()
    left, right, opposite = (here + 3) % 4, (here + 1) % 4, (here + 2) % 4
    to_left, to_right = row_device(left), row_device(right)

    def rows(owner, start=0, size=128):
        return pl.ds(pl.multiple_of(owner * 128 + start, 64), size)

    def copy(number, source, place, device):
        return pltpu.make_async_remote_copy(
            src_ref=source,
            dst_ref=place,
            send_sem=send_sem.at[number],
            recv_sem=recv_sem.at[number],
            device_id=device,
            device_id_type=MESH,
        )

    mine = normed.at[rows(here)]
    low, high = pl.ds(0, 64), pl.ds(64, 64)
    normed_right = copy(0, n_ref, mine, to_right)
    normed_left = copy(1, n_ref, mine, to_left)
    place = normed.at[rows(left, 0, 64)]
    normed_far_low = copy(2, place, place, to_right)
    place = normed.at[rows(right, 64, 64)]
    normed_far_high = copy(3, place, place, to_left)
    far_low = copy(4, partial.at[rows(opposite, 0, 64)], far.at[0], to_right)
    far_high = copy(5, partial.at[rows(opposite, 64, 64)], far.at[1], to_left)
    near_low = copy(6, partial.at[rows(left, 0, 64)], near_right.at[low], to_left)
    near_high = copy(7, partial.at[rows(right, 64, 64)], near_left.at[high], to_right)
    sum_low = copy(8, stage.at[0], near_left.at[low], to_right)
    sum_high = copy(9, stage.at[1], near_right.at[high], to_left)
    normed_right.start()
    normed_left.start()
    normed[rows(here), :] = n_ref[...]

    @pl.loop(0, 4)
    def _(step):
        turn = jnp.where(step == 1, 3, jnp.where(step == 2, 1, jnp.where(step == 3, 2, 0)))
        owner = (here + turn) % 4

        @pl.when(step == 1)
        def _():
            normed_right.wait_recv()
            normed_far_low.start()

        @pl.when(step == 2)
        def _():
            normed_left.wait_recv()
            normed_far_high.start()

        @pl.when(step == 3)
        def _():
            normed_far_low.wait_recv()
            normed_far_high.wait_recv()

        gate_vals = dot(normed[rows(owner), :], gu_ref[...])
        hidden_grad = dot(c_ref[rows(owner), :], down_ref[...])
        gate = gate_vals[:, :FF_QUARTER]
        upper = gate_vals[:, FF_QUARTER:]
        sigma = jax.nn.sigmoid(gate)
        silu_vals = gate * sigma
        hidden[rows(owner), :] = (silu_vals * upper).astype(jnp.bfloat16)
        gate_grad = hidden_grad * upper * sigma * (1.0 + gate * (1.0 - sigma))
        upper_grad = hidden_grad * silu_vals
        both = jnp.concatenate([gate_grad, upper_grad], axis=1).astype(jnp.bfloat16)
        gate_up_grad[rows(owner), :] = both
        partial[rows(owner), :] = dot(both, gu_ref[...], LAST).astype(jnp.bfloat16)

        @pl.when(step == 1)
        def _():
            near_low.start()

        @pl.when(step == 2)
        def _():
            near_high.start()

        @pl.when(step == 3)
        def _():
            far_low.start()
            far_high.start()

    @pl.loop(0, 4)
    def _(owner):
        part_ref[rows(owner), :] = dot(hidden[rows(owner), :], down_ref[...], LAST).astype(
            jnp.bfloat16
        )

    far_low.wait_recv()
    stage[0] = partial[rows(right, 0, 64), :] + far[0]
    sum_low.start()
    far_high.wait_recv()
    stage[1] = partial[rows(left, 64, 64), :] + far[1]
    sum_high.start()

    @pl.loop(0, PADDED // 256)
    def _(step):
        span = pl.ds(pl.multiple_of(step * 256, 256), 256)
        grad_gu_ref[span, :] = dot(normed[:, span], gate_up_grad[...], FIRST).astype(jnp.bfloat16)
        grad_down_ref[span, :] = dot(c_ref[:, span], hidden[...], FIRST).astype(jnp.bfloat16)

    for arrived in (near_low, near_high, sum_low, sum_high):
        arrived.wait_recv()
    total = partial[rows(here), :].astype(jnp.float32) + near_left[...].astype(jnp.float32)
    dn_ref[...] = total + near_right[...].astype(jnp.float32)
    for sent in (normed_right, normed_left, normed_far_low, normed_far_high, far_low, far_high):
        sent.wait_send()
    for sent in (near_low, near_high, sum_low, sum_high):
        sent.wait_send()


def feed_forward(normed, cotangent, weights, collective_id):
    kind = jnp.bfloat16
    return pl.pallas_call(
        feed_forward_kernel,
        out_shape=(
            jax.ShapeDtypeStruct((128, PADDED), jnp.float32),
            jax.ShapeDtypeStruct((512, PADDED), kind),
            jax.ShapeDtypeStruct((PADDED, 2 * FF_QUARTER), kind),
            jax.ShapeDtypeStruct((PADDED, FF_QUARTER), kind),
        ),
        in_specs=[pl.BlockSpec(memory_space=pltpu.VMEM)] * 3,
        out_specs=(pl.BlockSpec(memory_space=pltpu.VMEM),) * 4,
        scratch_shapes=[
            pltpu.VMEM((512, PADDED), kind),
            pltpu.VMEM((512, PADDED), kind),
            pltpu.VMEM((512, FF_QUARTER), kind),
            pltpu.VMEM((512, 2 * FF_QUARTER), kind),
            pltpu.VMEM((2, 64, PADDED), kind),
            pltpu.VMEM((128, PADDED), kind),
            pltpu.VMEM((128, PADDED), kind),
            pltpu.VMEM((2, 64, PADDED), kind),
            pltpu.SemaphoreType.DMA((10,)),
            pltpu.SemaphoreType.DMA((10,)),
        ],
        compiler_params=pltpu.CompilerParams(
            collective_id=collective_id, has_side_effects=True, vmem_limit_bytes=VMEM_LIMIT
        ),
        cost_estimate=pl.CostEstimate(
            flops=7 * 10**9, bytes_accessed=10**7, transcendentals=4 * 10**5
        ),
    )(normed, cotangent, weights)


def load_tiles(table_ref, kv_hbm, kv, sems, tiles):
    @pl.loop(0, tiles)
    def _(tile):
        for j in range(8):
            block = tile * 8 + j
            pltpu.make_async_copy(
                kv_hbm.at[table_ref[block]],
                kv.at[pl.ds(pl.multiple_of(block * 64, 64), 64)],
                sems.at[tile],
            ).start()


def wait_tile(kv, sems, tile):
    part = kv.at[pl.ds(pl.multiple_of(tile * TILE, TILE), TILE)]
    pltpu.make_async_copy(part, part, sems.at[tile]).wait()


def visible_keys(tile, pair, first_row, rows):
    shape = (rows, TILE)
    row = first_row + lax.broadcasted_iota(jnp.int32, shape, 0)
    key = tile * TILE + lax.broadcasted_iota(jnp.int32, shape, 1)
    order = jnp.where(row < QROWS // 2, pair, 127 - pair) * 64 + row % 64
    return key <= order


def head_parts():
    for g in range(KEY_VALUE_HEADS):
        for half in range(2):
            for h in range(GROUP):
                rows = slice((half * GROUP + h) * 64, (half * GROUP + h) * 64 + 64)
                column = (GROUP * g + h) * HEAD_SIZE
                yield g, rows, slice(half * 64, half * 64 + 64), slice(column, column + 64)


def run_tiles(pair, step):
    low_tiles = (pair + 8) // 8
    high_tiles = (135 - pair) // 8

    @pl.loop(0, low_tiles - 1)
    def _(tile):
        step(tile, 0, QROWS, False)

    step(low_tiles - 1, 0, QROWS, True)

    @pl.loop(low_tiles, high_tiles - 1)
    def _(tile):
        step(tile, QROWS // 2, QROWS // 2, False)

    step(high_tiles - 1, QROWS // 2, QROWS // 2, True)


def lane_parts(value):
    return [value[:, k * 128 : k * 128 + 128] for k in range(TILE // 128)]


def load_halves(w_hbm, place, sems, start):
    width = place.shape[-1]
    copies = []
    for k in range(2):
        columns = pl.ds(k * (IN_PAD + OUT_PAD) + start, width)
        copies.append(
            pltpu.make_async_copy(w_hbm.at[pl.ds(0, PADDED), columns], place.at[k], sems.at[k])
        )
        copies[-1].start()
    return copies


def held_lanes():
    return lax.broadcasted_iota(jnp.int32, (128, PADDED), 1) % ROWS < ROWS - 1


def norm_scale(values):
    return lax.rsqrt(jnp.sum(values * values, axis=-1, keepdims=True) / WIDTH + EPSILON)


def attend_kernel(
    table_ref,
    pair_ref,
    q_ref,
    start_ref,
    gain_ref,
    kv_hbm,
    w_hbm,
    out_ref,
    top_ref,
    sum_ref,
    mixed_ref,
    resid_ref,
    normed_ref,
    kv,
    q,
    acc,
    weight,
    sems,
    w_sems,
):
    pair = pair_ref[0]
    high_tiles = (135 - pair) // 8
    loads = load_halves(w_hbm, weight, w_sems, IN_PAD)
    load_tiles(table_ref, kv_hbm, kv, sems, high_tiles)
    q[...] = jnp.zeros(q.shape, q.dtype)
    for g, rows, tokens, columns in head_parts():
        q[g, rows, 0:64] = q_ref[tokens, columns]
    acc[...] = jnp.zeros(acc.shape, jnp.float32)
    top_ref[...] = jnp.full(top_ref.shape, -1e30, jnp.float32)
    sum_ref[...] = jnp.zeros(sum_ref.shape, jnp.float32)

    def step(tile, first_row, rows, masked):
        wait_tile(kv, sems, tile)
        span = slice(first_row, first_row + rows)
        if masked:
            seen = visible_keys(tile, pair, first_row, rows)
        heads = range(KEY_VALUE_HEADS)
        keys = [
            kv[pl.ds(pl.multiple_of(tile * TILE, TILE), TILE), g * 128 : g * 128 + 128]
            for g in heads
        ]
        scores = [dot(q[g, span, :], keys[g], LAST) for g in heads]
        if masked:
            scores = [jnp.where(seen, score, -1e30) for score in scores]
        parts = [lane_parts(score) for score in scores]
        best = [
            jnp.maximum(jnp.maximum(p[0], p[1]), jnp.maximum(p[2], p[3])) for p in parts
        ]
        before = [top_ref[g, span, :] for g in heads]
        highest = [
            jnp.maximum(before[g], jnp.max(best[g], axis=1, keepdims=True)) for g in heads
        ]
        shrink = [jnp.exp(before[g] - highest[g]) for g in heads]
        parts = [[jnp.exp(part - highest[g]) for part in parts[g]] for g in heads]
        for g in heads:
            p = parts[g]
            top_ref[g, span, :] = highest[g]
            sum_ref[g, span, :] = sum_ref[g, span, :] * shrink[g] + ((p[0] + p[1]) + (p[2] + p[3]))
        mixed = [
            dot(jnp.concatenate([p.astype(jnp.bfloat16) for p in parts[g]], axis=1), keys[g])
            for g in heads
        ]
        for g in heads:
            acc[g, span, :] = acc[g, span, :] * shrink[g] + mixed[g]

    run_tiles(pair, step)
    for g in range(KEY_VALUE_HEADS):
        total = jnp.sum(sum_ref[g], axis=1, keepdims=True)
        sum_ref[g] = jnp.broadcast_to(total, sum_ref.shape[1:])
        acc[g] = acc[g] / sum_ref[g]
    for g, rows, tokens, columns in head_parts():
        out_ref[tokens, columns] = acc[g, rows, 64:128]
    mixed_ref[...] = jnp.zeros(mixed_ref.shape, mixed_ref.dtype)
    mixed_ref[:, :OUT_HALF] = out_ref[:, :OUT_HALF].astype(jnp.bfloat16)
    mixed_ref[:, OUT_PAD : OUT_PAD + OUT_HALF] = out_ref[:, OUT_HALF:].astype(jnp.bfloat16)
    for copy in loads:
        copy.wait()
    branch = dot(mixed_ref[:, :OUT_PAD], weight[0], LAST)
    branch = branch + dot(mixed_ref[:, OUT_PAD:], weight[1], LAST)
    resid = start_ref[...] + jnp.where(held_lanes(), branch, 0.0)
    resid_ref[...] = resid
    normed_ref[...] = (resid * norm_scale(resid) * gain_ref[1:2, :]).astype(jnp.bfloat16)


def attend(table, pair, q, start, gains, kv, weights):
    heads = (KEY_VALUE_HEADS, QROWS, 128)
    return pl.pallas_call(
        attend_kernel,
        out_shape=(
            jax.ShapeDtypeStruct((128, WIDTH), jnp.float32),
            jax.ShapeDtypeStruct(heads, jnp.float32),
            jax.ShapeDtypeStruct(heads, jnp.float32),
            jax.ShapeDtypeStruct((128, PADDED), jnp.bfloat16),
            jax.ShapeDtypeStruct((128, PADDED), jnp.float32),
            jax.ShapeDtypeStruct((128, PADDED), jnp.bfloat16),
        ),
        in_specs=[pl.BlockSpec(memory_space=pltpu.SMEM)] * 2
        + [pl.BlockSpec(memory_space=pltpu.VMEM)] * 3
        + [pl.BlockSpec(memory_space=pl.ANY)] * 2,
        out_specs=(pl.BlockSpec(memory_space=pltpu.VMEM),) * 6,
        scratch_shapes=[
            pltpu.VMEM((8192, 640), jnp.bfloat16),
            pltpu.VMEM(heads, jnp.bfloat16),
            pltpu.VMEM(heads, jnp.float32),
            pltpu.VMEM((2, PADDED, OUT_PAD), jnp.bfloat16),
            pltpu.SemaphoreType.DMA((16,)),
            pltpu.SemaphoreType.DMA((2,)),
        ],
        compiler_params=pltpu.CompilerParams(vmem_limit_bytes=VMEM_LIMIT),
        cost_estimate=pl.CostEstimate(
            flops=4 * 10**9, bytes_accessed=10**7, transcendentals=8 * 10**6
        ),
    )(table, pair, q, start, gains, kv, weights)


def attend_back_kernel(
    table_ref,
    pair_ref,
    q_ref,
    normed_grad_ref,
    resid_ref,
    upstream_ref,
    gain_ref,
    out_ref,
    top_ref,
    sum_ref,
    kv_hbm,
    w_hbm,
    dq_ref,
    dkv_hbm,
    resid_grad_ref,
    branch_grad_ref,
    gain_grad_ref,
    grad_ref,
    weight,
    w_sems,
    kv,
    dkv,
    q,
    gs,
    q_turned,
    g_turned,
    shift,
    acc,
    sems,
    out_sems,
):
    pair = pair_ref[0]
    high_tiles = (135 - pair) // 8
    loads = load_halves(w_hbm, weight, w_sems, IN_PAD)
    load_tiles(table_ref, kv_hbm, kv, sems, high_tiles)

    def store(tile):
        for j in range(8):
            block = tile * 8 + j
            pltpu.make_async_copy(
                dkv.at[pl.ds(pl.multiple_of(block * 64, 64), 64)],
                dkv_hbm.at[table_ref[block]],
                out_sems.at[tile],
            ).start()

    @pl.loop(high_tiles, 16)
    def _(tile):
        dkv[pl.ds(pl.multiple_of(tile * TILE, TILE), TILE), :] = jnp.zeros(
            (TILE, 640), jnp.bfloat16
        )
        store(tile)

    resid, normed_grad = resid_ref[...], normed_grad_ref[...]
    scale = norm_scale(resid)
    gain_grad_ref[...] = jnp.sum(normed_grad * resid * scale, axis=0, keepdims=True)
    resid_grad = upstream_ref[...] + norm_backward(resid, scale, normed_grad * gain_ref[1:2, :])
    resid_grad_ref[...] = resid_grad
    branch_grad = resid_grad.astype(jnp.bfloat16)
    branch_grad_ref[...] = branch_grad
    for copy in loads:
        copy.wait()
    for k in range(2):
        mixed_grad = dot(branch_grad, weight[k])
        grad_ref[:, k * OUT_HALF : (k + 1) * OUT_HALF] = mixed_grad[:, :OUT_HALF]
    q[...] = jnp.zeros(q.shape, q.dtype)
    gs[...] = jnp.zeros(gs.shape, gs.dtype)
    for g, rows, tokens, columns in head_parts():
        q[g, rows, 0:64] = q_ref[tokens, columns]
        grad = grad_ref[tokens, columns]
        total = sum_ref[g, rows, :]
        gs[g, rows, 64:128] = (grad / total[:, 0:64]).astype(jnp.bfloat16)
        delta = jnp.sum(grad * out_ref[tokens, columns], axis=1, keepdims=True)
        shift[g, rows, :] = delta / total
    for g in range(KEY_VALUE_HEADS):
        q_turned[g] = q[g].T
        g_turned[g] = gs[g].T
    acc[...] = jnp.zeros(acc.shape, jnp.float32)

    def step(tile, first_row, rows, masked):
        wait_tile(kv, sems, tile)
        span = slice(first_row, first_row + rows)
        part = pl.ds(pl.multiple_of(tile * TILE, TILE), TILE)
        if masked:
            seen = visible_keys(tile, pair, first_row, rows)
        heads = range(KEY_VALUE_HEADS)
        keys = [kv[part, g * 128 : g * 128 + 128] for g in heads]
        scores = [dot(q[g, span, :], keys[g], LAST) for g in heads]
        prob_grad = [dot(gs[g, span, :], keys[g], LAST) for g in heads]
        if masked:
            scores = [jnp.where(seen, score, -1e30) for score in scores]
        for g in heads:
            top, moved = top_ref[g, span, :], shift[g, span, :]
            probs = [jnp.exp(part_ - top) for part_ in lane_parts(scores[g])]
            grads = [
                (probs[k] * (part_ - moved)).astype(jnp.bfloat16)
                for k, part_ in enumerate(lane_parts(prob_grad[g]))
            ]
            score_grad = jnp.concatenate(grads, axis=1)
            probs_low = jnp.concatenate([prob.astype(jnp.bfloat16) for prob in probs], axis=1)
            both = dot(
                jnp.concatenate([q_turned[g, :, span], g_turned[g, :, span]], axis=1),
                jnp.concatenate([score_grad, probs_low], axis=0),
            )
            acc[g, span, :] = acc[g, span, :] + dot(score_grad, keys[g])
            dkv[part, g * 128 : g * 128 + 128] = both.astype(jnp.bfloat16).T
        store(tile)

    run_tiles(pair, step)
    for g, rows, tokens, columns in head_parts():
        dq_ref[tokens, columns] = acc[g, rows, 0:64]

    @pl.loop(0, 16)
    def _(tile):
        part = dkv.at[pl.ds(pl.multiple_of(tile * TILE, TILE), TILE)]
        pltpu.make_async_copy(part, part, out_sems.at[tile]).wait()


def attend_back(table, pair, q, normed_grad, resid, upstream, gains, out, top, total, kv, weights):
    heads = (KEY_VALUE_HEADS, QROWS, 128)
    turned = (KEY_VALUE_HEADS, 128, QROWS)
    return pl.pallas_call(
        attend_back_kernel,
        out_shape=(
            jax.ShapeDtypeStruct((128, WIDTH), jnp.float32),
            jax.ShapeDtypeStruct((128, 64, 640), jnp.bfloat16),
            jax.ShapeDtypeStruct((128, PADDED), jnp.float32),
            jax.ShapeDtypeStruct((128, PADDED), jnp.bfloat16),
            jax.ShapeDtypeStruct((1, PADDED), jnp.float32),
        ),
        in_specs=[pl.BlockSpec(memory_space=pltpu.SMEM)] * 2
        + [pl.BlockSpec(memory_space=pltpu.VMEM)] * 8
        + [pl.BlockSpec(memory_space=pl.ANY)] * 2,
        out_specs=(
            pl.BlockSpec(memory_space=pltpu.VMEM),
            pl.BlockSpec(memory_space=pl.ANY),
        )
        + (pl.BlockSpec(memory_space=pltpu.VMEM),) * 3,
        scratch_shapes=[
            pltpu.VMEM((128, WIDTH), jnp.float32),
            pltpu.VMEM((2, PADDED, OUT_PAD), jnp.bfloat16),
            pltpu.SemaphoreType.DMA((2,)),
            pltpu.VMEM((8192, 640), jnp.bfloat16),
            pltpu.VMEM((8192, 640), jnp.bfloat16),
            pltpu.VMEM(heads, jnp.bfloat16),
            pltpu.VMEM(heads, jnp.bfloat16),
            pltpu.VMEM(turned, jnp.bfloat16),
            pltpu.VMEM(turned, jnp.bfloat16),
            pltpu.VMEM(heads, jnp.float32),
            pltpu.VMEM(heads, jnp.float32),
            pltpu.SemaphoreType.DMA((16,)),
            pltpu.SemaphoreType.DMA((16,)),
        ],
        compiler_params=pltpu.CompilerParams(vmem_limit_bytes=VMEM_LIMIT),
        cost_estimate=pl.CostEstimate(
            flops=10**10, bytes_accessed=2 * 10**7, transcendentals=8 * 10**6
        ),
    )(table, pair, q, normed_grad, resid, upstream, gains, out, top, total, kv, weights)


def pad_columns(value, columns):
    return jnp.pad(value, ((0, 0), (0, columns - value.shape[1])))


def pad_halves(value, half, padded):
    return jnp.concatenate(
        [pad_columns(value[:, :half], padded), pad_columns(value[:, half:], padded)], axis=1
    )


def norm_backward(rows, scale, weighted):
    inner = jnp.sum(weighted * rows, axis=-1, keepdims=True)
    return scale * weighted - rows * scale**3 * inner / WIDTH


def rotate_tiles(values, cosine, sine):
    lane = lax.broadcasted_iota(jnp.int32, (128, 128), 1)
    turned = []
    for k in range(values.shape[1] // 128):
        part = values[:, k * 128 : k * 128 + 128]
        partner = jnp.where(lane % 64 < 32, pltpu.roll(part, 96, 1), pltpu.roll(part, 32, 1))
        turned.append(part * cosine + partner * sine)
    return jnp.concatenate(turned, axis=1)


def project_kernel(
    start_ref,
    spare_ref,
    cos_ref,
    sin_ref,
    w_hbm,
    n_ref,
    q_ref,
    kv_ref,
    gain_ref,
    weight,
    w_sems,
):
    loads = load_halves(w_hbm, weight, w_sems, 0)
    lane = lax.broadcasted_iota(jnp.int32, (ROWS, PADDED), 1)
    row = lax.broadcasted_iota(jnp.int32, (ROWS, PADDED), 0)
    spread = dot(spare_ref[...], jnp.where(lane % ROWS == row, 1.0, 0.0).astype(jnp.bfloat16))
    lane = lax.broadcasted_iota(jnp.int32, (128, PADDED), 1)
    slot = lax.broadcasted_iota(jnp.int32, (128, PADDED), 0)
    spread = jnp.where(lane // ROWS == slot % 64, spread, 0.0)
    gain_first = jnp.sum(spread[:64], axis=0, keepdims=True)
    gain_ref[0:1, :] = gain_first
    gain_ref[1:2, :] = jnp.sum(spread[64:], axis=0, keepdims=True)
    start = start_ref[...]
    normed = (start * norm_scale(start) * gain_first).astype(jnp.bfloat16)
    n_ref[...] = normed
    for copy in loads:
        copy.wait()
    natural = jnp.concatenate([dot(normed, weight[k])[:, :IN_HALF] for k in range(2)], axis=1)
    key_width = KEY_VALUE_HEADS * HEAD_SIZE
    turned = rotate_tiles(natural[:, : WIDTH + key_width], cos_ref[...], sin_ref[...])
    q_ref[...] = turned[:, :WIDTH].astype(jnp.bfloat16) * jnp.bfloat16(0.125)
    keys, values = turned[:, WIDTH:], natural[:, WIDTH + key_width :]
    pieces = []
    for g in range(KEY_VALUE_HEADS):
        span = slice(g * HEAD_SIZE, (g + 1) * HEAD_SIZE)
        pieces += [keys[:, span], values[:, span]]
    kv_ref[...] = jnp.concatenate(pieces, axis=1).astype(jnp.bfloat16)


def local_call(kernel, shapes, operands, weights, flops):
    return pl.pallas_call(
        kernel,
        out_shape=tuple(jax.ShapeDtypeStruct(shape, kind) for shape, kind in shapes),
        in_specs=[pl.BlockSpec(memory_space=pltpu.VMEM)] * len(operands)
        + [pl.BlockSpec(memory_space=pl.ANY)],
        scratch_shapes=[
            pltpu.VMEM((2, PADDED, IN_PAD), jnp.bfloat16),
            pltpu.SemaphoreType.DMA((2,)),
        ],
        compiler_params=pltpu.CompilerParams(vmem_limit_bytes=VMEM_LIMIT),
        cost_estimate=pl.CostEstimate(flops=flops, bytes_accessed=6 * 10**6, transcendentals=0),
    )(*operands, weights)


def project(start, spare, cosine, sine, weights):
    low, full = jnp.bfloat16, jnp.float32
    shapes = (
        ((128, PADDED), low),
        ((128, WIDTH), low),
        ((128, 2 * KEY_VALUE_HEADS * HEAD_SIZE), low),
        ((2, PADDED), full),
    )
    return local_call(project_kernel, shapes, (start, spare, cosine, sine), weights, 5 * 10**8)


def project_back_kernel(
    dq_ref,
    kv_ref,
    start_ref,
    gain_ref,
    gain_two_ref,
    resid_grad_ref,
    n_ref,
    cos_ref,
    sin_ref,
    resid_ref,
    ffn_ref,
    map_ref,
    w_hbm,
    grad_ref,
    layer_ref,
    input_ref,
    weight,
    w_sems,
):
    loads = load_halves(w_hbm, weight, w_sems, 0)
    row = lax.broadcasted_iota(jnp.int32, (WIDTH, PADDED), 0)
    select = jnp.where(row == map_ref[...], 1.0, 0.0).astype(jnp.bfloat16)
    layer = (resid_ref[...] + ffn_ref[...]).astype(jnp.bfloat16)
    layer_ref[...] = dot(select, layer, LAST).astype(jnp.bfloat16)
    key_width = KEY_VALUE_HEADS * HEAD_SIZE
    kv = kv_ref[...]
    keys = [kv[:, g * 128 : g * 128 + 64] for g in range(KEY_VALUE_HEADS)]
    values = [kv[:, g * 128 + 64 : g * 128 + 128] for g in range(KEY_VALUE_HEADS)]
    turned = rotate_tiles(
        jnp.concatenate([dq_ref[...] * 0.125] + keys, axis=1), cos_ref[...], -sin_ref[...]
    )
    natural = jnp.concatenate([turned] + values, axis=1).astype(jnp.bfloat16)
    blank = jnp.zeros((128, IN_PAD - IN_HALF), jnp.bfloat16)
    grads = jnp.concatenate([natural[:, :IN_HALF], blank, natural[:, IN_HALF:], blank], axis=1)
    for copy in loads:
        copy.wait()
    back = dot(grads[:, :IN_PAD], weight[0], LAST) + dot(grads[:, IN_PAD:], weight[1], LAST)
    start = start_ref[...]
    scale = norm_scale(start)
    gain_grad = jnp.sum(back * start * scale, axis=0, keepdims=True)
    through = norm_backward(start, scale, back * gain_ref[0:1, :])
    change = (resid_grad_ref[...] + through).astype(jnp.bfloat16)
    input_ref[...] = dot(select, change, LAST).astype(jnp.bfloat16)
    for k in range(PADDED // 256):
        span = slice(k * 256, k * 256 + 256)
        grad_ref[span, :] = dot(n_ref[:, span], grads, FIRST).astype(jnp.bfloat16)
    slot = lax.broadcasted_iota(jnp.int32, (64, PADDED), 0)
    lane = lax.broadcasted_iota(jnp.int32, (64, PADDED), 1)
    picks = jnp.where((lane // ROWS == slot) & (lane % ROWS < ROWS - 1), 1.0, 0.0)
    row = lax.broadcasted_iota(jnp.int32, (PADDED, 128), 0)
    column = lax.broadcasted_iota(jnp.int32, (PADDED, 128), 1)
    fold = jnp.where(row % ROWS == column, 1.0, 0.0).astype(jnp.bfloat16)
    row = lax.broadcasted_iota(jnp.int32, (PADDED, 64), 0)
    column = lax.broadcasted_iota(jnp.int32, (PADDED, 64), 1)
    place = jnp.where(row == column * ROWS + ROWS - 1, 1.0, 0.0).astype(jnp.bfloat16)
    for start_column, gain in ((0, gain_grad), (IN_PAD, gain_two_ref[...])):
        by_slot = dot((picks * gain).astype(jnp.bfloat16), fold).astype(jnp.bfloat16)
        span = slice(start_column, start_column + 128)
        grad_ref[:, span] = grad_ref[:, span] + dot(place, by_slot).astype(jnp.bfloat16)


def project_back(operands, weights):
    low = jnp.bfloat16
    shapes = (((PADDED, IN_COLS), low), ((WIDTH, 128), low), ((WIDTH, 128), low))
    return local_call(project_back_kernel, shapes, operands, weights, 10**9)


def store_kernel(*refs):
    count = len(refs) // 2
    for source, place in zip(refs[:count], refs[count:]):
        place[...] = source[...]


def store(arrays):
    return pl.pallas_call(
        store_kernel,
        out_shape=tuple(jax.ShapeDtypeStruct(array.shape, array.dtype) for array in arrays),
        compiler_params=pltpu.CompilerParams(vmem_limit_bytes=VMEM_LIMIT),
    )(*arrays)


def on_device(
    inputs,
    cotangent,
    positions,
    pair_index,
    input_projection,
    project_out,
    gate_up,
    down_weight,
    norm_gains,
):
    half = lax.axis_index("fsdp")
    pair = pair_index[0, 0]
    key_width = KEY_VALUE_HEADS * HEAD_SIZE
    select = (
        lax.broadcasted_iota(jnp.int32, (WIDTH, PADDED), 0) == jnp.asarray(COLUMN_MAP)[None, :]
    ).astype(jnp.bfloat16)

    spare = jnp.pad(norm_gains.T, ((0, 0), (0, 1)))
    own_in = jnp.concatenate([input_projection, pad_columns(spare, IN_HALF)], axis=0)
    own_in = own_in.at[15, ROWS].set(pair.astype(jnp.bfloat16))
    own_out = jnp.pad(project_out, ((0, 1), (0, OUT_PAD - OUT_HALF)))
    own_att = jnp.concatenate([pad_columns(own_in, IN_PAD), own_out], axis=1)
    parts = jnp.concatenate([gate_up, down_weight[:, None]], axis=1)
    parts = parts.reshape(15, 3, 2, FF_QUARTER).transpose(2, 0, 1, 3)
    parts = jnp.pad(parts.reshape(2, 15, 3 * FF_QUARTER), ((0, 0), (0, 1), (0, 0)))
    upstream = dot(cotangent[0], select)
    weight_att, weight_ffn, row_cotangent = gather_blocks(
        (own_att, parts, upstream.astype(jnp.bfloat16)), 0
    )
    weight_att = weight_att.reshape(PADDED, 2 * (IN_PAD + OUT_PAD))
    weight_ffn = weight_ffn.reshape(PADDED, 3 * FF_QUARTER)
    row_cotangent = row_cotangent.reshape(512, PADDED)
    blocks_att = weight_att.reshape(64, ROWS, 2 * (IN_PAD + OUT_PAD))
    spare_first = blocks_att[:, 15, : 2 * ROWS]
    spare_second = blocks_att[:, 15, IN_PAD + OUT_PAD : IN_PAD + OUT_PAD + 2 * ROWS]
    labels = jnp.where(half == 0, spare_first, spare_second)[:, ROWS].astype(jnp.int32)
    slots = jnp.arange(64, dtype=jnp.int32)
    blocks = jnp.stack([labels, 127 - labels], axis=1).reshape(128)
    places = jnp.stack([2 * slots, 2 * slots + 1], axis=1).reshape(128)
    hits = blocks[None, :] == jnp.arange(128, dtype=jnp.int32)[:, None]
    table = jnp.sum(jnp.where(hits, places[None, :], 0), axis=1)

    start = dot(inputs[0], select)
    freqs = jnp.exp(
        -math.log(10000.0) * jnp.arange(HEAD_SIZE // 2, dtype=jnp.float32) * 2.0 / HEAD_SIZE
    )
    angle = positions[0].astype(jnp.float32)[:, None] * freqs[None, :]
    cosine = jnp.tile(jnp.cos(angle), (1, 4))
    sine = jnp.sin(angle)
    sine = jnp.tile(jnp.concatenate([-sine, sine], axis=1), (1, 2))
    spare = jnp.concatenate([spare_first[:, :ROWS], spare_second[:, :ROWS]], axis=0)
    normed_low, query_scaled, key_value, gains = project(
        start, spare, cosine, sine, weight_att
    )
    all_kv = gather_blocks((key_value,), 1)[0].reshape(128, 64, 2 * key_width)
    pair_one = pair.reshape(1)
    attention, top, total, mixed_low, resid, normed_two = attend(
        table, pair_one, query_scaled, start, gains, all_kv, weight_att
    )
    normed_two_grad, ffn_out, grad_gu, grad_down = feed_forward(
        normed_two, row_cotangent, weight_ffn, 2
    )
    query_grad, all_kv_grad, resid_grad, branch_grad_low, gain_two_grad = attend_back(
        table,
        pair_one,
        query_scaled,
        normed_two_grad,
        resid,
        upstream,
        gains,
        attention,
        top,
        total,
        all_kv,
        weight_att,
    )
    kv_grad, ffn_out, grad_out = scatter_blocks(
        (all_kv_grad.reshape(2, 4, 4, 2, 128, 2 * key_width),),
        ((0, 0, 2 * key_width, 0),),
        None,
        ffn_out.reshape(4, 128, PADDED),
        (
            weight_grad_work,
            (branch_grad_low, mixed_low),
            (jax.ShapeDtypeStruct((PADDED, 2 * OUT_PAD), jnp.bfloat16),),
        ),
        3,
    )
    grad_in, layer_out, input_grad = project_back(
        (
            query_grad,
            kv_grad,
            start,
            gains,
            gain_two_grad,
            resid_grad,
            normed_low,
            cosine,
            sine,
            resid,
            ffn_out,
            jnp.asarray(COLUMN_MAP)[None, :],
        ),
        weight_att,
    )
    own_cols = IN_PAD + OUT_PAD
    sums = scatter_blocks(
        tuple(
            grad.reshape(2, 4, 4, 2, ROWS, grad.shape[1])
            for grad in (grad_in, grad_out, grad_gu, grad_down)
        ),
        (
            (0, 0, IN_PAD, 0),
            (0, IN_PAD, IN_PAD, own_cols),
            (1, 0, OUT_PAD, IN_PAD),
            (1, OUT_PAD, OUT_PAD, own_cols + IN_PAD),
            (2, 0, 2 * FF_QUARTER, 2 * own_cols),
            (3, 0, FF_QUARTER, 2 * own_cols + 2 * FF_QUARTER),
        ),
        own_cols,
        None,
        (lambda ins, outs: None, (), ()),
        4,
    )
    sum_in, sum_out, sum_gu, sum_down, spare = store(sums)
    return (
        layer_out.T[None],
        input_grad.T[None],
        sum_in,
        sum_out,
        sum_gu,
        sum_down,
        spare[0, :15].reshape(15, 1),
    )


def solution(mesh):
    in_specs = (
        P("fsdp", "ctx", None),
        P("fsdp", "ctx", None),
        P("fsdp", "ctx"),
        P("fsdp", "ctx"),
        P("ctx", "fsdp"),
        P("ctx", "fsdp"),
        P("ctx", None, "fsdp"),
        P("ctx", "fsdp"),
        P("ctx", "fsdp"),
    )
    out_specs = (
        P("fsdp", "ctx", None),
        P("fsdp", "ctx", None),
        P("ctx", "fsdp"),
        P("ctx", "fsdp"),
        P("ctx", None, "fsdp"),
        P("ctx", "fsdp"),
        P("ctx", "fsdp"),
    )
    return jax.shard_map(
        on_device, mesh=mesh, in_specs=in_specs, out_specs=out_specs, check_vma=False
    )
```
